32 devices in a mesh: dp: 8 (over y, x, core), tensor: 4 (over z).
Axes of the slice: x: 2, y: 2, z: 4, core: 2. Of those that a mesh axis runs over, the one named last changes fastest.
Arguments:
- hidden_in: bfloat16 [6144, 2048], P('dp'), may hold values from -6 to 6
- segment_ids: int32 [6144], P('dp'), may hold values from 0 to 63, never falling along the last dimension, each value on 1 to 384 neighbouring positions
- modality: int32 [6144], P('dp'), may hold values from 0 to 1
- norm_gain: float32 [2048], replicated, may hold values from 0.5 to 1.5
- in_proj: bfloat16 [2, 2048, 2, 4096], P(None, None, None, 'tensor'), may hold values from -0.125 to 0.125
- conv_weight: float32 [4, 4096], P(None, 'tensor'), may hold values from -0.8 to 0.8
- conv_bias: float32 [4096], P('tensor'), may hold values from -1 to 1
- x_proj: bfloat16 [2, 4096, 160], P(None, 'tensor'), may hold values from -0.1875 to 0.1875
- dt_proj: bfloat16 [2, 128, 4096], P(None, None, 'tensor'), may hold values from -0.5 to 0.5
- dt_bias: float32 [2, 4096], P(None, 'tensor'), may hold values from -5 to -1
- a_log: float32 [16, 4096], P(None, 'tensor'), may hold values from -2 to 2.5
- skip_gain: float32 [4096], P('tensor'), may hold values from 0.5 to 1.5
- out_proj: bfloat16 [2, 4096, 2048], P(None, 'tensor'), may hold values from -0.1875 to 0.1875
- out_grad: bfloat16 [6144, 2048], P('dp'), may hold values from -6 to 6
Outputs:
- output: bfloat16 [6144, 2048], P('dp')
- input_grad: bfloat16 [6144, 2048], P('dp')
- norm_gain_grad: float32 [2048], replicated
- in_proj_grad: float32 [2, 2048, 2, 4096], P(None, None, None, 'tensor')
- conv_weight_grad: float32 [4, 4096], P(None, 'tensor')
- conv_bias_grad: float32 [4096], P('tensor')
- x_proj_grad: float32 [2, 4096, 160], P(None, 'tensor')
- dt_proj_grad: float32 [2, 128, 4096], P(None, None, 'tensor')
- dt_bias_grad: float32 [2, 4096], P(None, 'tensor')
- a_log_grad: float32 [16, 4096], P(None, 'tensor')
- skip_grad: float32 [4096], P('tensor')
- out_proj_grad: float32 [2, 4096, 2048], P(None, 'tensor')
The draws below stay inside these ranges and needn't reach their ends.
Inputs may be any that keep to these rules, and one draw needn't show every extreme that they name: `segment_ids`: segment ids never fall along the tokens; a segment holds 1 to 384 tokens and one holds exactly that many.
All inputs are finite; a program needn't handle non-finite values.
Results may differ from the reference program's by a relative error of at most 0.011.
Values may be sent and summed in bfloat16 or wider, within the bound.
A program may use at most 320 MiB of HBM per device.

```python
import math
import jax
import jax.numpy as jnp
import numpy as np
from jax import lax

D = 2048
INNER = 4096
NSTATE = 16
KCONV = 4
DT_RANK = 128
MODES = 2
TOK_DEV = 768
TOKENS = 6144
PROJ_OUT = 160
N_DP = 8


def touch_ends(drawn, own_key, least, top_value):
    shape = drawn.shape
    spot = [jax.random.randint(jax.random.fold_in(own_key, axis), (), 0, shape[axis]) for axis in range(len(shape))]
    drawn = drawn.at[tuple(spot)].set(least)
    longest = shape.index(max(shape))
    spot[longest] = (spot[longest] + 1) % shape[longest]
    return drawn.at[tuple(spot)].set(top_value)


def raised(entries, key, source, target, shards_of, factor):
    def block_of(position):
        return (jnp.arange(entries.shape[position]) // (entries.shape[position] // shards_of)).reshape((-1,) + (1,) * (entries.ndim - 1 - position))

    one_side = jax.random.permutation(key, shards_of)[block_of(target)]
    second = (block_of(target) + shards_of // 2) % shards_of
    return jnp.where((block_of(source) == one_side) | (block_of(source) == second), factor * entries, entries)


def level_of(key, dims, pieces, low, top_value):
    factor_of = 1.0
    for axis_at, shards_of in pieces:
        heights = jax.random.uniform(jax.random.fold_in(jax.random.fold_in(key, 6), axis_at), (shards_of,), jnp.float32, low / len(pieces), top_value / len(pieces))
        factor_of = factor_of * jnp.repeat(jnp.exp(heights), dims[axis_at] // shards_of).reshape((-1,) + (1,) * (len(dims) - 1 - axis_at))
    return factor_of


def length_profile(amount, total, reach, slope):
    loads = [(1 << 20) // math.isqrt(rank ** slope) + 1 for rank in range(2, amount + 1)]
    rest, holding = total - reach - (amount - 1), [1] * (amount - 1)
    while rest > 0:
        movable = [i for i in range(amount - 1) if holding[i] < reach]
        pool, budget = sum([loads[i] for i in movable]), rest
        for i in movable:
            addition = min(reach - holding[i], max(1, budget * loads[i] // pool), rest)
            holding[i] = holding[i] + addition
            rest = rest - addition
    return np.array([reach] + holding)


def uneven_parts(key, amount, total, reach, lean):
    if amount == 2:
        one = jax.random.randint(key, (), max(1, total - reach), min(reach, total - 1) + 1)
        return jnp.stack([one, total - one])
    lengths = jnp.asarray(length_profile(amount, total, reach, lean), jnp.int32)
    couples = (amount - 1) // 2
    donor, taker = lengths[1:1 + 2 * couples:2], lengths[2:2 + 2 * couples:2]
    slack = jnp.minimum(donor - 1, reach - taker)
    moved = jax.random.randint(jax.random.fold_in(key, 1), (couples,), 0, 1 << 20) % (slack + 1)
    lengths = lengths.at[1:1 + 2 * couples:2].set(donor - moved).at[2:2 + 2 * couples:2].set(taker + moved)
    return lengths[jax.random.permutation(jax.random.fold_in(key, 2), amount)]


def normal_values(stream_key, shape, deviation, reach, split=(), dtype=jnp.bfloat16):
    result = jax.random.normal(stream_key, shape, jnp.float32) * deviation
    if len(split) > 0:
        result = level_of(stream_key, shape, split, -0.22, 0.18) * result
    return jnp.clip(result, min=-reach, max=reach).astype(dtype)


def heavy_noise(key, extent, width, reach, pieces, heavy, dtype=jnp.bfloat16):
    entries = width * jax.random.normal(key, extent, jnp.float32)
    if pieces:
        entries = entries * level_of(key, extent, pieces, -0.22, 0.18)
    return jnp.clip(raised(entries, jax.random.fold_in(key, 3), *heavy), -reach, reach).astype(dtype)


def setup_inputs(seed: int = 0) -> dict:
    seeds = jax.random.split(jax.random.key(seed), 15)
    return {
        "hidden_in": normal_values(seeds[0], (TOKENS, D), 1.0, 6.0, ((0, 8),)),
        "segment_ids": jnp.searchsorted(jnp.cumsum(uneven_parts(seeds[1], 8 * N_DP, TOKENS, TOK_DEV // 2, 1)), jnp.arange(TOKENS), side="right").astype(jnp.int32),
        "modality": touch_ends(jax.random.randint(seeds[2], (TOKENS,), 0, 2), jax.random.fold_in(seeds[2], 1), 0, 1).astype(jnp.int32),
        "norm_gain": jnp.clip(1.0 + 0.1 * jax.random.normal(seeds[3], (D,), jnp.float32), 0.5, 1.5),
        "in_proj": normal_values(seeds[4], (MODES, D, 2, INNER), D ** -0.5, 0.125, ((3, 4),)),
        "conv_weight": jnp.clip(jax.random.uniform(seeds[5], (KCONV, INNER), jnp.float32, -0.8, 0.8) * level_of(seeds[5], (KCONV, INNER), ((1, 4),), -0.4, 0.0), -0.8, 0.8),
        "conv_bias": jnp.clip(jax.random.uniform(seeds[6], (INNER,), jnp.float32, -1.0, 1.0) * level_of(seeds[6], (INNER,), ((0, 4),), -0.4, 0.0), -1.0, 1.0),
        "x_proj": normal_values(seeds[7], (MODES, INNER, PROJ_OUT), (INNER // 4) ** -0.5, 0.1875, ((1, 4),)),
        "dt_proj": normal_values(seeds[8], (MODES, DT_RANK, INNER), DT_RANK ** -0.5, 0.5, ((2, 4),)),
        "dt_bias": jnp.clip(-5.0 + 4.0 * jax.random.uniform(seeds[9], (MODES, INNER), jnp.float32) ** level_of(seeds[9], (MODES, INNER), ((1, 4),), -0.2, 0.2), -5.0, -1.0),
        "a_log": jnp.clip(-2.0 + 4.5 * jax.random.uniform(seeds[10], (NSTATE, INNER), jnp.float32) ** level_of(seeds[10], (NSTATE, INNER), ((1, 4),), -0.2, 0.2), -2.0, 2.5),
        "skip_gain": jnp.clip(0.5 + 1.0 * jax.random.uniform(seeds[11], (INNER,), jnp.float32) ** level_of(seeds[11], (INNER,), ((0, 4),), -0.2, 0.2), 0.5, 1.5),
        "out_proj": normal_values(seeds[12], (MODES, INNER, D), (INNER // 4) ** -0.5, 0.1875, ((1, 4),)),
        "out_grad": heavy_noise(seeds[13], (TOKENS, D), 1.0, 6.0, ((0, 8),), (0, 1, 8, 2.0)),
    }


@jax.custom_vjp
def low(v):
    return lax.optimization_barrier(v.astype(jnp.bfloat16)).astype(jnp.float32)

@jax.custom_vjp
def low_back(v):
    return v

def low_keep(v):
    return (low(v), None)

def low_pass(kept, grad):
    return (grad,)

def back_keep(v):
    return (v, None)

def back_low(kept, grad):
    return (low(grad),)
low.defvjp(low_keep, low_pass)
low_back.defvjp(back_keep, back_low)
EPS = 1e-05
HIGH = lax.Precision.HIGHEST

def pick_dot(left_side, weights, first_mode):
    first_part = jnp.dot(left_side, weights[0], precision=HIGH)
    second_part = jnp.dot(left_side, weights[1], precision=HIGH)
    return jnp.where(first_mode, first_part, second_part)

def lagged(values, offset):
    padding = [(offset, 0)] + [(0, 0)] * (values.ndim - 1)
    return jnp.pad(values, padding)[:values.shape[0]]

def lagged_seg(segment, offset):
    return jnp.pad(segment, (offset, 0), constant_values=-1)[:segment.shape[0]]

def sequence_layer(params, hidden, segment, modal_ids):
    gain, in_w, conv_w, conv_b, xp_w, dt_w, dt_b, log_rate, skip, out_w = params
    first_mode = (modal_ids == 0)[:, None]
    mean_sq = lax.optimization_barrier(jnp.mean(hidden * hidden, axis=1, keepdims=True))
    normed = low(hidden * lax.rsqrt(mean_sq + EPS) * gain)
    both_parts = low_back(pick_dot(normed, in_w.reshape(2, D, 2 * INNER), first_mode))
    inner_x = both_parts[:, :INNER]
    gate_z = both_parts[:, INNER:]
    conv_sum = conv_b + conv_w[KCONV - 1] * inner_x
    for offset in range(1, KCONV):
        same_doc = (lagged_seg(segment, offset) == segment).astype(jnp.float32)[:, None]
        conv_sum = conv_sum + conv_w[KCONV - 1 - offset] * lagged(inner_x, offset) * same_doc
    activated = low(jax.nn.silu(conv_sum))
    projected = low_back(pick_dot(activated, xp_w, first_mode))
    rank_in = low(projected[:, :DT_RANK])
    b_coeff = projected[:, DT_RANK:DT_RANK + NSTATE]
    c_coeff = projected[:, DT_RANK + NSTATE:]
    step_pre = low_back(pick_dot(rank_in, dt_w, first_mode) + jnp.where(first_mode, dt_b[0], dt_b[1]))
    step_size = jax.nn.softplus(step_pre)
    decay = -jnp.exp(log_rate)
    keep_mask = (lagged_seg(segment, 1) == segment).astype(jnp.float32)

    def advance(state_now, inputs):
        step_t, act_t, b_t, c_t, keep_t = inputs
        state_now = jnp.exp(step_t[None, :] * decay) * keep_t * state_now + (step_t * act_t)[None, :] * b_t[:, None]
        return (state_now, jnp.dot(c_t, state_now, precision=HIGH))
    _, scanned = lax.scan(advance, jnp.zeros((NSTATE, INNER), jnp.float32), (step_size, activated, b_coeff, c_coeff, keep_mask))
    gated = low((scanned + skip * activated) * jax.nn.silu(gate_z))
    return hidden + pick_dot(gated, out_w, first_mode)

def reference(hidden_in, segment_ids, modality, norm_gain, in_proj, conv_weight, conv_bias, x_proj, dt_proj, dt_bias, a_log, skip_gain, out_proj, out_grad):
    params = (norm_gain, in_proj.astype(jnp.float32), conv_weight, conv_bias, x_proj.astype(jnp.float32), dt_proj.astype(jnp.float32), dt_bias, a_log, skip_gain, out_proj.astype(jnp.float32))

    def run_layer(hidden, weights):

        def visit_one(carried, item_now):
            return (carried, sequence_layer(weights, item_now[0], item_now[1], item_now[2]))
        _, results = lax.scan(jax.checkpoint(visit_one), jnp.zeros((), jnp.float32), (hidden.reshape(N_DP, TOK_DEV, D), segment_ids.reshape(N_DP, TOK_DEV), modality.reshape(N_DP, TOK_DEV)))
        return results.reshape(TOKENS, D)
    output, pullback = jax.vjp(run_layer, hidden_in.astype(jnp.float32), params)
    input_grad, grads = pullback(out_grad.astype(jnp.float32))
    return (output.astype(jnp.bfloat16), input_grad.astype(jnp.bfloat16), grads[0], grads[1], grads[2], grads[3], grads[4], grads[5], grads[6], grads[7], grads[8], grads[9])
```

```python
import functools

import jax
import jax.numpy as jnp
from jax import lax
from jax.experimental import pallas as pl
from jax.experimental.pallas import tpu as pltpu
from jax.sharding import PartitionSpec as P

EPS = 1e-05

LANES = 128
BIG = 1000.0
LOG2E = 1.4426950408889634


def softplus(v):
    return jnp.maximum(v, 0.0) + jnp.log1p(jnp.exp(-jnp.abs(v)))


def spread_rows(scratch, values, groups):
    rows = values.shape[0]
    for g in range(groups):
        scratch[pl.ds(g, rows, stride=groups), :] = values[:, g * LANES:(g + 1) * LANES]


def gather_rows(scratch, rows, groups):
    return jnp.concatenate(
        [scratch[pl.ds(g, rows, stride=groups), :] for g in range(groups)], axis=1)


def scan_forward_kernel(states, groups, rows, unroll,
                        bc_ref, pre_ref, act_ref, z_ref, gg_ref, keep_ref, alog_ref, skip_ref,
                        gated_ref, ggrad_ref, mixed_ref, h_ref, start_ref,
                        rate_scr, state_scr, sk_scr, u_scr, y_scr):
    chunk = pl.program_id(0)

    @pl.when(chunk == 0)
    def _():
        rate_scr[...] = jnp.exp(alog_ref[...]) * (-LOG2E)
        state_scr[...] = jnp.zeros_like(state_scr)

    step = softplus(pre_ref[...])
    act = act_ref[...].astype(jnp.float32)
    spread_rows(u_scr, step * act, groups)
    spread_rows(sk_scr, jnp.where(keep_ref[...] > 0.0, step, BIG), groups)
    start_ref[0] = state_scr[...]

    def one(t, held):
        at = pl.multiple_of(t * groups, groups)
        sk = sk_scr[pl.ds(at, groups), :]
        u = u_scr[pl.ds(at, groups), :]
        y = jnp.zeros_like(u)
        new = []
        for n in range(states):
            h = jnp.exp2(sk * rate_scr[n]) * held[n] + u * bc_ref[t, n]
            h_ref[t, n] = h
            y = y + h * bc_ref[t, states + n]
            new.append(h)
        y_scr[pl.ds(at, groups), :] = y
        return tuple(new)

    last = lax.fori_loop(0, rows, one, tuple(state_scr[n] for n in range(states)), unroll=unroll)
    for n in range(states):
        state_scr[n] = last[n]
    mixed_out = gather_rows(y_scr, rows, groups) + skip_ref[...] * act
    z = z_ref[...].astype(jnp.float32)
    gg = gg_ref[...].astype(jnp.float32)
    sig = jax.nn.sigmoid(z)
    silu = z * sig
    gated_ref[...] = (mixed_out * silu).astype(gated_ref.dtype)
    mixed_ref[...] = gg * silu
    ggrad_ref[...] = (gg * mixed_out * sig * (1.0 + z * (1.0 - sig))).astype(ggrad_ref.dtype)


def scan_forward(bc, pre, act, z, gg, keep, a_log3, skip, rows=64, unroll=4):
    tokens, channels = pre.shape
    groups = channels // LANES
    states = a_log3.shape[0]
    count = tokens // rows
    wide = pl.BlockSpec((rows, channels), lambda i: (i, 0))
    whole3 = pl.BlockSpec((states, groups, LANES), lambda i: (0, 0, 0))
    return pl.pallas_call(
        functools.partial(scan_forward_kernel, states, groups, rows, unroll),
        grid=(count,),
        in_specs=[
            pl.BlockSpec((rows, 2 * states), lambda i: (i, 0), memory_space=pltpu.SMEM),
            wide, wide, wide, wide,
            pl.BlockSpec((rows, 1), lambda i: (i, 0)),
            whole3,
            pl.BlockSpec((1, channels), lambda i: (0, 0)),
        ],
        out_specs=[
            wide, wide, wide,
            pl.BlockSpec((rows, states, groups, LANES), lambda i: (i, 0, 0, 0)),
            pl.BlockSpec((1, states, groups, LANES), lambda i: (i, 0, 0, 0)),
        ],
        out_shape=[
            jax.ShapeDtypeStruct((tokens, channels), jnp.bfloat16),
            jax.ShapeDtypeStruct((tokens, channels), jnp.bfloat16),
            jax.ShapeDtypeStruct((tokens, channels), jnp.float32),
            jax.ShapeDtypeStruct((tokens, states, groups, LANES), jnp.float32),
            jax.ShapeDtypeStruct((count, states, groups, LANES), jnp.float32),
        ],
        scratch_shapes=[
            pltpu.VMEM((states, groups, LANES), jnp.float32),
            pltpu.VMEM((states, groups, LANES), jnp.float32),
            pltpu.VMEM((rows * groups, LANES), jnp.float32),
            pltpu.VMEM((rows * groups, LANES), jnp.float32),
            pltpu.VMEM((rows * groups, LANES), jnp.float32),
        ],
        compiler_params=pltpu.CompilerParams(vmem_limit_bytes=48 * 1024 * 1024),
        name="scan_forward",
    )(bc, pre, act, z, gg, keep, a_log3, skip)


def scan_backward_kernel(states, groups, rows, unroll,
                         bc_ref, pre_ref, act_ref, mixed_ref, keep_ref, alog_ref, skip_ref, h_ref, start_ref,
                         pgrad_ref, apart_ref, bcg_ref, ratesum_ref, skipsum_ref,
                         rate_scr, decay_scr, carry_scr, sum_scr, sk_scr, u_scr, dy_scr, w_scr, s_scr, p_scr, q_scr):
    chunk = pl.program_id(0)
    count = pl.num_programs(0)

    @pl.when(chunk == 0)
    def _():
        decay = -jnp.exp(alog_ref[...])
        decay_scr[...] = decay
        rate_scr[...] = decay * LOG2E
        carry_scr[...] = jnp.zeros_like(carry_scr)
        sum_scr[...] = jnp.zeros_like(sum_scr)
        skipsum_ref[...] = jnp.zeros_like(skipsum_ref)

    step = softplus(pre_ref[...])
    act = act_ref[...].astype(jnp.float32)
    mixed = mixed_ref[...].astype(jnp.float32)
    spread_rows(u_scr, step * act, groups)
    spread_rows(dy_scr, mixed, groups)
    spread_rows(sk_scr, jnp.where(keep_ref[...] > 0.0, step, BIG), groups)
    skipsum_ref[...] += jnp.sum(mixed * act, axis=0, keepdims=True)

    def one(t, carried, before):
        at = pl.multiple_of(t * groups, groups)
        sk = sk_scr[pl.ds(at, groups), :]
        u = u_scr[pl.ds(at, groups), :]
        dy = dy_scr[pl.ds(at, groups), :]
        w = jnp.zeros_like(u)
        s = jnp.zeros_like(u)
        new, pb, pc = [], [], []
        for n in range(states):
            g = dy * bc_ref[t, states + n] + carried[n]
            pb.append(g * u)
            pc.append(dy * h_ref[t, n])
            w = w + g * bc_ref[t, n]
            fg = jnp.exp2(sk * rate_scr[n]) * g
            lg = fg * before(n)
            s = s + lg * decay_scr[n]
            sum_scr[n] += lg * sk
            new.append(fg)
        w_scr[pl.ds(at, groups), :] = w
        s_scr[pl.ds(at, groups), :] = s
        both = pb + pc
        batch = max(1, 16 // groups)
        for j in range(0, 2 * states, batch):
            p_scr[t, pl.ds(j * groups, batch * groups), :] = jnp.concatenate(
                both[j:j + batch], axis=0).astype(jnp.bfloat16)
        return tuple(new)

    def looped(i, carried):
        t = rows - 1 - i
        return one(t, carried, lambda n: h_ref[t - 1, n])

    last = lax.fori_loop(0, rows - 1, looped, tuple(carry_scr[n] for n in range(states)), unroll=unroll)
    last = one(0, last, lambda n: start_ref[0, n])
    for n in range(states):
        carry_scr[n] = last[n]

    ones = jnp.ones((16, LANES), jnp.bfloat16)

    def reduce_one(t, nothing):
        q = lax.dot_general(ones, p_scr[t], (((1,), (1,)), ((), ())), preferred_element_type=jnp.float32)
        q_scr[pl.ds(t, 1), :] = q[0:1]
        return nothing

    lax.fori_loop(0, rows, reduce_one, 0, unroll=4)
    pick = (lax.broadcasted_iota(jnp.int32, (2 * states * groups, 2 * states), 0) // groups
            == lax.broadcasted_iota(jnp.int32, (2 * states * groups, 2 * states), 1)).astype(jnp.float32).astype(jnp.bfloat16)
    q = q_scr[...]
    high = q.astype(jnp.bfloat16)
    low = (q - high.astype(jnp.float32)).astype(jnp.bfloat16)
    bcg_ref[...] = (jnp.dot(high, pick, preferred_element_type=jnp.float32)
                    + jnp.dot(low, pick, preferred_element_type=jnp.float32))
    w = gather_rows(w_scr, rows, groups)
    s = gather_rows(s_scr, rows, groups)
    pgrad_ref[...] = ((act * w + s) * jax.nn.sigmoid(pre_ref[...])).astype(pgrad_ref.dtype)
    apart_ref[...] = mixed * skip_ref[...] + step * w

    @pl.when(chunk == count - 1)
    def _():
        ratesum_ref[...] = sum_scr[...] * decay_scr[...]


def scan_backward(bc, pre, act, mixed, keep, a_log3, skip, h, starts, rows=64, unroll=3):
    tokens, channels = pre.shape
    groups = channels // LANES
    states = a_log3.shape[0]
    count = tokens // rows
    wide = pl.BlockSpec((rows, channels), lambda i: (count - 1 - i, 0))
    whole3 = pl.BlockSpec((states, groups, LANES), lambda i: (0, 0, 0))
    row = pl.BlockSpec((1, channels), lambda i: (0, 0))
    small = lambda: pltpu.VMEM((states, groups, LANES), jnp.float32)
    long = lambda: pltpu.VMEM((rows * groups, LANES), jnp.float32)
    return pl.pallas_call(
        functools.partial(scan_backward_kernel, states, groups, rows, unroll),
        grid=(count,),
        in_specs=[
            pl.BlockSpec((rows, 2 * states), lambda i: (count - 1 - i, 0), memory_space=pltpu.SMEM),
            wide, wide, wide,
            pl.BlockSpec((rows, 1), lambda i: (count - 1 - i, 0)),
            whole3, row,
            pl.BlockSpec((rows, states, groups, LANES), lambda i: (count - 1 - i, 0, 0, 0)),
            pl.BlockSpec((1, states, groups, LANES), lambda i: (count - 1 - i, 0, 0, 0)),
        ],
        out_specs=[
            wide, wide,
            pl.BlockSpec((rows, 2 * states), lambda i: (count - 1 - i, 0)),
            whole3, row,
        ],
        out_shape=[
            jax.ShapeDtypeStruct((tokens, channels), jnp.bfloat16),
            jax.ShapeDtypeStruct((tokens, channels), jnp.float32),
            jax.ShapeDtypeStruct((tokens, 2 * states), jnp.float32),
            jax.ShapeDtypeStruct((states, groups, LANES), jnp.float32),
            jax.ShapeDtypeStruct((1, channels), jnp.float32),
        ],
        scratch_shapes=[small(), small(), small(), small(), long(), long(), long(), long(), long(),
                        pltpu.VMEM((rows, 2 * states * groups, LANES), jnp.bfloat16),
                        pltpu.VMEM((rows, 2 * states * groups), jnp.float32)],
        compiler_params=pltpu.CompilerParams(vmem_limit_bytes=48 * 1024 * 1024),
        name="scan_backward",
    )(bc, pre, act, mixed, keep, a_log3, skip, h, starts)


def lagged(values, offset):
    padding = [(offset, 0)] + [(0, 0)] * (values.ndim - 1)
    return jnp.pad(values, padding)[: values.shape[0]]


def leading(values, offset):
    padding = [(0, offset)] + [(0, 0)] * (values.ndim - 1)
    return jnp.pad(values, padding)[offset:]


def pick_dot(left_side, weights, first_mode):
    first_part = jnp.dot(left_side, weights[0], preferred_element_type=jnp.float32)
    second_part = jnp.dot(left_side, weights[1], preferred_element_type=jnp.float32)
    return jnp.where(first_mode, first_part, second_part)


def pick_back(gradient, weights, first_mode):
    dims = (((1,), (1,)), ((), ()))
    first_part = lax.dot_general(gradient, weights[0], dims, preferred_element_type=jnp.float32)
    second_part = lax.dot_general(gradient, weights[1], dims, preferred_element_type=jnp.float32)
    return jnp.where(first_mode, first_part, second_part)


def weight_grads(left_side, gradient, first_mode):
    nothing = jnp.zeros_like(gradient)
    dims = (((0,), (0,)), ((), ()))
    first_part = lax.dot_general(
        left_side,
        jnp.where(first_mode, gradient, nothing),
        dims,
        preferred_element_type=jnp.float32,
    )
    second_part = lax.dot_general(
        left_side,
        jnp.where(first_mode, nothing, gradient),
        dims,
        preferred_element_type=jnp.float32,
    )
    return jnp.stack([first_part, second_part])


def finish_rows(normed_grad, hidden, inverse, cotan, norm_gain):
    scaled = normed_grad * norm_gain
    gain_terms = jnp.sum(normed_grad * hidden * inverse, axis=0)
    cubed = inverse * inverse * inverse
    rows = (
        cotan + inverse * scaled - hidden * cubed * jnp.mean(scaled * hidden, axis=1, keepdims=True)
    )
    return (rows.astype(jnp.bfloat16), gain_terms)


def shards(hidden_in, segment_ids, modality, norm_gain, in_proj, conv_weight, conv_bias, x_proj, dt_proj, dt_bias,
           a_log, skip_gain, out_proj, out_grad):
    tokens, model_width = hidden_in.shape
    conv_taps, channels = conv_weight.shape
    rank_dim = dt_proj.shape[1]
    state_dim = a_log.shape[0]
    groups = channels // LANES
    low = jnp.bfloat16
    first_mode = (modality == 0)[:, None]
    hidden = hidden_in.astype(jnp.float32)
    inverse = lax.rsqrt(jnp.mean(hidden * hidden, axis=1, keepdims=True) + EPS)
    normed_b = (hidden * inverse * norm_gain).astype(low)
    in_inner = in_proj[:, :, 0, :]
    in_gate = in_proj[:, :, 1, :]
    inner_x = pick_dot(normed_b, in_inner, first_mode)
    gate_z = pick_dot(normed_b, in_gate, first_mode)
    same_doc = [jnp.ones((tokens, 1), jnp.float32)]
    for offset in range(1, conv_taps):
        earlier_seg = jnp.pad(segment_ids, (offset, 0), constant_values=-1)[:tokens]
        same_doc.append((earlier_seg == segment_ids).astype(jnp.float32)[:, None])
    conv_sum = conv_bias + conv_weight[conv_taps - 1] * inner_x
    for offset in range(1, conv_taps):
        conv_sum = conv_sum + conv_weight[conv_taps - 1 - offset] * lagged(inner_x, offset) * same_doc[offset]
    activated_b = jax.nn.silu(conv_sum).astype(low)
    projected = lax.psum(pick_dot(activated_b, x_proj, first_mode), "tensor")
    rank_b = projected[:, :rank_dim].astype(low)
    coeffs = projected[:, rank_dim:]
    gated_grad = pick_back(out_grad, out_proj, first_mode)
    step_pre = pick_dot(rank_b, dt_proj, first_mode) + jnp.where(first_mode, dt_bias[0], dt_bias[1])
    keep = same_doc[1]
    a_log3 = a_log.reshape(state_dim, groups, LANES)
    skip_row = skip_gain[None]
    gated_b, gate_grad_b, mixed_grad, states, starts = scan_forward(
        coeffs, step_pre, activated_b, gate_z, gated_grad, keep, a_log3, skip_row)
    partial_out = pick_dot(gated_b, out_proj, first_mode).astype(low)
    summed_out = lax.psum(partial_out, "tensor")
    output = (hidden + summed_out.astype(jnp.float32)).astype(low)
    cotan = out_grad.astype(jnp.float32)
    out_proj_grad = weight_grads(gated_b, out_grad, first_mode).astype(low)
    out_proj_grad = lax.psum(out_proj_grad, "dp").astype(jnp.float32)
    gate_proj_grad = lax.psum(weight_grads(normed_b, gate_grad_b, first_mode).astype(low), "dp")
    pre_grad_b, act_part, coeff_grad, a_log_grad, skip_grad = scan_backward(
        coeffs, step_pre, activated_b, mixed_grad, keep, a_log3, skip_row, states, starts)
    a_log_grad = a_log_grad.reshape(state_dim, channels)
    pre_grad = pre_grad_b.astype(jnp.float32)
    dt_bias_grad = jnp.stack([
        jnp.sum(jnp.where(first_mode, pre_grad, 0.0), axis=0),
        jnp.sum(jnp.where(first_mode, 0.0, pre_grad), axis=0)])
    rank_part = pick_back(pre_grad_b, dt_proj, first_mode)
    proj_grad = lax.psum(jnp.concatenate([rank_part, coeff_grad], axis=1), "tensor")
    proj_grad_b = proj_grad.astype(low)
    act_grad = act_part + pick_back(proj_grad_b, x_proj, first_mode)
    sig_conv = jax.nn.sigmoid(conv_sum)
    conv_grad = act_grad * sig_conv * (1.0 + conv_sum * (1.0 - sig_conv))
    conv_bias_grad = jnp.sum(conv_grad, axis=0)
    weight_rows = []
    x_grad = jnp.zeros_like(inner_x)
    for tap_index in range(conv_taps):
        offset = conv_taps - 1 - tap_index
        masked = conv_grad * same_doc[offset]
        weight_rows.append(jnp.sum(masked * lagged(inner_x, offset), axis=0))
        x_grad = x_grad + conv_weight[tap_index] * leading(masked, offset)
    x_grad_b = x_grad.astype(low)
    normed_part = pick_back(x_grad_b, in_inner, first_mode) + pick_back(gate_grad_b, in_gate, first_mode)
    normed_grad = lax.psum(normed_part.astype(low), "tensor").astype(jnp.float32)
    inner_proj_grad = lax.psum(weight_grads(normed_b, x_grad_b, first_mode).astype(low), "dp")
    in_proj_grad = jnp.stack([inner_proj_grad, gate_proj_grad], axis=2).astype(jnp.float32)
    input_grad, norm_gain_grad = finish_rows(normed_grad, hidden, inverse, cotan, norm_gain)
    x_proj_grad = lax.psum(weight_grads(activated_b, proj_grad_b, first_mode).astype(low), "dp").astype(jnp.float32)
    dt_proj_grad = lax.psum(weight_grads(rank_b, pre_grad_b, first_mode).astype(low), "dp").astype(jnp.float32)
    rows = jnp.concatenate([jnp.stack(weight_rows), conv_bias_grad[None], dt_bias_grad, a_log_grad, skip_grad], axis=0)
    rows = lax.psum(rows, "dp")
    norm_gain_grad = lax.psum(norm_gain_grad, "dp")
    at = conv_taps + 1
    return (output, input_grad, norm_gain_grad, in_proj_grad, rows[:conv_taps], rows[conv_taps], x_proj_grad,
            dt_proj_grad, rows[at:at + 2], rows[at + 2:at + 2 + state_dim], rows[at + 2 + state_dim], out_proj_grad)


def solution(mesh):
    in_specs = (
        P("dp", None),
        P("dp"),
        P("dp"),
        P(),
        P(None, None, None, "tensor"),
        P(None, "tensor"),
        P("tensor"),
        P(None, "tensor", None),
        P(None, None, "tensor"),
        P(None, "tensor"),
        P(None, "tensor"),
        P("tensor"),
        P(None, "tensor", None),
        P("dp", None),
    )
    out_specs = (
        P("dp", None),
        P("dp", None),
        P(),
        P(None, None, None, "tensor"),
        P(None, "tensor"),
        P("tensor"),
        P(None, "tensor", None),
        P(None, None, "tensor"),
        P(None, "tensor"),
        P(None, "tensor"),
        P("tensor"),
        P(None, "tensor", None),
    )
    return jax.shard_map(shards, mesh=mesh, in_specs=in_specs, out_specs=out_specs, check_vma=False)
```

```python
import functools

import jax
import jax.numpy as jnp
from jax import lax
from jax.experimental import pallas as pl
from jax.experimental.pallas import tpu as pltpu
from jax.sharding import PartitionSpec as P

EPS = 1e-05

LANES = 128
BIG = 1000.0
LOG2E = 1.4426950408889634


def softplus(v):
    return jnp.maximum(v, 0.0) + jnp.log1p(jnp.exp(-jnp.abs(v)))


def spread_rows(scratch, values, groups):
    rows = values.shape[0]
    for g in range(groups):
        scratch[pl.ds(g, rows, stride=groups), :] = values[:, g * LANES:(g + 1) * LANES]


def gather_rows(scratch, rows, groups):
    return jnp.concatenate(
        [scratch[pl.ds(g, rows, stride=groups), :] for g in range(groups)], axis=1)


def scan_forward_kernel(states, groups, rows, unroll,
                        bc_ref, pre_ref, act_ref, z_ref, gg_ref, keep_ref, alog_ref, skip_ref,
                        gated_ref, ggrad_ref, mixed_ref, h_ref, start_ref,
                        rate_scr, state_scr, sk_scr, u_scr, y_scr):
    chunk = pl.program_id(0)

    @pl.when(chunk == 0)
    def _():
        rate_scr[...] = jnp.exp(alog_ref[...]) * (-LOG2E)
        state_scr[...] = jnp.zeros_like(state_scr)

    step = softplus(pre_ref[...])
    act = act_ref[...].astype(jnp.float32)
    spread_rows(u_scr, step * act, groups)
    spread_rows(sk_scr, jnp.where(keep_ref[...] > 0.0, step, BIG), groups)
    start_ref[0] = state_scr[...]

    def one(t, held):
        at = pl.multiple_of(t * groups, groups)
        sk = sk_scr[pl.ds(at, groups), :]
        u = u_scr[pl.ds(at, groups), :]
        y = jnp.zeros_like(u)
        new = []
        for n in range(states):
            h = jnp.exp2(sk * rate_scr[n]) * held[n] + u * bc_ref[t, n]
            h_ref[t, n] = h
            y = y + h * bc_ref[t, states + n]
            new.append(h)
        y_scr[pl.ds(at, groups), :] = y
        return tuple(new)

    last = lax.fori_loop(0, rows, one, tuple(state_scr[n] for n in range(states)), unroll=unroll)
    for n in range(states):
        state_scr[n] = last[n]
    mixed_out = gather_rows(y_scr, rows, groups) + skip_ref[...] * act
    z = z_ref[...].astype(jnp.float32)
    gg = gg_ref[...].astype(jnp.float32)
    sig = jax.nn.sigmoid(z)
    silu = z * sig
    gated_ref[...] = (mixed_out * silu).astype(gated_ref.dtype)
    mixed_ref[...] = gg * silu
    ggrad_ref[...] = (gg * mixed_out * sig * (1.0 + z * (1.0 - sig))).astype(ggrad_ref.dtype)


def scan_forward(bc, pre, act, z, gg, keep, a_log3, skip, rows=64, unroll=4):
    tokens, channels = pre.shape
    groups = channels // LANES
    states = a_log3.shape[0]
    count = tokens // rows
    wide = pl.BlockSpec((rows, channels), lambda i: (i, 0))
    whole3 = pl.BlockSpec((states, groups, LANES), lambda i: (0, 0, 0))
    return pl.pallas_call(
        functools.partial(scan_forward_kernel, states, groups, rows, unroll),
        grid=(count,),
        in_specs=[
            pl.BlockSpec((rows, 2 * states), lambda i: (i, 0), memory_space=pltpu.SMEM),
            wide, wide, wide, wide,
            pl.BlockSpec((rows, 1), lambda i: (i, 0)),
            whole3,
            pl.BlockSpec((1, channels), lambda i: (0, 0)),
        ],
        out_specs=[
            wide, wide, wide,
            pl.BlockSpec((rows, states, groups, LANES), lambda i: (i, 0, 0, 0)),
            pl.BlockSpec((1, states, groups, LANES), lambda i: (i, 0, 0, 0)),
        ],
        out_shape=[
            jax.ShapeDtypeStruct((tokens, channels), jnp.bfloat16),
            jax.ShapeDtypeStruct((tokens, channels), jnp.bfloat16),
            jax.ShapeDtypeStruct((tokens, channels), jnp.float32),
            jax.ShapeDtypeStruct((tokens, states, groups, LANES), jnp.float32),
            jax.ShapeDtypeStruct((count, states, groups, LANES), jnp.float32),
        ],
        scratch_shapes=[
            pltpu.VMEM((states, groups, LANES), jnp.float32),
            pltpu.VMEM((states, groups, LANES), jnp.float32),
            pltpu.VMEM((rows * groups, LANES), jnp.float32),
            pltpu.VMEM((rows * groups, LANES), jnp.float32),
            pltpu.VMEM((rows * groups, LANES), jnp.float32),
        ],
        compiler_params=pltpu.CompilerParams(vmem_limit_bytes=48 * 1024 * 1024),
        name="scan_forward",
    )(bc, pre, act, z, gg, keep, a_log3, skip)


MESH = pl.DeviceIdType.MESH
DMA = pltpu.SemaphoreType.DMA


def add_rows(target, left, right, rows, slab):
    def body(i, nothing):
        at = pl.ds(pl.multiple_of(i * slab, slab), slab)
        target[at, :] = (left[at, :].astype(jnp.float32) + right[at, :].astype(jnp.float32)).astype(jnp.bfloat16)
        return nothing
    lax.fori_loop(0, rows // slab, body, 0)


def place():
    dp = lax.axis_index("dp")
    x, y, core = (dp // 2) % 2, dp // 4, dp % 2
    return x, y, {"dp": dp + 2 - 4 * x}, {"dp": dp + 4 - 8 * y}, {"dp": dp + 1 - 2 * core}


def greet():
    z = lax.axis_index("tensor")
    barrier = pltpu.get_barrier_semaphore()
    for target in place()[2:]:
        pl.semaphore_signal(barrier, inc=1, device_id=target, device_id_type=MESH)

    @pl.when(z > 0)
    def _():
        pl.semaphore_signal(barrier, inc=1, device_id={"tensor": z - 1}, device_id_type=MESH)

    @pl.when(z < 3)
    def _():
        pl.semaphore_signal(barrier, inc=1, device_id={"tensor": z + 1}, device_id_type=MESH)

    @pl.when((z > 0) & (z < 3))
    def _():
        pl.semaphore_wait(barrier, 5)

    @pl.when((z == 0) | (z == 3))
    def _():
        pl.semaphore_wait(barrier, 4)


class Exchange:
    def __init__(self, prod, out, held, half_buf, quarter_buf, sems, summed=None):
        self.summed = summed
        self.prod, self.out, self.held, self.half_buf, self.quarter_buf = prod, out, held, half_buf, quarter_buf
        (self.half_send, self.half_recv, self.quarter_send, self.quarter_recv,
         self.share_send, self.share_recv, self.core_send, self.core_recv, self.local) = sems
        x, y, self.to_x, self.to_y, self.to_core = place()
        self.firsts, self.seconds = (x, y), (y, x)
        self.ways = ((self.to_x, self.to_y), (self.to_y, self.to_x))
        self.side = half_buf.shape[2]

    @staticmethod
    def scratch(side, depth):
        low = jnp.bfloat16
        return [pltpu.VMEM((2, 2, side, depth), low), pltpu.VMEM((2, 2, side, depth), low), pltpu.VMEM((2, side, depth), low),
                DMA((2, 2)), DMA((2, 2)), DMA((2,)), DMA((2,)), DMA((2, 4)), DMA((2, 4)), DMA((2, 4)), DMA((2, 4)), DMA((2, 3))]

    def rows(self, mode, k, mine):
        first, second = self.firsts[mode], self.seconds[mode]
        half = first if mine else 1 - first
        quarter = 1 - second if k == 0 else second
        return pl.ds(pl.multiple_of((half * 2 + quarter) * self.side, self.side), self.side)

    def half_copy(self, mode, k):
        return pltpu.make_async_remote_copy(
            src_ref=self.prod.at[mode, self.rows(mode, k, False)], dst_ref=self.half_buf.at[mode, k],
            send_sem=self.half_send.at[mode, k], recv_sem=self.half_recv.at[mode, k],
            device_id=self.ways[mode][0], device_id_type=MESH)

    def keep_copy(self, mode, k):
        return pltpu.make_async_copy(self.prod.at[mode, self.rows(mode, k, True)], self.held.at[mode, k], self.local.at[mode, k])

    def quarter_copy(self, mode):
        return pltpu.make_async_remote_copy(
            src_ref=self.half_buf.at[mode, 0], dst_ref=self.quarter_buf.at[mode],
            send_sem=self.quarter_send.at[mode], recv_sem=self.quarter_recv.at[mode],
            device_id=self.ways[mode][1], device_id_type=MESH)

    def share_copy(self, mode, k):
        own = self.held.at[mode, 1]
        if k == 3:
            source, way = (self.out.at[mode, 0, 1], self.to_x) if mode == 0 else (self.out.at[mode, 0, 2], self.to_y)
        else:
            source, way = own, self.to_y if k == 1 else self.to_x
        return pltpu.make_async_remote_copy(
            src_ref=source, dst_ref=self.out.at[mode, 0, k], send_sem=self.share_send.at[mode, k],
            recv_sem=self.share_recv.at[mode, k], device_id=way, device_id_type=MESH)

    def core_copy(self, mode, k):
        return pltpu.make_async_remote_copy(
            src_ref=self.held.at[mode, 1] if k == 0 else self.out.at[mode, 0, k], dst_ref=self.out.at[mode, 1, k],
            send_sem=self.core_send.at[mode, k], recv_sem=self.core_recv.at[mode, k],
            device_id=self.to_core, device_id_type=MESH)

    def out_copy(self, mode):
        return pltpu.make_async_copy(self.held.at[mode, 1], self.out.at[mode, 0, 0], self.local.at[mode, 2])

    def start_shares(self, mode):
        for k in ((1, 2) if mode == 0 else (2, 1)):
            self.share_copy(mode, k).start()
        self.core_copy(mode, 0).start()
        self.out_copy(mode).start()

    def event(self, number):
        if number == 0:
            for k in range(2):
                for mode in range(2):
                    self.half_copy(mode, k).start()
                    self.keep_copy(mode, k).start()
        elif number == 1:
            for mode in range(2):
                self.keep_copy(mode, 0).wait()
                self.half_copy(mode, 0).wait_recv()
                add_rows(self.half_buf.at[mode, 0], self.half_buf.at[mode, 0], self.held.at[mode, 0], self.side, 32)
                self.quarter_copy(mode).start()
        elif number == 2:
            for mode in range(2):
                self.keep_copy(mode, 1).wait()
                self.half_copy(mode, 1).wait_recv()
                add_rows(self.half_buf.at[mode, 1], self.half_buf.at[mode, 1], self.held.at[mode, 1], self.side, 32)
        elif number == 3:
            for mode in range(2):
                self.quarter_copy(mode).wait_recv()
                add_rows(self.held.at[mode, 1], self.half_buf.at[mode, 1], self.quarter_buf.at[mode], self.side, 32)
                self.start_shares(mode)
        elif number == 4:
            for mode in range(2):
                k = 1 if mode == 0 else 2
                self.share_copy(mode, k).wait_recv()
                self.share_copy(mode, 3).start()
                self.core_copy(mode, k).start()
        elif number == 5:
            for mode in range(2):
                k = 2 if mode == 0 else 1
                self.share_copy(mode, k).wait_recv()
                self.core_copy(mode, k).start()
        elif number == 6:
            for mode in range(2):
                self.share_copy(mode, 3).wait_recv()
                self.core_copy(mode, 3).start()
        elif number == 8:
            for mode in range(2):
                pltpu.make_async_copy(self.prod.at[mode], self.held.at[mode, 1], self.local.at[mode, 1]).start()
        elif number == 9:
            for mode in range(2):
                pltpu.make_async_copy(self.prod.at[mode], self.held.at[mode, 1], self.local.at[mode, 1]).wait()
                self.start_shares(mode)
        elif number == 7:
            for mode in range(2):
                if self.summed is None:
                    for k in range(2):
                        self.half_copy(mode, k).wait_send()
                    self.quarter_copy(mode).wait_send()
                for k in range(1, 4):
                    self.share_copy(mode, k).wait_send()
                for k in range(4):
                    self.core_copy(mode, k).wait_send()
                    self.core_copy(mode, k).wait_recv()
                self.out_copy(mode).wait()


class LineSum:
    def __init__(self, part, res, acc, red, sems):
        self.part, self.res, self.acc, self.red = part, res, acc, red
        self.red_send, self.red_recv, self.back_send, self.back_recv, self.local = sems
        self.z = lax.axis_index("tensor")
        self.near = jnp.where(self.z < 2, 1, 0)
        self.pieces, self.rows = acc.shape[1], acc.shape[2]
        self.turns = 2 * self.pieces + 2

    @staticmethod
    def scratch(pieces, rows, width):
        low = jnp.bfloat16
        return [pltpu.VMEM((2, pieces, rows, width), low), pltpu.VMEM((2, pieces, rows, width), low),
                DMA((2, pieces)), DMA((2, pieces)), DMA((2, pieces)), DMA((2, pieces)), DMA((2,))]

    def place_of(self, half):
        along = jnp.where(half == 0, 3 - self.z, self.z)
        return along == 0, along == 3

    def red_copy(self, half, c):
        return pltpu.make_async_remote_copy(
            src_ref=self.acc.at[half, c], dst_ref=self.red.at[half, c], send_sem=self.red_send.at[half, c],
            recv_sem=self.red_recv.at[half, c], device_id={"tensor": self.z + 2 * half - 1}, device_id_type=MESH)

    def back_copy(self, half, c, source):
        return pltpu.make_async_remote_copy(
            src_ref=source, dst_ref=self.res.at[half, c], send_sem=self.back_send.at[half, c],
            recv_sem=self.back_recv.at[half, c], device_id={"tensor": self.z - 2 * half + 1}, device_id_type=MESH)

    def load(self):
        return pltpu.make_async_copy(self.part, self.acc, self.local.at[0])

    def own(self, half):
        return pltpu.make_async_copy(self.acc.at[half], self.res.at[half], self.local.at[1])

    def begin(self):
        self.load().wait()
        for half in range(2):
            begins, _ = self.place_of(half)

            @pl.when(begins)
            def _():
                for c in range(self.pieces):
                    self.red_copy(half, c).start()

    def reduce_step(self, c, half):
        begins, ends = self.place_of(half)

        @pl.when(jnp.logical_not(begins))
        def _():
            self.red_copy(half, c).wait_recv()
            add_rows(self.acc.at[half, c], self.acc.at[half, c], self.red.at[half, c], self.rows, 16)

            @pl.when(ends)
            def _():
                self.back_copy(half, c, self.acc.at[half, c]).start()

            @pl.when(jnp.logical_not(ends))
            def _():
                self.red_copy(half, c).start()

    def back_step(self, c, half):
        begins, ends = self.place_of(half)

        @pl.when(jnp.logical_not(ends))
        def _():
            self.back_copy(half, c, self.res.at[half, c]).wait_recv()

            @pl.when(jnp.logical_not(begins))
            def _():
                self.back_copy(half, c, self.res.at[half, c]).start()

    def turn(self, turn):
        near, far = self.near, 1 - self.near
        if turn < self.pieces:
            self.reduce_step(turn, near)
        if 1 <= turn <= self.pieces:
            self.reduce_step(turn - 1, far)
        back = turn - self.pieces
        if 0 <= back < self.pieces:
            self.back_step(back, far)
        if 1 <= back <= self.pieces:
            self.back_step(back - 1, near)

    def finish(self):
        for half in range(2):
            begins, ends = self.place_of(half)

            @pl.when(ends)
            def _():
                self.own(half).start()
                self.own(half).wait()

            @pl.when(jnp.logical_not(ends))
            def _():
                for c in range(self.pieces):
                    self.red_copy(half, c).wait_send()

            @pl.when(jnp.logical_not(begins))
            def _():
                for c in range(self.pieces):
                    self.back_copy(half, c, self.res.at[half, c]).wait_send()


def tail_kernel(count, *refs):
    prods, part = refs[:count], refs[count]
    outs, res = refs[count + 1:2 * count + 1], refs[2 * count + 1]
    scr = refs[2 * count + 2:]
    line = LineSum(part, res, scr[0], scr[1], scr[2:7])
    swaps = [Exchange(prods[i], outs[i], *scr[7 + 12 * i:10 + 12 * i], scr[10 + 12 * i:19 + 12 * i]) for i in range(count)]
    swaps[0].summed = True
    line.load().start()
    swaps[0].event(8)
    greet()
    swaps[1].event(0)
    swaps[0].event(9)
    line.begin()
    last = line.turns
    plan = {4: [(1, 1)], 6: [(0, 4)], 8: [(1, 2)], 10: [(0, 5)], 12: [(1, 3)], 15: [(0, 6)], 17: [(1, 4)], 20: [(1, 5)],
            24: [(1, 6)]}
    for turn in range(last):
        line.turn(turn)
        for which, number in plan.get(turn, []):
            swaps[which].event(number)
    for swapped in swaps:
        swapped.event(7)
    line.finish()


def tail_exchange(products, normed_part, pieces=12):
    count = len(products)
    side, depth = products[0].shape[1:]
    tokens, width = normed_part.shape
    part = normed_part.reshape(2, pieces, tokens // 2 // pieces, width)
    low = jnp.bfloat16
    anywhere = pl.BlockSpec(memory_space=pl.ANY)
    scratch = LineSum.scratch(*part.shape[1:])
    for _ in products:
        scratch = scratch + Exchange.scratch(side, depth)
    outs = pl.pallas_call(
        functools.partial(tail_kernel, count),
        in_specs=[anywhere] * (count + 1),
        out_specs=[anywhere] * (count + 1),
        out_shape=[jax.ShapeDtypeStruct((2, 2, 4, side, depth), low)] * count + [jax.ShapeDtypeStruct(part.shape, low)],
        scratch_shapes=scratch,
        cost_estimate=pl.CostEstimate(flops=100_000_000, bytes_accessed=300_000_000, transcendentals=0),
        compiler_params=pltpu.CompilerParams(collective_id=1, has_side_effects=True, vmem_limit_bytes=40 * 1024 * 1024),
        name="tail_exchange",
    )(*products, part)
    return outs[:count], outs[count].reshape(tokens, width)


NT = (((1,), (1,)), ((), ()))
TN = (((0,), (0,)), ((), ()))


def dot_f32(left, right, dims=(((1,), (0,)), ((), ()))):
    return lax.dot_general(left, right, dims, preferred_element_type=jnp.float32)


def widened(column_block, width):
    return jnp.concatenate([column_block] * (width // LANES), axis=1)


def middle_kernel(pre_grad, act_part, coeff, conv_sum, inner_x, act_b, rank_b, dt_proj, x_wide, conv_w, docs, modes,
                  gate_pair, normed_t, inv, extra, hidden, in_gate, in_inner,
                  rows_out, normed_out, gate_own, inner_prod, gate_prod,
                  w_buf, mask_buf, pair_buf, conv_buf, stage, stage_n, hid_buf, proj_buf, proj_recv, proj_fin, gain_buf, gain_recv,
                  held, half_buf, quarter_buf,
                  half_send, half_recv, quarter_send, quarter_recv, keep_sems,
                  red_send, red_recv, all_send, all_recv, core_sems, gain_send, gain_recv_sem, w_sems, stage_sems, n_sems, hid_sems):
    tokens, channels = pre_grad.shape
    low = jnp.bfloat16
    rank_dim = dt_proj.shape[1]
    z = lax.axis_index("tensor")
    x, y, to_x, to_y, to_core = place()
    share = tokens // 4
    gate = Exchange(gate_prod, None, held, half_buf, quarter_buf,
                    (half_send, half_recv, quarter_send, quarter_recv, None, None, None, None, keep_sems))
    width = hidden.shape[1]
    slices = width // w_buf.shape[2]
    cut = w_buf.shape[2]

    def z_at(off):
        return {"tensor": (z + off) % 4}

    barrier = pltpu.get_barrier_semaphore()
    for target in (to_x, to_y, to_core, z_at(1), z_at(2), z_at(3)):
        pl.semaphore_signal(barrier, inc=1, device_id=target, device_id_type=MESH)
    pl.semaphore_wait(barrier, 6)

    def weight_copies(i):
        slot = i % 2
        found = []
        for j, source in enumerate((in_gate, in_inner)):
            for m in range(2):
                found.append(pltpu.make_async_copy(source.at[m, pl.ds(i * cut, cut)], w_buf.at[slot, 2 * j + m],
                                                   w_sems.at[slot, 2 * j + m]))
        found.append(pltpu.make_async_copy(hidden.at[:, pl.ds(i * cut, cut)], hid_buf.at[slot], hid_sems.at[slot]))
        return found

    for i in range(2):
        for copy in weight_copies(i):
            copy.start()

    block = 128

    def proj_block(i, nothing):
        at = pl.ds(pl.multiple_of(i * block, block), block)
        grad = pre_grad[at, :]
        part = dot_f32(grad * widened(modes[0, at, :], channels), dt_proj[0], NT)
        part = part + dot_f32(grad * widened(modes[1, at, :], channels), dt_proj[1], NT)
        proj_buf[at, 0:rank_dim] = part.astype(low)
        proj_buf[at, rank_dim:rank_dim + LANES] = coeff[at, :].astype(low)
        return nothing

    lax.fori_loop(0, tokens // block, proj_block, 0)

    def red_copy(off):
        return pltpu.make_async_remote_copy(
            src_ref=proj_buf.at[pl.ds(pl.multiple_of(((z + off) % 4) * share, share), share)], dst_ref=proj_recv.at[off - 1],
            send_sem=red_send.at[off - 1], recv_sem=red_recv.at[off - 1], device_id=z_at(off), device_id_type=MESH)

    for off in (1, 2, 3):
        red_copy(off).start()

    def product(pair, target, number):
        pair_tokens = pair.shape[0]
        tall = stage.shape[1]
        turns = normed_t.shape[0] // tall
        for m in range(2):
            def mask_rows(i, nothing):
                at = pl.ds(pl.multiple_of(i * block, block), block)
                mask_buf[at, :] = pair[at, :] * widened(modes[m, at, :], channels)
                return nothing
            lax.fori_loop(0, pair_tokens // block, mask_rows, 0)
            for j in range(turns):
                slot = (m * turns + j) % 2
                copy = pltpu.make_async_copy(stage.at[slot], target.at[m, pl.ds(j * tall, tall)], stage_sems.at[slot])
                if m * turns + j >= 2:
                    copy.wait()
                stage[slot] = dot_f32(normed_t[pl.ds(j * tall, tall), :], mask_buf[...]).astype(low)
                copy.start()
        for slot in range(2):
            pltpu.make_async_copy(stage.at[slot], target.at[0, pl.ds(0, tall)], stage_sems.at[slot]).wait()

    product(gate_pair, gate_prod, 0)
    gate.event(0)

    for off in (1, 2, 3):
        red_copy(off).wait_recv()
    mine = pl.ds(pl.multiple_of(z * share, share), share)
    total = proj_buf[mine, :].astype(jnp.float32)
    for k in range(3):
        total = total + proj_recv[k].astype(jnp.float32)
    proj_fin[mine, :] = total.astype(low)

    def all_copy(off):
        return pltpu.make_async_remote_copy(
            src_ref=proj_fin.at[mine], dst_ref=proj_fin.at[mine], send_sem=all_send.at[off - 1],
            recv_sem=all_recv.at[off - 1], device_id=z_at(off), device_id_type=MESH)

    for off in (1, 2, 3):
        all_copy(off).start()
    span = x_wide.shape[1] - 96
    mode_rows = span + rank_dim
    for m in range(2):
        ranks = rank_b[...] * modes[m, pl.ds(0, tokens), :]
        rows_out[pl.ds(m * mode_rows + span, rank_dim), :] = dot_f32(ranks, pre_grad[...], TN).astype(low)
    def dt_sums(i, carried):
        at = pl.ds(pl.multiple_of(i * block, block), block)
        grad = pre_grad[at, :].astype(jnp.float32)
        first = jnp.sum(grad * widened(modes[0, at, :].astype(jnp.float32), channels), axis=0, keepdims=True)
        return carried[0] + first, carried[1] + jnp.sum(grad, axis=0, keepdims=True) - first

    none_row = jnp.zeros((1, channels), jnp.float32)
    bias0, bias1 = lax.fori_loop(0, tokens // block, dt_sums, (none_row, none_row))
    for off in (1, 2, 3):
        all_copy(off).wait_recv()

    def act_block(i, bias):
        at = pl.ds(pl.multiple_of(i * block, block), block)
        proj = proj_fin[at, :]
        two = proj.shape[1]
        back = dot_f32(proj * widened(modes[0, at, :], two), x_wide[0])
        back = back + dot_f32(proj * widened(modes[1, at, :], two), x_wide[1])
        value = conv_sum[at, :]
        sig = jax.nn.sigmoid(value)
        grad = (act_part[at, :] + back) * sig * (1.0 + value * (1.0 - sig))
        conv_buf[at, :] = grad
        return bias + jnp.sum(grad, axis=0, keepdims=True)

    conv_buf[pl.ds(tokens, 8), :] = jnp.zeros((8, channels), jnp.float32)
    bias = lax.fori_loop(0, tokens // block, act_block, none_row)
    gate.event(1)
    taps = conv_w.shape[0]
    thin = 64

    def conv_block(i, sums):
        base = pl.multiple_of(i * thin, thin)
        grads = conv_buf[pl.ds(base, thin + 8), :]
        doc = docs[pl.ds(base, thin), :]
        inner = inner_x[pl.ds(base, thin), :]
        result = jnp.zeros((thin, channels), jnp.float32)
        new = []
        for offset in range(taps):
            moved = grads[offset:offset + thin, :] * doc[:, offset:offset + 1]
            tap = taps - 1 - offset
            result = result + moved * conv_w[tap:tap + 1, :]
            new.append(sums[offset] + jnp.sum(moved * inner, axis=0, keepdims=True))
        pair_buf[pl.ds(base, thin), :] = result.astype(low)
        return tuple(new)

    sums = lax.fori_loop(0, tokens // thin, conv_block, (none_row,) * taps)

    def core_copy():
        return pltpu.make_async_remote_copy(
            src_ref=pair_buf.at[pl.ds(0, tokens)], dst_ref=pair_buf.at[pl.ds(tokens, tokens)],
            send_sem=core_sems.at[0], recv_sem=core_sems.at[1], device_id=to_core, device_id_type=MESH)

    core_copy().start()

    for i in range(slices):
        slot = i % 2
        for copy in weight_copies(i):
            copy.wait()
        third = tokens // 3
        out_copy = pltpu.make_async_copy(stage_n.at[slot], normed_out.at[:, pl.ds(i * cut, cut)], n_sems.at[slot])
        if i >= 2:
            out_copy.wait()

        def normed_rows(j, gain, slot=slot):
            at = pl.ds(pl.multiple_of(j * third, third), third)
            gate_grad, grad = gate_pair[at, :], pair_buf[at, :]
            zero = dot_f32(gate_grad, w_buf[slot, 0], NT) + dot_f32(grad, w_buf[slot, 2], NT)
            one = dot_f32(gate_grad, w_buf[slot, 1], NT) + dot_f32(grad, w_buf[slot, 3], NT)
            picked = jnp.where(inv[at, 1:2] > 0.5, zero, one)
            stage_n[slot, at, :] = picked.astype(low)
            return gain + jnp.sum(picked * hid_buf[slot, at, :].astype(jnp.float32) * inv[at, 0:1], axis=0, keepdims=True)

        gain = lax.fori_loop(0, 3, normed_rows, jnp.zeros((1, cut), jnp.float32))
        gain_buf[:, pl.ds(i * cut, cut)] = jnp.broadcast_to(gain, (8, cut))
        out_copy.start()
        if i + 2 < slices:
            for copy in weight_copies(i + 2):
                copy.start()
        if i == 1:
            gate.event(2)
    for slot in range(2):
        pltpu.make_async_copy(stage_n.at[slot], normed_out.at[:, pl.ds(0, cut)], n_sems.at[slot]).wait()

    def gain_copy(off):
        return pltpu.make_async_remote_copy(
            src_ref=gain_buf, dst_ref=gain_recv.at[off - 1], send_sem=gain_send.at[off - 1],
            recv_sem=gain_recv_sem.at[off - 1], device_id=z_at(off), device_id_type=MESH)

    for off in (1, 2, 3):
        gain_copy(off).start()
    core_copy().wait_recv()
    product(pair_buf, inner_prod, 1)
    for m in range(2):
        proj = proj_fin[...] * widened(modes[m, pl.ds(0, tokens), :], proj_fin.shape[1])
        rows_out[pl.ds(m * mode_rows, span), :] = dot_f32(proj, act_b[...], TN)[:span].astype(low)
    for off in (1, 2, 3):
        gain_copy(off).wait_recv()
    gain = gain_buf[0:1, :] + gain_recv[0, 0:1, :] + gain_recv[1, 0:1, :] + gain_recv[2, 0:1, :]
    gains = [gain[:, k * channels:(k + 1) * channels] for k in range(width // channels)]
    tail_rows = list(sums[::-1]) + [bias, bias0, bias1, extra[...]] + gains
    used = taps + 3 + extra.shape[0] + len(gains)
    tail_rows.append(jnp.zeros((32 - used, channels), jnp.float32))
    rows_out[pl.ds(2 * mode_rows, 32), :] = jnp.concatenate(tail_rows, axis=0).astype(low)
    for mode in range(2):
        gate.quarter_copy(mode).wait_recv()
        add_rows(gate_own.at[mode], half_buf.at[mode, 1], quarter_buf.at[mode], gate.side, 32)
        gate.quarter_copy(mode).wait_send()
        for k in range(2):
            gate.half_copy(mode, k).wait_send()
    for off in (1, 2, 3):
        red_copy(off).wait_send()
        all_copy(off).wait_send()
        gain_copy(off).wait_send()
    core_copy().wait_send()


def middle(pre_grad, act_part, coeff, conv_sum, inner_x, act_b, rank_b, dt_proj, x_wide, conv_w, docs, modes,
           gate_pair, normed_t, inv, extra, hidden, in_gate, in_inner):
    tokens, channels = pre_grad.shape
    width = hidden.shape[1]
    low = jnp.bfloat16
    side = normed_t.shape[0] // 4
    cut = 512
    mode_rows = x_wide.shape[1] - 96 + dt_proj.shape[1]
    vmem, anywhere = pl.BlockSpec(memory_space=pltpu.VMEM), pl.BlockSpec(memory_space=pl.ANY)
    return pl.pallas_call(
        middle_kernel,
        in_specs=[vmem] * 16 + [anywhere] * 3,
        out_specs=[vmem, anywhere, vmem, anywhere, anywhere],
        out_shape=[
            jax.ShapeDtypeStruct((2 * mode_rows + 32, channels), low),
            jax.ShapeDtypeStruct((tokens, width), low),
            jax.ShapeDtypeStruct((2, side, channels), low),
            jax.ShapeDtypeStruct((2, 4 * side, channels), low),
            jax.ShapeDtypeStruct((2, 4 * side, channels), low),
        ],
        scratch_shapes=[
            pltpu.VMEM((2, 4, cut, channels), low),
            pltpu.VMEM((2 * tokens, channels), low),
            pltpu.VMEM((2 * tokens, channels), low),
            pltpu.VMEM((tokens + 8, channels), jnp.float32),
            pltpu.VMEM((2, 2 * side, channels), low),
            pltpu.VMEM((2, tokens, cut), low),
            pltpu.VMEM((2, tokens, cut), low),
            pltpu.VMEM((tokens, 2 * LANES), low),
            pltpu.VMEM((3, tokens // 4, 2 * LANES), low),
            pltpu.VMEM((tokens, 2 * LANES), low),
            pltpu.VMEM((8, width), jnp.float32),
            pltpu.VMEM((3, 8, width), jnp.float32),
            pltpu.VMEM((2, 2, side, channels), low),
            pltpu.VMEM((2, 2, side, channels), low),
            pltpu.VMEM((2, side, channels), low),
            DMA((2, 2)), DMA((2, 2)), DMA((2,)), DMA((2,)), DMA((2, 3)),
            DMA((3,)), DMA((3,)), DMA((3,)), DMA((3,)), DMA((2,)), DMA((3,)), DMA((3,)),
            DMA((2, 4)), DMA((2,)), DMA((2,)), DMA((2,)),
        ],
        cost_estimate=pl.CostEstimate(flops=27_000_000_000, bytes_accessed=60_000_000, transcendentals=1_000_000),
        compiler_params=pltpu.CompilerParams(collective_id=3, has_side_effects=True, vmem_limit_bytes=61 * 1024 * 1024),
        name="middle",
    )(pre_grad, act_part, coeff, conv_sum, inner_x, act_b, rank_b, dt_proj, x_wide, conv_w, docs, modes,
      gate_pair, normed_t, inv, extra, hidden, in_gate, in_inner)


def split_tail(part, count):
    lane = lax.broadcasted_iota(jnp.int32, part.shape, 1)
    high = part.astype(jnp.bfloat16).astype(jnp.float32)
    rest = pltpu.roll(part - high, count, axis=1)
    return jnp.where(lane < count, high, jnp.where(lane < 2 * count, rest, 0.0)).astype(jnp.bfloat16)


def join_tail(block, count):
    return block + pltpu.roll(block, block.shape[1] - count, axis=1)


def front_kernel(coeffs_wide, hidden, gain, conv_w, conv_b, docs, modes, x_wide, out_grad, view, out_proj,
                 w_inner, w_gate, normed, inverse, conv_sum, inner_x, act_b, gate_z, gated_grad, rank_out, coeff_out,
                 acc, view_buf, wide, stage, w_out, proj_buf, proj_recv, proj_fin,
                 view_sems, stage_sems, out_sems, red_send, red_recv, all_send, all_recv):
    tokens, width = hidden.shape
    channels = conv_w.shape[1]
    groups = channels // LANES
    low = jnp.bfloat16
    z = lax.axis_index("tensor")
    share = tokens // 4
    deep = stage.shape[2] // 2
    turns = width // deep
    block = 128

    def z_at(off):
        return {"tensor": (z + off) % 4}

    barrier = pltpu.get_barrier_semaphore()
    for off in (1, 2, 3):
        pl.semaphore_signal(barrier, inc=1, device_id=z_at(off), device_id_type=MESH)

    def view_copy(i, m):
        tall = deep * 2 * groups
        return pltpu.make_async_copy(view.at[m, pl.ds(pl.multiple_of(i * tall, tall), tall)], view_buf.at[i % 2, m],
                                     view_sems.at[i % 2, m])

    def stage_copy(i, half, m):
        target = w_inner if half == 0 else w_gate
        return pltpu.make_async_copy(stage.at[i % 2, half, pl.ds(m * deep, deep)],
                                     target.at[m, pl.ds(pl.multiple_of(i * deep, deep), deep)], stage_sems.at[i % 2, half, m])

    def out_copy(m):
        return pltpu.make_async_copy(out_proj.at[m], w_out.at[m], out_sems.at[m])

    for m in range(2):
        view_copy(0, m).start()
    for m in range(2):
        view_copy(1, m).start()
        out_copy(m).start()

    def norm_block(i, nothing):
        at = pl.ds(pl.multiple_of(i * block, block), block)
        rows = hidden[at, :].astype(jnp.float32)
        scale = lax.rsqrt(jnp.mean(rows * rows, axis=1, keepdims=True) + EPS)
        inverse[at, :] = jnp.broadcast_to(scale, (block, LANES))
        normed[at, :] = (rows * scale * gain[...]).astype(low)
        return nothing

    lax.fori_loop(0, tokens // block, norm_block, 0)
    acc[0:8, :] = jnp.zeros((8, channels), jnp.float32)

    def unpack(i):
        for m in range(2):
            wide[m] = view_buf[i % 2, m].astype(jnp.float32)
            for half in range(2):
                stage[i % 2, half, m * deep:(m + 1) * deep, :] = jnp.concatenate(
                    [wide[m, pl.ds(g * 2 + half, deep, stride=2 * groups), :] for g in range(groups)], axis=1).astype(low)

    def multiply(i, first):
        columns = normed[:, pl.ds(pl.multiple_of(i * deep, deep), deep)]
        left = jnp.concatenate([columns * widened(modes[0], deep), columns * widened(modes[1], deep)], axis=1)
        for half in range(2):
            product = dot_f32(left, stage[i % 2, half])
            if half == 0:
                acc[8:8 + tokens, :] = product if first else acc[8:8 + tokens, :] + product
            else:
                gate_z[...] = product if first else gate_z[...] + product

    def turn(i):
        for m in range(2):
            view_copy(i, m).wait()
        unpack(i)
        for m in range(2):
            for half in range(2):
                stage_copy(i, half, m).start()

    turn(0)
    multiply(0, True)
    for m in range(2):
        view_copy(2, m).start()
    turn(1)
    for m in range(2):
        view_copy(3, m).start()

    def looped(i, nothing):
        for m in range(2):
            for half in range(2):
                stage_copy(i, half, m).wait()
        multiply(i + 1, False)
        turn(i + 2)

        @pl.when(i + 4 < turns)
        def _():
            for m in range(2):
                view_copy(i + 4, m).start()
        return nothing

    lax.fori_loop(0, turns - 2, looped, 0)
    multiply(turns - 1, False)
    for i in (turns - 2, turns - 1):
        for m in range(2):
            for half in range(2):
                stage_copy(i, half, m).wait()

    taps = conv_w.shape[0]

    def conv_block(i, nothing):
        base = pl.multiple_of(i * block, block)
        at = pl.ds(base, block)
        rows = acc[pl.ds(base, block + 8), :]
        doc = docs[at, :]
        total = conv_b[...] + conv_w[taps - 1:taps, :] * rows[8:8 + block, :]
        for offset in range(1, taps):
            total = total + conv_w[taps - 1 - offset:taps - offset, :] * rows[8 - offset:8 - offset + block, :] * doc[:, offset:offset + 1]
        conv_sum[at, :] = total
        inner_x[at, :] = rows[8:8 + block, :]
        active = (total * jax.nn.sigmoid(total)).astype(low)
        act_b[at, :] = active
        part = dot_f32(active * widened(modes[0, at, :], channels), x_wide[0], NT)
        part = part + dot_f32(active * widened(modes[1, at, :], channels), x_wide[1], NT)
        proj_buf[at, 0:LANES] = part[:, :LANES].astype(low)
        proj_buf[at, LANES:2 * LANES] = split_tail(part[:, LANES:], coeffs_wide)
        return nothing

    lax.fori_loop(0, tokens // block, conv_block, 0)

    def red_copy(off):
        return pltpu.make_async_remote_copy(
            src_ref=proj_buf.at[pl.ds(pl.multiple_of(((z + off) % 4) * share, share), share)], dst_ref=proj_recv.at[off - 1],
            send_sem=red_send.at[off - 1], recv_sem=red_recv.at[off - 1], device_id=z_at(off), device_id_type=MESH)

    mine = pl.ds(pl.multiple_of(z * share, share), share)

    def all_copy(off):
        return pltpu.make_async_remote_copy(
            src_ref=proj_fin.at[mine], dst_ref=proj_fin.at[mine], send_sem=all_send.at[off - 1],
            recv_sem=all_recv.at[off - 1], device_id=z_at(off), device_id_type=MESH)

    pl.semaphore_wait(barrier, 3)
    for off in (1, 2, 3):
        red_copy(off).start()
    third = tokens // 3

    def grad_block(i):
        at = pl.ds(i * third, third)
        zero = dot_f32(out_grad[at, :], w_out[0], NT)
        one = dot_f32(out_grad[at, :], w_out[1], NT)
        gated_grad[at, :] = jnp.where(docs[at, 0:1] > 0.5, zero, one)

    for m in range(2):
        out_copy(m).wait()
    grad_block(0)
    for off in (1, 2, 3):
        red_copy(off).wait_recv()
    total = proj_buf[mine, :].astype(jnp.float32)
    for k in range(3):
        total = total + proj_recv[k].astype(jnp.float32)
    proj_fin[mine, 0:LANES] = total[:, :LANES].astype(low)
    proj_fin[mine, LANES:2 * LANES] = split_tail(join_tail(total[:, LANES:], coeffs_wide), coeffs_wide)
    for off in (1, 2, 3):
        all_copy(off).start()
    grad_block(1)
    grad_block(2)
    for off in (1, 2, 3):
        all_copy(off).wait_recv()
    rank_out[...] = proj_fin[:, 0:LANES]
    coeff_out[...] = join_tail(proj_fin[:, LANES:2 * LANES].astype(jnp.float32), coeffs_wide)
    for off in (1, 2, 3):
        red_copy(off).wait_send()
        all_copy(off).wait_send()


def front(hidden, gain, conv_w, conv_b, docs, modes, x_wide, out_grad, in_proj, out_proj, coeffs_wide):
    tokens, width = hidden.shape
    channels = conv_w.shape[1]
    groups = channels // LANES
    low, f32 = jnp.bfloat16, jnp.float32
    view = in_proj.reshape(2, width, 2, groups, LANES).transpose(0, 1, 3, 2, 4).reshape(2, width * 2 * groups, LANES)
    deep = 256
    vmem, anywhere = pl.BlockSpec(memory_space=pltpu.VMEM), pl.BlockSpec(memory_space=pl.ANY)
    shape = jax.ShapeDtypeStruct
    return pl.pallas_call(
        functools.partial(front_kernel, coeffs_wide),
        in_specs=[vmem] * 8 + [anywhere] * 2,
        out_specs=[anywhere] * 2 + [vmem] * 9,
        out_shape=[
            shape((2, width, channels), low), shape((2, width, channels), low), shape((tokens, width), low),
            shape((tokens, LANES), f32), shape((tokens, channels), f32), shape((tokens, channels), f32),
            shape((tokens, channels), low), shape((tokens, channels), f32), shape((tokens, channels), f32),
            shape((tokens, LANES), low), shape((tokens, LANES), f32),
        ],
        scratch_shapes=[
            pltpu.VMEM((tokens + 8, channels), f32),
            pltpu.VMEM((2, 2, deep * 2 * groups, LANES), low),
            pltpu.VMEM((2, deep * 2 * groups, LANES), f32),
            pltpu.VMEM((2, 2, 2 * deep, channels), low),
            pltpu.VMEM((2, channels, width), low),
            pltpu.VMEM((tokens, 2 * LANES), low),
            pltpu.VMEM((3, tokens // 4, 2 * LANES), low),
            pltpu.VMEM((tokens, 2 * LANES), low),
            DMA((2, 2)), DMA((2, 2, 2)), DMA((2,)), DMA((3,)), DMA((3,)), DMA((3,)), DMA((3,)),
        ],
        cost_estimate=pl.CostEstimate(flops=20_000_000_000, bytes_accessed=80_000_000, transcendentals=1_000_000),
        compiler_params=pltpu.CompilerParams(collective_id=4, has_side_effects=True, vmem_limit_bytes=60 * 1024 * 1024),
        name="front",
    )(hidden, gain, conv_w, conv_b, docs, modes, x_wide, out_grad, view, out_proj)


def finish_kernel(hidden, out_grad, inverse, gain, summed_out, normed_sum, output, input_grad):
    rows = hidden[...].astype(jnp.float32)
    output[...] = (rows + summed_out[...].astype(jnp.float32)).astype(output.dtype)
    scale = inverse[:, 0:1]
    scaled = normed_sum[...].astype(jnp.float32) * gain[...]
    mean = jnp.mean(scaled * rows, axis=1, keepdims=True)
    input_grad[...] = (out_grad[...].astype(jnp.float32) + scale * scaled - rows * (scale * scale * scale) * mean).astype(input_grad.dtype)


def finish(hidden, out_grad, inverse, gain, summed_out, normed_sum):
    tokens, width = hidden.shape
    rows = 128
    wide = pl.BlockSpec((rows, width), lambda i: (i, 0))
    return pl.pallas_call(
        finish_kernel,
        grid=(tokens // rows,),
        in_specs=[wide, wide, pl.BlockSpec((rows, LANES), lambda i: (i, 0)), pl.BlockSpec((1, width), lambda i: (0, 0)), wide, wide],
        out_specs=[wide, wide],
        out_shape=[jax.ShapeDtypeStruct((tokens, width), jnp.bfloat16)] * 2,
        cost_estimate=pl.CostEstimate(flops=16 * tokens * width, bytes_accessed=12 * tokens * width, transcendentals=0),
        name="finish_rows",
    )(hidden, out_grad, inverse, gain, summed_out, normed_sum)


def scan_backward_kernel(states, groups, rows, unroll, count, joined,
                         bc_ref, pre_ref, act_ref, mixed_ref, keep_ref, alog_ref, skip_ref, h_ref, start_ref, *rest):
    if joined:
        prod_ref, part_ref, rest = rest[0], rest[1], rest[2:]
    pgrad_ref, apart_ref, bcg_ref, sum_ref, skipsum_ref = rest[:5]
    rest = rest[5:]
    if joined:
        shared_ref, res_ref, rest = rest[0], rest[1], rest[2:]
    carry_ref, rate_scr, decay_scr, sk_scr, u_scr, dy_scr, w_scr, s_scr, p_scr, q_scr = rest[:10]
    rest = rest[10:]
    chunk = pl.program_id(0)
    if joined:
        line = LineSum(part_ref, res_ref, rest[0], rest[1], rest[2:7])
        swapped = Exchange(prod_ref, shared_ref, *rest[7:10], rest[10:19])

        @pl.when(chunk == 0)
        def _():
            line.load().start()
            greet()
            swapped.event(0)
            line.begin()

        for number, at in enumerate((2, 4, 7, 9, 11), start=1):
            @pl.when(chunk == min(at, count - 1))
            def _():
                swapped.event(number)

        for at in range(1, count):
            @pl.when(chunk == at)
            def _():
                for turn in range(line.turns * (at - 1) // (count - 1), line.turns * at // (count - 1)):
                    line.turn(turn)

    @pl.when(chunk == 0)
    def _():
        decay = -jnp.exp(alog_ref[...])
        decay_scr[...] = decay
        rate_scr[...] = decay * LOG2E
        carry_ref[...] = jnp.zeros_like(carry_ref)
        sum_ref[...] = jnp.zeros_like(sum_ref)
        skipsum_ref[...] = jnp.zeros_like(skipsum_ref)

    step = softplus(pre_ref[...])
    act = act_ref[...].astype(jnp.float32)
    mixed = mixed_ref[...].astype(jnp.float32)
    spread_rows(u_scr, step * act, groups)
    spread_rows(dy_scr, mixed, groups)
    spread_rows(sk_scr, jnp.where(keep_ref[...] > 0.0, step, BIG), groups)
    skipsum_ref[...] += jnp.sum(mixed * act, axis=0, keepdims=True)

    def one(t, carried, before):
        at = pl.multiple_of(t * groups, groups)
        sk = sk_scr[pl.ds(at, groups), :]
        u = u_scr[pl.ds(at, groups), :]
        dy = dy_scr[pl.ds(at, groups), :]
        w = jnp.zeros_like(u)
        s = jnp.zeros_like(u)
        new, pb, pc = [], [], []
        for n in range(states):
            g = dy * bc_ref[t, states + n] + carried[n]
            pb.append(g * u)
            pc.append(dy * h_ref[t, n])
            w = w + g * bc_ref[t, n]
            fg = jnp.exp2(sk * rate_scr[n]) * g
            lg = fg * before(n)
            s = s + lg * decay_scr[n]
            sum_ref[n] += lg * sk
            new.append(fg)
        w_scr[pl.ds(at, groups), :] = w
        s_scr[pl.ds(at, groups), :] = s
        both = pb + pc
        batch = max(1, 16 // groups)
        for j in range(0, 2 * states, batch):
            p_scr[t, pl.ds(j * groups, batch * groups), :] = jnp.concatenate(
                both[j:j + batch], axis=0).astype(jnp.bfloat16)
        return tuple(new)

    def looped(i, carried):
        t = rows - 1 - i
        return one(t, carried, lambda n: h_ref[t - 1, n])

    last = lax.fori_loop(0, rows - 1, looped, tuple(carry_ref[n] for n in range(states)), unroll=unroll)
    last = one(0, last, lambda n: start_ref[0, n])
    for n in range(states):
        carry_ref[n] = last[n]

    ones = jnp.ones((16, LANES), jnp.bfloat16)

    def reduce_one(t, nothing):
        q = lax.dot_general(ones, p_scr[t], (((1,), (1,)), ((), ())), preferred_element_type=jnp.float32)
        q_scr[pl.ds(t, 1), :] = q[0:1]
        return nothing

    lax.fori_loop(0, rows, reduce_one, 0, unroll=4)
    shape = (2 * states * groups, LANES)
    pick = (lax.broadcasted_iota(jnp.int32, shape, 0) // groups == lax.broadcasted_iota(jnp.int32, shape, 1))
    pick = pick.astype(jnp.float32).astype(jnp.bfloat16)
    q = q_scr[...]
    high = q.astype(jnp.bfloat16)
    low = (q - high.astype(jnp.float32)).astype(jnp.bfloat16)
    bcg_ref[...] = (jnp.dot(high, pick, preferred_element_type=jnp.float32)
                    + jnp.dot(low, pick, preferred_element_type=jnp.float32))
    w = gather_rows(w_scr, rows, groups)
    s = gather_rows(s_scr, rows, groups)
    pgrad_ref[...] = ((act * w + s) * jax.nn.sigmoid(pre_ref[...])).astype(pgrad_ref.dtype)
    apart_ref[...] = mixed * skip_ref[...] + step * w

    if joined:
        @pl.when(chunk == count - 1)
        def _():
            swapped.event(6)
            swapped.event(7)
            line.finish()


def scan_backward(bc, pre, act, mixed, keep, a_log3, skip, h, starts, product=None, z_part=None, rows=64, unroll=3, pieces=6):
    tokens, channels = pre.shape
    groups = channels // LANES
    states = a_log3.shape[0]
    count = tokens // rows
    joined = product is not None
    wide = pl.BlockSpec((rows, channels), lambda i: (count - 1 - i, 0))
    whole3 = pl.BlockSpec((states, groups, LANES), lambda i: (0, 0, 0))
    row = pl.BlockSpec((1, channels), lambda i: (0, 0))
    anywhere = pl.BlockSpec(memory_space=pl.ANY)
    small = lambda: pltpu.VMEM((states, groups, LANES), jnp.float32)
    long = lambda: pltpu.VMEM((rows * groups, LANES), jnp.float32)
    extra, extra_shapes, extra_scratch = [], [], []
    if joined:
        side, depth = product.shape[1] // 4, product.shape[2]
        part = z_part.reshape(2, pieces, tokens // 2 // pieces, z_part.shape[1])
        extra = [product, part]
        extra_shapes = [jax.ShapeDtypeStruct((2, 2, 4, side, depth), jnp.bfloat16), jax.ShapeDtypeStruct(part.shape, jnp.bfloat16)]
        extra_scratch = LineSum.scratch(*part.shape[1:]) + Exchange.scratch(side, depth)
    settings = dict(collective_id=2, has_side_effects=True) if joined else {}
    outs = pl.pallas_call(
        functools.partial(scan_backward_kernel, states, groups, rows, unroll, count, joined),
        grid=(count,),
        in_specs=[
            pl.BlockSpec((rows, 2 * states), lambda i: (count - 1 - i, 0), memory_space=pltpu.SMEM),
            wide, wide, wide,
            pl.BlockSpec((rows, 1), lambda i: (count - 1 - i, 0)),
            whole3, row,
            pl.BlockSpec((rows, states, groups, LANES), lambda i: (count - 1 - i, 0, 0, 0)),
            pl.BlockSpec((1, states, groups, LANES), lambda i: (count - 1 - i, 0, 0, 0)),
        ] + [anywhere] * len(extra),
        out_specs=[wide, wide, pl.BlockSpec((rows, LANES), lambda i: (count - 1 - i, 0)), whole3, row]
        + [anywhere] * len(extra),
        out_shape=[
            jax.ShapeDtypeStruct((tokens, channels), jnp.bfloat16),
            jax.ShapeDtypeStruct((tokens, channels), jnp.float32),
            jax.ShapeDtypeStruct((tokens, LANES), jnp.float32),
            jax.ShapeDtypeStruct((states, groups, LANES), jnp.float32),
            jax.ShapeDtypeStruct((1, channels), jnp.float32),
        ] + extra_shapes,
        scratch_shapes=[small(), small(), small(), long(), long(), long(), long(), long(),
                        pltpu.VMEM((rows, 2 * states * groups, LANES), jnp.bfloat16),
                        pltpu.VMEM((rows, 2 * states * groups), jnp.float32)] + extra_scratch,
        cost_estimate=pl.CostEstimate(flops=60 * tokens * channels * states,
                                      bytes_accessed=4 * tokens * channels * states,
                                      transcendentals=tokens * channels * states),
        compiler_params=pltpu.CompilerParams(vmem_limit_bytes=52 * 1024 * 1024, **settings),
        name="scan_backward",
    )(bc, pre, act, mixed, keep, a_log3, skip, h, starts, *extra)
    if joined:
        outs = list(outs[:6]) + [outs[6].reshape(tokens, z_part.shape[1])]
    return outs


def writer_kernel(place, side, depth, where_ref, pieces_ref, *rest):
    out_ref, wide_scr, sems = rest[-3:]
    x, y, core = where_ref[0], where_ref[1], where_ref[2]
    copies = []
    for mode in range(2):
        for owner in range(2):
            c = core if owner == 0 else 1 - core
            for k in range(4):
                qx = x if k in (0, 1) else 1 - x
                qy = y if k in (0, 2) else 1 - y
                row = (qx * 2 + qy if mode == 0 else qy * 2 + qx) * side
                at = (mode * 2 + owner) * 4 + k
                wide_scr[at] = pieces_ref[mode, owner, k].astype(jnp.float32)
                if place == "columns":
                    target = out_ref.at[mode, pl.ds(pl.multiple_of(row, side), side),
                                        pl.ds(pl.multiple_of(c * depth, depth), depth)]
                else:
                    target = out_ref.at[mode, pl.ds(pl.multiple_of(c * 4 * side + row, side), side), place, :]
                copies.append(pltpu.make_async_copy(wide_scr.at[at], target, sems.at[at]))
                copies[-1].start()
    for copy in copies:
        copy.wait()


def write_out(place, shape, where, pieces, filled):
    side, depth = pieces.shape[3:]
    held = [] if filled is None else [filled]
    return pl.pallas_call(
        functools.partial(writer_kernel, place, side, depth),
        in_specs=[pl.BlockSpec(memory_space=pltpu.SMEM), pl.BlockSpec(memory_space=pltpu.VMEM)]
        + [pl.BlockSpec(memory_space=pl.ANY)] * len(held),
        out_specs=pl.BlockSpec(memory_space=pl.ANY),
        out_shape=jax.ShapeDtypeStruct(shape, jnp.float32),
        input_output_aliases={2: 0} if held else {},
        scratch_shapes=[pltpu.VMEM((16, side, depth), jnp.float32), pltpu.SemaphoreType.DMA((16,))],
        cost_estimate=pl.CostEstimate(flops=16 * side * depth, bytes_accessed=16 * side * depth * 6, transcendentals=0),
        compiler_params=pltpu.CompilerParams(vmem_limit_bytes=48 * 1024 * 1024),
        name="write_grads",
    )(where, pieces, *held)


def lagged(values, offset):
    padding = [(offset, 0)] + [(0, 0)] * (values.ndim - 1)
    return jnp.pad(values, padding)[: values.shape[0]]


def leading(values, offset):
    padding = [(0, offset)] + [(0, 0)] * (values.ndim - 1)
    return jnp.pad(values, padding)[offset:]


def pick_dot(left_side, weights, first_mode):
    first_part = jnp.dot(left_side, weights[0], preferred_element_type=jnp.float32)
    second_part = jnp.dot(left_side, weights[1], preferred_element_type=jnp.float32)
    return jnp.where(first_mode, first_part, second_part)


def pick_back(gradient, weights, first_mode):
    dims = (((1,), (1,)), ((), ()))
    first_part = lax.dot_general(gradient, weights[0], dims, preferred_element_type=jnp.float32)
    second_part = lax.dot_general(gradient, weights[1], dims, preferred_element_type=jnp.float32)
    return jnp.where(first_mode, first_part, second_part)


def weight_grads(left_side, gradient, first_mode):
    nothing = jnp.zeros_like(gradient)
    dims = (((0,), (0,)), ((), ()))
    first_part = lax.dot_general(
        left_side,
        jnp.where(first_mode, gradient, nothing),
        dims,
        preferred_element_type=jnp.float32,
    )
    second_part = lax.dot_general(
        left_side,
        jnp.where(first_mode, nothing, gradient),
        dims,
        preferred_element_type=jnp.float32,
    )
    return jnp.stack([first_part, second_part])


def finish_rows(normed_grad, hidden, inverse, cotan, norm_gain):
    scaled = normed_grad * norm_gain
    gain_terms = jnp.sum(normed_grad * hidden * inverse, axis=0)
    cubed = inverse * inverse * inverse
    rows = (
        cotan + inverse * scaled - hidden * cubed * jnp.mean(scaled * hidden, axis=1, keepdims=True)
    )
    return (rows.astype(jnp.bfloat16), gain_terms)


def swap(values, distance):
    return lax.ppermute(values, "dp", [(i, i ^ distance) for i in range(8)])


CORE = 1


def tie(values, *others):
    return lax.optimization_barrier((values,) + others)[0]


def z_sum(values, size, dtype=jnp.bfloat16):
    distance = 1
    while distance < size:
        low = values.astype(dtype)
        got = lax.ppermute(low, "tensor", [(i, i ^ distance) for i in range(size)])
        values = low.astype(jnp.float32) + got.astype(jnp.float32)
        distance *= 2
    return values


def shards(names, hidden_in, segment_ids, modality, norm_gain, in_proj, conv_weight, conv_bias, x_proj, dt_proj, dt_bias,
           a_log, skip_gain, out_proj, out_grad):
    tokens, model_width = hidden_in.shape
    conv_taps, channels = conv_weight.shape
    rank_dim = dt_proj.shape[1]
    state_dim = a_log.shape[0]
    groups = channels // LANES
    ways = names["tensor"]
    by_hand = names["dp"] == 8 and names["tensor"] == 4
    low = jnp.bfloat16
    rank = lax.axis_index("dp")
    core, x_at, y_at = rank % 2, (rank // 2) % 2, rank // 4
    where = jnp.stack([x_at, y_at, core]).astype(jnp.int32)
    half_width = model_width // 2
    first_mode = (modality == 0)[:, None]
    nothing = jnp.zeros((), low)
    dims = (((0,), (0,)), ((), ()))

    def col_half(values, which):
        return lax.dynamic_slice_in_dim(values, which * half_width, half_width, 1)

    def pair_half(values):
        return jnp.concatenate([col_half(values, core), swap(col_half(values, 1 - core), CORE)], axis=0)

    def pair_all(values):
        return jnp.concatenate([values, swap(values, CORE)], axis=0)

    def masked_products(left, right, modes, mask_left):
        products = []
        for chosen in (modes, jnp.logical_not(modes)):
            one = jnp.where(chosen, left, nothing) if mask_left else left
            two = right if mask_left else jnp.where(chosen, right, nothing)
            products.append(lax.dot_general(one, two, dims, preferred_element_type=jnp.float32).astype(low))
        return jnp.stack(products)

    same_doc = [jnp.ones((tokens, 1), jnp.float32)]
    for offset in range(1, conv_taps):
        earlier_seg = jnp.pad(segment_ids, (offset, 0), constant_values=-1)[:tokens]
        same_doc.append((earlier_seg == segment_ids).astype(jnp.float32)[:, None])
    if by_hand:
        modes_own = jnp.broadcast_to(jnp.stack([first_mode, jnp.logical_not(first_mode)]), (2, tokens, LANES)).astype(low)
        x_wide = jnp.pad(jnp.swapaxes(x_proj, 1, 2), ((0, 0), (0, 96), (0, 0)))
        facts = jnp.concatenate([first_mode.astype(jnp.float32)] + same_doc[1:], axis=1)
        (in_inner, in_gate, normed_b, inverse, conv_sum, inner_x, activated_b, gate_z, gated_grad, rank_b, coeffs) = front(
            hidden_in, norm_gain[None], conv_weight, conv_bias[None], facts, modes_own, x_wide, out_grad, in_proj, out_proj,
            2 * state_dim)
        coeffs = coeffs[:, :2 * state_dim]
        sib_mode = swap(first_mode.astype(jnp.float32), CORE) > 0.5
        pair_mode = jnp.concatenate([first_mode, sib_mode], axis=0)
        normed_pair = pair_half(normed_b)
        cotan_pair = pair_half(tie(out_grad, rank_b))
    else:
        hidden = hidden_in.astype(jnp.float32)
        inverse = lax.rsqrt(jnp.mean(hidden * hidden, axis=1, keepdims=True) + EPS)
        normed_b = (hidden * inverse * norm_gain).astype(low)
        in_inner = in_proj[:, :, 0, :]
        in_gate = in_proj[:, :, 1, :]
        inner_x = pick_dot(normed_b, in_inner, first_mode)
        conv_sum = conv_bias + conv_weight[conv_taps - 1] * inner_x
        for offset in range(1, conv_taps):
            conv_sum = conv_sum + conv_weight[conv_taps - 1 - offset] * lagged(inner_x, offset) * same_doc[offset]
        activated_b = jax.nn.silu(conv_sum).astype(low)
        projected = z_sum(pick_dot(activated_b, x_proj, first_mode), ways)
        rank_b = projected[:, :rank_dim].astype(low)
        coeffs = projected[:, rank_dim:]
        gate_z = pick_dot(normed_b, in_gate, first_mode)
        gated_grad = pick_back(out_grad, out_proj, first_mode)
    step_pre = pick_dot(rank_b, dt_proj, first_mode) + jnp.where(first_mode, dt_bias[0], dt_bias[1])
    keep = same_doc[1]
    a_log3 = a_log.reshape(state_dim, groups, LANES)
    skip_row = skip_gain[None]
    gated_b, gate_grad_b, mixed_grad, states, starts = scan_forward(
        coeffs, step_pre, activated_b, gate_z, gated_grad, keep, a_log3, skip_row)
    partial_out = pick_dot(gated_b, out_proj, first_mode).astype(low)
    if by_hand:
        gated_pair = pair_all(gated_b)
        ggrad_pair = pair_all(gate_grad_b)
        out_product = masked_products(gated_pair, cotan_pair, pair_mode, True)
        back = scan_backward(coeffs, step_pre, activated_b, mixed_grad, keep, a_log3, skip_row, states, starts,
                             out_product, partial_out)
        summed_out, out_shared = back[6], back[5]
    else:
        back = scan_backward(coeffs, step_pre, activated_b, mixed_grad, keep, a_log3, skip_row, states, starts)
        summed_out = lax.psum(partial_out, "tensor")
        out_proj_grad = lax.psum(weight_grads(gated_b, out_grad, first_mode).astype(low), "dp").astype(jnp.float32)
        gate_proj_grad = lax.psum(weight_grads(normed_b, gate_grad_b, first_mode).astype(low), "dp")
    pre_grad_b, act_part, coeff_grad, sums, skips = back[:5]
    a_log_grad = sums.reshape(state_dim, channels) * -jnp.exp(a_log)
    mode_rows = x_proj.shape[2] + rank_dim
    if by_hand:
        later = jnp.stack([same_doc[0]] + [leading(same_doc[k], k) for k in range(1, conv_taps)], axis=1)[:, :, 0]
        modes = jnp.broadcast_to(jnp.stack([pair_mode, jnp.logical_not(pair_mode)]), (2, 2 * tokens, LANES)).astype(low)
        row_facts = jnp.concatenate([inverse[:, :1], first_mode.astype(jnp.float32)], axis=1)
        rows, normed_low, gate_own, inner_product, _ = middle(
            pre_grad_b, act_part, coeff_grad, conv_sum, inner_x, activated_b, rank_b, dt_proj, x_wide, conv_weight, later, modes,
            ggrad_pair, jnp.swapaxes(normed_pair, 0, 1), row_facts, jnp.concatenate([a_log_grad, skips], axis=0), hidden_in,
            in_gate, in_inner)
    else:
        pre_grad = pre_grad_b.astype(jnp.float32)
        dt_bias_grad = jnp.stack([
            jnp.sum(jnp.where(first_mode, pre_grad, 0.0), axis=0),
            jnp.sum(jnp.where(first_mode, 0.0, pre_grad), axis=0)])
        rank_part = pick_back(pre_grad_b, dt_proj, first_mode)
        proj_grad_b = z_sum(jnp.concatenate([rank_part, coeff_grad[:, :2 * state_dim]], axis=1), ways).astype(low)
        act_grad = act_part + pick_back(proj_grad_b, x_proj, first_mode)
        sig_conv = jax.nn.sigmoid(conv_sum)
        conv_grad = act_grad * sig_conv * (1.0 + conv_sum * (1.0 - sig_conv))
        conv_bias_grad = jnp.sum(conv_grad, axis=0)
        weight_rows = []
        x_grad = jnp.zeros_like(inner_x)
        for tap_index in range(conv_taps):
            offset = conv_taps - 1 - tap_index
            masked = conv_grad * same_doc[offset]
            weight_rows.append(jnp.sum(masked * lagged(inner_x, offset), axis=0))
            x_grad = x_grad + conv_weight[tap_index] * leading(masked, offset)
        x_grad_b = x_grad.astype(low)
        normed_part = pick_back(x_grad_b, in_inner, first_mode) + pick_back(gate_grad_b, in_gate, first_mode)
        gain_part = jnp.sum(normed_part * (hidden * inverse), axis=0).reshape(-1, channels)
        gain_part = lax.psum(gain_part, "tensor")
        small_modes = jnp.concatenate([
            weight_grads(proj_grad_b, activated_b, first_mode), weight_grads(rank_b, pre_grad_b, first_mode)], axis=1)
        rows = jnp.concatenate([small_modes.reshape(-1, channels), jnp.stack(weight_rows), conv_bias_grad[None], dt_bias_grad,
                                a_log_grad, skips, gain_part], axis=0).astype(low)
    summed_rows = lax.psum(rows, "dp")
    if by_hand:
        (gate_shared, inner_shared), normed_sum = tail_exchange([gate_own, inner_product], normed_low)

        output, input_grad = finish(hidden_in, out_grad, inverse, norm_gain[None], summed_out, normed_sum)
        where = tie(where, summed_rows)
        out_proj_grad = write_out("columns", (2, channels, model_width), where, out_shared, None)
        in_shape = (2, model_width, 2, channels)
        in_proj_grad = write_out(1, in_shape, where, gate_shared, None)
        in_proj_grad = write_out(0, in_shape, where, inner_shared, in_proj_grad)
    else:
        inner_proj_grad = lax.psum(weight_grads(normed_b, x_grad_b, first_mode).astype(low), "dp")
        in_proj_grad = jnp.stack([inner_proj_grad, gate_proj_grad], axis=2).astype(jnp.float32)
        normed_sum = lax.psum(normed_part.astype(low), "tensor")
        output = (hidden + summed_out.astype(jnp.float32)).astype(low)
        cotan = out_grad.astype(jnp.float32)
        input_grad, _ = finish_rows(normed_sum.astype(jnp.float32), hidden, inverse, cotan, norm_gain)
    summed_rows = summed_rows.astype(jnp.float32)
    small_modes, rows = summed_rows[:2 * mode_rows].reshape(2, mode_rows, channels), summed_rows[2 * mode_rows:]
    x_proj_grad = jnp.swapaxes(small_modes[:, :-rank_dim], 1, 2)
    dt_proj_grad = small_modes[:, -rank_dim:]
    norm_gain_grad = rows[conv_taps + 4 + state_dim:].reshape(-1)[:model_width]
    at = conv_taps + 1
    return (output, input_grad, norm_gain_grad, in_proj_grad, rows[:conv_taps], rows[conv_taps], x_proj_grad,
            dt_proj_grad, rows[at:at + 2], rows[at + 2:at + 2 + state_dim], rows[at + 2 + state_dim], out_proj_grad)


def solution(mesh):
    in_specs = (
        P("dp", None),
        P("dp"),
        P("dp"),
        P(),
        P(None, None, None, "tensor"),
        P(None, "tensor"),
        P("tensor"),
        P(None, "tensor", None),
        P(None, None, "tensor"),
        P(None, "tensor"),
        P(None, "tensor"),
        P("tensor"),
        P(None, "tensor", None),
        P("dp", None),
    )
    out_specs = (
        P("dp", None),
        P("dp", None),
        P(),
        P(None, None, None, "tensor"),
        P(None, "tensor"),
        P("tensor"),
        P(None, "tensor", None),
        P(None, None, "tensor"),
        P(None, "tensor"),
        P(None, "tensor"),
        P("tensor"),
        P(None, "tensor", None),
    )
    names = dict(mesh.shape)
    return jax.shard_map(functools.partial(shards, names), mesh=mesh, in_specs=in_specs, out_specs=out_specs, check_vma=False)
```

```python
import functools

import jax
import jax.numpy as jnp
from jax import lax
from jax.experimental import pallas as pl
from jax.experimental.pallas import tpu as pltpu
from jax.sharding import PartitionSpec as P

EPS = 1e-05

LANES = 128
BIG = 1000.0
LOG2E = 1.4426950408889634


def softplus(v):
    return jnp.maximum(v, 0.0) + jnp.log1p(jnp.exp(-jnp.abs(v)))


def spread_rows(scratch, values, groups):
    rows = values.shape[0]
    for g in range(groups):
        scratch[pl.ds(g, rows, stride=groups), :] = values[:, g * LANES:(g + 1) * LANES]


def gather_rows(scratch, rows, groups):
    return jnp.concatenate(
        [scratch[pl.ds(g, rows, stride=groups), :] for g in range(groups)], axis=1)


def scan_forward_kernel(states, groups, rows, unroll, count, joined,
                        bc_ref, pre_ref, act_ref, z_ref, gg_ref, keep_ref, alog_ref, skip_ref, mode_ref,
                        gated_ref, ggrad_ref, mixed_ref, h_ref, start_ref, *rest):
    chunk = pl.program_id(0)
    if joined:
        split_ref, rate_scr, state_scr, sk_scr, u_scr, y_scr, gated_all, ggrad_all, send_sems, recv_sems, local_sems = rest
        tokens = rows * count
        to_core = place()[4]

        def pair_copies(at, i):
            source, target = ((gated_all, gated_ref), (ggrad_all, ggrad_ref))[i]
            base = at * rows
            return (pltpu.make_async_copy(source.at[pl.ds(base, rows)], target.at[pl.ds(base, rows)], local_sems.at[at, i]),
                    pltpu.make_async_remote_copy(
                        src_ref=source.at[pl.ds(base, rows)], dst_ref=target.at[pl.ds(tokens + base, rows)],
                        send_sem=send_sems.at[at, i], recv_sem=recv_sems.at[at, i], device_id=to_core, device_id_type=MESH))

        @pl.when(chunk == 0)
        def _():
            barrier = pltpu.get_barrier_semaphore()
            pl.semaphore_signal(barrier, inc=1, device_id=to_core, device_id_type=MESH)
            pl.semaphore_wait(barrier, 1)
    else:
        rate_scr, state_scr, sk_scr, u_scr, y_scr = rest

    @pl.when(chunk == 0)
    def _():
        rate_scr[...] = jnp.exp(alog_ref[...]) * (-LOG2E)
        state_scr[...] = jnp.zeros_like(state_scr)

    step = softplus(pre_ref[...])
    act = act_ref[...].astype(jnp.float32)
    spread_rows(u_scr, step * act, groups)
    spread_rows(sk_scr, jnp.where(keep_ref[...] > 0.0, step, BIG), groups)
    start_ref[0] = state_scr[...]

    def one(t, held):
        at = pl.multiple_of(t * groups, groups)
        sk = sk_scr[pl.ds(at, groups), :]
        u = u_scr[pl.ds(at, groups), :]
        y = jnp.zeros_like(u)
        new = []
        for n in range(states):
            h = jnp.exp2(sk * rate_scr[n]) * held[n] + u * bc_ref[t, n]
            h_ref[t, n] = h
            y = y + h * bc_ref[t, states + n]
            new.append(h)
        y_scr[pl.ds(at, groups), :] = y
        return tuple(new)

    last = lax.fori_loop(0, rows, one, tuple(state_scr[n] for n in range(states)), unroll=unroll)
    for n in range(states):
        state_scr[n] = last[n]
    mixed_out = gather_rows(y_scr, rows, groups) + skip_ref[...] * act
    z = z_ref[...].astype(jnp.float32)
    gg = gg_ref[...].astype(jnp.float32)
    sig = jax.nn.sigmoid(z)
    silu = z * sig
    gated = mixed_out * silu
    gate_grad = (gg * mixed_out * sig * (1.0 + z * (1.0 - sig))).astype(ggrad_ref.dtype)
    mixed_ref[...] = gg * silu
    if joined:
        channels = gated.shape[1]
        first = mode_ref[...]
        split_ref[:, 0:channels] = (gated * first).astype(split_ref.dtype)
        split_ref[:, channels:2 * channels] = (gated * (1.0 - first)).astype(split_ref.dtype)
        at = pl.ds(pl.multiple_of(chunk * rows, rows), rows)
        gated_all[at, :] = gated.astype(gated_ref.dtype)
        ggrad_all[at, :] = gate_grad
        for k in range(count):
            @pl.when(chunk == k)
            def _():
                for i in range(2):
                    for copy in pair_copies(k, i):
                        copy.start()

        @pl.when(chunk == count - 1)
        def _():
            for k in range(count):
                for i in range(2):
                    for copy in pair_copies(k, i):
                        copy.wait()
    else:
        gated_ref[...] = gated.astype(gated_ref.dtype)
        ggrad_ref[...] = gate_grad


def scan_forward(bc, pre, act, z, gg, keep, a_log3, skip, mode, joined, rows=64, unroll=4):
    tokens, channels = pre.shape
    groups = channels // LANES
    states = a_log3.shape[0]
    count = tokens // rows
    wide = pl.BlockSpec((rows, channels), lambda i: (i, 0))
    thin = pl.BlockSpec((rows, 1), lambda i: (i, 0))
    whole3 = pl.BlockSpec((states, groups, LANES), lambda i: (0, 0, 0))
    low, f32 = jnp.bfloat16, jnp.float32
    long = lambda: pltpu.VMEM((rows * groups, LANES), f32)
    small = lambda: pltpu.VMEM((states, groups, LANES), f32)
    anywhere = pl.BlockSpec(memory_space=pl.ANY)
    tall = 2 * tokens if joined else tokens
    settings = dict(collective_id=5, has_side_effects=True) if joined else {}
    return pl.pallas_call(
        functools.partial(scan_forward_kernel, states, groups, rows, unroll, count, joined),
        grid=(count,),
        in_specs=[
            pl.BlockSpec((rows, 2 * states), lambda i: (i, 0), memory_space=pltpu.SMEM),
            wide, wide, wide, wide, thin, whole3,
            pl.BlockSpec((1, channels), lambda i: (0, 0)), thin,
        ],
        out_specs=[
            anywhere if joined else wide, anywhere if joined else wide, wide,
            pl.BlockSpec((rows, states, groups, LANES), lambda i: (i, 0, 0, 0)),
            pl.BlockSpec((1, states, groups, LANES), lambda i: (i, 0, 0, 0)),
        ] + ([pl.BlockSpec((rows, 2 * channels), lambda i: (i, 0))] if joined else []),
        out_shape=[
            jax.ShapeDtypeStruct((tall, channels), low),
            jax.ShapeDtypeStruct((tall, channels), low),
            jax.ShapeDtypeStruct((tokens, channels), f32),
            jax.ShapeDtypeStruct((tokens, states, groups, LANES), f32),
            jax.ShapeDtypeStruct((count, states, groups, LANES), f32),
        ] + ([jax.ShapeDtypeStruct((tokens, 2 * channels), low)] if joined else []),
        scratch_shapes=[small(), small(), long(), long(), long()] + ([
            pltpu.VMEM((tokens, channels), low), pltpu.VMEM((tokens, channels), low),
            pltpu.SemaphoreType.DMA((count, 2)), pltpu.SemaphoreType.DMA((count, 2)), pltpu.SemaphoreType.DMA((count, 2)),
        ] if joined else []),
        compiler_params=pltpu.CompilerParams(vmem_limit_bytes=48 * 1024 * 1024, **settings),
        name="scan_forward",
    )(bc, pre, act, z, gg, keep, a_log3, skip, mode)


MESH = pl.DeviceIdType.MESH
DMA = pltpu.SemaphoreType.DMA


def add_rows(target, left, right, rows, slab):
    def body(i, nothing):
        at = pl.ds(pl.multiple_of(i * slab, slab), slab)
        target[at, :] = (left[at, :].astype(jnp.float32) + right[at, :].astype(jnp.float32)).astype(jnp.bfloat16)
        return nothing
    lax.fori_loop(0, rows // slab, body, 0)


def place():
    dp = lax.axis_index("dp")
    x, y, core = (dp // 2) % 2, dp // 4, dp % 2
    return x, y, {"dp": dp + 2 - 4 * x}, {"dp": dp + 4 - 8 * y}, {"dp": dp + 1 - 2 * core}


def greet():
    z = lax.axis_index("tensor")
    barrier = pltpu.get_barrier_semaphore()
    for target in place()[2:]:
        pl.semaphore_signal(barrier, inc=1, device_id=target, device_id_type=MESH)

    @pl.when(z > 0)
    def _():
        pl.semaphore_signal(barrier, inc=1, device_id={"tensor": z - 1}, device_id_type=MESH)

    @pl.when(z < 3)
    def _():
        pl.semaphore_signal(barrier, inc=1, device_id={"tensor": z + 1}, device_id_type=MESH)

    @pl.when((z > 0) & (z < 3))
    def _():
        pl.semaphore_wait(barrier, 5)

    @pl.when((z == 0) | (z == 3))
    def _():
        pl.semaphore_wait(barrier, 4)


class Exchange:
    def __init__(self, prod, out, held, half_buf, quarter_buf, sems, summed=None):
        self.summed = summed
        self.prod, self.held, self.half_buf, self.quarter_buf = prod, held, half_buf, quarter_buf
        self.out, self.own = out
        (self.half_send, self.half_recv, self.quarter_send, self.quarter_recv,
         self.share_send, self.share_recv, self.core_send, self.core_recv, self.local) = sems
        x, y, self.to_x, self.to_y, self.to_core = place()
        self.firsts, self.seconds = (x, y), (y, x)
        self.ways = ((self.to_x, self.to_y), (self.to_y, self.to_x))
        self.side = half_buf.shape[2]

    @staticmethod
    def scratch(side, depth):
        low = jnp.bfloat16
        return [pltpu.VMEM((2, 2, side, depth), low), pltpu.VMEM((2, 2, side, depth), low), pltpu.VMEM((2, side, depth), low),
                DMA((2, 2)), DMA((2, 2)), DMA((2,)), DMA((2,)), DMA((2, 4)), DMA((2, 4)), DMA((2, 4)), DMA((2, 4)), DMA((2, 3))]

    def rows(self, mode, k, mine):
        first, second = self.firsts[mode], self.seconds[mode]
        half = first if mine else 1 - first
        quarter = 1 - second if k == 0 else second
        return pl.ds(pl.multiple_of((half * 2 + quarter) * self.side, self.side), self.side)

    def half_copy(self, mode, k):
        return pltpu.make_async_remote_copy(
            src_ref=self.prod[mode].at[self.rows(mode, k, False)], dst_ref=self.half_buf.at[mode, k],
            send_sem=self.half_send.at[mode, k], recv_sem=self.half_recv.at[mode, k],
            device_id=self.ways[mode][0], device_id_type=MESH)

    def keep_copy(self, mode, k):
        return pltpu.make_async_copy(self.prod[mode].at[self.rows(mode, k, True)], self.held.at[mode, k], self.local.at[mode, k])

    def quarter_copy(self, mode):
        return pltpu.make_async_remote_copy(
            src_ref=self.half_buf.at[mode, 0], dst_ref=self.quarter_buf.at[mode],
            send_sem=self.quarter_send.at[mode], recv_sem=self.quarter_recv.at[mode],
            device_id=self.ways[mode][1], device_id_type=MESH)

    def share_copy(self, mode, k):
        own = self.held.at[mode, 1]
        if k == 3:
            source, way = (self.out.at[mode, 0, 1], self.to_x) if mode == 0 else (self.out.at[mode, 0, 2], self.to_y)
        else:
            source, way = own, self.to_y if k == 1 else self.to_x
        return pltpu.make_async_remote_copy(
            src_ref=source, dst_ref=self.out.at[mode, 0, k], send_sem=self.share_send.at[mode, k],
            recv_sem=self.share_recv.at[mode, k], device_id=way, device_id_type=MESH)

    def core_copy(self, mode, k):
        return pltpu.make_async_remote_copy(
            src_ref=self.held.at[mode, 1] if k == 0 else self.out.at[mode, 0, k], dst_ref=self.out.at[mode, 1, k],
            send_sem=self.core_send.at[mode, k], recv_sem=self.core_recv.at[mode, k],
            device_id=self.to_core, device_id_type=MESH)

    def out_copy(self, mode):
        return pltpu.make_async_copy(self.held.at[mode, 1], self.own.at[mode], self.local.at[mode, 2])

    def start_shares(self, mode):
        for k in ((1, 2) if mode == 0 else (2, 1)):
            self.share_copy(mode, k).start()
        self.core_copy(mode, 0).start()
        self.out_copy(mode).start()

    def event(self, number):
        if number == 0:
            for k in range(2):
                for mode in range(2):
                    self.half_copy(mode, k).start()
                    self.keep_copy(mode, k).start()
        elif number == 1:
            for mode in range(2):
                self.keep_copy(mode, 0).wait()
                self.half_copy(mode, 0).wait_recv()
                add_rows(self.half_buf.at[mode, 0], self.half_buf.at[mode, 0], self.held.at[mode, 0], self.side, 32)
                self.quarter_copy(mode).start()
        elif number == 2:
            for mode in range(2):
                self.keep_copy(mode, 1).wait()
                self.half_copy(mode, 1).wait_recv()
                add_rows(self.half_buf.at[mode, 1], self.half_buf.at[mode, 1], self.held.at[mode, 1], self.side, 32)
        elif number == 3:
            for mode in range(2):
                self.quarter_copy(mode).wait_recv()
                add_rows(self.held.at[mode, 1], self.half_buf.at[mode, 1], self.quarter_buf.at[mode], self.side, 32)
                self.start_shares(mode)
        elif number == 4:
            for mode in range(2):
                k = 1 if mode == 0 else 2
                self.share_copy(mode, k).wait_recv()
                self.share_copy(mode, 3).start()
                self.core_copy(mode, k).start()
        elif number == 5:
            for mode in range(2):
                k = 2 if mode == 0 else 1
                self.share_copy(mode, k).wait_recv()
                self.core_copy(mode, k).start()
        elif number == 6:
            for mode in range(2):
                self.share_copy(mode, 3).wait_recv()
                self.core_copy(mode, 3).start()
        elif number == 8:
            for mode in range(2):
                pltpu.make_async_copy(self.prod.at[mode], self.held.at[mode, 1], self.local.at[mode, 1]).start()
        elif number == 9:
            for mode in range(2):
                pltpu.make_async_copy(self.prod.at[mode], self.held.at[mode, 1], self.local.at[mode, 1]).wait()
                self.start_shares(mode)
        elif number == 7:
            for mode in range(2):
                if self.summed is None:
                    for k in range(2):
                        self.half_copy(mode, k).wait_send()
                    self.quarter_copy(mode).wait_send()
                for k in range(1, 4):
                    self.share_copy(mode, k).wait_send()
                for k in range(4):
                    self.core_copy(mode, k).wait_send()
                    self.core_copy(mode, k).wait_recv()
                self.out_copy(mode).wait()


class Share:
    def __init__(self, own, out, sems):
        self.own, self.out = own, out
        self.share_send, self.share_recv, self.core_send, self.core_recv = sems
        _, _, self.to_x, self.to_y, self.to_core = place()

    @staticmethod
    def scratch():
        return [DMA((2, 4)), DMA((2, 4)), DMA((2, 4)), DMA((2, 4))]

    def share_copy(self, mode, k):
        if k == 3:
            source, way = (self.out.at[mode, 0, 1], self.to_x) if mode == 0 else (self.out.at[mode, 0, 2], self.to_y)
        else:
            source, way = self.own.at[mode], self.to_y if k == 1 else self.to_x
        return pltpu.make_async_remote_copy(
            src_ref=source, dst_ref=self.out.at[mode, 0, k], send_sem=self.share_send.at[mode, k],
            recv_sem=self.share_recv.at[mode, k], device_id=way, device_id_type=MESH)

    def core_copy(self, mode, k):
        return pltpu.make_async_remote_copy(
            src_ref=self.own.at[mode] if k == 0 else self.out.at[mode, 0, k], dst_ref=self.out.at[mode, 1, k],
            send_sem=self.core_send.at[mode, k], recv_sem=self.core_recv.at[mode, k],
            device_id=self.to_core, device_id_type=MESH)

    def event(self, number):
        for mode in range(2):
            early, late = (1, 2) if mode == 0 else (2, 1)
            if number == 0:
                self.share_copy(mode, early).start()
                self.share_copy(mode, late).start()
                self.core_copy(mode, 0).start()
            elif number == 1:
                self.share_copy(mode, early).wait_recv()
                self.share_copy(mode, 3).start()
                self.core_copy(mode, early).start()
            elif number == 2:
                self.share_copy(mode, late).wait_recv()
                self.core_copy(mode, late).start()
            elif number == 3:
                self.share_copy(mode, 3).wait_recv()
                self.core_copy(mode, 3).start()
            else:
                for k in range(1, 4):
                    self.share_copy(mode, k).wait_send()
                for k in range(4):
                    self.core_copy(mode, k).wait_send()
                    self.core_copy(mode, k).wait_recv()


class Reduce(Exchange):
    def __init__(self, prod, own, held, half_buf, quarter_buf, sems):
        half_send, half_recv, quarter_send, quarter_recv, keep = sems
        super().__init__(prod, (None, own), held, half_buf, quarter_buf,
                         (half_send, half_recv, quarter_send, quarter_recv, None, None, None, None, keep))

    @staticmethod
    def scratch(side, depth):
        low = jnp.bfloat16
        return [pltpu.VMEM((2, 2, side, depth), low), pltpu.VMEM((2, 2, side, depth), low), pltpu.VMEM((2, side, depth), low),
                DMA((2, 2)), DMA((2, 2)), DMA((2,)), DMA((2,)), DMA((2, 3))]

    def last(self):
        for mode in range(2):
            self.quarter_copy(mode).wait_recv()
            add_rows(self.held.at[mode, 1], self.half_buf.at[mode, 1], self.quarter_buf.at[mode], self.side, 32)
            pltpu.make_async_copy(self.held.at[mode, 1], self.own.at[mode], self.local.at[mode, 2]).start()

    def done(self):
        for mode in range(2):
            for k in range(2):
                self.half_copy(mode, k).wait_send()
            self.quarter_copy(mode).wait_send()
            pltpu.make_async_copy(self.held.at[mode, 1], self.own.at[mode], self.local.at[mode, 2]).wait()


class LineReduce:
    def __init__(self, part, own, acc, red, sems):
        red_send, red_recv, local = sems
        self.line = LineSum(part, own, acc, red, (red_send, red_recv, None, None, local))

    @staticmethod
    def scratch(pieces, rows, width):
        low = jnp.bfloat16
        return [pltpu.VMEM((2, pieces, rows, width), low), pltpu.VMEM((2, pieces, rows, width), low),
                DMA((2, pieces)), DMA((2, pieces)), DMA((2,))]

    def step(self, c, half):
        line = self.line
        begins, ends = line.place_of(half)

        @pl.when(jnp.logical_not(begins))
        def _():
            line.red_copy(half, c).wait_recv()
            add_rows(line.acc.at[half, c], line.acc.at[half, c], line.red.at[half, c], line.rows, 16)

            @pl.when(jnp.logical_not(ends))
            def _():
                line.red_copy(half, c).start()

    def turn(self, turn):
        line = self.line
        at_end = (line.z == 0) | (line.z == 3)
        if 0 <= turn - 2 < line.pieces:
            self.step(turn - 2, line.near)
        if 0 <= turn - 4 < line.pieces:
            @pl.when(jnp.logical_not(at_end))
            def _():
                self.step(turn - 4, 1 - line.near)
        if 0 <= turn - 6 < line.pieces:
            @pl.when(at_end)
            def _():
                self.step(turn - 6, 1 - line.near)

    def done(self):
        line = self.line
        for half in range(2):
            begins, ends = line.place_of(half)

            @pl.when(ends)
            def _():
                line.own(half).start()
                line.own(half).wait()

            @pl.when(jnp.logical_not(ends))
            def _():
                for c in range(line.pieces):
                    line.red_copy(half, c).wait_send()


class LineBack:
    def __init__(self, res, sems):
        self.res = res
        self.send, self.recv = sems
        self.z = lax.axis_index("tensor")
        self.near = jnp.where(self.z < 2, 1, 0)
        self.pieces = res.shape[1]

    @staticmethod
    def scratch(pieces):
        return [DMA((2, pieces)), DMA((2, pieces))]

    def place_of(self, half):
        along = jnp.where(half == 0, 3 - self.z, self.z)
        return along == 0, along == 3

    def copy(self, half, c):
        return pltpu.make_async_remote_copy(
            src_ref=self.res.at[half, c], dst_ref=self.res.at[half, c], send_sem=self.send.at[half, c],
            recv_sem=self.recv.at[half, c], device_id={"tensor": self.z - 2 * half + 1}, device_id_type=MESH)

    def begin(self, pieces):
        for half in range(2):
            _, ends = self.place_of(half)

            @pl.when(ends)
            def _():
                for c in pieces:
                    self.copy(half, c).start()

    def step(self, c, half):
        begins, ends = self.place_of(half)

        @pl.when(jnp.logical_not(ends | begins))
        def _():
            self.copy(half, c).wait_recv()
            self.copy(half, c).start()

    def some(self, pieces, far):
        for c in pieces:
            self.step(c, 1 - self.near if far else self.near)

    def done(self):
        for half in range(2):
            begins, ends = self.place_of(half)

            @pl.when(begins)
            def _():
                for c in range(self.pieces):
                    self.copy(half, c).wait_recv()

            @pl.when(jnp.logical_not(begins))
            def _():
                for c in range(self.pieces):
                    self.copy(half, c).wait_send()


AHEAD = 2


class LineSum:
    def __init__(self, part, res, acc, red, sems):
        self.part, self.res, self.acc, self.red = part, res, acc, red
        self.red_send, self.red_recv, self.back_send, self.back_recv, self.local = sems
        self.z = lax.axis_index("tensor")
        self.near = jnp.where(self.z < 2, 1, 0)
        self.pieces, self.rows = acc.shape[1], acc.shape[2]
        self.turns = 2 * self.pieces + 2

    @staticmethod
    def scratch(pieces, rows, width):
        low = jnp.bfloat16
        return [pltpu.VMEM((2, pieces, rows, width), low), pltpu.VMEM((2, pieces, rows, width), low),
                DMA((2, pieces)), DMA((2, pieces)), DMA((2, pieces)), DMA((2, pieces)), DMA((2,))]

    def place_of(self, half):
        along = jnp.where(half == 0, 3 - self.z, self.z)
        return along == 0, along == 3

    def red_copy(self, half, c):
        return pltpu.make_async_remote_copy(
            src_ref=self.acc.at[half, c], dst_ref=self.red.at[half, c], send_sem=self.red_send.at[half, c],
            recv_sem=self.red_recv.at[half, c], device_id={"tensor": self.z + 2 * half - 1}, device_id_type=MESH)

    def back_copy(self, half, c, source):
        return pltpu.make_async_remote_copy(
            src_ref=source, dst_ref=self.res.at[half, c], send_sem=self.back_send.at[half, c],
            recv_sem=self.back_recv.at[half, c], device_id={"tensor": self.z - 2 * half + 1}, device_id_type=MESH)

    def load(self):
        return pltpu.make_async_copy(self.part, self.acc, self.local.at[0])

    def own(self, half):
        return pltpu.make_async_copy(self.acc.at[half], self.res.at[half], self.local.at[1])

    def begin(self, pieces):
        for half in range(2):
            begins, _ = self.place_of(half)

            @pl.when(begins)
            def _():
                for c in pieces:
                    self.red_copy(half, c).start()

    def reduce_step(self, c, half):
        begins, ends = self.place_of(half)

        @pl.when(jnp.logical_not(begins))
        def _():
            self.red_copy(half, c).wait_recv()
            add_rows(self.acc.at[half, c], self.acc.at[half, c], self.red.at[half, c], self.rows, 16)

            @pl.when(ends)
            def _():
                self.back_copy(half, c, self.acc.at[half, c]).start()

            @pl.when(jnp.logical_not(ends))
            def _():
                self.red_copy(half, c).start()

    def back_step(self, c, half):
        begins, ends = self.place_of(half)

        @pl.when(jnp.logical_not(ends | begins))
        def _():
            self.back_copy(half, c, self.res.at[half, c]).wait_recv()
            self.back_copy(half, c, self.res.at[half, c]).start()

    def turn(self, turn):
        near, far = self.near, 1 - self.near
        if turn + AHEAD < self.pieces:
            self.begin((turn + AHEAD,))
        if turn < self.pieces:
            self.reduce_step(turn, near)
        if 1 <= turn <= self.pieces:
            self.reduce_step(turn - 1, far)
        back = turn - self.pieces
        if 0 <= back < self.pieces:
            self.back_step(back, far)
        if 1 <= back <= self.pieces:
            self.back_step(back - 1, near)

    def finish(self):
        for half in range(2):
            begins, ends = self.place_of(half)

            @pl.when(ends)
            def _():
                self.own(half).start()
                self.own(half).wait()

            @pl.when(begins)
            def _():
                for c in range(self.pieces):
                    self.back_copy(half, c, self.res.at[half, c]).wait_recv()

            @pl.when(jnp.logical_not(ends))
            def _():
                for c in range(self.pieces):
                    self.red_copy(half, c).wait_send()

            @pl.when(jnp.logical_not(begins))
            def _():
                for c in range(self.pieces):
                    self.back_copy(half, c, self.res.at[half, c]).wait_send()


def tail_kernel(count, *refs):
    prods, part = refs[:count], refs[count]
    outs, res, owns = refs[count + 1:2 * count + 1], refs[2 * count + 1], refs[2 * count + 2:3 * count + 2]
    scr = refs[3 * count + 2:]
    line = LineSum(part, res, scr[0], scr[1], scr[2:7])
    swaps = [Exchange([prods[i].at[0], prods[i].at[1]], (outs[i], owns[i]), *scr[7 + 12 * i:10 + 12 * i], scr[10 + 12 * i:19 + 12 * i]) for i in range(count)]
    line.load().start()
    greet()
    swaps[0].event(0)
    line.load().wait()
    line.begin(range(AHEAD))
    last = line.turns
    plan = {3: [(0, 1)], 5: [(0, 2)], 9: [(0, 3)], 13: [(0, 4)], 17: [(0, 5)], 21: [(0, 6)]}
    for turn in range(last):
        line.turn(turn)
        for which, number in plan.get(turn, []):
            swaps[which].event(number)
    for swapped in swaps:
        swapped.event(7)
    line.finish()


def tail_exchange(products, normed_part, pieces=12):
    count = len(products)
    side, depth = products[0].shape[1] // 4, products[0].shape[2]
    tokens, width = normed_part.shape
    part = normed_part.reshape(2, pieces, tokens // 2 // pieces, width)
    low = jnp.bfloat16
    anywhere = pl.BlockSpec(memory_space=pl.ANY)
    scratch = LineSum.scratch(*part.shape[1:])
    for _ in products:
        scratch = scratch + Exchange.scratch(side, depth)
    outs = pl.pallas_call(
        functools.partial(tail_kernel, count),
        in_specs=[anywhere] * (count + 1),
        out_specs=[anywhere] * (2 * count + 1),
        out_shape=[jax.ShapeDtypeStruct((2, 2, 4, side, depth), low)] * count + [jax.ShapeDtypeStruct(part.shape, low)]
        + [jax.ShapeDtypeStruct((2, side, depth), low)] * count,
        scratch_shapes=scratch,
        cost_estimate=pl.CostEstimate(flops=100_000_000, bytes_accessed=300_000_000, transcendentals=0),
        compiler_params=pltpu.CompilerParams(collective_id=1, has_side_effects=True, vmem_limit_bytes=40 * 1024 * 1024),
        name="tail_exchange",
    )(*products, part)
    return outs[:count], outs[count + 1:], outs[count].reshape(tokens, width)


NT = (((1,), (1,)), ((), ()))
TN = (((0,), (0,)), ((), ()))


def dot_f32(left, right, dims=(((1,), (0,)), ((), ()))):
    return lax.dot_general(left, right, dims, preferred_element_type=jnp.float32)


def widened(column_block, width):
    return jnp.concatenate([column_block] * (width // LANES), axis=1)


def middle_kernel(pre_grad, act_part, coeff, conv_sum, inner_x, act_b, rank_b, dt_proj, x_wide, conv_w, docs, modes,
                  gate_grads, normed_t, inv, extra, hidden, in_gate, in_inner, out_own, gate_own, z_own,
                  rows_out, normed_out, inner_prod, out_shared, gate_shared, z_res,
                  w_buf, mask_buf, pair_buf, conv_buf, stage, stage_n, hid_buf, proj_buf, proj_recv, proj_fin, gain_buf, gain_recv,
                  red_send, red_recv, all_send, all_recv, core_sems, gain_send, gain_recv_sem, w_sems, stage_sems, n_sems, hid_sems,
                  *share_sems):
    tokens, channels = pre_grad.shape
    low = jnp.bfloat16
    rank_dim = dt_proj.shape[1]
    z = lax.axis_index("tensor")
    x, y, to_x, to_y, to_core = place()
    share = tokens // 4
    outs = Share(out_own, out_shared, share_sems[0:4])
    gate = Share(gate_own, gate_shared, share_sems[4:8])
    back = LineBack(z_res, share_sems[8:10])
    width = hidden.shape[1]
    slices = width // w_buf.shape[2]
    cut = w_buf.shape[2]

    def z_at(off):
        return {"tensor": (z + off) % 4}

    barrier = pltpu.get_barrier_semaphore()
    for target in (to_x, to_y, to_core, z_at(1), z_at(2), z_at(3)):
        pl.semaphore_signal(barrier, inc=1, device_id=target, device_id_type=MESH)
    pl.semaphore_wait(barrier, 6)

    def weight_copies(i):
        slot = i % 2
        found = []
        for j, source in enumerate((in_gate, in_inner)):
            for m in range(2):
                found.append(pltpu.make_async_copy(source.at[m, pl.ds(i * cut, cut)], w_buf.at[slot, 2 * j + m],
                                                   w_sems.at[slot, 2 * j + m]))
        found.append(pltpu.make_async_copy(hidden.at[:, pl.ds(i * cut, cut)], hid_buf.at[slot], hid_sems.at[slot]))
        return found

    for i in range(2):
        for copy in weight_copies(i):
            copy.start()

    block = 128

    def proj_block(i, nothing):
        at = pl.ds(pl.multiple_of(i * block, block), block)
        grad = pre_grad[at, :]
        part = dot_f32(grad * widened(modes[0, at, :], channels), dt_proj[0], NT)
        part = part + dot_f32(grad * widened(modes[1, at, :], channels), dt_proj[1], NT)
        proj_buf[at, 0:rank_dim] = part.astype(low)
        proj_buf[at, rank_dim:rank_dim + LANES] = coeff[at, :].astype(low)
        return nothing

    lax.fori_loop(0, tokens // block, proj_block, 0)

    def red_copy(off):
        return pltpu.make_async_remote_copy(
            src_ref=proj_buf.at[pl.ds(pl.multiple_of(((z + off) % 4) * share, share), share)], dst_ref=proj_recv.at[off - 1],
            send_sem=red_send.at[off - 1], recv_sem=red_recv.at[off - 1], device_id=z_at(off), device_id_type=MESH)

    for off in (1, 2, 3):
        red_copy(off).start()
    outs.event(0)

    def product(pair, target, number):
        pair_tokens = pair.shape[0]
        tall = stage.shape[1]
        turns = normed_t.shape[0] // tall
        for m in range(2):
            def mask_rows(i, nothing):
                at = pl.ds(pl.multiple_of(i * block, block), block)
                mask_buf[at, :] = pair[at, :] * widened(modes[m, at, :], channels)
                return nothing
            lax.fori_loop(0, pair_tokens // block, mask_rows, 0)
            for j in range(turns):
                slot = (m * turns + j) % 2
                copy = pltpu.make_async_copy(stage.at[slot], target.at[m, pl.ds(j * tall, tall)], stage_sems.at[slot])
                if m * turns + j >= 2:
                    copy.wait()
                stage[slot] = dot_f32(normed_t[pl.ds(j * tall, tall), :], mask_buf[...]).astype(low)
                copy.start()
        for slot in range(2):
            pltpu.make_async_copy(stage.at[slot], target.at[0, pl.ds(0, tall)], stage_sems.at[slot]).wait()

    for off in (1, 2, 3):
        red_copy(off).wait_recv()
    mine = pl.ds(pl.multiple_of(z * share, share), share)
    total = proj_buf[mine, :].astype(jnp.float32)
    for k in range(3):
        total = total + proj_recv[k].astype(jnp.float32)
    proj_fin[mine, :] = total.astype(low)

    def all_copy(off):
        return pltpu.make_async_remote_copy(
            src_ref=proj_fin.at[mine], dst_ref=proj_fin.at[mine], send_sem=all_send.at[off - 1],
            recv_sem=all_recv.at[off - 1], device_id=z_at(off), device_id_type=MESH)

    for off in (1, 2, 3):
        all_copy(off).start()
    span = x_wide.shape[1] - 96
    mode_rows = span + rank_dim
    for m in range(2):
        ranks = rank_b[...] * modes[m, pl.ds(0, tokens), :]
        rows_out[pl.ds(m * mode_rows + span, rank_dim), :] = dot_f32(ranks, pre_grad[...], TN).astype(low)
    def dt_sums(i, carried):
        at = pl.ds(pl.multiple_of(i * block, block), block)
        grad = pre_grad[at, :].astype(jnp.float32)
        first = jnp.sum(grad * widened(modes[0, at, :].astype(jnp.float32), channels), axis=0, keepdims=True)
        return carried[0] + first, carried[1] + jnp.sum(grad, axis=0, keepdims=True) - first

    none_row = jnp.zeros((1, channels), jnp.float32)
    bias0, bias1 = lax.fori_loop(0, tokens // block, dt_sums, (none_row, none_row))
    for off in (1, 2, 3):
        all_copy(off).wait_recv()
    back.begin((0, 1))

    def act_block(i, bias):
        at = pl.ds(pl.multiple_of(i * block, block), block)
        proj = proj_fin[at, :]
        two = proj.shape[1]
        back = dot_f32(proj * widened(modes[0, at, :], two), x_wide[0])
        back = back + dot_f32(proj * widened(modes[1, at, :], two), x_wide[1])
        value = conv_sum[at, :]
        sig = jax.nn.sigmoid(value)
        grad = (act_part[at, :] + back) * sig * (1.0 + value * (1.0 - sig))
        conv_buf[at, :] = grad
        return bias + jnp.sum(grad, axis=0, keepdims=True)

    conv_buf[pl.ds(tokens, 8), :] = jnp.zeros((8, channels), jnp.float32)
    bias = lax.fori_loop(0, tokens // block, act_block, none_row)
    outs.event(1)
    gate.event(0)
    back.some((0,), True)
    back.begin((2,))
    taps = conv_w.shape[0]
    thin = 64

    def conv_block(i, sums):
        base = pl.multiple_of(i * thin, thin)
        grads = conv_buf[pl.ds(base, thin + 8), :]
        doc = docs[pl.ds(base, thin), :]
        inner = inner_x[pl.ds(base, thin), :]
        result = jnp.zeros((thin, channels), jnp.float32)
        new = []
        for offset in range(taps):
            moved = grads[offset:offset + thin, :] * doc[:, offset:offset + 1]
            tap = taps - 1 - offset
            result = result + moved * conv_w[tap:tap + 1, :]
            new.append(sums[offset] + jnp.sum(moved * inner, axis=0, keepdims=True))
        pair_buf[pl.ds(base, thin), :] = result.astype(low)
        return tuple(new)

    sums = lax.fori_loop(0, tokens // thin, conv_block, (none_row,) * taps)

    def core_copy():
        return pltpu.make_async_remote_copy(
            src_ref=pair_buf.at[pl.ds(0, tokens)], dst_ref=pair_buf.at[pl.ds(tokens, tokens)],
            send_sem=core_sems.at[0], recv_sem=core_sems.at[1], device_id=to_core, device_id_type=MESH)

    core_copy().start()
    back.some((1,), True)
    back.begin((3,))

    for i in range(slices):
        slot = i % 2
        for copy in weight_copies(i):
            copy.wait()
        third = tokens // 3
        out_copy = pltpu.make_async_copy(stage_n.at[slot], normed_out.at[:, pl.ds(i * cut, cut)], n_sems.at[slot])
        if i >= 2:
            out_copy.wait()

        def normed_rows(j, gain, slot=slot):
            at = pl.ds(pl.multiple_of(j * third, third), third)
            gate_grad, grad = gate_grads[at, :], pair_buf[at, :]
            zero = dot_f32(gate_grad, w_buf[slot, 0], NT) + dot_f32(grad, w_buf[slot, 2], NT)
            one = dot_f32(gate_grad, w_buf[slot, 1], NT) + dot_f32(grad, w_buf[slot, 3], NT)
            picked = jnp.where(inv[at, 1:2] > 0.5, zero, one)
            stage_n[slot, at, :] = picked.astype(low)
            return gain + jnp.sum(picked * hid_buf[slot, at, :].astype(jnp.float32) * inv[at, 0:1], axis=0, keepdims=True)

        gain = lax.fori_loop(0, 3, normed_rows, jnp.zeros((1, cut), jnp.float32))
        gain_buf[:, pl.ds(i * cut, cut)] = jnp.broadcast_to(gain, (8, cut))
        out_copy.start()
        if i + 2 < slices:
            for copy in weight_copies(i + 2):
                copy.start()
        if i == 0:
            back.some((2,), True)
            back.some((0,), False)
            back.begin((4,))
        elif i == 1:
            back.some((3,), True)
            back.some((1,), False)
            back.begin((5,))
        elif i == 2:
            outs.event(2)
            back.some((4,), True)
            back.some((2,), False)
        elif i == 3:
            back.some((5,), True)
            back.some((3,), False)
    for slot in range(2):
        pltpu.make_async_copy(stage_n.at[slot], normed_out.at[:, pl.ds(0, cut)], n_sems.at[slot]).wait()

    def gain_copy(off):
        return pltpu.make_async_remote_copy(
            src_ref=gain_buf, dst_ref=gain_recv.at[off - 1], send_sem=gain_send.at[off - 1],
            recv_sem=gain_recv_sem.at[off - 1], device_id=z_at(off), device_id_type=MESH)

    for off in (1, 2, 3):
        gain_copy(off).start()
    core_copy().wait_recv()
    product(pair_buf, inner_prod, 1)
    back.some((4, 5), False)
    gate.event(1)
    outs.event(3)
    for m in range(2):
        proj = proj_fin[...] * widened(modes[m, pl.ds(0, tokens), :], proj_fin.shape[1])
        rows_out[pl.ds(m * mode_rows, span), :] = dot_f32(proj, act_b[...], TN)[:span].astype(low)
    for off in (1, 2, 3):
        gain_copy(off).wait_recv()
    gain = gain_buf[0:1, :] + gain_recv[0, 0:1, :] + gain_recv[1, 0:1, :] + gain_recv[2, 0:1, :]
    gains = [gain[:, k * channels:(k + 1) * channels] for k in range(width // channels)]
    tail_rows = list(sums[::-1]) + [bias, bias0, bias1, extra[...]] + gains
    used = taps + 3 + extra.shape[0] + len(gains)
    tail_rows.append(jnp.zeros((32 - used, channels), jnp.float32))
    rows_out[pl.ds(2 * mode_rows, 32), :] = jnp.concatenate(tail_rows, axis=0).astype(low)
    gate.event(2)
    gate.event(3)
    outs.event(4)
    gate.event(4)
    back.done()
    for off in (1, 2, 3):
        red_copy(off).wait_send()
        all_copy(off).wait_send()
        gain_copy(off).wait_send()
    core_copy().wait_send()


def middle(pre_grad, act_part, coeff, conv_sum, inner_x, act_b, rank_b, dt_proj, x_wide, conv_w, docs, modes,
           gate_grads, normed_t, inv, extra, hidden, in_gate, in_inner, out_own, gate_own, z_own):
    tokens, channels = pre_grad.shape
    width = hidden.shape[1]
    low = jnp.bfloat16
    side = normed_t.shape[0] // 4
    cut = 512
    mode_rows = x_wide.shape[1] - 96 + dt_proj.shape[1]
    vmem, anywhere = pl.BlockSpec(memory_space=pltpu.VMEM), pl.BlockSpec(memory_space=pl.ANY)
    return pl.pallas_call(
        middle_kernel,
        in_specs=[vmem] * 16 + [anywhere] * 6,
        out_specs=[vmem] + [anywhere] * 5,
        out_shape=[
            jax.ShapeDtypeStruct((2 * mode_rows + 32, channels), low),
            jax.ShapeDtypeStruct((tokens, width), low),
            jax.ShapeDtypeStruct((2, 4 * side, channels), low),
            jax.ShapeDtypeStruct((2, 2, 4) + out_own.shape[1:], low),
            jax.ShapeDtypeStruct((2, 2, 4) + gate_own.shape[1:], low),
            jax.ShapeDtypeStruct(z_own.shape, low),
        ],
        scratch_shapes=[
            pltpu.VMEM((2, 4, cut, channels), low),
            pltpu.VMEM((2 * tokens, channels), low),
            pltpu.VMEM((2 * tokens, channels), low),
            pltpu.VMEM((tokens + 8, channels), jnp.float32),
            pltpu.VMEM((2, 2 * side, channels), low),
            pltpu.VMEM((2, tokens, cut), low),
            pltpu.VMEM((2, tokens, cut), low),
            pltpu.VMEM((tokens, 2 * LANES), low),
            pltpu.VMEM((3, tokens // 4, 2 * LANES), low),
            pltpu.VMEM((tokens, 2 * LANES), low),
            pltpu.VMEM((8, width), jnp.float32),
            pltpu.VMEM((3, 8, width), jnp.float32),
            DMA((3,)), DMA((3,)), DMA((3,)), DMA((3,)), DMA((2,)), DMA((3,)), DMA((3,)),
            DMA((2, 4)), DMA((2,)), DMA((2,)), DMA((2,)),
        ] + Share.scratch() + Share.scratch() + LineBack.scratch(z_own.shape[1]),
        input_output_aliases={21: 5},
        cost_estimate=pl.CostEstimate(flops=27_000_000_000, bytes_accessed=60_000_000, transcendentals=1_000_000),
        compiler_params=pltpu.CompilerParams(collective_id=3, has_side_effects=True, vmem_limit_bytes=61 * 1024 * 1024),
        name="middle",
    )(pre_grad, act_part, coeff, conv_sum, inner_x, act_b, rank_b, dt_proj, x_wide, conv_w, docs, modes,
      gate_grads, normed_t, inv, extra, hidden, in_gate, in_inner, out_own, gate_own, z_own)


def split_tail(part, count):
    lane = lax.broadcasted_iota(jnp.int32, part.shape, 1)
    high = part.astype(jnp.bfloat16).astype(jnp.float32)
    rest = pltpu.roll(part - high, count, axis=1)
    return jnp.where(lane < count, high, jnp.where(lane < 2 * count, rest, 0.0)).astype(jnp.bfloat16)


def join_tail(block, count):
    return block + pltpu.roll(block, block.shape[1] - count, axis=1)


def front_kernel(coeffs_wide, hidden, gain, conv_w, conv_b, docs, modes, x_wide, out_grad, view, out_proj,
                 w_inner, w_gate, normed_pair, cotan_pair, modes_pair,
                 normed, inverse, conv_sum, inner_x, act_b, gate_z, gated_grad, rank_out, coeff_out,
                 acc, view_buf, wide, stage, w_out, proj_buf, proj_recv, proj_fin,
                 view_sems, stage_sems, out_sems, red_send, red_recv, all_send, all_recv, pair_send, pair_recv, pair_local):
    tokens, width = hidden.shape
    channels = conv_w.shape[1]
    groups = channels // LANES
    low = jnp.bfloat16
    z = lax.axis_index("tensor")
    share = tokens // 4
    deep = stage.shape[2] // 2
    turns = width // deep
    block = 128

    def z_at(off):
        return {"tensor": (z + off) % 4}

    barrier = pltpu.get_barrier_semaphore()
    for off in (1, 2, 3):
        pl.semaphore_signal(barrier, inc=1, device_id=z_at(off), device_id_type=MESH)
    core, to_core = lax.axis_index("dp") % 2, place()[4]
    pl.semaphore_signal(barrier, inc=1, device_id=to_core, device_id_type=MESH)

    def half_of(ref, which):
        return ref.at[:, pl.ds(pl.multiple_of(which * (width // 2), width // 2), width // 2)]

    own_rows, other_rows = pl.ds(0, tokens), pl.ds(tokens, tokens)
    pairs = ((half_of(normed, core), half_of(normed, 1 - core), normed_pair.at[own_rows], normed_pair.at[other_rows]),
             (half_of(out_grad, core), half_of(out_grad, 1 - core), cotan_pair.at[own_rows], cotan_pair.at[other_rows]),
             (modes, modes, modes_pair.at[:, own_rows], modes_pair.at[:, other_rows]))

    def pair_copies(i):
        mine, theirs, here, there = pairs[i]
        return (pltpu.make_async_copy(mine, here, pair_local.at[i]),
                pltpu.make_async_remote_copy(src_ref=theirs, dst_ref=there, send_sem=pair_send.at[i], recv_sem=pair_recv.at[i],
                                             device_id=to_core, device_id_type=MESH))

    def view_copy(i, m):
        tall = deep * 2 * groups
        return pltpu.make_async_copy(view.at[m, pl.ds(pl.multiple_of(i * tall, tall), tall)], view_buf.at[i % 2, m],
                                     view_sems.at[i % 2, m])

    def stage_copy(i, half, m):
        target = w_inner if half == 0 else w_gate
        return pltpu.make_async_copy(stage.at[i % 2, half, pl.ds(m * deep, deep)],
                                     target.at[m, pl.ds(pl.multiple_of(i * deep, deep), deep)], stage_sems.at[i % 2, half, m])

    def out_copy(m):
        return pltpu.make_async_copy(out_proj.at[m], w_out.at[m], out_sems.at[m])

    for m in range(2):
        view_copy(0, m).start()
    for m in range(2):
        view_copy(1, m).start()
        out_copy(m).start()

    def norm_block(i, nothing):
        at = pl.ds(pl.multiple_of(i * block, block), block)
        rows = hidden[at, :].astype(jnp.float32)
        scale = lax.rsqrt(jnp.mean(rows * rows, axis=1, keepdims=True) + EPS)
        inverse[at, :] = jnp.broadcast_to(scale, (block, LANES))
        normed[at, :] = (rows * scale * gain[...]).astype(low)
        return nothing

    lax.fori_loop(0, tokens // block, norm_block, 0)
    acc[0:8, :] = jnp.zeros((8, channels), jnp.float32)

    def unpack(i):
        for m in range(2):
            wide[m] = view_buf[i % 2, m].astype(jnp.float32)
            for half in range(2):
                stage[i % 2, half, m * deep:(m + 1) * deep, :] = jnp.concatenate(
                    [wide[m, pl.ds(g * 2 + half, deep, stride=2 * groups), :] for g in range(groups)], axis=1).astype(low)

    def multiply(i, first):
        columns = normed[:, pl.ds(pl.multiple_of(i * deep, deep), deep)]
        left = jnp.concatenate([columns * widened(modes[0], deep), columns * widened(modes[1], deep)], axis=1)
        for half in range(2):
            product = dot_f32(left, stage[i % 2, half])
            if half == 0:
                acc[8:8 + tokens, :] = product if first else acc[8:8 + tokens, :] + product
            else:
                gate_z[...] = product if first else gate_z[...] + product

    def turn(i):
        for m in range(2):
            view_copy(i, m).wait()
        unpack(i)
        for m in range(2):
            for half in range(2):
                stage_copy(i, half, m).start()

    turn(0)
    multiply(0, True)
    for m in range(2):
        view_copy(2, m).start()
    turn(1)
    for m in range(2):
        view_copy(3, m).start()

    def looped(i, nothing):
        for m in range(2):
            for half in range(2):
                stage_copy(i, half, m).wait()
        multiply(i + 1, False)
        turn(i + 2)

        @pl.when(i + 4 < turns)
        def _():
            for m in range(2):
                view_copy(i + 4, m).start()
        return nothing

    lax.fori_loop(0, turns - 2, looped, 0)
    multiply(turns - 1, False)
    for i in (turns - 2, turns - 1):
        for m in range(2):
            for half in range(2):
                stage_copy(i, half, m).wait()

    taps = conv_w.shape[0]

    def conv_block(i, nothing):
        base = pl.multiple_of(i * block, block)
        at = pl.ds(base, block)
        rows = acc[pl.ds(base, block + 8), :]
        doc = docs[at, :]
        total = conv_b[...] + conv_w[taps - 1:taps, :] * rows[8:8 + block, :]
        for offset in range(1, taps):
            total = total + conv_w[taps - 1 - offset:taps - offset, :] * rows[8 - offset:8 - offset + block, :] * doc[:, offset:offset + 1]
        conv_sum[at, :] = total
        inner_x[at, :] = rows[8:8 + block, :]
        active = (total * jax.nn.sigmoid(total)).astype(low)
        act_b[at, :] = active
        part = dot_f32(active * widened(modes[0, at, :], channels), x_wide[0], NT)
        part = part + dot_f32(active * widened(modes[1, at, :], channels), x_wide[1], NT)
        proj_buf[at, 0:LANES] = part[:, :LANES].astype(low)
        proj_buf[at, LANES:2 * LANES] = split_tail(part[:, LANES:], coeffs_wide)
        return nothing

    lax.fori_loop(0, tokens // block, conv_block, 0)

    def red_copy(off):
        return pltpu.make_async_remote_copy(
            src_ref=proj_buf.at[pl.ds(pl.multiple_of(((z + off) % 4) * share, share), share)], dst_ref=proj_recv.at[off - 1],
            send_sem=red_send.at[off - 1], recv_sem=red_recv.at[off - 1], device_id=z_at(off), device_id_type=MESH)

    mine = pl.ds(pl.multiple_of(z * share, share), share)

    def all_copy(off):
        return pltpu.make_async_remote_copy(
            src_ref=proj_fin.at[mine], dst_ref=proj_fin.at[mine], send_sem=all_send.at[off - 1],
            recv_sem=all_recv.at[off - 1], device_id=z_at(off), device_id_type=MESH)

    pl.semaphore_wait(barrier, 4)
    for off in (1, 2, 3):
        red_copy(off).start()
    for i in range(3):
        for copy in pair_copies(i):
            copy.start()
    third = tokens // 3

    def grad_block(i):
        at = pl.ds(i * third, third)
        zero = dot_f32(out_grad[at, :], w_out[0], NT)
        one = dot_f32(out_grad[at, :], w_out[1], NT)
        gated_grad[at, :] = jnp.where(docs[at, 0:1] > 0.5, zero, one)

    for m in range(2):
        out_copy(m).wait()
    grad_block(0)
    for off in (1, 2, 3):
        red_copy(off).wait_recv()
    total = proj_buf[mine, :].astype(jnp.float32)
    for k in range(3):
        total = total + proj_recv[k].astype(jnp.float32)
    proj_fin[mine, 0:LANES] = total[:, :LANES].astype(low)
    proj_fin[mine, LANES:2 * LANES] = split_tail(join_tail(total[:, LANES:], coeffs_wide), coeffs_wide)
    for off in (1, 2, 3):
        all_copy(off).start()
    grad_block(1)
    grad_block(2)
    for off in (1, 2, 3):
        all_copy(off).wait_recv()
    rank_out[...] = proj_fin[:, 0:LANES]
    coeff_out[...] = join_tail(proj_fin[:, LANES:2 * LANES].astype(jnp.float32), coeffs_wide)
    for off in (1, 2, 3):
        red_copy(off).wait_send()
        all_copy(off).wait_send()
    for i in range(3):
        for copy in pair_copies(i):
            copy.wait()


def front(hidden, gain, conv_w, conv_b, docs, modes, x_wide, out_grad, in_proj, out_proj, coeffs_wide):
    tokens, width = hidden.shape
    channels = conv_w.shape[1]
    groups = channels // LANES
    low, f32 = jnp.bfloat16, jnp.float32
    view = in_proj.reshape(2, width, 2, groups, LANES).transpose(0, 1, 3, 2, 4).reshape(2, width * 2 * groups, LANES)
    deep = 256
    vmem, anywhere = pl.BlockSpec(memory_space=pltpu.VMEM), pl.BlockSpec(memory_space=pl.ANY)
    shape = jax.ShapeDtypeStruct
    return pl.pallas_call(
        functools.partial(front_kernel, coeffs_wide),
        in_specs=[vmem] * 8 + [anywhere] * 2,
        out_specs=[anywhere] * 5 + [vmem] * 9,
        out_shape=[
            shape((2, width, channels), low), shape((2, width, channels), low), shape((2 * tokens, width // 2), low),
            shape((2 * tokens, width // 2), low), shape((2, 2 * tokens, LANES), low), shape((tokens, width), low),
            shape((tokens, LANES), f32), shape((tokens, channels), f32), shape((tokens, channels), f32),
            shape((tokens, channels), low), shape((tokens, channels), f32), shape((tokens, channels), f32),
            shape((tokens, LANES), low), shape((tokens, LANES), f32),
        ],
        scratch_shapes=[
            pltpu.VMEM((tokens + 8, channels), f32),
            pltpu.VMEM((2, 2, deep * 2 * groups, LANES), low),
            pltpu.VMEM((2, deep * 2 * groups, LANES), f32),
            pltpu.VMEM((2, 2, 2 * deep, channels), low),
            pltpu.VMEM((2, channels, width), low),
            pltpu.VMEM((tokens, 2 * LANES), low),
            pltpu.VMEM((3, tokens // 4, 2 * LANES), low),
            pltpu.VMEM((tokens, 2 * LANES), low),
            DMA((2, 2)), DMA((2, 2, 2)), DMA((2,)), DMA((3,)), DMA((3,)), DMA((3,)), DMA((3,)), DMA((3,)), DMA((3,)), DMA((3,)),
        ],
        cost_estimate=pl.CostEstimate(flops=20_000_000_000, bytes_accessed=80_000_000, transcendentals=1_000_000),
        compiler_params=pltpu.CompilerParams(collective_id=4, has_side_effects=True, vmem_limit_bytes=60 * 1024 * 1024),
        name="front",
    )(hidden, gain, conv_w, conv_b, docs, modes, x_wide, out_grad, view, out_proj)


def finish_kernel(hidden, out_grad, inverse, gain, summed_out, normed_sum, output, input_grad):
    rows = hidden[...].astype(jnp.float32)
    output[...] = (rows + summed_out[...].astype(jnp.float32)).astype(output.dtype)
    scale = inverse[:, 0:1]
    scaled = normed_sum[...].astype(jnp.float32) * gain[...]
    mean = jnp.mean(scaled * rows, axis=1, keepdims=True)
    input_grad[...] = (out_grad[...].astype(jnp.float32) + scale * scaled - rows * (scale * scale * scale) * mean).astype(input_grad.dtype)


def finish(hidden, out_grad, inverse, gain, summed_out, normed_sum):
    tokens, width = hidden.shape
    rows = 128
    wide = pl.BlockSpec((rows, width), lambda i: (i, 0))
    return pl.pallas_call(
        finish_kernel,
        grid=(tokens // rows,),
        in_specs=[wide, wide, pl.BlockSpec((rows, LANES), lambda i: (i, 0)), pl.BlockSpec((1, width), lambda i: (0, 0)), wide, wide],
        out_specs=[wide, wide],
        out_shape=[jax.ShapeDtypeStruct((tokens, width), jnp.bfloat16)] * 2,
        cost_estimate=pl.CostEstimate(flops=16 * tokens * width, bytes_accessed=12 * tokens * width, transcendentals=0),
        name="finish_rows",
    )(hidden, out_grad, inverse, gain, summed_out, normed_sum)


def scan_backward_kernel(states, groups, rows, unroll, count, joined,
                         bc_ref, pre_ref, act_ref, mixed_ref, keep_ref, alog_ref, skip_ref, h_ref, start_ref, *rest):
    if joined:
        prods, part_ref, rest = rest[:4], rest[4], rest[5:]
    pgrad_ref, apart_ref, bcg_ref, sum_ref, skipsum_ref = rest[:5]
    rest = rest[5:]
    if joined:
        out_own, gate_own, z_own, rest = rest[0], rest[1], rest[2], rest[3:]
    carry_ref, rate_scr, decay_scr, sk_scr, u_scr, dy_scr, w_scr, s_scr, p_scr, q_scr = rest[:10]
    rest = rest[10:]
    chunk = pl.program_id(0)
    if joined:
        line = LineReduce(part_ref, z_own, rest[0], rest[1], rest[2:5])
        outs = Reduce(prods[:2], out_own, *rest[5:8], rest[8:13])
        gate = Reduce(prods[2:], gate_own, *rest[13:16], rest[16:21])

        @pl.when(chunk == 0)
        def _():
            line.line.load().start()
            greet()
            outs.event(0)
            line.line.load().wait()
            line.line.begin((0,))

        for at in range(1, count):
            @pl.when(chunk == at)
            def _():
                if at < line.line.pieces:
                    line.line.begin((at,))
                if at == 2:
                    outs.event(1)
                elif at == 3:
                    gate.event(0)
                elif at == 5:
                    outs.event(2)
                elif at == 6:
                    outs.last()
                elif at == 8:
                    gate.event(1)
                elif at == 10:
                    gate.event(2)
                line.turn(at)

    @pl.when(chunk == 0)
    def _():
        decay = -jnp.exp(alog_ref[...])
        decay_scr[...] = decay
        rate_scr[...] = decay * LOG2E
        carry_ref[...] = jnp.zeros_like(carry_ref)
        sum_ref[...] = jnp.zeros_like(sum_ref)
        skipsum_ref[...] = jnp.zeros_like(skipsum_ref)

    step = softplus(pre_ref[...])
    act = act_ref[...].astype(jnp.float32)
    mixed = mixed_ref[...].astype(jnp.float32)
    spread_rows(u_scr, step * act, groups)
    spread_rows(dy_scr, mixed, groups)
    spread_rows(sk_scr, jnp.where(keep_ref[...] > 0.0, step, BIG), groups)
    skipsum_ref[...] += jnp.sum(mixed * act, axis=0, keepdims=True)

    def one(t, carried, before):
        at = pl.multiple_of(t * groups, groups)
        sk = sk_scr[pl.ds(at, groups), :]
        u = u_scr[pl.ds(at, groups), :]
        dy = dy_scr[pl.ds(at, groups), :]
        w = jnp.zeros_like(u)
        s = jnp.zeros_like(u)
        new, pb, pc = [], [], []
        for n in range(states):
            g = dy * bc_ref[t, states + n] + carried[n]
            pb.append(g * u)
            pc.append(dy * h_ref[t, n])
            w = w + g * bc_ref[t, n]
            fg = jnp.exp2(sk * rate_scr[n]) * g
            lg = fg * before(n)
            s = s + lg * decay_scr[n]
            sum_ref[n] += lg * sk
            new.append(fg)
        w_scr[pl.ds(at, groups), :] = w
        s_scr[pl.ds(at, groups), :] = s
        both = pb + pc
        batch = max(1, 16 // groups)
        for j in range(0, 2 * states, batch):
            p_scr[t, pl.ds(j * groups, batch * groups), :] = jnp.concatenate(
                both[j:j + batch], axis=0).astype(jnp.bfloat16)
        return tuple(new)

    def looped(i, carried):
        t = rows - 1 - i
        return one(t, carried, lambda n: h_ref[t - 1, n])

    last = lax.fori_loop(0, rows - 1, looped, tuple(carry_ref[n] for n in range(states)), unroll=unroll)
    last = one(0, last, lambda n: start_ref[0, n])
    for n in range(states):
        carry_ref[n] = last[n]

    ones = jnp.ones((16, LANES), jnp.bfloat16)

    def reduce_one(t, nothing):
        q = lax.dot_general(ones, p_scr[t], (((1,), (1,)), ((), ())), preferred_element_type=jnp.float32)
        q_scr[pl.ds(t, 1), :] = q[0:1]
        return nothing

    lax.fori_loop(0, rows, reduce_one, 0, unroll=4)
    shape = (2 * states * groups, LANES)
    pick = (lax.broadcasted_iota(jnp.int32, shape, 0) // groups == lax.broadcasted_iota(jnp.int32, shape, 1))
    pick = pick.astype(jnp.float32).astype(jnp.bfloat16)
    q = q_scr[...]
    high = q.astype(jnp.bfloat16)
    low = (q - high.astype(jnp.float32)).astype(jnp.bfloat16)
    bcg_ref[...] = (jnp.dot(high, pick, preferred_element_type=jnp.float32)
                    + jnp.dot(low, pick, preferred_element_type=jnp.float32))
    w = gather_rows(w_scr, rows, groups)
    s = gather_rows(s_scr, rows, groups)
    pgrad_ref[...] = ((act * w + s) * jax.nn.sigmoid(pre_ref[...])).astype(pgrad_ref.dtype)
    apart_ref[...] = mixed * skip_ref[...] + step * w

    if joined:
        @pl.when(chunk == count - 1)
        def _():
            gate.last()
            outs.done()
            gate.done()
            line.done()


def scan_backward(bc, pre, act, mixed, keep, a_log3, skip, h, starts, products=None, z_part=None, rows=64, unroll=3, pieces=6):
    tokens, channels = pre.shape
    groups = channels // LANES
    states = a_log3.shape[0]
    count = tokens // rows
    joined = products is not None
    wide = pl.BlockSpec((rows, channels), lambda i: (count - 1 - i, 0))
    whole3 = pl.BlockSpec((states, groups, LANES), lambda i: (0, 0, 0))
    row = pl.BlockSpec((1, channels), lambda i: (0, 0))
    anywhere = pl.BlockSpec(memory_space=pl.ANY)
    small = lambda: pltpu.VMEM((states, groups, LANES), jnp.float32)
    long = lambda: pltpu.VMEM((rows * groups, LANES), jnp.float32)
    extra, extra_shapes, extra_scratch = [], [], []
    if joined:
        side, depth = products[0].shape[0] // 4, products[0].shape[1]
        part = z_part.reshape(2, pieces, tokens // 2 // pieces, z_part.shape[1])
        extra = list(products) + [part]
        extra_shapes = [jax.ShapeDtypeStruct((2, side, depth), jnp.bfloat16)] * 2 + [jax.ShapeDtypeStruct(part.shape, jnp.bfloat16)]
        extra_scratch = LineReduce.scratch(*part.shape[1:]) + Reduce.scratch(side, depth) + Reduce.scratch(side, depth)
    settings = dict(collective_id=2, has_side_effects=True) if joined else {}
    outs = pl.pallas_call(
        functools.partial(scan_backward_kernel, states, groups, rows, unroll, count, joined),
        grid=(count,),
        in_specs=[
            pl.BlockSpec((rows, 2 * states), lambda i: (count - 1 - i, 0), memory_space=pltpu.SMEM),
            wide, wide, wide,
            pl.BlockSpec((rows, 1), lambda i: (count - 1 - i, 0)),
            whole3, row,
            pl.BlockSpec((rows, states, groups, LANES), lambda i: (count - 1 - i, 0, 0, 0)),
            pl.BlockSpec((1, states, groups, LANES), lambda i: (count - 1 - i, 0, 0, 0)),
        ] + [anywhere] * len(extra),
        out_specs=[wide, wide, pl.BlockSpec((rows, LANES), lambda i: (count - 1 - i, 0)), whole3, row]
        + [anywhere] * len(extra_shapes),
        out_shape=[
            jax.ShapeDtypeStruct((tokens, channels), jnp.bfloat16),
            jax.ShapeDtypeStruct((tokens, channels), jnp.float32),
            jax.ShapeDtypeStruct((tokens, LANES), jnp.float32),
            jax.ShapeDtypeStruct((states, groups, LANES), jnp.float32),
            jax.ShapeDtypeStruct((1, channels), jnp.float32),
        ] + extra_shapes,
        scratch_shapes=[small(), small(), small(), long(), long(), long(), long(), long(),
                        pltpu.VMEM((rows, 2 * states * groups, LANES), jnp.bfloat16),
                        pltpu.VMEM((rows, 2 * states * groups), jnp.float32)] + extra_scratch,
        cost_estimate=pl.CostEstimate(flops=60 * tokens * channels * states,
                                      bytes_accessed=4 * tokens * channels * states,
                                      transcendentals=tokens * channels * states),
        compiler_params=pltpu.CompilerParams(vmem_limit_bytes=52 * 1024 * 1024, **settings),
        name="scan_backward",
    )(bc, pre, act, mixed, keep, a_log3, skip, h, starts, *extra)
    return outs


def writer_kernel(place, side, depth, where_ref, pieces_ref, own_ref, *rest):
    out_ref, wide_scr, sems = rest[-3:]
    x, y, core = where_ref[0], where_ref[1], where_ref[2]
    copies = []
    for mode in range(2):
        for owner in range(2):
            c = core if owner == 0 else 1 - core
            for k in range(4):
                qx = x if k in (0, 1) else 1 - x
                qy = y if k in (0, 2) else 1 - y
                row = (qx * 2 + qy if mode == 0 else qy * 2 + qx) * side
                at = (mode * 2 + owner) * 4 + k
                piece = own_ref[mode] if owner == 0 and k == 0 else pieces_ref[mode, owner, k]
                wide_scr[at] = piece.astype(jnp.float32)
                if place == "columns":
                    target = out_ref.at[mode, pl.ds(pl.multiple_of(row, side), side),
                                        pl.ds(pl.multiple_of(c * depth, depth), depth)]
                else:
                    target = out_ref.at[mode, pl.ds(pl.multiple_of(c * 4 * side + row, side), side), place, :]
                copies.append(pltpu.make_async_copy(wide_scr.at[at], target, sems.at[at]))
                copies[-1].start()
    for copy in copies:
        copy.wait()


def write_out(place, shape, where, pieces, own, filled):
    side, depth = pieces.shape[3:]
    held = [] if filled is None else [filled]
    return pl.pallas_call(
        functools.partial(writer_kernel, place, side, depth),
        in_specs=[pl.BlockSpec(memory_space=pltpu.SMEM), pl.BlockSpec(memory_space=pltpu.VMEM), pl.BlockSpec(memory_space=pltpu.VMEM)]
        + [pl.BlockSpec(memory_space=pl.ANY)] * len(held),
        out_specs=pl.BlockSpec(memory_space=pl.ANY),
        out_shape=jax.ShapeDtypeStruct(shape, jnp.float32),
        input_output_aliases={3: 0} if held else {},
        scratch_shapes=[pltpu.VMEM((16, side, depth), jnp.float32), pltpu.SemaphoreType.DMA((16,))],
        cost_estimate=pl.CostEstimate(flops=16 * side * depth, bytes_accessed=16 * side * depth * 6, transcendentals=0),
        compiler_params=pltpu.CompilerParams(vmem_limit_bytes=48 * 1024 * 1024),
        name="write_grads",
    )(where, pieces, own, *held)


def lagged(values, offset):
    padding = [(offset, 0)] + [(0, 0)] * (values.ndim - 1)
    return jnp.pad(values, padding)[: values.shape[0]]


def leading(values, offset):
    padding = [(0, offset)] + [(0, 0)] * (values.ndim - 1)
    return jnp.pad(values, padding)[offset:]


def pick_dot(left_side, weights, first_mode):
    first_part = jnp.dot(left_side, weights[0], preferred_element_type=jnp.float32)
    second_part = jnp.dot(left_side, weights[1], preferred_element_type=jnp.float32)
    return jnp.where(first_mode, first_part, second_part)


def pick_back(gradient, weights, first_mode):
    dims = (((1,), (1,)), ((), ()))
    first_part = lax.dot_general(gradient, weights[0], dims, preferred_element_type=jnp.float32)
    second_part = lax.dot_general(gradient, weights[1], dims, preferred_element_type=jnp.float32)
    return jnp.where(first_mode, first_part, second_part)


def weight_grads(left_side, gradient, first_mode):
    nothing = jnp.zeros_like(gradient)
    dims = (((0,), (0,)), ((), ()))
    first_part = lax.dot_general(
        left_side,
        jnp.where(first_mode, gradient, nothing),
        dims,
        preferred_element_type=jnp.float32,
    )
    second_part = lax.dot_general(
        left_side,
        jnp.where(first_mode, nothing, gradient),
        dims,
        preferred_element_type=jnp.float32,
    )
    return jnp.stack([first_part, second_part])


def finish_rows(normed_grad, hidden, inverse, cotan, norm_gain):
    scaled = normed_grad * norm_gain
    gain_terms = jnp.sum(normed_grad * hidden * inverse, axis=0)
    cubed = inverse * inverse * inverse
    rows = (
        cotan + inverse * scaled - hidden * cubed * jnp.mean(scaled * hidden, axis=1, keepdims=True)
    )
    return (rows.astype(jnp.bfloat16), gain_terms)


def swap(values, distance):
    return lax.ppermute(values, "dp", [(i, i ^ distance) for i in range(8)])


CORE = 1


def tie(values, *others):
    return lax.optimization_barrier((values,) + others)[0]


def z_sum(values, size, dtype=jnp.bfloat16):
    distance = 1
    while distance < size:
        low = values.astype(dtype)
        got = lax.ppermute(low, "tensor", [(i, i ^ distance) for i in range(size)])
        values = low.astype(jnp.float32) + got.astype(jnp.float32)
        distance *= 2
    return values


def shards(names, hidden_in, segment_ids, modality, norm_gain, in_proj, conv_weight, conv_bias, x_proj, dt_proj, dt_bias,
           a_log, skip_gain, out_proj, out_grad):
    tokens, model_width = hidden_in.shape
    conv_taps, channels = conv_weight.shape
    rank_dim = dt_proj.shape[1]
    state_dim = a_log.shape[0]
    groups = channels // LANES
    ways = names["tensor"]
    by_hand = names["dp"] == 8 and names["tensor"] == 4
    low = jnp.bfloat16
    rank = lax.axis_index("dp")
    core, x_at, y_at = rank % 2, (rank // 2) % 2, rank // 4
    where = jnp.stack([x_at, y_at, core]).astype(jnp.int32)
    half_width = model_width // 2
    first_mode = (modality == 0)[:, None]
    nothing = jnp.zeros((), low)
    dims = (((0,), (0,)), ((), ()))

    def masked_products(left, right, modes, mask_left):
        products = []
        for chosen in (modes, jnp.logical_not(modes)):
            one = jnp.where(chosen, left, nothing) if mask_left else left
            two = right if mask_left else jnp.where(chosen, right, nothing)
            products.append(lax.dot_general(one, two, dims, preferred_element_type=jnp.float32).astype(low))
        return jnp.stack(products)

    same_doc = [jnp.ones((tokens, 1), jnp.float32)]
    for offset in range(1, conv_taps):
        earlier_seg = jnp.pad(segment_ids, (offset, 0), constant_values=-1)[:tokens]
        same_doc.append((earlier_seg == segment_ids).astype(jnp.float32)[:, None])
    if by_hand:
        modes_own = jnp.broadcast_to(jnp.stack([first_mode, jnp.logical_not(first_mode)]), (2, tokens, LANES)).astype(low)
        x_wide = jnp.pad(jnp.swapaxes(x_proj, 1, 2), ((0, 0), (0, 96), (0, 0)))
        facts = jnp.concatenate([first_mode.astype(jnp.float32)] + same_doc[1:], axis=1)
        (in_inner, in_gate, normed_pair, cotan_pair, modes, _, inverse, conv_sum, inner_x, activated_b, gate_z, gated_grad, rank_b, coeffs) = front(
            hidden_in, norm_gain[None], conv_weight, conv_bias[None], facts, modes_own, x_wide, out_grad, in_proj, out_proj,
            2 * state_dim)
        coeffs = coeffs[:, :2 * state_dim]
    else:
        hidden = hidden_in.astype(jnp.float32)
        inverse = lax.rsqrt(jnp.mean(hidden * hidden, axis=1, keepdims=True) + EPS)
        normed_b = (hidden * inverse * norm_gain).astype(low)
        in_inner = in_proj[:, :, 0, :]
        in_gate = in_proj[:, :, 1, :]
        inner_x = pick_dot(normed_b, in_inner, first_mode)
        conv_sum = conv_bias + conv_weight[conv_taps - 1] * inner_x
        for offset in range(1, conv_taps):
            conv_sum = conv_sum + conv_weight[conv_taps - 1 - offset] * lagged(inner_x, offset) * same_doc[offset]
        activated_b = jax.nn.silu(conv_sum).astype(low)
        projected = z_sum(pick_dot(activated_b, x_proj, first_mode), ways)
        rank_b = projected[:, :rank_dim].astype(low)
        coeffs = projected[:, rank_dim:]
        gate_z = pick_dot(normed_b, in_gate, first_mode)
        gated_grad = pick_back(out_grad, out_proj, first_mode)
    step_pre = pick_dot(rank_b, dt_proj, first_mode) + jnp.where(first_mode, dt_bias[0], dt_bias[1])
    keep = same_doc[1]
    a_log3 = a_log.reshape(state_dim, groups, LANES)
    skip_row = skip_gain[None]
    forward = scan_forward(coeffs, step_pre, activated_b, gate_z, gated_grad, keep, a_log3, skip_row,
                           first_mode.astype(jnp.float32), by_hand)
    gated_b, gate_grad_b, mixed_grad, states, starts = forward[:5]
    if by_hand:
        masks = [modes[m, :, :1] for m in range(2)]
        products = [lax.dot_general(gated_b * masks[m], cotan_pair, dims, preferred_element_type=jnp.float32).astype(low)
                    for m in range(2)]
        products += [lax.dot_general(normed_pair, gate_grad_b * masks[m], dims, preferred_element_type=jnp.float32).astype(low)
                     for m in range(2)]
        partial_out = jnp.dot(forward[5], out_proj.reshape(2 * channels, model_width), preferred_element_type=jnp.float32).astype(low)
        back = scan_backward(coeffs, step_pre, activated_b, mixed_grad, keep, a_log3, skip_row, states, starts,
                             products, partial_out)
        out_own, gate_own, z_own = back[5:]
    else:
        partial_out = pick_dot(gated_b, out_proj, first_mode).astype(low)
        back = scan_backward(coeffs, step_pre, activated_b, mixed_grad, keep, a_log3, skip_row, states, starts)
        summed_out = lax.psum(partial_out, "tensor")
        out_proj_grad = lax.psum(weight_grads(gated_b, out_grad, first_mode).astype(low), "dp").astype(jnp.float32)
        gate_proj_grad = lax.psum(weight_grads(normed_b, gate_grad_b, first_mode).astype(low), "dp")
    pre_grad_b, act_part, coeff_grad, sums, skips = back[:5]
    a_log_grad = sums.reshape(state_dim, channels) * -jnp.exp(a_log)
    mode_rows = x_proj.shape[2] + rank_dim
    if by_hand:
        later = jnp.stack([same_doc[0]] + [leading(same_doc[k], k) for k in range(1, conv_taps)], axis=1)[:, :, 0]
        row_facts = jnp.concatenate([inverse[:, :1], first_mode.astype(jnp.float32)], axis=1)
        rows, normed_low, inner_product, out_shared, gate_shared, z_res = middle(
            pre_grad_b, act_part, coeff_grad, conv_sum, inner_x, activated_b, rank_b, dt_proj, x_wide, conv_weight, later, modes,
            gate_grad_b[:tokens], jnp.swapaxes(normed_pair, 0, 1), row_facts, jnp.concatenate([a_log_grad, skips], axis=0),
            hidden_in, in_gate, in_inner, out_own, gate_own, z_own)
        summed_out = z_res.reshape(tokens, model_width)
    else:
        pre_grad = pre_grad_b.astype(jnp.float32)
        dt_bias_grad = jnp.stack([
            jnp.sum(jnp.where(first_mode, pre_grad, 0.0), axis=0),
            jnp.sum(jnp.where(first_mode, 0.0, pre_grad), axis=0)])
        rank_part = pick_back(pre_grad_b, dt_proj, first_mode)
        proj_grad_b = z_sum(jnp.concatenate([rank_part, coeff_grad[:, :2 * state_dim]], axis=1), ways).astype(low)
        act_grad = act_part + pick_back(proj_grad_b, x_proj, first_mode)
        sig_conv = jax.nn.sigmoid(conv_sum)
        conv_grad = act_grad * sig_conv * (1.0 + conv_sum * (1.0 - sig_conv))
        conv_bias_grad = jnp.sum(conv_grad, axis=0)
        weight_rows = []
        x_grad = jnp.zeros_like(inner_x)
        for tap_index in range(conv_taps):
            offset = conv_taps - 1 - tap_index
            masked = conv_grad * same_doc[offset]
            weight_rows.append(jnp.sum(masked * lagged(inner_x, offset), axis=0))
            x_grad = x_grad + conv_weight[tap_index] * leading(masked, offset)
        x_grad_b = x_grad.astype(low)
        normed_part = pick_back(x_grad_b, in_inner, first_mode) + pick_back(gate_grad_b, in_gate, first_mode)
        gain_part = jnp.sum(normed_part * (hidden * inverse), axis=0).reshape(-1, channels)
        gain_part = lax.psum(gain_part, "tensor")
        small_modes = jnp.concatenate([
            weight_grads(proj_grad_b, activated_b, first_mode), weight_grads(rank_b, pre_grad_b, first_mode)], axis=1)
        rows = jnp.concatenate([small_modes.reshape(-1, channels), jnp.stack(weight_rows), conv_bias_grad[None], dt_bias_grad,
                                a_log_grad, skips, gain_part], axis=0).astype(low)
    summed_rows = lax.psum(rows, "dp")
    if by_hand:
        (inner_shared,), (inner_own,), normed_sum = tail_exchange([inner_product], normed_low)

        output, input_grad = finish(hidden_in, out_grad, inverse, norm_gain[None], summed_out, normed_sum)
        where = tie(where, summed_rows)
        out_proj_grad = write_out("columns", (2, channels, model_width), where, out_shared, out_own, None)
        in_shape = (2, model_width, 2, channels)
        in_proj_grad = write_out(1, in_shape, where, gate_shared, gate_own, None)
        in_proj_grad = write_out(0, in_shape, where, inner_shared, inner_own, in_proj_grad)
    else:
        inner_proj_grad = lax.psum(weight_grads(normed_b, x_grad_b, first_mode).astype(low), "dp")
        in_proj_grad = jnp.stack([inner_proj_grad, gate_proj_grad], axis=2).astype(jnp.float32)
        normed_sum = lax.psum(normed_part.astype(low), "tensor")
        output = (hidden + summed_out.astype(jnp.float32)).astype(low)
        cotan = out_grad.astype(jnp.float32)
        input_grad, _ = finish_rows(normed_sum.astype(jnp.float32), hidden, inverse, cotan, norm_gain)
    summed_rows = summed_rows.astype(jnp.float32)
    small_modes, rows = summed_rows[:2 * mode_rows].reshape(2, mode_rows, channels), summed_rows[2 * mode_rows:]
    x_proj_grad = jnp.swapaxes(small_modes[:, :-rank_dim], 1, 2)
    dt_proj_grad = small_modes[:, -rank_dim:]
    norm_gain_grad = rows[conv_taps + 4 + state_dim:].reshape(-1)[:model_width]
    at = conv_taps + 1
    return (output, input_grad, norm_gain_grad, in_proj_grad, rows[:conv_taps], rows[conv_taps], x_proj_grad,
            dt_proj_grad, rows[at:at + 2], rows[at + 2:at + 2 + state_dim], rows[at + 2 + state_dim], out_proj_grad)


def solution(mesh):
    in_specs = (
        P("dp", None),
        P("dp"),
        P("dp"),
        P(),
        P(None, None, None, "tensor"),
        P(None, "tensor"),
        P("tensor"),
        P(None, "tensor", None),
        P(None, None, "tensor"),
        P(None, "tensor"),
        P(None, "tensor"),
        P("tensor"),
        P(None, "tensor", None),
        P("dp", None),
    )
    out_specs = (
        P("dp", None),
        P("dp", None),
        P(),
        P(None, None, None, "tensor"),
        P(None, "tensor"),
        P("tensor"),
        P(None, "tensor", None),
        P(None, None, "tensor"),
        P(None, "tensor"),
        P(None, "tensor"),
        P("tensor"),
        P(None, "tensor", None),
    )
    names = dict(mesh.shape)
    return jax.shard_map(functools.partial(shards, names), mesh=mesh, in_specs=in_specs, out_specs=out_specs, check_vma=False)
```

```python
import functools

import jax
import jax.numpy as jnp
from jax import lax
from jax.experimental import pallas as pl
from jax.experimental.pallas import tpu as pltpu
from jax.sharding import PartitionSpec as P

EPS = 1e-05

LANES = 128
BIG = 1000.0
LOG2E = 1.4426950408889634


def softplus(v):
    return jnp.maximum(v, 0.0) + jnp.log1p(jnp.exp(-jnp.abs(v)))


def spread_rows(scratch, values, groups):
    rows = values.shape[0]
    for g in range(groups):
        scratch[pl.ds(g, rows, stride=groups), :] = values[:, g * LANES:(g + 1) * LANES]


def gather_rows(scratch, rows, groups):
    return jnp.concatenate(
        [scratch[pl.ds(g, rows, stride=groups), :] for g in range(groups)], axis=1)


def scan_forward_kernel(states, groups, rows, unroll, count, joined,
                        bc_ref, pre_ref, act_ref, z_ref, gg_ref, keep_ref, alog_ref, skip_ref, mode_ref,
                        gated_ref, ggrad_ref, mixed_ref, h_ref, start_ref, *rest):
    chunk = pl.program_id(0)
    if joined:
        split_ref, rate_scr, state_scr, sk_scr, u_scr, y_scr, gated_all, ggrad_all, send_sems, recv_sems, local_sems = rest
        tokens = rows * count
        to_core = place()[4]

        def pair_copies(at, i):
            source, target = ((gated_all, gated_ref), (ggrad_all, ggrad_ref))[i]
            base = at * rows
            return (pltpu.make_async_copy(source.at[pl.ds(base, rows)], target.at[pl.ds(base, rows)], local_sems.at[at, i]),
                    pltpu.make_async_remote_copy(
                        src_ref=source.at[pl.ds(base, rows)], dst_ref=target.at[pl.ds(tokens + base, rows)],
                        send_sem=send_sems.at[at, i], recv_sem=recv_sems.at[at, i], device_id=to_core, device_id_type=MESH))

        @pl.when(chunk == 0)
        def _():
            barrier = pltpu.get_barrier_semaphore()
            pl.semaphore_signal(barrier, inc=1, device_id=to_core, device_id_type=MESH)
            pl.semaphore_wait(barrier, 1)
    else:
        rate_scr, state_scr, sk_scr, u_scr, y_scr = rest

    @pl.when(chunk == 0)
    def _():
        rate_scr[...] = jnp.exp(alog_ref[...]) * (-LOG2E)
        state_scr[...] = jnp.zeros_like(state_scr)

    step = softplus(pre_ref[...])
    act = act_ref[...].astype(jnp.float32)
    spread_rows(u_scr, step * act, groups)
    spread_rows(sk_scr, jnp.where(keep_ref[...] > 0.0, step, BIG), groups)
    start_ref[0] = state_scr[...]

    def one(t, held):
        at = pl.multiple_of(t * groups, groups)
        sk = sk_scr[pl.ds(at, groups), :]
        u = u_scr[pl.ds(at, groups), :]
        y = jnp.zeros_like(u)
        new = []
        for n in range(states):
            h = jnp.exp2(sk * rate_scr[n]) * held[n] + u * bc_ref[t, n]
            h_ref[t, n] = h
            y = y + h * bc_ref[t, states + n]
            new.append(h)
        y_scr[pl.ds(at, groups), :] = y
        return tuple(new)

    last = lax.fori_loop(0, rows, one, tuple(state_scr[n] for n in range(states)), unroll=unroll)
    for n in range(states):
        state_scr[n] = last[n]
    mixed_out = gather_rows(y_scr, rows, groups) + skip_ref[...] * act
    z = z_ref[...].astype(jnp.float32)
    gg = gg_ref[...].astype(jnp.float32)
    sig = jax.nn.sigmoid(z)
    silu = z * sig
    gated = mixed_out * silu
    gate_grad = (gg * mixed_out * sig * (1.0 + z * (1.0 - sig))).astype(ggrad_ref.dtype)
    mixed_ref[...] = gg * silu
    if joined:
        channels = gated.shape[1]
        first = mode_ref[...]
        split_ref[:, 0:channels] = (gated * first).astype(split_ref.dtype)
        split_ref[:, channels:2 * channels] = (gated * (1.0 - first)).astype(split_ref.dtype)
        at = pl.ds(pl.multiple_of(chunk * rows, rows), rows)
        gated_all[at, :] = gated.astype(gated_ref.dtype)
        ggrad_all[at, :] = gate_grad
        for k in range(count):
            @pl.when(chunk == k)
            def _():
                for i in range(2):
                    for copy in pair_copies(k, i):
                        copy.start()

        @pl.when(chunk == count - 1)
        def _():
            for k in range(count):
                for i in range(2):
                    for copy in pair_copies(k, i):
                        copy.wait()
    else:
        gated_ref[...] = gated.astype(gated_ref.dtype)
        ggrad_ref[...] = gate_grad


def scan_forward(bc, pre, act, z, gg, keep, a_log3, skip, mode, joined, rows=64, unroll=4):
    tokens, channels = pre.shape
    groups = channels // LANES
    states = a_log3.shape[0]
    count = tokens // rows
    wide = pl.BlockSpec((rows, channels), lambda i: (i, 0))
    thin = pl.BlockSpec((rows, 1), lambda i: (i, 0))
    whole3 = pl.BlockSpec((states, groups, LANES), lambda i: (0, 0, 0))
    low, f32 = jnp.bfloat16, jnp.float32
    long = lambda: pltpu.VMEM((rows * groups, LANES), f32)
    small = lambda: pltpu.VMEM((states, groups, LANES), f32)
    anywhere = pl.BlockSpec(memory_space=pl.ANY)
    tall = 2 * tokens if joined else tokens
    settings = dict(collective_id=5, has_side_effects=True) if joined else {}
    return pl.pallas_call(
        functools.partial(scan_forward_kernel, states, groups, rows, unroll, count, joined),
        grid=(count,),
        in_specs=[
            pl.BlockSpec((rows, 2 * states), lambda i: (i, 0), memory_space=pltpu.SMEM),
            wide, wide, wide, wide, thin, whole3,
            pl.BlockSpec((1, channels), lambda i: (0, 0)), thin,
        ],
        out_specs=[
            anywhere if joined else wide, anywhere if joined else wide, wide,
            pl.BlockSpec((rows, states, groups, LANES), lambda i: (i, 0, 0, 0)),
            pl.BlockSpec((1, states, groups, LANES), lambda i: (i, 0, 0, 0)),
        ] + ([pl.BlockSpec((rows, 2 * channels), lambda i: (i, 0))] if joined else []),
        out_shape=[
            jax.ShapeDtypeStruct((tall, channels), low),
            jax.ShapeDtypeStruct((tall, channels), low),
            jax.ShapeDtypeStruct((tokens, channels), f32),
            jax.ShapeDtypeStruct((tokens, states, groups, LANES), f32),
            jax.ShapeDtypeStruct((count, states, groups, LANES), f32),
        ] + ([jax.ShapeDtypeStruct((tokens, 2 * channels), low)] if joined else []),
        scratch_shapes=[small(), small(), long(), long(), long()] + ([
            pltpu.VMEM((tokens, channels), low), pltpu.VMEM((tokens, channels), low),
            pltpu.SemaphoreType.DMA((count, 2)), pltpu.SemaphoreType.DMA((count, 2)), pltpu.SemaphoreType.DMA((count, 2)),
        ] if joined else []),
        compiler_params=pltpu.CompilerParams(vmem_limit_bytes=48 * 1024 * 1024, **settings),
        name="scan_forward",
    )(bc, pre, act, z, gg, keep, a_log3, skip, mode)


MESH = pl.DeviceIdType.MESH
DMA = pltpu.SemaphoreType.DMA


def add_rows(target, left, right, rows, slab):
    def body(i, nothing):
        at = pl.ds(pl.multiple_of(i * slab, slab), slab)
        target[at, :] = (left[at, :].astype(jnp.float32) + right[at, :].astype(jnp.float32)).astype(jnp.bfloat16)
        return nothing
    lax.fori_loop(0, rows // slab, body, 0)


def place():
    dp = lax.axis_index("dp")
    x, y, core = (dp // 2) % 2, dp // 4, dp % 2
    return x, y, {"dp": dp + 2 - 4 * x}, {"dp": dp + 4 - 8 * y}, {"dp": dp + 1 - 2 * core}


def greet():
    z = lax.axis_index("tensor")
    barrier = pltpu.get_barrier_semaphore()
    for target in place()[2:]:
        pl.semaphore_signal(barrier, inc=1, device_id=target, device_id_type=MESH)

    @pl.when(z > 0)
    def _():
        pl.semaphore_signal(barrier, inc=1, device_id={"tensor": z - 1}, device_id_type=MESH)

    @pl.when(z < 3)
    def _():
        pl.semaphore_signal(barrier, inc=1, device_id={"tensor": z + 1}, device_id_type=MESH)

    @pl.when((z > 0) & (z < 3))
    def _():
        pl.semaphore_wait(barrier, 5)

    @pl.when((z == 0) | (z == 3))
    def _():
        pl.semaphore_wait(barrier, 4)


class Exchange:
    def __init__(self, prod, out, held, half_buf, quarter_buf, sems, summed=None):
        self.summed = summed
        self.prod, self.held, self.half_buf, self.quarter_buf = prod, held, half_buf, quarter_buf
        self.out, self.own = out
        (self.half_send, self.half_recv, self.quarter_send, self.quarter_recv,
         self.share_send, self.share_recv, self.core_send, self.core_recv, self.local) = sems
        x, y, self.to_x, self.to_y, self.to_core = place()
        self.firsts, self.seconds = (x, y), (y, x)
        self.ways = ((self.to_x, self.to_y), (self.to_y, self.to_x))
        self.side = half_buf.shape[2]

    @staticmethod
    def scratch(side, depth):
        low = jnp.bfloat16
        return [pltpu.VMEM((2, 2, side, depth), low), pltpu.VMEM((2, 2, side, depth), low), pltpu.VMEM((2, side, depth), low),
                DMA((2, 2)), DMA((2, 2)), DMA((2,)), DMA((2,)), DMA((2, 4)), DMA((2, 4)), DMA((2, 4)), DMA((2, 4)), DMA((2, 3))]

    def rows(self, mode, k, mine):
        first, second = self.firsts[mode], self.seconds[mode]
        half = first if mine else 1 - first
        quarter = 1 - second if k == 0 else second
        return pl.ds(pl.multiple_of((half * 2 + quarter) * self.side, self.side), self.side)

    def half_copy(self, mode, k):
        return pltpu.make_async_remote_copy(
            src_ref=self.prod[mode].at[self.rows(mode, k, False)], dst_ref=self.half_buf.at[mode, k],
            send_sem=self.half_send.at[mode, k], recv_sem=self.half_recv.at[mode, k],
            device_id=self.ways[mode][0], device_id_type=MESH)

    def keep_copy(self, mode, k):
        return pltpu.make_async_copy(self.prod[mode].at[self.rows(mode, k, True)], self.held.at[mode, k], self.local.at[mode, k])

    def quarter_copy(self, mode):
        return pltpu.make_async_remote_copy(
            src_ref=self.half_buf.at[mode, 0], dst_ref=self.quarter_buf.at[mode],
            send_sem=self.quarter_send.at[mode], recv_sem=self.quarter_recv.at[mode],
            device_id=self.ways[mode][1], device_id_type=MESH)

    def share_copy(self, mode, k):
        own = self.held.at[mode, 1]
        if k == 3:
            source, way = (self.out.at[mode, 0, 1], self.to_x) if mode == 0 else (self.out.at[mode, 0, 2], self.to_y)
        else:
            source, way = own, self.to_y if k == 1 else self.to_x
        return pltpu.make_async_remote_copy(
            src_ref=source, dst_ref=self.out.at[mode, 0, k], send_sem=self.share_send.at[mode, k],
            recv_sem=self.share_recv.at[mode, k], device_id=way, device_id_type=MESH)

    def core_copy(self, mode, k):
        return pltpu.make_async_remote_copy(
            src_ref=self.held.at[mode, 1] if k == 0 else self.out.at[mode, 0, k], dst_ref=self.out.at[mode, 1, k],
            send_sem=self.core_send.at[mode, k], recv_sem=self.core_recv.at[mode, k],
            device_id=self.to_core, device_id_type=MESH)

    def out_copy(self, mode):
        return pltpu.make_async_copy(self.held.at[mode, 1], self.own.at[mode], self.local.at[mode, 2])

    def start_shares(self, mode):
        for k in ((1, 2) if mode == 0 else (2, 1)):
            self.share_copy(mode, k).start()
        self.core_copy(mode, 0).start()
        self.out_copy(mode).start()

    def event(self, number):
        if number == 0:
            for k in range(2):
                for mode in range(2):
                    self.half_copy(mode, k).start()
                    self.keep_copy(mode, k).start()
        elif number == 1:
            for mode in range(2):
                self.keep_copy(mode, 0).wait()
                self.half_copy(mode, 0).wait_recv()
                add_rows(self.half_buf.at[mode, 0], self.half_buf.at[mode, 0], self.held.at[mode, 0], self.side, 32)
                self.quarter_copy(mode).start()
        elif number == 2:
            for mode in range(2):
                self.keep_copy(mode, 1).wait()
                self.half_copy(mode, 1).wait_recv()
                add_rows(self.half_buf.at[mode, 1], self.half_buf.at[mode, 1], self.held.at[mode, 1], self.side, 32)
        elif number == 3:
            for mode in range(2):
                self.quarter_copy(mode).wait_recv()
                add_rows(self.held.at[mode, 1], self.half_buf.at[mode, 1], self.quarter_buf.at[mode], self.side, 32)
                self.start_shares(mode)
        elif number == 4:
            for mode in range(2):
                k = 1 if mode == 0 else 2
                self.share_copy(mode, k).wait_recv()
                self.share_copy(mode, 3).start()
                self.core_copy(mode, k).start()
        elif number == 5:
            for mode in range(2):
                k = 2 if mode == 0 else 1
                self.share_copy(mode, k).wait_recv()
                self.core_copy(mode, k).start()
        elif number == 6:
            for mode in range(2):
                self.share_copy(mode, 3).wait_recv()
                self.core_copy(mode, 3).start()
        elif number == 8:
            for mode in range(2):
                pltpu.make_async_copy(self.prod.at[mode], self.held.at[mode, 1], self.local.at[mode, 1]).start()
        elif number == 9:
            for mode in range(2):
                pltpu.make_async_copy(self.prod.at[mode], self.held.at[mode, 1], self.local.at[mode, 1]).wait()
                self.start_shares(mode)
        elif number == 7:
            for mode in range(2):
                if self.summed is None:
                    for k in range(2):
                        self.half_copy(mode, k).wait_send()
                    self.quarter_copy(mode).wait_send()
                for k in range(1, 4):
                    self.share_copy(mode, k).wait_send()
                for k in range(4):
                    self.core_copy(mode, k).wait_send()
                    self.core_copy(mode, k).wait_recv()
                self.out_copy(mode).wait()


class Share:
    def __init__(self, own, out, sems):
        self.own, self.out = own, out
        self.share_send, self.share_recv, self.core_send, self.core_recv = sems
        _, _, self.to_x, self.to_y, self.to_core = place()

    @staticmethod
    def scratch():
        return [DMA((2, 4)), DMA((2, 4)), DMA((2, 4)), DMA((2, 4))]

    def share_copy(self, mode, k):
        if k == 3:
            source, way = (self.out.at[mode, 0, 1], self.to_x) if mode == 0 else (self.out.at[mode, 0, 2], self.to_y)
        else:
            source, way = self.own.at[mode], self.to_y if k == 1 else self.to_x
        return pltpu.make_async_remote_copy(
            src_ref=source, dst_ref=self.out.at[mode, 0, k], send_sem=self.share_send.at[mode, k],
            recv_sem=self.share_recv.at[mode, k], device_id=way, device_id_type=MESH)

    def core_copy(self, mode, k):
        return pltpu.make_async_remote_copy(
            src_ref=self.own.at[mode] if k == 0 else self.out.at[mode, 0, k], dst_ref=self.out.at[mode, 1, k],
            send_sem=self.core_send.at[mode, k], recv_sem=self.core_recv.at[mode, k],
            device_id=self.to_core, device_id_type=MESH)

    def event(self, number):
        for mode in range(2):
            early, late = (1, 2) if mode == 0 else (2, 1)
            if number == 0:
                self.share_copy(mode, early).start()
                self.share_copy(mode, late).start()
                self.core_copy(mode, 0).start()
            elif number == 1:
                self.share_copy(mode, early).wait_recv()
                self.share_copy(mode, 3).start()
                self.core_copy(mode, early).start()
            elif number == 2:
                self.share_copy(mode, late).wait_recv()
                self.core_copy(mode, late).start()
            elif number == 3:
                self.share_copy(mode, 3).wait_recv()
                self.core_copy(mode, 3).start()
            else:
                for k in range(1, 4):
                    self.share_copy(mode, k).wait_send()
                for k in range(4):
                    self.core_copy(mode, k).wait_send()
                    self.core_copy(mode, k).wait_recv()


class Reduce(Exchange):
    def __init__(self, prod, own, held, half_buf, quarter_buf, sems):
        half_send, half_recv, quarter_send, quarter_recv, keep = sems
        super().__init__(prod, (None, own), held, half_buf, quarter_buf,
                         (half_send, half_recv, quarter_send, quarter_recv, None, None, None, None, keep))

    @staticmethod
    def scratch(side, depth):
        low = jnp.bfloat16
        return [pltpu.VMEM((2, 2, side, depth), low), pltpu.VMEM((2, 2, side, depth), low), pltpu.VMEM((2, side, depth), low),
                DMA((2, 2)), DMA((2, 2)), DMA((2,)), DMA((2,)), DMA((2, 3))]

    def last(self):
        for mode in range(2):
            self.quarter_copy(mode).wait_recv()
            add_rows(self.held.at[mode, 1], self.half_buf.at[mode, 1], self.quarter_buf.at[mode], self.side, 32)
            pltpu.make_async_copy(self.held.at[mode, 1], self.own.at[mode], self.local.at[mode, 2]).start()

    def done(self):
        for mode in range(2):
            for k in range(2):
                self.half_copy(mode, k).wait_send()
            self.quarter_copy(mode).wait_send()
            pltpu.make_async_copy(self.held.at[mode, 1], self.own.at[mode], self.local.at[mode, 2]).wait()


class LineReduce:
    def __init__(self, part, own, acc, red, sems):
        red_send, red_recv, local = sems
        self.line = LineSum(part, own, acc, red, (red_send, red_recv, None, None, local))

    @staticmethod
    def scratch(pieces, rows, width):
        low = jnp.bfloat16
        return [pltpu.VMEM((2, pieces, rows, width), low), pltpu.VMEM((2, pieces, rows, width), low),
                DMA((2, pieces)), DMA((2, pieces)), DMA((2,))]

    def step(self, c, half):
        line = self.line
        begins, ends = line.place_of(half)

        @pl.when(jnp.logical_not(begins))
        def _():
            line.red_copy(half, c).wait_recv()
            add_rows(line.acc.at[half, c], line.acc.at[half, c], line.red.at[half, c], line.rows, 16)

            @pl.when(jnp.logical_not(ends))
            def _():
                line.red_copy(half, c).start()

    def turn(self, turn):
        line = self.line
        at_end = (line.z == 0) | (line.z == 3)
        if 0 <= turn - 2 < line.pieces:
            self.step(turn - 2, line.near)
        if 0 <= turn - 4 < line.pieces:
            @pl.when(jnp.logical_not(at_end))
            def _():
                self.step(turn - 4, 1 - line.near)
        if 0 <= turn - 6 < line.pieces:
            @pl.when(at_end)
            def _():
                self.step(turn - 6, 1 - line.near)

    def done(self):
        line = self.line
        for half in range(2):
            begins, ends = line.place_of(half)

            @pl.when(ends)
            def _():
                line.own(half).start()
                line.own(half).wait()

            @pl.when(jnp.logical_not(ends))
            def _():
                for c in range(line.pieces):
                    line.red_copy(half, c).wait_send()


class LineBack:
    def __init__(self, res, sems):
        self.res = res
        self.send, self.recv = sems
        self.z = lax.axis_index("tensor")
        self.near = jnp.where(self.z < 2, 1, 0)
        self.pieces = res.shape[1]

    @staticmethod
    def scratch(pieces):
        return [DMA((2, pieces)), DMA((2, pieces))]

    def place_of(self, half):
        along = jnp.where(half == 0, 3 - self.z, self.z)
        return along == 0, along == 3

    def copy(self, half, c):
        return pltpu.make_async_remote_copy(
            src_ref=self.res.at[half, c], dst_ref=self.res.at[half, c], send_sem=self.send.at[half, c],
            recv_sem=self.recv.at[half, c], device_id={"tensor": self.z - 2 * half + 1}, device_id_type=MESH)

    def begin(self, pieces):
        for half in range(2):
            _, ends = self.place_of(half)

            @pl.when(ends)
            def _():
                for c in pieces:
                    self.copy(half, c).start()

    def step(self, c, half):
        begins, ends = self.place_of(half)

        @pl.when(jnp.logical_not(ends | begins))
        def _():
            self.copy(half, c).wait_recv()
            self.copy(half, c).start()

    def some(self, pieces, far):
        for c in pieces:
            self.step(c, 1 - self.near if far else self.near)

    def done(self):
        for half in range(2):
            begins, ends = self.place_of(half)

            @pl.when(begins)
            def _():
                for c in range(self.pieces):
                    self.copy(half, c).wait_recv()

            @pl.when(jnp.logical_not(begins))
            def _():
                for c in range(self.pieces):
                    self.copy(half, c).wait_send()


AHEAD = 2


class LineSum:
    def __init__(self, part, res, acc, red, sems):
        self.part, self.res, self.acc, self.red = part, res, acc, red
        self.red_send, self.red_recv, self.back_send, self.back_recv, self.local = sems
        self.z = lax.axis_index("tensor")
        self.near = jnp.where(self.z < 2, 1, 0)
        self.pieces, self.rows = acc.shape[1], acc.shape[2]
        self.turns = 2 * self.pieces + 2

    @staticmethod
    def scratch(pieces, rows, width):
        low = jnp.bfloat16
        return [pltpu.VMEM((2, pieces, rows, width), low), pltpu.VMEM((2, pieces, rows, width), low),
                DMA((2, pieces)), DMA((2, pieces)), DMA((2, pieces)), DMA((2, pieces)), DMA((2,))]

    def place_of(self, half):
        along = jnp.where(half == 0, 3 - self.z, self.z)
        return along == 0, along == 3

    def red_copy(self, half, c):
        return pltpu.make_async_remote_copy(
            src_ref=self.acc.at[half, c], dst_ref=self.red.at[half, c], send_sem=self.red_send.at[half, c],
            recv_sem=self.red_recv.at[half, c], device_id={"tensor": self.z + 2 * half - 1}, device_id_type=MESH)

    def back_copy(self, half, c, source):
        return pltpu.make_async_remote_copy(
            src_ref=source, dst_ref=self.res.at[half, c], send_sem=self.back_send.at[half, c],
            recv_sem=self.back_recv.at[half, c], device_id={"tensor": self.z - 2 * half + 1}, device_id_type=MESH)

    def load(self):
        return pltpu.make_async_copy(self.part, self.acc, self.local.at[0])

    def own(self, half):
        return pltpu.make_async_copy(self.acc.at[half], self.res.at[half], self.local.at[1])

    def begin(self, pieces):
        for half in range(2):
            begins, _ = self.place_of(half)

            @pl.when(begins)
            def _():
                for c in pieces:
                    self.red_copy(half, c).start()

    def reduce_step(self, c, half):
        begins, ends = self.place_of(half)

        @pl.when(jnp.logical_not(begins))
        def _():
            self.red_copy(half, c).wait_recv()
            add_rows(self.acc.at[half, c], self.acc.at[half, c], self.red.at[half, c], self.rows, 16)

            @pl.when(ends)
            def _():
                self.back_copy(half, c, self.acc.at[half, c]).start()

            @pl.when(jnp.logical_not(ends))
            def _():
                self.red_copy(half, c).start()

    def back_step(self, c, half):
        begins, ends = self.place_of(half)

        @pl.when(jnp.logical_not(ends | begins))
        def _():
            self.back_copy(half, c, self.res.at[half, c]).wait_recv()
            self.back_copy(half, c, self.res.at[half, c]).start()

    def turn(self, turn):
        near, far = self.near, 1 - self.near
        if turn + AHEAD < self.pieces:
            self.begin((turn + AHEAD,))
        if turn < self.pieces:
            self.reduce_step(turn, near)
        if 1 <= turn <= self.pieces:
            self.reduce_step(turn - 1, far)
        back = turn - self.pieces
        if 0 <= back < self.pieces:
            self.back_step(back, far)
        if 1 <= back <= self.pieces:
            self.back_step(back - 1, near)

    def finish(self):
        for half in range(2):
            begins, ends = self.place_of(half)

            @pl.when(ends)
            def _():
                self.own(half).start()
                self.own(half).wait()

            @pl.when(begins)
            def _():
                for c in range(self.pieces):
                    self.back_copy(half, c, self.res.at[half, c]).wait_recv()

            @pl.when(jnp.logical_not(ends))
            def _():
                for c in range(self.pieces):
                    self.red_copy(half, c).wait_send()

            @pl.when(jnp.logical_not(begins))
            def _():
                for c in range(self.pieces):
                    self.back_copy(half, c, self.res.at[half, c]).wait_send()


def tail_kernel(count, *refs):
    prods, part = refs[:count], refs[count]
    outs, res, owns = refs[count + 1:2 * count + 1], refs[2 * count + 1], refs[2 * count + 2:3 * count + 2]
    scr = refs[3 * count + 2:]
    line = LineSum(part, res, scr[0], scr[1], scr[2:7])
    swaps = [Exchange([prods[i].at[0], prods[i].at[1]], (outs[i], owns[i]), *scr[7 + 12 * i:10 + 12 * i], scr[10 + 12 * i:19 + 12 * i]) for i in range(count)]
    line.load().start()
    greet()
    swaps[0].event(0)
    line.load().wait()
    line.begin(range(AHEAD))
    last = line.turns
    plan = {3: [(0, 1)], 5: [(0, 2)], 9: [(0, 3)], 13: [(0, 4)], 17: [(0, 5)], 21: [(0, 6)]}
    for turn in range(last):
        line.turn(turn)
        for which, number in plan.get(turn, []):
            swaps[which].event(number)
    for swapped in swaps:
        swapped.event(7)
    line.finish()


def tail_exchange(products, normed_part, pieces=12):
    count = len(products)
    side, depth = products[0].shape[1] // 4, products[0].shape[2]
    tokens, width = normed_part.shape
    part = normed_part.reshape(2, pieces, tokens // 2 // pieces, width)
    low = jnp.bfloat16
    anywhere = pl.BlockSpec(memory_space=pl.ANY)
    scratch = LineSum.scratch(*part.shape[1:])
    for _ in products:
        scratch = scratch + Exchange.scratch(side, depth)
    outs = pl.pallas_call(
        functools.partial(tail_kernel, count),
        in_specs=[anywhere] * (count + 1),
        out_specs=[anywhere] * (2 * count + 1),
        out_shape=[jax.ShapeDtypeStruct((2, 2, 4, side, depth), low)] * count + [jax.ShapeDtypeStruct(part.shape, low)]
        + [jax.ShapeDtypeStruct((2, side, depth), low)] * count,
        scratch_shapes=scratch,
        cost_estimate=pl.CostEstimate(flops=100_000_000, bytes_accessed=300_000_000, transcendentals=0),
        compiler_params=pltpu.CompilerParams(collective_id=1, has_side_effects=True, vmem_limit_bytes=40 * 1024 * 1024),
        name="tail_exchange",
    )(*products, part)
    return outs[:count], outs[count + 1:], outs[count].reshape(tokens, width)


NT = (((1,), (1,)), ((), ()))
TN = (((0,), (0,)), ((), ()))


def dot_f32(left, right, dims=(((1,), (0,)), ((), ()))):
    return lax.dot_general(left, right, dims, preferred_element_type=jnp.float32)


def widened(column_block, width):
    return jnp.concatenate([column_block] * (width // LANES), axis=1)


def middle_kernel(pre_grad, act_part, coeff, conv_sum, inner_x, act_b, rank_b, dt_proj, x_wide, conv_w, docs, modes,
                  gate_grads, normed_t, inv, extra, hidden, in_gate, in_inner, out_own, gate_own, z_own,
                  rows_out, normed_out, inner_prod, out_shared, gate_shared, z_res,
                  w_buf, mask_buf, pair_buf, conv_buf, stage, stage_n, hid_buf, proj_buf, proj_recv, proj_fin, gain_buf, gain_recv,
                  red_send, red_recv, all_send, all_recv, core_sems, gain_send, gain_recv_sem, w_sems, stage_sems, n_sems, hid_sems,
                  *share_sems):
    tokens, channels = pre_grad.shape
    low = jnp.bfloat16
    rank_dim = dt_proj.shape[1]
    z = lax.axis_index("tensor")
    x, y, to_x, to_y, to_core = place()
    share = tokens // 4
    outs = Share(out_own, out_shared, share_sems[0:4])
    gate = Share(gate_own, gate_shared, share_sems[4:8])
    back = LineBack(z_res, share_sems[8:10])
    width = hidden.shape[1]
    slices = width // w_buf.shape[2]
    cut = w_buf.shape[2]

    def z_at(off):
        return {"tensor": (z + off) % 4}

    barrier = pltpu.get_barrier_semaphore()
    for target in (to_x, to_y, to_core, z_at(1), z_at(2), z_at(3)):
        pl.semaphore_signal(barrier, inc=1, device_id=target, device_id_type=MESH)
    pl.semaphore_wait(barrier, 6)

    def weight_copies(i):
        slot = i % 2
        found = []
        for j, source in enumerate((in_gate, in_inner)):
            for m in range(2):
                found.append(pltpu.make_async_copy(source.at[m, pl.ds(i * cut, cut)], w_buf.at[slot, 2 * j + m],
                                                   w_sems.at[slot, 2 * j + m]))
        found.append(pltpu.make_async_copy(hidden.at[:, pl.ds(i * cut, cut)], hid_buf.at[slot], hid_sems.at[slot]))
        return found

    for i in range(2):
        for copy in weight_copies(i):
            copy.start()

    block = 128

    def proj_block(i, nothing):
        at = pl.ds(pl.multiple_of(i * block, block), block)
        grad = pre_grad[at, :]
        part = dot_f32(grad * widened(modes[0, at, :], channels), dt_proj[0], NT)
        part = part + dot_f32(grad * widened(modes[1, at, :], channels), dt_proj[1], NT)
        proj_buf[at, 0:rank_dim] = part.astype(low)
        proj_buf[at, rank_dim:rank_dim + LANES] = coeff[at, :].astype(low)
        return nothing

    lax.fori_loop(0, tokens // block, proj_block, 0)

    def red_copy(off):
        return pltpu.make_async_remote_copy(
            src_ref=proj_buf.at[pl.ds(pl.multiple_of(((z + off) % 4) * share, share), share)], dst_ref=proj_recv.at[off - 1],
            send_sem=red_send.at[off - 1], recv_sem=red_recv.at[off - 1], device_id=z_at(off), device_id_type=MESH)

    for off in (1, 2, 3):
        red_copy(off).start()
    outs.event(0)

    def product(pair, target, number):
        pair_tokens = pair.shape[0]
        tall = stage.shape[1]
        turns = normed_t.shape[0] // tall
        for m in range(2):
            def mask_rows(i, nothing):
                at = pl.ds(pl.multiple_of(i * block, block), block)
                mask_buf[at, :] = pair[at, :] * widened(modes[m, at, :], channels)
                return nothing
            lax.fori_loop(0, pair_tokens // block, mask_rows, 0)
            for j in range(turns):
                slot = (m * turns + j) % 2
                copy = pltpu.make_async_copy(stage.at[slot], target.at[m, pl.ds(j * tall, tall)], stage_sems.at[slot])
                if m * turns + j >= 2:
                    copy.wait()
                stage[slot] = dot_f32(normed_t[pl.ds(j * tall, tall), :], mask_buf[...]).astype(low)
                copy.start()
        for slot in range(2):
            pltpu.make_async_copy(stage.at[slot], target.at[0, pl.ds(0, tall)], stage_sems.at[slot]).wait()

    for off in (1, 2, 3):
        red_copy(off).wait_recv()
    mine = pl.ds(pl.multiple_of(z * share, share), share)
    total = proj_buf[mine, :].astype(jnp.float32)
    for k in range(3):
        total = total + proj_recv[k].astype(jnp.float32)
    proj_fin[mine, :] = total.astype(low)

    def all_copy(off):
        return pltpu.make_async_remote_copy(
            src_ref=proj_fin.at[mine], dst_ref=proj_fin.at[mine], send_sem=all_send.at[off - 1],
            recv_sem=all_recv.at[off - 1], device_id=z_at(off), device_id_type=MESH)

    for off in (1, 2, 3):
        all_copy(off).start()
    span = x_wide.shape[1] - 96
    mode_rows = span + rank_dim
    for m in range(2):
        ranks = rank_b[...] * modes[m, pl.ds(0, tokens), :]
        rows_out[pl.ds(m * mode_rows + span, rank_dim), :] = dot_f32(ranks, pre_grad[...], TN).astype(low)
    def dt_sums(i, carried):
        at = pl.ds(pl.multiple_of(i * block, block), block)
        grad = pre_grad[at, :].astype(jnp.float32)
        first = jnp.sum(grad * widened(modes[0, at, :].astype(jnp.float32), channels), axis=0, keepdims=True)
        return carried[0] + first, carried[1] + jnp.sum(grad, axis=0, keepdims=True) - first

    none_row = jnp.zeros((1, channels), jnp.float32)
    bias0, bias1 = lax.fori_loop(0, tokens // block, dt_sums, (none_row, none_row))
    for off in (1, 2, 3):
        all_copy(off).wait_recv()
    back.begin((0, 1))

    def act_block(i, bias):
        at = pl.ds(pl.multiple_of(i * block, block), block)
        proj = proj_fin[at, :]
        two = proj.shape[1]
        back = dot_f32(proj * widened(modes[0, at, :], two), x_wide[0])
        back = back + dot_f32(proj * widened(modes[1, at, :], two), x_wide[1])
        value = conv_sum[at, :]
        sig = jax.nn.sigmoid(value)
        grad = (act_part[at, :] + back) * sig * (1.0 + value * (1.0 - sig))
        conv_buf[at, :] = grad
        return bias + jnp.sum(grad, axis=0, keepdims=True)

    conv_buf[pl.ds(tokens, 8), :] = jnp.zeros((8, channels), jnp.float32)
    bias = lax.fori_loop(0, tokens // block, act_block, none_row)
    outs.event(1)
    gate.event(0)
    back.some((0,), True)
    back.begin((2,))
    taps = conv_w.shape[0]
    thin = 64

    def conv_block(i, sums):
        base = pl.multiple_of(i * thin, thin)
        grads = conv_buf[pl.ds(base, thin + 8), :]
        doc = docs[pl.ds(base, thin), :]
        inner = inner_x[pl.ds(base, thin), :]
        result = jnp.zeros((thin, channels), jnp.float32)
        new = []
        for offset in range(taps):
            moved = grads[offset:offset + thin, :] * doc[:, offset:offset + 1]
            tap = taps - 1 - offset
            result = result + moved * conv_w[tap:tap + 1, :]
            new.append(sums[offset] + jnp.sum(moved * inner, axis=0, keepdims=True))
        pair_buf[pl.ds(base, thin), :] = result.astype(low)
        return tuple(new)

    sums = lax.fori_loop(0, tokens // thin, conv_block, (none_row,) * taps)

    def core_copy():
        return pltpu.make_async_remote_copy(
            src_ref=pair_buf.at[pl.ds(0, tokens)], dst_ref=pair_buf.at[pl.ds(tokens, tokens)],
            send_sem=core_sems.at[0], recv_sem=core_sems.at[1], device_id=to_core, device_id_type=MESH)

    core_copy().start()
    back.some((1,), True)
    back.begin((3,))

    for i in range(slices):
        slot = i % 2
        for copy in weight_copies(i):
            copy.wait()
        third = tokens // 3
        out_copy = pltpu.make_async_copy(stage_n.at[slot], normed_out.at[:, pl.ds(i * cut, cut)], n_sems.at[slot])
        if i >= 2:
            out_copy.wait()

        def normed_rows(j, gain, slot=slot):
            at = pl.ds(pl.multiple_of(j * third, third), third)
            gate_grad, grad = gate_grads[at, :], pair_buf[at, :]
            zero = dot_f32(gate_grad, w_buf[slot, 0], NT) + dot_f32(grad, w_buf[slot, 2], NT)
            one = dot_f32(gate_grad, w_buf[slot, 1], NT) + dot_f32(grad, w_buf[slot, 3], NT)
            picked = jnp.where(inv[at, 1:2] > 0.5, zero, one)
            stage_n[slot, at, :] = picked.astype(low)
            return gain + jnp.sum(picked * hid_buf[slot, at, :].astype(jnp.float32) * inv[at, 0:1], axis=0, keepdims=True)

        gain = lax.fori_loop(0, 3, normed_rows, jnp.zeros((1, cut), jnp.float32))
        gain_buf[:, pl.ds(i * cut, cut)] = jnp.broadcast_to(gain, (8, cut))
        out_copy.start()
        if i + 2 < slices:
            for copy in weight_copies(i + 2):
                copy.start()
        if i == 0:
            back.some((2,), True)
            back.some((0,), False)
            back.begin((4,))
        elif i == 1:
            back.some((3,), True)
            back.some((1,), False)
            back.begin((5,))
        elif i == 2:
            outs.event(2)
            back.some((4,), True)
            back.some((2,), False)
        elif i == 3:
            back.some((5,), True)
            back.some((3,), False)
    for slot in range(2):
        pltpu.make_async_copy(stage_n.at[slot], normed_out.at[:, pl.ds(0, cut)], n_sems.at[slot]).wait()

    def gain_copy(off):
        return pltpu.make_async_remote_copy(
            src_ref=gain_buf, dst_ref=gain_recv.at[off - 1], send_sem=gain_send.at[off - 1],
            recv_sem=gain_recv_sem.at[off - 1], device_id=z_at(off), device_id_type=MESH)

    for off in (1, 2, 3):
        gain_copy(off).start()
    core_copy().wait_recv()
    product(pair_buf, inner_prod, 1)
    back.some((4, 5), False)
    gate.event(1)
    outs.event(3)
    for m in range(2):
        proj = proj_fin[...] * widened(modes[m, pl.ds(0, tokens), :], proj_fin.shape[1])
        rows_out[pl.ds(m * mode_rows, span), :] = dot_f32(proj, act_b[...], TN)[:span].astype(low)
    for off in (1, 2, 3):
        gain_copy(off).wait_recv()
    gain = gain_buf[0:1, :] + gain_recv[0, 0:1, :] + gain_recv[1, 0:1, :] + gain_recv[2, 0:1, :]
    gains = [gain[:, k * channels:(k + 1) * channels] for k in range(width // channels)]
    tail_rows = list(sums[::-1]) + [bias, bias0, bias1, extra[...]] + gains
    used = taps + 3 + extra.shape[0] + len(gains)
    tail_rows.append(jnp.zeros((32 - used, channels), jnp.float32))
    rows_out[pl.ds(2 * mode_rows, 32), :] = jnp.concatenate(tail_rows, axis=0).astype(low)
    gate.event(2)
    gate.event(3)
    outs.event(4)
    gate.event(4)
    back.done()
    for off in (1, 2, 3):
        red_copy(off).wait_send()
        all_copy(off).wait_send()
        gain_copy(off).wait_send()
    core_copy().wait_send()


def middle(pre_grad, act_part, coeff, conv_sum, inner_x, act_b, rank_b, dt_proj, x_wide, conv_w, docs, modes,
           gate_grads, normed_t, inv, extra, hidden, in_gate, in_inner, out_own, gate_own, z_own):
    tokens, channels = pre_grad.shape
    width = hidden.shape[1]
    low = jnp.bfloat16
    side = normed_t.shape[0] // 4
    cut = 512
    mode_rows = x_wide.shape[1] - 96 + dt_proj.shape[1]
    vmem, anywhere = pl.BlockSpec(memory_space=pltpu.VMEM), pl.BlockSpec(memory_space=pl.ANY)
    return pl.pallas_call(
        middle_kernel,
        in_specs=[vmem] * 16 + [anywhere] * 6,
        out_specs=[vmem] + [anywhere] * 5,
        out_shape=[
            jax.ShapeDtypeStruct((2 * mode_rows + 32, channels), low),
            jax.ShapeDtypeStruct((tokens, width), low),
            jax.ShapeDtypeStruct((2, 4 * side, channels), low),
            jax.ShapeDtypeStruct((2, 2, 4) + out_own.shape[1:], low),
            jax.ShapeDtypeStruct((2, 2, 4) + gate_own.shape[1:], low),
            jax.ShapeDtypeStruct(z_own.shape, low),
        ],
        scratch_shapes=[
            pltpu.VMEM((2, 4, cut, channels), low),
            pltpu.VMEM((2 * tokens, channels), low),
            pltpu.VMEM((2 * tokens, channels), low),
            pltpu.VMEM((tokens + 8, channels), jnp.float32),
            pltpu.VMEM((2, 2 * side, channels), low),
            pltpu.VMEM((2, tokens, cut), low),
            pltpu.VMEM((2, tokens, cut), low),
            pltpu.VMEM((tokens, 2 * LANES), low),
            pltpu.VMEM((3, tokens // 4, 2 * LANES), low),
            pltpu.VMEM((tokens, 2 * LANES), low),
            pltpu.VMEM((8, width), jnp.float32),
            pltpu.VMEM((3, 8, width), jnp.float32),
            DMA((3,)), DMA((3,)), DMA((3,)), DMA((3,)), DMA((2,)), DMA((3,)), DMA((3,)),
            DMA((2, 4)), DMA((2,)), DMA((2,)), DMA((2,)),
        ] + Share.scratch() + Share.scratch() + LineBack.scratch(z_own.shape[1]),
        input_output_aliases={21: 5},
        cost_estimate=pl.CostEstimate(flops=27_000_000_000, bytes_accessed=60_000_000, transcendentals=1_000_000),
        compiler_params=pltpu.CompilerParams(collective_id=3, has_side_effects=True, vmem_limit_bytes=61 * 1024 * 1024),
        name="middle",
    )(pre_grad, act_part, coeff, conv_sum, inner_x, act_b, rank_b, dt_proj, x_wide, conv_w, docs, modes,
      gate_grads, normed_t, inv, extra, hidden, in_gate, in_inner, out_own, gate_own, z_own)


def split_tail(part, count):
    lane = lax.broadcasted_iota(jnp.int32, part.shape, 1)
    high = part.astype(jnp.bfloat16).astype(jnp.float32)
    rest = pltpu.roll(part - high, count, axis=1)
    return jnp.where(lane < count, high, jnp.where(lane < 2 * count, rest, 0.0)).astype(jnp.bfloat16)


def join_tail(block, count):
    return block + pltpu.roll(block, block.shape[1] - count, axis=1)


def front_kernel(coeffs_wide, hidden, gain, conv_w, conv_b, docs, modes, x_wide, out_grad, view, out_proj,
                 w_inner, w_gate, normed_pair, cotan_pair, modes_pair,
                 normed, inverse, conv_sum, inner_x, act_b, gate_z, gated_grad, rank_out, coeff_out,
                 acc, view_buf, wide, stage, w_out, proj_buf, proj_recv, proj_fin,
                 view_sems, stage_sems, out_sems, red_send, red_recv, all_send, all_recv, pair_send, pair_recv, pair_local):
    tokens, width = hidden.shape
    channels = conv_w.shape[1]
    groups = channels // LANES
    low = jnp.bfloat16
    z = lax.axis_index("tensor")
    share = tokens // 4
    deep = stage.shape[2] // 2
    turns = width // deep
    block = 128

    def z_at(off):
        return {"tensor": (z + off) % 4}

    barrier = pltpu.get_barrier_semaphore()
    for off in (1, 2, 3):
        pl.semaphore_signal(barrier, inc=1, device_id=z_at(off), device_id_type=MESH)
    core, to_core = lax.axis_index("dp") % 2, place()[4]
    pl.semaphore_signal(barrier, inc=1, device_id=to_core, device_id_type=MESH)

    def half_of(ref, which):
        return ref.at[:, pl.ds(pl.multiple_of(which * (width // 2), width // 2), width // 2)]

    own_rows, other_rows = pl.ds(0, tokens), pl.ds(tokens, tokens)
    pairs = ((half_of(normed, core), half_of(normed, 1 - core), normed_pair.at[own_rows], normed_pair.at[other_rows]),
             (half_of(out_grad, core), half_of(out_grad, 1 - core), cotan_pair.at[own_rows], cotan_pair.at[other_rows]),
             (modes, modes, modes_pair.at[:, own_rows], modes_pair.at[:, other_rows]))

    def pair_copies(i):
        mine, theirs, here, there = pairs[i]
        return (pltpu.make_async_copy(mine, here, pair_local.at[i]),
                pltpu.make_async_remote_copy(src_ref=theirs, dst_ref=there, send_sem=pair_send.at[i], recv_sem=pair_recv.at[i],
                                             device_id=to_core, device_id_type=MESH))

    def view_copy(i, m):
        tall = deep * 2 * groups
        return pltpu.make_async_copy(view.at[m, pl.ds(pl.multiple_of(i * tall, tall), tall)], view_buf.at[i % 2, m],
                                     view_sems.at[i % 2, m])

    def stage_copy(i, half, m):
        target = w_inner if half == 0 else w_gate
        return pltpu.make_async_copy(stage.at[i % 2, half, pl.ds(m * deep, deep)],
                                     target.at[m, pl.ds(pl.multiple_of(i * deep, deep), deep)], stage_sems.at[i % 2, half, m])

    def out_copy(m):
        return pltpu.make_async_copy(out_proj.at[m], w_out.at[m], out_sems.at[m])

    for m in range(2):
        view_copy(0, m).start()
    for m in range(2):
        view_copy(1, m).start()
        out_copy(m).start()

    def norm_block(i, nothing):
        at = pl.ds(pl.multiple_of(i * block, block), block)
        rows = hidden[at, :].astype(jnp.float32)
        scale = lax.rsqrt(jnp.mean(rows * rows, axis=1, keepdims=True) + EPS)
        inverse[at, :] = jnp.broadcast_to(scale, (block, LANES))
        normed[at, :] = (rows * scale * gain[...]).astype(low)
        return nothing

    lax.fori_loop(0, tokens // block, norm_block, 0)
    acc[0:8, :] = jnp.zeros((8, channels), jnp.float32)

    def unpack(i):
        for m in range(2):
            wide[m] = view_buf[i % 2, m].astype(jnp.float32)
            for half in range(2):
                stage[i % 2, half, m * deep:(m + 1) * deep, :] = jnp.concatenate(
                    [wide[m, pl.ds(g * 2 + half, deep, stride=2 * groups), :] for g in range(groups)], axis=1).astype(low)

    def multiply(i, first):
        columns = normed[:, pl.ds(pl.multiple_of(i * deep, deep), deep)]
        left = jnp.concatenate([columns * widened(modes[0], deep), columns * widened(modes[1], deep)], axis=1)
        for half in range(2):
            product = dot_f32(left, stage[i % 2, half])
            if half == 0:
                acc[8:8 + tokens, :] = product if first else acc[8:8 + tokens, :] + product
            else:
                gate_z[...] = product if first else gate_z[...] + product

    def turn(i):
        for m in range(2):
            view_copy(i, m).wait()
        unpack(i)
        for m in range(2):
            for half in range(2):
                stage_copy(i, half, m).start()

    turn(0)
    multiply(0, True)
    for m in range(2):
        view_copy(2, m).start()
    turn(1)
    for m in range(2):
        view_copy(3, m).start()

    def looped(i, nothing):
        for m in range(2):
            for half in range(2):
                stage_copy(i, half, m).wait()
        multiply(i + 1, False)
        turn(i + 2)

        @pl.when(i + 4 < turns)
        def _():
            for m in range(2):
                view_copy(i + 4, m).start()
        return nothing

    lax.fori_loop(0, turns - 2, looped, 0)
    multiply(turns - 1, False)
    for i in (turns - 2, turns - 1):
        for m in range(2):
            for half in range(2):
                stage_copy(i, half, m).wait()

    taps = conv_w.shape[0]

    def conv_block(i, nothing):
        base = pl.multiple_of(i * block, block)
        at = pl.ds(base, block)
        rows = acc[pl.ds(base, block + 8), :]
        doc = docs[at, :]
        total = conv_b[...] + conv_w[taps - 1:taps, :] * rows[8:8 + block, :]
        for offset in range(1, taps):
            total = total + conv_w[taps - 1 - offset:taps - offset, :] * rows[8 - offset:8 - offset + block, :] * doc[:, offset:offset + 1]
        conv_sum[at, :] = total
        inner_x[at, :] = rows[8:8 + block, :]
        active = (total * jax.nn.sigmoid(total)).astype(low)
        act_b[at, :] = active
        part = dot_f32(active * widened(modes[0, at, :], channels), x_wide[0], NT)
        part = part + dot_f32(active * widened(modes[1, at, :], channels), x_wide[1], NT)
        proj_buf[at, 0:LANES] = part[:, :LANES].astype(low)
        proj_buf[at, LANES:2 * LANES] = split_tail(part[:, LANES:], coeffs_wide)
        return nothing

    lax.fori_loop(0, tokens // block, conv_block, 0)

    def red_copy(off):
        return pltpu.make_async_remote_copy(
            src_ref=proj_buf.at[pl.ds(pl.multiple_of(((z + off) % 4) * share, share), share)], dst_ref=proj_recv.at[off - 1],
            send_sem=red_send.at[off - 1], recv_sem=red_recv.at[off - 1], device_id=z_at(off), device_id_type=MESH)

    mine = pl.ds(pl.multiple_of(z * share, share), share)

    def all_copy(off):
        return pltpu.make_async_remote_copy(
            src_ref=proj_fin.at[mine], dst_ref=proj_fin.at[mine], send_sem=all_send.at[off - 1],
            recv_sem=all_recv.at[off - 1], device_id=z_at(off), device_id_type=MESH)

    pl.semaphore_wait(barrier, 4)
    for off in (1, 2, 3):
        red_copy(off).start()
    for i in range(3):
        for copy in pair_copies(i):
            copy.start()
    third = tokens // 3

    def grad_block(i):
        at = pl.ds(i * third, third)
        zero = dot_f32(out_grad[at, :], w_out[0], NT)
        one = dot_f32(out_grad[at, :], w_out[1], NT)
        gated_grad[at, :] = jnp.where(docs[at, 0:1] > 0.5, zero, one)

    for m in range(2):
        out_copy(m).wait()
    grad_block(0)
    for off in (1, 2, 3):
        red_copy(off).wait_recv()
    total = proj_buf[mine, :].astype(jnp.float32)
    for k in range(3):
        total = total + proj_recv[k].astype(jnp.float32)
    proj_fin[mine, 0:LANES] = total[:, :LANES].astype(low)
    proj_fin[mine, LANES:2 * LANES] = split_tail(join_tail(total[:, LANES:], coeffs_wide), coeffs_wide)
    for off in (1, 2, 3):
        all_copy(off).start()
    grad_block(1)
    grad_block(2)
    for off in (1, 2, 3):
        all_copy(off).wait_recv()
    rank_out[...] = proj_fin[:, 0:LANES]
    coeff_out[...] = join_tail(proj_fin[:, LANES:2 * LANES].astype(jnp.float32), coeffs_wide)
    for off in (1, 2, 3):
        red_copy(off).wait_send()
        all_copy(off).wait_send()
    for i in range(3):
        for copy in pair_copies(i):
            copy.wait()


def front(hidden, gain, conv_w, conv_b, docs, modes, x_wide, out_grad, in_proj, out_proj, coeffs_wide):
    tokens, width = hidden.shape
    channels = conv_w.shape[1]
    groups = channels // LANES
    low, f32 = jnp.bfloat16, jnp.float32
    view = in_proj.reshape(2, width, 2, groups, LANES).transpose(0, 1, 3, 2, 4).reshape(2, width * 2 * groups, LANES)
    deep = 256
    vmem, anywhere = pl.BlockSpec(memory_space=pltpu.VMEM), pl.BlockSpec(memory_space=pl.ANY)
    shape = jax.ShapeDtypeStruct
    return pl.pallas_call(
        functools.partial(front_kernel, coeffs_wide),
        in_specs=[vmem] * 8 + [anywhere] * 2,
        out_specs=[anywhere] * 5 + [vmem] * 9,
        out_shape=[
            shape((2, width, channels), low), shape((2, width, channels), low), shape((2 * tokens, width // 2), low),
            shape((2 * tokens, width // 2), low), shape((2, 2 * tokens, LANES), low), shape((tokens, width), low),
            shape((tokens, LANES), f32), shape((tokens, channels), f32), shape((tokens, channels), f32),
            shape((tokens, channels), low), shape((tokens, channels), f32), shape((tokens, channels), f32),
            shape((tokens, LANES), low), shape((tokens, LANES), f32),
        ],
        scratch_shapes=[
            pltpu.VMEM((tokens + 8, channels), f32),
            pltpu.VMEM((2, 2, deep * 2 * groups, LANES), low),
            pltpu.VMEM((2, deep * 2 * groups, LANES), f32),
            pltpu.VMEM((2, 2, 2 * deep, channels), low),
            pltpu.VMEM((2, channels, width), low),
            pltpu.VMEM((tokens, 2 * LANES), low),
            pltpu.VMEM((3, tokens // 4, 2 * LANES), low),
            pltpu.VMEM((tokens, 2 * LANES), low),
            DMA((2, 2)), DMA((2, 2, 2)), DMA((2,)), DMA((3,)), DMA((3,)), DMA((3,)), DMA((3,)), DMA((3,)), DMA((3,)), DMA((3,)),
        ],
        cost_estimate=pl.CostEstimate(flops=20_000_000_000, bytes_accessed=80_000_000, transcendentals=1_000_000),
        compiler_params=pltpu.CompilerParams(collective_id=4, has_side_effects=True, vmem_limit_bytes=60 * 1024 * 1024),
        name="front",
    )(hidden, gain, conv_w, conv_b, docs, modes, x_wide, out_grad, view, out_proj)


def products_kernel(gated, cotan, normed, gate, modes, split, weights,
                    out0, out1, gate0, gate1, partial, normed_t,
                    left_buf, right_buf, mode_buf, split_buf, w_buf, turned, mask_buf, stage, stage_wide,
                    load_sems, w_sems, stage_sems, wide_sems, turned_sem):
    pair_tokens, channels = left_buf.shape[1:]
    tokens, deep = split_buf.shape
    low = jnp.bfloat16
    block = 128
    loads = [pltpu.make_async_copy(source, target, load_sems.at[i]) for i, (source, target) in enumerate((
        (gated, left_buf.at[0]), (cotan, right_buf.at[0]), (modes, mode_buf), (normed, left_buf.at[1]), (gate, right_buf.at[1]),
        (split, split_buf)))]
    for copy in loads:
        copy.start()
    half = w_buf.shape[0] // 2
    w_loads = [pltpu.make_async_copy(weights.at[m], w_buf.at[pl.ds(m * half, half)], w_sems.at[m]) for m in range(2)]
    for copy in w_loads:
        copy.start()
    tall = stage.shape[1]
    turns = channels // tall
    flights = [None, None]

    def turn_left(which):
        def body(i, nothing):
            at = pl.ds(pl.multiple_of(i * block, block), block)
            turned[at, :] = left_buf[which, :, at].T
            return nothing
        lax.fori_loop(0, channels // block, body, 0)

    def multiply(which, targets):
        for m in range(2):
            def mask_rows(i, nothing):
                at = pl.ds(pl.multiple_of(i * block, block), block)
                mask_buf[at, :] = right_buf[which, at, :] * widened(mode_buf[m, at, :], channels)
                return nothing
            lax.fori_loop(0, pair_tokens // block, mask_rows, 0)
            for j in range(turns):
                slot = (m * turns + j) % 2
                if flights[slot] is not None:
                    flights[slot].wait()
                stage[slot] = dot_f32(turned[pl.ds(j * tall, tall), :], mask_buf[...]).astype(low)
                flights[slot] = pltpu.make_async_copy(stage.at[slot], targets[m].at[pl.ds(j * tall, tall)], stage_sems.at[slot])
                flights[slot].start()

    for copy in loads[:3]:
        copy.wait()
    turn_left(0)
    multiply(0, (out0, out1))
    for copy in loads[3:5]:
        copy.wait()
    turn_left(1)
    out_turned = pltpu.make_async_copy(turned, normed_t, turned_sem)
    out_turned.start()
    multiply(1, (gate0, gate1))
    loads[5].wait()
    for copy in w_loads:
        copy.wait()
    part = stage_wide.shape[1]
    wide_flights = [None, None]
    for j in range(tokens // part):
        slot = j % 2
        if wide_flights[slot] is not None:
            wide_flights[slot].wait()
        stage_wide[slot] = dot_f32(split_buf[pl.ds(j * part, part), :], w_buf[...]).astype(low)
        wide_flights[slot] = pltpu.make_async_copy(stage_wide.at[slot], partial.at[pl.ds(j * part, part)], wide_sems.at[slot])
        wide_flights[slot].start()
    for copy in flights + wide_flights + [out_turned]:
        copy.wait()


def make_products(gated, cotan, normed, gate, modes, split, weights):
    pair_tokens, channels = gated.shape
    tokens, deep = split.shape
    width = weights.shape[2]
    low = jnp.bfloat16
    anywhere = pl.BlockSpec(memory_space=pl.ANY)
    square = jax.ShapeDtypeStruct((channels, channels), low)
    return pl.pallas_call(
        products_kernel,
        in_specs=[anywhere] * 7,
        out_specs=[anywhere] * 6,
        out_shape=[square] * 4 + [jax.ShapeDtypeStruct((tokens, width), low), jax.ShapeDtypeStruct((channels, pair_tokens), low)],
        scratch_shapes=[
            pltpu.VMEM((2, pair_tokens, channels), low), pltpu.VMEM((2, pair_tokens, channels), low),
            pltpu.VMEM((2, pair_tokens, LANES), low), pltpu.VMEM((tokens, deep), low), pltpu.VMEM((deep, width), low),
            pltpu.VMEM((channels, pair_tokens), low), pltpu.VMEM((pair_tokens, channels), low),
            pltpu.VMEM((2, channels // 2, channels), low), pltpu.VMEM((2, tokens // 3, width), low),
            DMA((6,)), DMA((2,)), DMA((2,)), DMA((2,)), DMA,
        ],
        cost_estimate=pl.CostEstimate(flops=20_000_000_000, bytes_accessed=45_000_000, transcendentals=0),
        compiler_params=pltpu.CompilerParams(vmem_limit_bytes=56 * 1024 * 1024),
        name="products",
    )(gated, cotan, normed, gate, modes, split, weights)


def final_kernel(side, depth, where_ref, out_shared, out_own, gate_shared, gate_own, inner_shared, inner_own,
                 hidden, out_grad, inverse, gain, summed_out, normed_sum,
                 out_ref, in_ref, output, input_grad,
                 narrow, wide, row_in, row_out, in_sems, out_sems, row_in_sems, row_out_sems):
    x, y, core = where_ref[0], where_ref[1], where_ref[2]
    low, f32 = jnp.bfloat16, jnp.float32
    block = row_in.shape[2]
    jobs = []
    for which, (shared, own) in enumerate(((out_shared, out_own), (gate_shared, gate_own), (inner_shared, inner_own))):
        for mode in range(2):
            for owner in range(2):
                c = core if owner == 0 else 1 - core
                for k in range(4):
                    qx = x if k in (0, 1) else 1 - x
                    qy = y if k in (0, 2) else 1 - y
                    row = (qx * 2 + qy if mode == 0 else qy * 2 + qx) * side
                    if which == 0:
                        target = out_ref.at[mode, pl.ds(pl.multiple_of(row, side), side),
                                            pl.ds(pl.multiple_of(c * depth, depth), depth)]
                    else:
                        target = in_ref.at[mode, pl.ds(pl.multiple_of(c * 4 * side + row, side), side), 2 - which, :]
                    source = own.at[mode] if owner == 0 and k == 0 else shared.at[mode, owner, k]
                    jobs.append((source, target))
    slots = narrow.shape[0]
    loads = [pltpu.make_async_copy(jobs[i][0], narrow.at[i % slots], in_sems.at[i % slots]) for i in range(len(jobs))]
    stores = [pltpu.make_async_copy(wide.at[i % slots], jobs[i][1], out_sems.at[i % slots]) for i in range(len(jobs))]
    count = hidden.shape[0] // block

    def row_loads(i):
        at = pl.ds(i * block, block)
        return [pltpu.make_async_copy(ref.at[at], row_in.at[i % 2, j], row_in_sems.at[i % 2, j])
                for j, ref in enumerate((hidden, out_grad, summed_out, normed_sum))]

    def row_stores(i):
        at = pl.ds(i * block, block)
        return [pltpu.make_async_copy(row_out.at[i % 2, j], ref.at[at], row_out_sems.at[i % 2, j])
                for j, ref in enumerate((output, input_grad))]

    for copy in row_loads(0) + row_loads(1):
        copy.start()
    for i in range(slots):
        loads[i].start()
    per = -(-len(jobs) // count)
    for i in range(count):
        for copy in row_loads(i):
            copy.wait()
        if i >= 2:
            for copy in row_stores(i - 2):
                copy.wait()
        rows = row_in[i % 2, 0].astype(f32)
        scale = inverse[pl.ds(i * block, block), 0:1]
        scaled = row_in[i % 2, 3].astype(f32) * gain[...]
        mean = jnp.mean(scaled * rows, axis=1, keepdims=True)
        row_out[i % 2, 0] = (rows + row_in[i % 2, 2].astype(f32)).astype(low)
        row_out[i % 2, 1] = (row_in[i % 2, 1].astype(f32) + scale * scaled - rows * (scale * scale * scale) * mean).astype(low)
        for copy in row_stores(i):
            copy.start()
        if i + 2 < count:
            for copy in row_loads(i + 2):
                copy.start()
        for p in range(i * per, min((i + 1) * per, len(jobs))):
            loads[p].wait()
            if p >= slots:
                stores[p - slots].wait()
            wide[p % slots] = narrow[p % slots].astype(f32)
            stores[p].start()
            if p + slots < len(jobs):
                loads[p + slots].start()
    for p in range(len(jobs) - slots, len(jobs)):
        stores[p].wait()
    for i in (count - 2, count - 1):
        for copy in row_stores(i):
            copy.wait()


def final(where, out_shared, out_own, gate_shared, gate_own, inner_shared, inner_own, hidden, out_grad, inverse, gain,
          summed_out, normed_sum):
    side, depth = out_own.shape[1:]
    tokens, width = hidden.shape
    channels = 4 * side
    low, f32 = jnp.bfloat16, jnp.float32
    anywhere, vmem = pl.BlockSpec(memory_space=pl.ANY), pl.BlockSpec(memory_space=pltpu.VMEM)
    block, slots = 128, 6
    return pl.pallas_call(
        functools.partial(final_kernel, side, depth),
        in_specs=[pl.BlockSpec(memory_space=pltpu.SMEM)] + [anywhere] * 8 + [vmem] * 2 + [anywhere] * 2,
        out_specs=[anywhere] * 4,
        out_shape=[
            jax.ShapeDtypeStruct((2, channels, width), f32), jax.ShapeDtypeStruct((2, width, 2, channels), f32),
            jax.ShapeDtypeStruct((tokens, width), low), jax.ShapeDtypeStruct((tokens, width), low),
        ],
        scratch_shapes=[
            pltpu.VMEM((slots, side, depth), low), pltpu.VMEM((slots, side, depth), f32),
            pltpu.VMEM((2, 4, block, width), low), pltpu.VMEM((2, 2, block, width), low),
            DMA((slots,)), DMA((slots,)), DMA((2, 4)), DMA((2, 2)),
        ],
        cost_estimate=pl.CostEstimate(flops=50_000_000, bytes_accessed=91_000_000, transcendentals=0),
        compiler_params=pltpu.CompilerParams(vmem_limit_bytes=40 * 1024 * 1024),
        name="final_rows",
    )(where, out_shared, out_own, gate_shared, gate_own, inner_shared, inner_own, hidden, out_grad, inverse, gain,
      summed_out, normed_sum)


def scan_backward_kernel(states, groups, rows, unroll, count, joined,
                         bc_ref, pre_ref, act_ref, mixed_ref, keep_ref, alog_ref, skip_ref, h_ref, start_ref, *rest):
    if joined:
        prods, part_ref, rest = rest[:4], rest[4], rest[5:]
    pgrad_ref, apart_ref, bcg_ref, sum_ref, skipsum_ref = rest[:5]
    rest = rest[5:]
    if joined:
        out_own, gate_own, z_own, rest = rest[0], rest[1], rest[2], rest[3:]
    carry_ref, rate_scr, decay_scr, sk_scr, u_scr, dy_scr, w_scr, s_scr, p_scr, q_scr = rest[:10]
    rest = rest[10:]
    chunk = pl.program_id(0)
    if joined:
        line = LineReduce(part_ref, z_own, rest[0], rest[1], rest[2:5])
        outs = Reduce(prods[:2], out_own, *rest[5:8], rest[8:13])
        gate = Reduce(prods[2:], gate_own, *rest[13:16], rest[16:21])

        @pl.when(chunk == 0)
        def _():
            line.line.load().start()
            greet()
            outs.event(0)
            line.line.load().wait()
            line.line.begin((0,))

        for at in range(1, count):
            @pl.when(chunk == at)
            def _():
                if at < line.line.pieces:
                    line.line.begin((at,))
                if at == 2:
                    outs.event(1)
                elif at == 3:
                    gate.event(0)
                elif at == 5:
                    outs.event(2)
                elif at == 6:
                    outs.last()
                elif at == 8:
                    gate.event(1)
                elif at == 10:
                    gate.event(2)
                line.turn(at)

    @pl.when(chunk == 0)
    def _():
        decay = -jnp.exp(alog_ref[...])
        decay_scr[...] = decay
        rate_scr[...] = decay * LOG2E
        carry_ref[...] = jnp.zeros_like(carry_ref)
        sum_ref[...] = jnp.zeros_like(sum_ref)
        skipsum_ref[...] = jnp.zeros_like(skipsum_ref)

    step = softplus(pre_ref[...])
    act = act_ref[...].astype(jnp.float32)
    mixed = mixed_ref[...].astype(jnp.float32)
    spread_rows(u_scr, step * act, groups)
    spread_rows(dy_scr, mixed, groups)
    spread_rows(sk_scr, jnp.where(keep_ref[...] > 0.0, step, BIG), groups)
    skipsum_ref[...] += jnp.sum(mixed * act, axis=0, keepdims=True)

    def one(t, carried, before):
        at = pl.multiple_of(t * groups, groups)
        sk = sk_scr[pl.ds(at, groups), :]
        u = u_scr[pl.ds(at, groups), :]
        dy = dy_scr[pl.ds(at, groups), :]
        w = jnp.zeros_like(u)
        s = jnp.zeros_like(u)
        new, pb, pc = [], [], []
        for n in range(states):
            g = dy * bc_ref[t, states + n] + carried[n]
            pb.append(g * u)
            pc.append(dy * h_ref[t, n])
            w = w + g * bc_ref[t, n]
            fg = jnp.exp2(sk * rate_scr[n]) * g
            lg = fg * before(n)
            s = s + lg * decay_scr[n]
            sum_ref[n] += lg * sk
            new.append(fg)
        w_scr[pl.ds(at, groups), :] = w
        s_scr[pl.ds(at, groups), :] = s
        both = pb + pc
        batch = max(1, 16 // groups)
        for j in range(0, 2 * states, batch):
            p_scr[t, pl.ds(j * groups, batch * groups), :] = jnp.concatenate(
                both[j:j + batch], axis=0).astype(jnp.bfloat16)
        return tuple(new)

    def looped(i, carried):
        t = rows - 1 - i
        return one(t, carried, lambda n: h_ref[t - 1, n])

    last = lax.fori_loop(0, rows - 1, looped, tuple(carry_ref[n] for n in range(states)), unroll=unroll)
    last = one(0, last, lambda n: start_ref[0, n])
    for n in range(states):
        carry_ref[n] = last[n]

    ones = jnp.ones((16, LANES), jnp.bfloat16)

    def reduce_one(t, nothing):
        q = lax.dot_general(ones, p_scr[t], (((1,), (1,)), ((), ())), preferred_element_type=jnp.float32)
        q_scr[pl.ds(t, 1), :] = q[0:1]
        return nothing

    lax.fori_loop(0, rows, reduce_one, 0, unroll=4)
    shape = (2 * states * groups, LANES)
    pick = (lax.broadcasted_iota(jnp.int32, shape, 0) // groups == lax.broadcasted_iota(jnp.int32, shape, 1))
    pick = pick.astype(jnp.float32).astype(jnp.bfloat16)
    q = q_scr[...]
    high = q.astype(jnp.bfloat16)
    low = (q - high.astype(jnp.float32)).astype(jnp.bfloat16)
    bcg_ref[...] = (jnp.dot(high, pick, preferred_element_type=jnp.float32)
                    + jnp.dot(low, pick, preferred_element_type=jnp.float32))
    w = gather_rows(w_scr, rows, groups)
    s = gather_rows(s_scr, rows, groups)
    pgrad_ref[...] = ((act * w + s) * jax.nn.sigmoid(pre_ref[...])).astype(pgrad_ref.dtype)
    apart_ref[...] = mixed * skip_ref[...] + step * w

    if joined:
        @pl.when(chunk == count - 1)
        def _():
            gate.last()
            outs.done()
            gate.done()
            line.done()


def scan_backward(bc, pre, act, mixed, keep, a_log3, skip, h, starts, products=None, z_part=None, rows=64, unroll=3, pieces=6):
    tokens, channels = pre.shape
    groups = channels // LANES
    states = a_log3.shape[0]
    count = tokens // rows
    joined = products is not None
    wide = pl.BlockSpec((rows, channels), lambda i: (count - 1 - i, 0))
    whole3 = pl.BlockSpec((states, groups, LANES), lambda i: (0, 0, 0))
    row = pl.BlockSpec((1, channels), lambda i: (0, 0))
    anywhere = pl.BlockSpec(memory_space=pl.ANY)
    small = lambda: pltpu.VMEM((states, groups, LANES), jnp.float32)
    long = lambda: pltpu.VMEM((rows * groups, LANES), jnp.float32)
    extra, extra_shapes, extra_scratch = [], [], []
    if joined:
        side, depth = products[0].shape[0] // 4, products[0].shape[1]
        part = z_part.reshape(2, pieces, tokens // 2 // pieces, z_part.shape[1])
        extra = list(products) + [part]
        extra_shapes = [jax.ShapeDtypeStruct((2, side, depth), jnp.bfloat16)] * 2 + [jax.ShapeDtypeStruct(part.shape, jnp.bfloat16)]
        extra_scratch = LineReduce.scratch(*part.shape[1:]) + Reduce.scratch(side, depth) + Reduce.scratch(side, depth)
    settings = dict(collective_id=2, has_side_effects=True) if joined else {}
    outs = pl.pallas_call(
        functools.partial(scan_backward_kernel, states, groups, rows, unroll, count, joined),
        grid=(count,),
        in_specs=[
            pl.BlockSpec((rows, 2 * states), lambda i: (count - 1 - i, 0), memory_space=pltpu.SMEM),
            wide, wide, wide,
            pl.BlockSpec((rows, 1), lambda i: (count - 1 - i, 0)),
            whole3, row,
            pl.BlockSpec((rows, states, groups, LANES), lambda i: (count - 1 - i, 0, 0, 0)),
            pl.BlockSpec((1, states, groups, LANES), lambda i: (count - 1 - i, 0, 0, 0)),
        ] + [anywhere] * len(extra),
        out_specs=[wide, wide, pl.BlockSpec((rows, LANES), lambda i: (count - 1 - i, 0)), whole3, row]
        + [anywhere] * len(extra_shapes),
        out_shape=[
            jax.ShapeDtypeStruct((tokens, channels), jnp.bfloat16),
            jax.ShapeDtypeStruct((tokens, channels), jnp.float32),
            jax.ShapeDtypeStruct((tokens, LANES), jnp.float32),
            jax.ShapeDtypeStruct((states, groups, LANES), jnp.float32),
            jax.ShapeDtypeStruct((1, channels), jnp.float32),
        ] + extra_shapes,
        scratch_shapes=[small(), small(), small(), long(), long(), long(), long(), long(),
                        pltpu.VMEM((rows, 2 * states * groups, LANES), jnp.bfloat16),
                        pltpu.VMEM((rows, 2 * states * groups), jnp.float32)] + extra_scratch,
        cost_estimate=pl.CostEstimate(flops=60 * tokens * channels * states,
                                      bytes_accessed=4 * tokens * channels * states,
                                      transcendentals=tokens * channels * states),
        compiler_params=pltpu.CompilerParams(vmem_limit_bytes=52 * 1024 * 1024, **settings),
        name="scan_backward",
    )(bc, pre, act, mixed, keep, a_log3, skip, h, starts, *extra)
    return outs


def lagged(values, offset):
    padding = [(offset, 0)] + [(0, 0)] * (values.ndim - 1)
    return jnp.pad(values, padding)[: values.shape[0]]


def leading(values, offset):
    padding = [(0, offset)] + [(0, 0)] * (values.ndim - 1)
    return jnp.pad(values, padding)[offset:]


def pick_dot(left_side, weights, first_mode):
    first_part = jnp.dot(left_side, weights[0], preferred_element_type=jnp.float32)
    second_part = jnp.dot(left_side, weights[1], preferred_element_type=jnp.float32)
    return jnp.where(first_mode, first_part, second_part)


def pick_back(gradient, weights, first_mode):
    dims = (((1,), (1,)), ((), ()))
    first_part = lax.dot_general(gradient, weights[0], dims, preferred_element_type=jnp.float32)
    second_part = lax.dot_general(gradient, weights[1], dims, preferred_element_type=jnp.float32)
    return jnp.where(first_mode, first_part, second_part)


def weight_grads(left_side, gradient, first_mode):
    nothing = jnp.zeros_like(gradient)
    dims = (((0,), (0,)), ((), ()))
    first_part = lax.dot_general(
        left_side,
        jnp.where(first_mode, gradient, nothing),
        dims,
        preferred_element_type=jnp.float32,
    )
    second_part = lax.dot_general(
        left_side,
        jnp.where(first_mode, nothing, gradient),
        dims,
        preferred_element_type=jnp.float32,
    )
    return jnp.stack([first_part, second_part])


def finish_rows(normed_grad, hidden, inverse, cotan, norm_gain):
    scaled = normed_grad * norm_gain
    gain_terms = jnp.sum(normed_grad * hidden * inverse, axis=0)
    cubed = inverse * inverse * inverse
    rows = (
        cotan + inverse * scaled - hidden * cubed * jnp.mean(scaled * hidden, axis=1, keepdims=True)
    )
    return (rows.astype(jnp.bfloat16), gain_terms)


def swap(values, distance):
    return lax.ppermute(values, "dp", [(i, i ^ distance) for i in range(8)])


CORE = 1


def tie(values, *others):
    return lax.optimization_barrier((values,) + others)[0]


def z_sum(values, size, dtype=jnp.bfloat16):
    distance = 1
    while distance < size:
        low = values.astype(dtype)
        got = lax.ppermute(low, "tensor", [(i, i ^ distance) for i in range(size)])
        values = low.astype(jnp.float32) + got.astype(jnp.float32)
        distance *= 2
    return values


def shards(names, hidden_in, segment_ids, modality, norm_gain, in_proj, conv_weight, conv_bias, x_proj, dt_proj, dt_bias,
           a_log, skip_gain, out_proj, out_grad):
    tokens, model_width = hidden_in.shape
    conv_taps, channels = conv_weight.shape
    rank_dim = dt_proj.shape[1]
    state_dim = a_log.shape[0]
    groups = channels // LANES
    ways = names["tensor"]
    by_hand = names["dp"] == 8 and names["tensor"] == 4
    low = jnp.bfloat16
    rank = lax.axis_index("dp")
    core, x_at, y_at = rank % 2, (rank // 2) % 2, rank // 4
    where = jnp.stack([x_at, y_at, core]).astype(jnp.int32)
    first_mode = (modality == 0)[:, None]
    nothing = jnp.zeros((), low)
    dims = (((0,), (0,)), ((), ()))

    def masked_products(left, right, modes, mask_left):
        products = []
        for chosen in (modes, jnp.logical_not(modes)):
            one = jnp.where(chosen, left, nothing) if mask_left else left
            two = right if mask_left else jnp.where(chosen, right, nothing)
            products.append(lax.dot_general(one, two, dims, preferred_element_type=jnp.float32).astype(low))
        return jnp.stack(products)

    same_doc = [jnp.ones((tokens, 1), jnp.float32)]
    for offset in range(1, conv_taps):
        earlier_seg = jnp.pad(segment_ids, (offset, 0), constant_values=-1)[:tokens]
        same_doc.append((earlier_seg == segment_ids).astype(jnp.float32)[:, None])
    if by_hand:
        modes_own = jnp.broadcast_to(jnp.stack([first_mode, jnp.logical_not(first_mode)]), (2, tokens, LANES)).astype(low)
        x_wide = jnp.pad(jnp.swapaxes(x_proj, 1, 2), ((0, 0), (0, 96), (0, 0)))
        facts = jnp.concatenate([first_mode.astype(jnp.float32)] + same_doc[1:], axis=1)
        (in_inner, in_gate, normed_pair, cotan_pair, modes, _, inverse, conv_sum, inner_x, activated_b, gate_z, gated_grad, rank_b, coeffs) = front(
            hidden_in, norm_gain[None], conv_weight, conv_bias[None], facts, modes_own, x_wide, out_grad, in_proj, out_proj,
            2 * state_dim)
        coeffs = coeffs[:, :2 * state_dim]
    else:
        hidden = hidden_in.astype(jnp.float32)
        inverse = lax.rsqrt(jnp.mean(hidden * hidden, axis=1, keepdims=True) + EPS)
        normed_b = (hidden * inverse * norm_gain).astype(low)
        in_inner = in_proj[:, :, 0, :]
        in_gate = in_proj[:, :, 1, :]
        inner_x = pick_dot(normed_b, in_inner, first_mode)
        conv_sum = conv_bias + conv_weight[conv_taps - 1] * inner_x
        for offset in range(1, conv_taps):
            conv_sum = conv_sum + conv_weight[conv_taps - 1 - offset] * lagged(inner_x, offset) * same_doc[offset]
        activated_b = jax.nn.silu(conv_sum).astype(low)
        projected = z_sum(pick_dot(activated_b, x_proj, first_mode), ways)
        rank_b = projected[:, :rank_dim].astype(low)
        coeffs = projected[:, rank_dim:]
        gate_z = pick_dot(normed_b, in_gate, first_mode)
        gated_grad = pick_back(out_grad, out_proj, first_mode)
    step_pre = pick_dot(rank_b, dt_proj, first_mode) + jnp.where(first_mode, dt_bias[0], dt_bias[1])
    keep = same_doc[1]
    a_log3 = a_log.reshape(state_dim, groups, LANES)
    skip_row = skip_gain[None]
    forward = scan_forward(coeffs, step_pre, activated_b, gate_z, gated_grad, keep, a_log3, skip_row,
                           first_mode.astype(jnp.float32), by_hand)
    gated_b, gate_grad_b, mixed_grad, states, starts = forward[:5]
    if by_hand:
        made = make_products(gated_b, cotan_pair, normed_pair, gate_grad_b, modes, forward[5], out_proj)
        products, partial_out, normed_t = made[:4], made[4], made[5]
        back = scan_backward(coeffs, step_pre, activated_b, mixed_grad, keep, a_log3, skip_row, states, starts,
                             products, partial_out)
        out_own, gate_own, z_own = back[5:]
    else:
        partial_out = pick_dot(gated_b, out_proj, first_mode).astype(low)
        back = scan_backward(coeffs, step_pre, activated_b, mixed_grad, keep, a_log3, skip_row, states, starts)
        summed_out = lax.psum(partial_out, "tensor")
        out_proj_grad = lax.psum(weight_grads(gated_b, out_grad, first_mode).astype(low), "dp").astype(jnp.float32)
        gate_proj_grad = lax.psum(weight_grads(normed_b, gate_grad_b, first_mode).astype(low), "dp")
    pre_grad_b, act_part, coeff_grad, sums, skips = back[:5]
    a_log_grad = sums.reshape(state_dim, channels) * -jnp.exp(a_log)
    mode_rows = x_proj.shape[2] + rank_dim
    if by_hand:
        later = jnp.stack([same_doc[0]] + [leading(same_doc[k], k) for k in range(1, conv_taps)], axis=1)[:, :, 0]
        row_facts = jnp.concatenate([inverse[:, :1], first_mode.astype(jnp.float32)], axis=1)
        rows, normed_low, inner_product, out_shared, gate_shared, z_res = middle(
            pre_grad_b, act_part, coeff_grad, conv_sum, inner_x, activated_b, rank_b, dt_proj, x_wide, conv_weight, later, modes,
            gate_grad_b, normed_t, row_facts, jnp.concatenate([a_log_grad, skips], axis=0),
            hidden_in, in_gate, in_inner, out_own, gate_own, z_own)
        summed_out = z_res.reshape(tokens, model_width)
    else:
        pre_grad = pre_grad_b.astype(jnp.float32)
        dt_bias_grad = jnp.stack([
            jnp.sum(jnp.where(first_mode, pre_grad, 0.0), axis=0),
            jnp.sum(jnp.where(first_mode, 0.0, pre_grad), axis=0)])
        rank_part = pick_back(pre_grad_b, dt_proj, first_mode)
        proj_grad_b = z_sum(jnp.concatenate([rank_part, coeff_grad[:, :2 * state_dim]], axis=1), ways).astype(low)
        act_grad = act_part + pick_back(proj_grad_b, x_proj, first_mode)
        sig_conv = jax.nn.sigmoid(conv_sum)
        conv_grad = act_grad * sig_conv * (1.0 + conv_sum * (1.0 - sig_conv))
        conv_bias_grad = jnp.sum(conv_grad, axis=0)
        weight_rows = []
        x_grad = jnp.zeros_like(inner_x)
        for tap_index in range(conv_taps):
            offset = conv_taps - 1 - tap_index
            masked = conv_grad * same_doc[offset]
            weight_rows.append(jnp.sum(masked * lagged(inner_x, offset), axis=0))
            x_grad = x_grad + conv_weight[tap_index] * leading(masked, offset)
        x_grad_b = x_grad.astype(low)
        normed_part = pick_back(x_grad_b, in_inner, first_mode) + pick_back(gate_grad_b, in_gate, first_mode)
        gain_part = jnp.sum(normed_part * (hidden * inverse), axis=0).reshape(-1, channels)
        gain_part = lax.psum(gain_part, "tensor")
        small_modes = jnp.concatenate([
            weight_grads(proj_grad_b, activated_b, first_mode), weight_grads(rank_b, pre_grad_b, first_mode)], axis=1)
        rows = jnp.concatenate([small_modes.reshape(-1, channels), jnp.stack(weight_rows), conv_bias_grad[None], dt_bias_grad,
                                a_log_grad, skips, gain_part], axis=0).astype(low)
    summed_rows = lax.psum(rows, "dp")
    if by_hand:
        (inner_shared,), (inner_own,), normed_sum = tail_exchange([inner_product], normed_low)

        out_proj_grad, in_proj_grad, output, input_grad = final(
            tie(where, summed_rows), out_shared, out_own, gate_shared, gate_own, inner_shared, inner_own,
            hidden_in, out_grad, inverse, norm_gain[None], summed_out, normed_sum)
    else:
        inner_proj_grad = lax.psum(weight_grads(normed_b, x_grad_b, first_mode).astype(low), "dp")
        in_proj_grad = jnp.stack([inner_proj_grad, gate_proj_grad], axis=2).astype(jnp.float32)
        normed_sum = lax.psum(normed_part.astype(low), "tensor")
        output = (hidden + summed_out.astype(jnp.float32)).astype(low)
        cotan = out_grad.astype(jnp.float32)
        input_grad, _ = finish_rows(normed_sum.astype(jnp.float32), hidden, inverse, cotan, norm_gain)
    summed_rows = summed_rows.astype(jnp.float32)
    small_modes, rows = summed_rows[:2 * mode_rows].reshape(2, mode_rows, channels), summed_rows[2 * mode_rows:]
    x_proj_grad = jnp.swapaxes(small_modes[:, :-rank_dim], 1, 2)
    dt_proj_grad = small_modes[:, -rank_dim:]
    norm_gain_grad = rows[conv_taps + 4 + state_dim:].reshape(-1)[:model_width]
    at = conv_taps + 1
    return (output, input_grad, norm_gain_grad, in_proj_grad, rows[:conv_taps], rows[conv_taps], x_proj_grad,
            dt_proj_grad, rows[at:at + 2], rows[at + 2:at + 2 + state_dim], rows[at + 2 + state_dim], out_proj_grad)


def solution(mesh):
    in_specs = (
        P("dp", None),
        P("dp"),
        P("dp"),
        P(),
        P(None, None, None, "tensor"),
        P(None, "tensor"),
        P("tensor"),
        P(None, "tensor", None),
        P(None, None, "tensor"),
        P(None, "tensor"),
        P(None, "tensor"),
        P("tensor"),
        P(None, "tensor", None),
        P("dp", None),
    )
    out_specs = (
        P("dp", None),
        P("dp", None),
        P(),
        P(None, None, None, "tensor"),
        P(None, "tensor"),
        P("tensor"),
        P(None, "tensor", None),
        P(None, None, "tensor"),
        P(None, "tensor"),
        P(None, "tensor"),
        P("tensor"),
        P(None, "tensor", None),
    )
    names = dict(mesh.shape)
    return jax.shard_map(functools.partial(shards, names), mesh=mesh, in_specs=in_specs, out_specs=out_specs, check_vma=False)
```

```python
import functools

import jax
import jax.numpy as jnp
from jax import lax
from jax.experimental import pallas as pl
from jax.experimental.pallas import tpu as pltpu
from jax.sharding import PartitionSpec as P

EPS = 1e-05

LANES = 128
BIG = 1000.0
LOG2E = 1.4426950408889634


def softplus(v):
    return jnp.maximum(v, 0.0) + jnp.log1p(jnp.exp(-jnp.abs(v)))


def spread_rows(scratch, values, groups):
    rows = values.shape[0]
    for g in range(groups):
        scratch[pl.ds(g, rows, stride=groups), :] = values[:, g * LANES:(g + 1) * LANES]


def gather_rows(scratch, rows, groups):
    return jnp.concatenate(
        [scratch[pl.ds(g, rows, stride=groups), :] for g in range(groups)], axis=1)


def scan_forward_kernel(states, groups, rows, unroll, count, joined,
                        bc_ref, pre_ref, act_ref, z_ref, gg_ref, keep_ref, alog_ref, skip_ref, mode_ref,
                        gated_ref, ggrad_ref, mixed_ref, h_ref, start_ref, *rest):
    chunk = pl.program_id(0)
    if joined:
        split_ref, rate_scr, state_scr, sk_scr, u_scr, y_scr, gated_all, ggrad_all, send_sems, recv_sems, local_sems = rest
        tokens = rows * count
        to_core = place()[4]

        def pair_copies(at, i):
            source, target = ((gated_all, gated_ref), (ggrad_all, ggrad_ref))[i]
            base = at * rows
            return (pltpu.make_async_copy(source.at[pl.ds(base, rows)], target.at[pl.ds(base, rows)], local_sems.at[at, i]),
                    pltpu.make_async_remote_copy(
                        src_ref=source.at[pl.ds(base, rows)], dst_ref=target.at[pl.ds(tokens + base, rows)],
                        send_sem=send_sems.at[at, i], recv_sem=recv_sems.at[at, i], device_id=to_core, device_id_type=MESH))

        @pl.when(chunk == 0)
        def _():
            barrier = pltpu.get_barrier_semaphore()
            pl.semaphore_signal(barrier, inc=1, device_id=to_core, device_id_type=MESH)
            pl.semaphore_wait(barrier, 1)
    else:
        rate_scr, state_scr, sk_scr, u_scr, y_scr = rest

    @pl.when(chunk == 0)
    def _():
        rate_scr[...] = jnp.exp(alog_ref[...]) * (-LOG2E)
        state_scr[...] = jnp.zeros_like(state_scr)

    step = softplus(pre_ref[...])
    act = act_ref[...].astype(jnp.float32)
    spread_rows(u_scr, step * act, groups)
    spread_rows(sk_scr, jnp.where(keep_ref[...] > 0.0, step, BIG), groups)
    start_ref[0] = state_scr[...]

    def one(t, held):
        at = pl.multiple_of(t * groups, groups)
        sk = sk_scr[pl.ds(at, groups), :]
        u = u_scr[pl.ds(at, groups), :]
        y = jnp.zeros_like(u)
        new = []
        for n in range(states):
            h = jnp.exp2(sk * rate_scr[n]) * held[n] + u * bc_ref[t, n]
            h_ref[t, n] = h
            y = y + h * bc_ref[t, states + n]
            new.append(h)
        y_scr[pl.ds(at, groups), :] = y
        return tuple(new)

    last = lax.fori_loop(0, rows, one, tuple(state_scr[n] for n in range(states)), unroll=unroll)
    for n in range(states):
        state_scr[n] = last[n]
    mixed_out = gather_rows(y_scr, rows, groups) + skip_ref[...] * act
    z = z_ref[...].astype(jnp.float32)
    gg = gg_ref[...].astype(jnp.float32)
    sig = jax.nn.sigmoid(z)
    silu = z * sig
    gated = mixed_out * silu
    gate_grad = (gg * mixed_out * sig * (1.0 + z * (1.0 - sig))).astype(ggrad_ref.dtype)
    mixed_ref[...] = gg * silu
    if joined:
        channels = gated.shape[1]
        first = mode_ref[...]
        split_ref[:, 0:channels] = (gated * first).astype(split_ref.dtype)
        split_ref[:, channels:2 * channels] = (gated * (1.0 - first)).astype(split_ref.dtype)
        at = pl.ds(pl.multiple_of(chunk * rows, rows), rows)
        gated_all[at, :] = gated.astype(gated_ref.dtype)
        ggrad_all[at, :] = gate_grad
        for k in range(count):
            @pl.when(chunk == k)
            def _():
                for i in range(2):
                    for copy in pair_copies(k, i):
                        copy.start()

        @pl.when(chunk == count - 1)
        def _():
            for k in range(count):
                for i in range(2):
                    for copy in pair_copies(k, i):
                        copy.wait()
    else:
        gated_ref[...] = gated.astype(gated_ref.dtype)
        ggrad_ref[...] = gate_grad


def scan_forward(bc, pre, act, z, gg, keep, a_log3, skip, mode, joined, rows=64, unroll=8):
    tokens, channels = pre.shape
    groups = channels // LANES
    states = a_log3.shape[0]
    count = tokens // rows
    wide = pl.BlockSpec((rows, channels), lambda i: (i, 0))
    thin = pl.BlockSpec((rows, 1), lambda i: (i, 0))
    whole3 = pl.BlockSpec((states, groups, LANES), lambda i: (0, 0, 0))
    low, f32 = jnp.bfloat16, jnp.float32
    long = lambda: pltpu.VMEM((rows * groups, LANES), f32)
    small = lambda: pltpu.VMEM((states, groups, LANES), f32)
    anywhere = pl.BlockSpec(memory_space=pl.ANY)
    tall = 2 * tokens if joined else tokens
    settings = dict(collective_id=5, has_side_effects=True) if joined else {}
    return pl.pallas_call(
        functools.partial(scan_forward_kernel, states, groups, rows, unroll, count, joined),
        grid=(count,),
        in_specs=[
            pl.BlockSpec((rows, 2 * states), lambda i: (i, 0), memory_space=pltpu.SMEM),
            wide, wide, wide, wide, thin, whole3,
            pl.BlockSpec((1, channels), lambda i: (0, 0)), thin,
        ],
        out_specs=[
            anywhere if joined else wide, anywhere if joined else wide, wide,
            pl.BlockSpec((rows, states, groups, LANES), lambda i: (i, 0, 0, 0)),
            pl.BlockSpec((1, states, groups, LANES), lambda i: (i, 0, 0, 0)),
        ] + ([pl.BlockSpec((rows, 2 * channels), lambda i: (i, 0))] if joined else []),
        out_shape=[
            jax.ShapeDtypeStruct((tall, channels), low),
            jax.ShapeDtypeStruct((tall, channels), low),
            jax.ShapeDtypeStruct((tokens, channels), f32),
            jax.ShapeDtypeStruct((tokens, states, groups, LANES), f32),
            jax.ShapeDtypeStruct((count, states, groups, LANES), f32),
        ] + ([jax.ShapeDtypeStruct((tokens, 2 * channels), low)] if joined else []),
        scratch_shapes=[small(), small(), long(), long(), long()] + ([
            pltpu.VMEM((tokens, channels), low), pltpu.VMEM((tokens, channels), low),
            pltpu.SemaphoreType.DMA((count, 2)), pltpu.SemaphoreType.DMA((count, 2)), pltpu.SemaphoreType.DMA((count, 2)),
        ] if joined else []),
        compiler_params=pltpu.CompilerParams(vmem_limit_bytes=48 * 1024 * 1024, **settings),
        name="scan_forward",
    )(bc, pre, act, z, gg, keep, a_log3, skip, mode)


MESH = pl.DeviceIdType.MESH
DMA = pltpu.SemaphoreType.DMA


def add_rows(target, left, right, rows, slab):
    def body(i, nothing):
        at = pl.ds(pl.multiple_of(i * slab, slab), slab)
        target[at, :] = (left[at, :].astype(jnp.float32) + right[at, :].astype(jnp.float32)).astype(jnp.bfloat16)
        return nothing
    lax.fori_loop(0, rows // slab, body, 0)


def place():
    dp = lax.axis_index("dp")
    x, y, core = (dp // 2) % 2, dp // 4, dp % 2
    return x, y, {"dp": dp + 2 - 4 * x}, {"dp": dp + 4 - 8 * y}, {"dp": dp + 1 - 2 * core}


def greet():
    z = lax.axis_index("tensor")
    barrier = pltpu.get_barrier_semaphore()
    for target in place()[2:]:
        pl.semaphore_signal(barrier, inc=1, device_id=target, device_id_type=MESH)

    @pl.when(z > 0)
    def _():
        pl.semaphore_signal(barrier, inc=1, device_id={"tensor": z - 1}, device_id_type=MESH)

    @pl.when(z < 3)
    def _():
        pl.semaphore_signal(barrier, inc=1, device_id={"tensor": z + 1}, device_id_type=MESH)

    @pl.when((z > 0) & (z < 3))
    def _():
        pl.semaphore_wait(barrier, 5)

    @pl.when((z == 0) | (z == 3))
    def _():
        pl.semaphore_wait(barrier, 4)


class Exchange:
    def __init__(self, prod, out, held, half_buf, quarter_buf, sems, summed=None):
        self.summed = summed
        self.prod, self.held, self.half_buf, self.quarter_buf = prod, held, half_buf, quarter_buf
        self.out, self.own = out
        (self.half_send, self.half_recv, self.quarter_send, self.quarter_recv,
         self.share_send, self.share_recv, self.core_send, self.core_recv, self.local) = sems
        x, y, self.to_x, self.to_y, self.to_core = place()
        self.firsts, self.seconds = (x, y), (y, x)
        self.ways = ((self.to_x, self.to_y), (self.to_y, self.to_x))
        self.side = half_buf.shape[2]

    @staticmethod
    def scratch(side, depth):
        low = jnp.bfloat16
        return [pltpu.VMEM((2, 2, side, depth), low), pltpu.VMEM((2, 2, side, depth), low), pltpu.VMEM((2, side, depth), low),
                DMA((2, 2)), DMA((2, 2)), DMA((2,)), DMA((2,)), DMA((2, 4)), DMA((2, 4)), DMA((2, 4)), DMA((2, 4)), DMA((2, 3))]

    def rows(self, mode, k, mine):
        first, second = self.firsts[mode], self.seconds[mode]
        half = first if mine else 1 - first
        quarter = 1 - second if k == 0 else second
        return pl.ds(pl.multiple_of((half * 2 + quarter) * self.side, self.side), self.side)

    def half_copy(self, mode, k):
        return pltpu.make_async_remote_copy(
            src_ref=self.prod[mode].at[self.rows(mode, k, False)], dst_ref=self.half_buf.at[mode, k],
            send_sem=self.half_send.at[mode, k], recv_sem=self.half_recv.at[mode, k],
            device_id=self.ways[mode][0], device_id_type=MESH)

    def keep_copy(self, mode, k):
        return pltpu.make_async_copy(self.prod[mode].at[self.rows(mode, k, True)], self.held.at[mode, k], self.local.at[mode, k])

    def quarter_copy(self, mode):
        return pltpu.make_async_remote_copy(
            src_ref=self.half_buf.at[mode, 0], dst_ref=self.quarter_buf.at[mode],
            send_sem=self.quarter_send.at[mode], recv_sem=self.quarter_recv.at[mode],
            device_id=self.ways[mode][1], device_id_type=MESH)

    def share_copy(self, mode, k):
        own = self.held.at[mode, 1]
        if k == 3:
            source, way = (self.out.at[mode, 0, 1], self.to_x) if mode == 0 else (self.out.at[mode, 0, 2], self.to_y)
        else:
            source, way = own, self.to_y if k == 1 else self.to_x
        return pltpu.make_async_remote_copy(
            src_ref=source, dst_ref=self.out.at[mode, 0, k], send_sem=self.share_send.at[mode, k],
            recv_sem=self.share_recv.at[mode, k], device_id=way, device_id_type=MESH)

    def core_copy(self, mode, k):
        return pltpu.make_async_remote_copy(
            src_ref=self.held.at[mode, 1] if k == 0 else self.out.at[mode, 0, k], dst_ref=self.out.at[mode, 1, k],
            send_sem=self.core_send.at[mode, k], recv_sem=self.core_recv.at[mode, k],
            device_id=self.to_core, device_id_type=MESH)

    def out_copy(self, mode):
        return pltpu.make_async_copy(self.held.at[mode, 1], self.own.at[mode], self.local.at[mode, 2])

    def start_shares(self, mode):
        for k in ((1, 2) if mode == 0 else (2, 1)):
            self.share_copy(mode, k).start()
        self.core_copy(mode, 0).start()
        self.out_copy(mode).start()

    def event(self, number):
        if number == 0:
            for k in range(2):
                for mode in range(2):
                    self.half_copy(mode, k).start()
                    self.keep_copy(mode, k).start()
        elif number == 1:
            for mode in range(2):
                self.keep_copy(mode, 0).wait()
                self.half_copy(mode, 0).wait_recv()
                add_rows(self.half_buf.at[mode, 0], self.half_buf.at[mode, 0], self.held.at[mode, 0], self.side, 32)
                self.quarter_copy(mode).start()
        elif number == 2:
            for mode in range(2):
                self.keep_copy(mode, 1).wait()
                self.half_copy(mode, 1).wait_recv()
                add_rows(self.half_buf.at[mode, 1], self.half_buf.at[mode, 1], self.held.at[mode, 1], self.side, 32)
        elif number == 3:
            for mode in range(2):
                self.quarter_copy(mode).wait_recv()
                add_rows(self.held.at[mode, 1], self.half_buf.at[mode, 1], self.quarter_buf.at[mode], self.side, 32)
                self.start_shares(mode)
        elif number == 4:
            for mode in range(2):
                k = 1 if mode == 0 else 2
                self.share_copy(mode, k).wait_recv()
                self.share_copy(mode, 3).start()
                self.core_copy(mode, k).start()
        elif number == 5:
            for mode in range(2):
                k = 2 if mode == 0 else 1
                self.share_copy(mode, k).wait_recv()
                self.core_copy(mode, k).start()
        elif number == 6:
            for mode in range(2):
                self.share_copy(mode, 3).wait_recv()
                self.core_copy(mode, 3).start()
        elif number == 8:
            for mode in range(2):
                pltpu.make_async_copy(self.prod.at[mode], self.held.at[mode, 1], self.local.at[mode, 1]).start()
        elif number == 9:
            for mode in range(2):
                pltpu.make_async_copy(self.prod.at[mode], self.held.at[mode, 1], self.local.at[mode, 1]).wait()
                self.start_shares(mode)
        elif number == 7:
            for mode in range(2):
                if self.summed is None:
                    for k in range(2):
                        self.half_copy(mode, k).wait_send()
                    self.quarter_copy(mode).wait_send()
                for k in range(1, 4):
                    self.share_copy(mode, k).wait_send()
                for k in range(4):
                    self.core_copy(mode, k).wait_send()
                    self.core_copy(mode, k).wait_recv()
                self.out_copy(mode).wait()


class Share:
    def __init__(self, own, out, sems):
        self.own, self.out = own, out
        self.share_send, self.share_recv, self.core_send, self.core_recv = sems
        _, _, self.to_x, self.to_y, self.to_core = place()

    @staticmethod
    def scratch():
        return [DMA((2, 4)), DMA((2, 4)), DMA((2, 4)), DMA((2, 4))]

    def share_copy(self, mode, k):
        if k == 3:
            source, way = (self.out.at[mode, 0, 1], self.to_x) if mode == 0 else (self.out.at[mode, 0, 2], self.to_y)
        else:
            source, way = self.own.at[mode], self.to_y if k == 1 else self.to_x
        return pltpu.make_async_remote_copy(
            src_ref=source, dst_ref=self.out.at[mode, 0, k], send_sem=self.share_send.at[mode, k],
            recv_sem=self.share_recv.at[mode, k], device_id=way, device_id_type=MESH)

    def core_copy(self, mode, k):
        return pltpu.make_async_remote_copy(
            src_ref=self.own.at[mode] if k == 0 else self.out.at[mode, 0, k], dst_ref=self.out.at[mode, 1, k],
            send_sem=self.core_send.at[mode, k], recv_sem=self.core_recv.at[mode, k],
            device_id=self.to_core, device_id_type=MESH)

    def event(self, number):
        for mode in range(2):
            early, late = (1, 2) if mode == 0 else (2, 1)
            if number == 0:
                self.share_copy(mode, early).start()
                self.share_copy(mode, late).start()
                self.core_copy(mode, 0).start()
            elif number == 1:
                self.share_copy(mode, early).wait_recv()
                self.share_copy(mode, 3).start()
                self.core_copy(mode, early).start()
            elif number == 2:
                self.share_copy(mode, late).wait_recv()
                self.core_copy(mode, late).start()
            elif number == 3:
                self.share_copy(mode, 3).wait_recv()
                self.core_copy(mode, 3).start()
            else:
                for k in range(1, 4):
                    self.share_copy(mode, k).wait_send()
                for k in range(4):
                    self.core_copy(mode, k).wait_send()
                    self.core_copy(mode, k).wait_recv()


class Reduce(Exchange):
    def __init__(self, prod, own, held, half_buf, quarter_buf, sems):
        half_send, half_recv, quarter_send, quarter_recv, keep = sems
        super().__init__(prod, (None, own), held, half_buf, quarter_buf,
                         (half_send, half_recv, quarter_send, quarter_recv, None, None, None, None, keep))

    @staticmethod
    def scratch(side, depth):
        low = jnp.bfloat16
        return [pltpu.VMEM((2, 2, side, depth), low), pltpu.VMEM((2, 2, side, depth), low), pltpu.VMEM((2, side, depth), low),
                DMA((2, 2)), DMA((2, 2)), DMA((2,)), DMA((2,)), DMA((2, 3))]

    def last(self):
        for mode in range(2):
            self.quarter_copy(mode).wait_recv()
            add_rows(self.held.at[mode, 1], self.half_buf.at[mode, 1], self.quarter_buf.at[mode], self.side, 32)
            pltpu.make_async_copy(self.held.at[mode, 1], self.own.at[mode], self.local.at[mode, 2]).start()

    def done(self):
        for mode in range(2):
            for k in range(2):
                self.half_copy(mode, k).wait_send()
            self.quarter_copy(mode).wait_send()
            pltpu.make_async_copy(self.held.at[mode, 1], self.own.at[mode], self.local.at[mode, 2]).wait()


class LineReduce:
    def __init__(self, part, own, acc, red, sems):
        red_send, red_recv, local = sems
        self.line = LineSum(part, own, acc, red, (red_send, red_recv, None, None, local))

    @staticmethod
    def scratch(pieces, rows, width):
        low = jnp.bfloat16
        return [pltpu.VMEM((2, pieces, rows, width), low), pltpu.VMEM((2, pieces, rows, width), low),
                DMA((2, pieces)), DMA((2, pieces)), DMA((2,))]

    def step(self, c, half):
        line = self.line
        begins, ends = line.place_of(half)

        @pl.when(jnp.logical_not(begins))
        def _():
            line.red_copy(half, c).wait_recv()
            add_rows(line.acc.at[half, c], line.acc.at[half, c], line.red.at[half, c], line.rows, 16)

            @pl.when(jnp.logical_not(ends))
            def _():
                line.red_copy(half, c).start()

    def turn(self, turn):
        line = self.line
        at_end = (line.z == 0) | (line.z == 3)
        if 0 <= turn - 2 < line.pieces:
            self.step(turn - 2, line.near)
        if 0 <= turn - 4 < line.pieces:
            @pl.when(jnp.logical_not(at_end))
            def _():
                self.step(turn - 4, 1 - line.near)
        if 0 <= turn - 6 < line.pieces:
            @pl.when(at_end)
            def _():
                self.step(turn - 6, 1 - line.near)

    def done(self):
        line = self.line
        for half in range(2):
            begins, ends = line.place_of(half)

            @pl.when(ends)
            def _():
                line.own(half).start()
                line.own(half).wait()

            @pl.when(jnp.logical_not(ends))
            def _():
                for c in range(line.pieces):
                    line.red_copy(half, c).wait_send()


class LineBack:
    def __init__(self, res, sems):
        self.res = res
        self.send, self.recv = sems
        self.z = lax.axis_index("tensor")
        self.near = jnp.where(self.z < 2, 1, 0)
        self.pieces = res.shape[1]

    @staticmethod
    def scratch(pieces):
        return [DMA((2, pieces)), DMA((2, pieces))]

    def place_of(self, half):
        along = jnp.where(half == 0, 3 - self.z, self.z)
        return along == 0, along == 3

    def copy(self, half, c):
        return pltpu.make_async_remote_copy(
            src_ref=self.res.at[half, c], dst_ref=self.res.at[half, c], send_sem=self.send.at[half, c],
            recv_sem=self.recv.at[half, c], device_id={"tensor": self.z - 2 * half + 1}, device_id_type=MESH)

    def begin(self, pieces):
        for half in range(2):
            _, ends = self.place_of(half)

            @pl.when(ends)
            def _():
                for c in pieces:
                    self.copy(half, c).start()

    def step(self, c, half):
        begins, ends = self.place_of(half)

        @pl.when(jnp.logical_not(ends | begins))
        def _():
            self.copy(half, c).wait_recv()
            self.copy(half, c).start()

    def some(self, pieces, far):
        for c in pieces:
            self.step(c, 1 - self.near if far else self.near)

    def done(self):
        for half in range(2):
            begins, ends = self.place_of(half)

            @pl.when(begins)
            def _():
                for c in range(self.pieces):
                    self.copy(half, c).wait_recv()

            @pl.when(jnp.logical_not(begins))
            def _():
                for c in range(self.pieces):
                    self.copy(half, c).wait_send()


AHEAD = 4


class LineSum:
    def __init__(self, part, res, acc, red, sems):
        self.part, self.res, self.acc, self.red = part, res, acc, red
        self.red_send, self.red_recv, self.back_send, self.back_recv, self.local = sems
        self.z = lax.axis_index("tensor")
        self.near = jnp.where(self.z < 2, 1, 0)
        self.pieces, self.rows = acc.shape[1], acc.shape[2]
        self.turns = 2 * self.pieces + 2

    @staticmethod
    def scratch(pieces, rows, width):
        low = jnp.bfloat16
        return [pltpu.VMEM((2, pieces, rows, width), low), pltpu.VMEM((2, pieces, rows, width), low),
                DMA((2, pieces)), DMA((2, pieces)), DMA((2, pieces)), DMA((2, pieces)), DMA((2,))]

    def place_of(self, half):
        along = jnp.where(half == 0, 3 - self.z, self.z)
        return along == 0, along == 3

    def red_copy(self, half, c):
        return pltpu.make_async_remote_copy(
            src_ref=self.acc.at[half, c], dst_ref=self.red.at[half, c], send_sem=self.red_send.at[half, c],
            recv_sem=self.red_recv.at[half, c], device_id={"tensor": self.z + 2 * half - 1}, device_id_type=MESH)

    def back_copy(self, half, c, source):
        return pltpu.make_async_remote_copy(
            src_ref=source, dst_ref=self.res.at[half, c], send_sem=self.back_send.at[half, c],
            recv_sem=self.back_recv.at[half, c], device_id={"tensor": self.z - 2 * half + 1}, device_id_type=MESH)

    def load(self):
        return pltpu.make_async_copy(self.part, self.acc, self.local.at[0])

    def own(self, half):
        return pltpu.make_async_copy(self.acc.at[half], self.res.at[half], self.local.at[1])

    def begin(self, pieces):
        for half in range(2):
            begins, _ = self.place_of(half)

            @pl.when(begins)
            def _():
                for c in pieces:
                    self.red_copy(half, c).start()

    def reduce_step(self, c, half):
        begins, ends = self.place_of(half)

        @pl.when(jnp.logical_not(begins))
        def _():
            self.red_copy(half, c).wait_recv()
            add_rows(self.acc.at[half, c], self.acc.at[half, c], self.red.at[half, c], self.rows, 16)

            @pl.when(ends)
            def _():
                self.back_copy(half, c, self.acc.at[half, c]).start()

            @pl.when(jnp.logical_not(ends))
            def _():
                self.red_copy(half, c).start()

    def back_step(self, c, half):
        begins, ends = self.place_of(half)

        @pl.when(jnp.logical_not(ends | begins))
        def _():
            self.back_copy(half, c, self.res.at[half, c]).wait_recv()
            self.back_copy(half, c, self.res.at[half, c]).start()

    def turn(self, turn):
        near, far = self.near, 1 - self.near
        if turn + AHEAD < self.pieces:
            self.begin((turn + AHEAD,))
        if turn < self.pieces:
            self.reduce_step(turn, near)
        if 1 <= turn <= self.pieces:
            self.reduce_step(turn - 1, far)
        back = turn - self.pieces
        if 0 <= back < self.pieces:
            self.back_step(back, far)
        if 1 <= back <= self.pieces:
            self.back_step(back - 1, near)

    def finish(self):
        for half in range(2):
            begins, ends = self.place_of(half)

            @pl.when(ends)
            def _():
                self.own(half).start()
                self.own(half).wait()

            @pl.when(begins)
            def _():
                for c in range(self.pieces):
                    self.back_copy(half, c, self.res.at[half, c]).wait_recv()

            @pl.when(jnp.logical_not(ends))
            def _():
                for c in range(self.pieces):
                    self.red_copy(half, c).wait_send()

            @pl.when(jnp.logical_not(begins))
            def _():
                for c in range(self.pieces):
                    self.back_copy(half, c, self.res.at[half, c]).wait_send()


def tail_kernel(count, *refs):
    prods, part = refs[:count], refs[count]
    outs, res, owns = refs[count + 1:2 * count + 1], refs[2 * count + 1], refs[2 * count + 2:3 * count + 2]
    scr = refs[3 * count + 2:]
    line = LineSum(part, res, scr[0], scr[1], scr[2:7])
    swaps = [Exchange([prods[i].at[0], prods[i].at[1]], (outs[i], owns[i]), *scr[7 + 12 * i:10 + 12 * i], scr[10 + 12 * i:19 + 12 * i]) for i in range(count)]
    line.load().start()
    greet()
    swaps[0].event(0)
    line.load().wait()
    line.begin(range(AHEAD))
    last = line.turns
    plan = {3: [(0, 1)], 5: [(0, 2)], 9: [(0, 3)], 13: [(0, 4)], 17: [(0, 5)], 21: [(0, 6)]}
    for turn in range(last):
        line.turn(turn)
        for which, number in plan.get(turn, []):
            swaps[which].event(number)
    for swapped in swaps:
        swapped.event(7)
    line.finish()


def tail_exchange(products, normed_part, pieces=12):
    count = len(products)
    side, depth = products[0].shape[1] // 4, products[0].shape[2]
    tokens, width = normed_part.shape
    part = normed_part.reshape(2, pieces, tokens // 2 // pieces, width)
    low = jnp.bfloat16
    anywhere = pl.BlockSpec(memory_space=pl.ANY)
    scratch = LineSum.scratch(*part.shape[1:])
    for _ in products:
        scratch = scratch + Exchange.scratch(side, depth)
    outs = pl.pallas_call(
        functools.partial(tail_kernel, count),
        in_specs=[anywhere] * (count + 1),
        out_specs=[anywhere] * (2 * count + 1),
        out_shape=[jax.ShapeDtypeStruct((2, 2, 4, side, depth), low)] * count + [jax.ShapeDtypeStruct(part.shape, low)]
        + [jax.ShapeDtypeStruct((2, side, depth), low)] * count,
        scratch_shapes=scratch,
        cost_estimate=pl.CostEstimate(flops=100_000_000, bytes_accessed=300_000_000, transcendentals=0),
        compiler_params=pltpu.CompilerParams(collective_id=1, has_side_effects=True, vmem_limit_bytes=60 * 1024 * 1024),
        name="tail_exchange",
    )(*products, part)
    return outs[:count], outs[count + 1:], outs[count].reshape(tokens, width)


NT = (((1,), (1,)), ((), ()))
TN = (((0,), (0,)), ((), ()))


def dot_f32(left, right, dims=(((1,), (0,)), ((), ()))):
    return lax.dot_general(left, right, dims, preferred_element_type=jnp.float32)


def widened(column_block, width):
    return jnp.concatenate([column_block] * (width // LANES), axis=1)


def middle_kernel(pre_grad, act_part, coeff, conv_sum, inner_x, act_b, rank_b, dt_proj, x_wide, conv_w, docs, modes,
                  gate_grads, normed_t, inv, extra, hidden, in_gate, in_inner, out_own, gate_own, z_own,
                  rows_out, normed_out, inner_prod, out_shared, gate_shared, z_res,
                  w_buf, mask_buf, pair_buf, conv_buf, stage, stage_n, hid_buf, proj_buf, proj_recv, proj_fin, gain_buf, gain_recv,
                  red_send, red_recv, all_send, all_recv, core_sems, gain_send, gain_recv_sem, w_sems, stage_sems, n_sems, hid_sems,
                  *share_sems):
    tokens, channels = pre_grad.shape
    low = jnp.bfloat16
    rank_dim = dt_proj.shape[1]
    z = lax.axis_index("tensor")
    x, y, to_x, to_y, to_core = place()
    share = tokens // 4
    outs = Share(out_own, out_shared, share_sems[0:4])
    gate = Share(gate_own, gate_shared, share_sems[4:8])
    back = LineBack(z_res, share_sems[8:10])
    width = hidden.shape[1]
    slices = width // w_buf.shape[2]
    cut = w_buf.shape[2]

    def z_at(off):
        return {"tensor": (z + off) % 4}

    barrier = pltpu.get_barrier_semaphore()
    for target in (to_x, to_y, to_core, z_at(1), z_at(2), z_at(3)):
        pl.semaphore_signal(barrier, inc=1, device_id=target, device_id_type=MESH)
    pl.semaphore_wait(barrier, 6)

    def weight_copies(i):
        slot = i % 2
        found = []
        for j, source in enumerate((in_gate, in_inner)):
            for m in range(2):
                found.append(pltpu.make_async_copy(source.at[m, pl.ds(i * cut, cut)], w_buf.at[slot, 2 * j + m],
                                                   w_sems.at[slot, 2 * j + m]))
        found.append(pltpu.make_async_copy(hidden.at[:, pl.ds(i * cut, cut)], hid_buf.at[slot], hid_sems.at[slot]))
        return found

    for i in range(2):
        for copy in weight_copies(i):
            copy.start()

    block = 128

    def proj_block(i, nothing):
        at = pl.ds(pl.multiple_of(i * block, block), block)
        grad = pre_grad[at, :]
        part = dot_f32(grad * widened(modes[0, at, :], channels), dt_proj[0], NT)
        part = part + dot_f32(grad * widened(modes[1, at, :], channels), dt_proj[1], NT)
        proj_buf[at, 0:rank_dim] = part.astype(low)
        proj_buf[at, rank_dim:rank_dim + LANES] = coeff[at, :].astype(low)
        return nothing

    lax.fori_loop(0, tokens // block, proj_block, 0)

    def red_copy(off):
        return pltpu.make_async_remote_copy(
            src_ref=proj_buf.at[pl.ds(pl.multiple_of(((z + off) % 4) * share, share), share)], dst_ref=proj_recv.at[off - 1],
            send_sem=red_send.at[off - 1], recv_sem=red_recv.at[off - 1], device_id=z_at(off), device_id_type=MESH)

    for off in (1, 2, 3):
        red_copy(off).start()
    outs.event(0)

    def product(pair, target, number):
        pair_tokens = pair.shape[0]
        tall = stage.shape[1]
        turns = normed_t.shape[0] // tall
        for m in range(2):
            def mask_rows(i, nothing):
                at = pl.ds(pl.multiple_of(i * block, block), block)
                mask_buf[at, :] = pair[at, :] * widened(modes[m, at, :], channels)
                return nothing
            lax.fori_loop(0, pair_tokens // block, mask_rows, 0)
            for j in range(turns):
                slot = (m * turns + j) % 2
                copy = pltpu.make_async_copy(stage.at[slot], target.at[m, pl.ds(j * tall, tall)], stage_sems.at[slot])
                if m * turns + j >= 2:
                    copy.wait()
                stage[slot] = dot_f32(normed_t[pl.ds(j * tall, tall), :], mask_buf[...]).astype(low)
                copy.start()
        for slot in range(2):
            pltpu.make_async_copy(stage.at[slot], target.at[0, pl.ds(0, tall)], stage_sems.at[slot]).wait()

    for off in (1, 2, 3):
        red_copy(off).wait_recv()
    mine = pl.ds(pl.multiple_of(z * share, share), share)
    total = proj_buf[mine, :].astype(jnp.float32)
    for k in range(3):
        total = total + proj_recv[k].astype(jnp.float32)
    proj_fin[mine, :] = total.astype(low)

    def all_copy(off):
        return pltpu.make_async_remote_copy(
            src_ref=proj_fin.at[mine], dst_ref=proj_fin.at[mine], send_sem=all_send.at[off - 1],
            recv_sem=all_recv.at[off - 1], device_id=z_at(off), device_id_type=MESH)

    for off in (1, 2, 3):
        all_copy(off).start()
    span = x_wide.shape[1] - 96
    mode_rows = span + rank_dim
    for m in range(2):
        ranks = rank_b[...] * modes[m, pl.ds(0, tokens), :]
        rows_out[pl.ds(m * mode_rows + span, rank_dim), :] = dot_f32(ranks, pre_grad[...], TN).astype(low)
    def dt_sums(i, carried):
        at = pl.ds(pl.multiple_of(i * block, block), block)
        grad = pre_grad[at, :].astype(jnp.float32)
        first = jnp.sum(grad * widened(modes[0, at, :].astype(jnp.float32), channels), axis=0, keepdims=True)
        return carried[0] + first, carried[1] + jnp.sum(grad, axis=0, keepdims=True) - first

    none_row = jnp.zeros((1, channels), jnp.float32)
    bias0, bias1 = lax.fori_loop(0, tokens // block, dt_sums, (none_row, none_row))
    for off in (1, 2, 3):
        all_copy(off).wait_recv()
    back.begin((0, 1))

    def act_block(i, bias):
        at = pl.ds(pl.multiple_of(i * block, block), block)
        proj = proj_fin[at, :]
        two = proj.shape[1]
        back = dot_f32(proj * widened(modes[0, at, :], two), x_wide[0])
        back = back + dot_f32(proj * widened(modes[1, at, :], two), x_wide[1])
        value = conv_sum[at, :]
        sig = jax.nn.sigmoid(value)
        grad = (act_part[at, :] + back) * sig * (1.0 + value * (1.0 - sig))
        conv_buf[at, :] = grad
        return bias + jnp.sum(grad, axis=0, keepdims=True)

    conv_buf[pl.ds(tokens, 8), :] = jnp.zeros((8, channels), jnp.float32)
    bias = lax.fori_loop(0, tokens // block, act_block, none_row)
    outs.event(1)
    gate.event(0)
    back.some((0,), True)
    back.begin((2,))
    taps = conv_w.shape[0]
    thin = 64

    def conv_block(i, sums):
        base = pl.multiple_of(i * thin, thin)
        grads = conv_buf[pl.ds(base, thin + 8), :]
        doc = docs[pl.ds(base, thin), :]
        inner = inner_x[pl.ds(base, thin), :]
        result = jnp.zeros((thin, channels), jnp.float32)
        new = []
        for offset in range(taps):
            moved = grads[offset:offset + thin, :] * doc[:, offset:offset + 1]
            tap = taps - 1 - offset
            result = result + moved * conv_w[tap:tap + 1, :]
            new.append(sums[offset] + jnp.sum(moved * inner, axis=0, keepdims=True))
        pair_buf[pl.ds(base, thin), :] = result.astype(low)
        return tuple(new)

    sums = lax.fori_loop(0, tokens // thin, conv_block, (none_row,) * taps)

    def core_copy():
        return pltpu.make_async_remote_copy(
            src_ref=pair_buf.at[pl.ds(0, tokens)], dst_ref=pair_buf.at[pl.ds(tokens, tokens)],
            send_sem=core_sems.at[0], recv_sem=core_sems.at[1], device_id=to_core, device_id_type=MESH)

    core_copy().start()
    back.some((1,), True)
    back.begin((3,))

    for i in range(slices):
        slot = i % 2
        for copy in weight_copies(i):
            copy.wait()
        third = tokens // 3
        out_copy = pltpu.make_async_copy(stage_n.at[slot], normed_out.at[:, pl.ds(i * cut, cut)], n_sems.at[slot])
        if i >= 2:
            out_copy.wait()

        def normed_rows(j, gain, slot=slot):
            at = pl.ds(pl.multiple_of(j * third, third), third)
            gate_grad, grad = gate_grads[at, :], pair_buf[at, :]
            zero = dot_f32(gate_grad, w_buf[slot, 0], NT) + dot_f32(grad, w_buf[slot, 2], NT)
            one = dot_f32(gate_grad, w_buf[slot, 1], NT) + dot_f32(grad, w_buf[slot, 3], NT)
            picked = jnp.where(inv[at, 1:2] > 0.5, zero, one)
            stage_n[slot, at, :] = picked.astype(low)
            return gain + jnp.sum(picked * hid_buf[slot, at, :].astype(jnp.float32) * inv[at, 0:1], axis=0, keepdims=True)

        gain = lax.fori_loop(0, 3, normed_rows, jnp.zeros((1, cut), jnp.float32))
        gain_buf[:, pl.ds(i * cut, cut)] = jnp.broadcast_to(gain, (8, cut))
        out_copy.start()
        if i + 2 < slices:
            for copy in weight_copies(i + 2):
                copy.start()
        if i == 0:
            back.some((2,), True)
            back.some((0,), False)
            back.begin((4,))
        elif i == 1:
            back.some((3,), True)
            back.some((1,), False)
            back.begin((5,))
        elif i == 2:
            outs.event(2)
            back.some((4,), True)
            back.some((2,), False)
        elif i == 3:
            back.some((5,), True)
            back.some((3,), False)
    for slot in range(2):
        pltpu.make_async_copy(stage_n.at[slot], normed_out.at[:, pl.ds(0, cut)], n_sems.at[slot]).wait()

    def gain_copy(off):
        return pltpu.make_async_remote_copy(
            src_ref=gain_buf, dst_ref=gain_recv.at[off - 1], send_sem=gain_send.at[off - 1],
            recv_sem=gain_recv_sem.at[off - 1], device_id=z_at(off), device_id_type=MESH)

    for off in (1, 2, 3):
        gain_copy(off).start()
    core_copy().wait_recv()
    product(pair_buf, inner_prod, 1)
    back.some((4, 5), False)
    gate.event(1)
    outs.event(3)
    for m in range(2):
        proj = proj_fin[...] * widened(modes[m, pl.ds(0, tokens), :], proj_fin.shape[1])
        rows_out[pl.ds(m * mode_rows, span), :] = dot_f32(proj, act_b[...], TN)[:span].astype(low)
    for off in (1, 2, 3):
        gain_copy(off).wait_recv()
    gain = gain_buf[0:1, :] + gain_recv[0, 0:1, :] + gain_recv[1, 0:1, :] + gain_recv[2, 0:1, :]
    gains = [gain[:, k * channels:(k + 1) * channels] for k in range(width // channels)]
    tail_rows = list(sums[::-1]) + [bias, bias0, bias1, extra[...]] + gains
    used = taps + 3 + extra.shape[0] + len(gains)
    tail_rows.append(jnp.zeros((32 - used, channels), jnp.float32))
    rows_out[pl.ds(2 * mode_rows, 32), :] = jnp.concatenate(tail_rows, axis=0).astype(low)
    gate.event(2)
    gate.event(3)
    outs.event(4)
    gate.event(4)
    back.done()
    for off in (1, 2, 3):
        red_copy(off).wait_send()
        all_copy(off).wait_send()
        gain_copy(off).wait_send()
    core_copy().wait_send()


def middle(pre_grad, act_part, coeff, conv_sum, inner_x, act_b, rank_b, dt_proj, x_wide, conv_w, docs, modes,
           gate_grads, normed_t, inv, extra, hidden, in_gate, in_inner, out_own, gate_own, z_own):
    tokens, channels = pre_grad.shape
    width = hidden.shape[1]
    low = jnp.bfloat16
    side = normed_t.shape[0] // 4
    cut = 512
    mode_rows = x_wide.shape[1] - 96 + dt_proj.shape[1]
    vmem, anywhere = pl.BlockSpec(memory_space=pltpu.VMEM), pl.BlockSpec(memory_space=pl.ANY)
    return pl.pallas_call(
        middle_kernel,
        in_specs=[vmem] * 16 + [anywhere] * 6,
        out_specs=[vmem] + [anywhere] * 5,
        out_shape=[
            jax.ShapeDtypeStruct((2 * mode_rows + 32, channels), low),
            jax.ShapeDtypeStruct((tokens, width), low),
            jax.ShapeDtypeStruct((2, 4 * side, channels), low),
            jax.ShapeDtypeStruct((2, 2, 4) + out_own.shape[1:], low),
            jax.ShapeDtypeStruct((2, 2, 4) + gate_own.shape[1:], low),
            jax.ShapeDtypeStruct(z_own.shape, low),
        ],
        scratch_shapes=[
            pltpu.VMEM((2, 4, cut, channels), low),
            pltpu.VMEM((2 * tokens, channels), low),
            pltpu.VMEM((2 * tokens, channels), low),
            pltpu.VMEM((tokens + 8, channels), jnp.float32),
            pltpu.VMEM((2, 2 * side, channels), low),
            pltpu.VMEM((2, tokens, cut), low),
            pltpu.VMEM((2, tokens, cut), low),
            pltpu.VMEM((tokens, 2 * LANES), low),
            pltpu.VMEM((3, tokens // 4, 2 * LANES), low),
            pltpu.VMEM((tokens, 2 * LANES), low),
            pltpu.VMEM((8, width), jnp.float32),
            pltpu.VMEM((3, 8, width), jnp.float32),
            DMA((3,)), DMA((3,)), DMA((3,)), DMA((3,)), DMA((2,)), DMA((3,)), DMA((3,)),
            DMA((2, 4)), DMA((2,)), DMA((2,)), DMA((2,)),
        ] + Share.scratch() + Share.scratch() + LineBack.scratch(z_own.shape[1]),
        input_output_aliases={21: 5},
        cost_estimate=pl.CostEstimate(flops=27_000_000_000, bytes_accessed=60_000_000, transcendentals=1_000_000),
        compiler_params=pltpu.CompilerParams(collective_id=3, has_side_effects=True, vmem_limit_bytes=61 * 1024 * 1024),
        name="middle",
    )(pre_grad, act_part, coeff, conv_sum, inner_x, act_b, rank_b, dt_proj, x_wide, conv_w, docs, modes,
      gate_grads, normed_t, inv, extra, hidden, in_gate, in_inner, out_own, gate_own, z_own)


def split_tail(part, count):
    lane = lax.broadcasted_iota(jnp.int32, part.shape, 1)
    high = part.astype(jnp.bfloat16).astype(jnp.float32)
    rest = pltpu.roll(part - high, count, axis=1)
    return jnp.where(lane < count, high, jnp.where(lane < 2 * count, rest, 0.0)).astype(jnp.bfloat16)


def join_tail(block, count):
    return block + pltpu.roll(block, block.shape[1] - count, axis=1)


def front_kernel(coeffs_wide, hidden, gain, conv_w, conv_b, docs, modes, x_wide, out_grad, view, out_proj,
                 w_inner, w_gate, normed_pair, cotan_pair, modes_pair,
                 inverse, conv_sum_out, inner_x_out, act_out, gate_z_out, gated_grad, rank_out, coeff_out,
                 normed, conv_sum, act_b, gate_z, acc, view_a, view_b, wide, stage_a, stage_b, w_out, proj_buf, proj_recv, proj_fin,
                 view_sems, stage_sems, out_sems, red_send, red_recv, all_send, all_recv, pair_send, pair_recv, pair_local, early_sems):
    tokens, width = hidden.shape
    channels = conv_w.shape[1]
    groups = channels // LANES
    low = jnp.bfloat16
    z = lax.axis_index("tensor")
    share = tokens // 4
    deep = stage_a.shape[1] // 2
    turns = width // deep
    views, stages = (view_a, view_b), (stage_a, stage_b)
    block = 128

    def z_at(off):
        return {"tensor": (z + off) % 4}

    barrier = pltpu.get_barrier_semaphore()
    for off in (1, 2, 3):
        pl.semaphore_signal(barrier, inc=1, device_id=z_at(off), device_id_type=MESH)
    core, to_core = lax.axis_index("dp") % 2, place()[4]
    pl.semaphore_signal(barrier, inc=1, device_id=to_core, device_id_type=MESH)

    def half_of(ref, which):
        return ref.at[:, pl.ds(pl.multiple_of(which * (width // 2), width // 2), width // 2)]

    own_rows, other_rows = pl.ds(0, tokens), pl.ds(tokens, tokens)
    pairs = ((half_of(normed, core), half_of(normed, 1 - core), normed_pair.at[own_rows], normed_pair.at[other_rows]),
             (half_of(out_grad, core), half_of(out_grad, 1 - core), cotan_pair.at[own_rows], cotan_pair.at[other_rows]),
             (modes, modes, modes_pair.at[:, own_rows], modes_pair.at[:, other_rows]))

    def pair_copies(i):
        mine, theirs, here, there = pairs[i]
        return (pltpu.make_async_copy(mine, here, pair_local.at[i]),
                pltpu.make_async_remote_copy(src_ref=theirs, dst_ref=there, send_sem=pair_send.at[i], recv_sem=pair_recv.at[i],
                                             device_id=to_core, device_id_type=MESH))

    def view_copy(i, slot, m):
        tall = deep * 2 * groups
        return pltpu.make_async_copy(view.at[m, pl.ds(pl.multiple_of(i * tall, tall), tall)], views[slot].at[m],
                                     view_sems.at[slot, m])

    def stage_copy(i, slot, half, m):
        target = w_inner if half == 0 else w_gate
        return pltpu.make_async_copy(stages[slot].at[half, pl.ds(m * deep, deep)],
                                     target.at[m, pl.ds(pl.multiple_of(i * deep, deep), deep)], stage_sems.at[slot, half, m])

    def out_copy(m):
        return pltpu.make_async_copy(out_proj.at[m], w_out.at[m], out_sems.at[m])

    for slot in range(2):
        for m in range(2):
            view_copy(slot, slot, m).start()
    for m in range(2):
        out_copy(m).start()

    def norm_block(i, nothing):
        at = pl.ds(pl.multiple_of(i * block, block), block)
        rows = hidden[at, :].astype(jnp.float32)
        scale = lax.rsqrt(jnp.mean(rows * rows, axis=1, keepdims=True) + EPS)
        inverse[at, :] = jnp.broadcast_to(scale, (block, LANES))
        normed[at, :] = (rows * scale * gain[...]).astype(low)
        return nothing

    lax.fori_loop(0, tokens // block, norm_block, 0)
    acc[0:8, :] = jnp.zeros((8, channels), jnp.float32)

    def unpack(slot):
        for m in range(2):
            wide[m] = views[slot][m].astype(jnp.float32)
            for half in range(2):
                stages[slot][half, m * deep:(m + 1) * deep, :] = jnp.concatenate(
                    [wide[m, pl.ds(g * 2 + half, deep, stride=2 * groups), :] for g in range(groups)], axis=1).astype(low)

    def multiply(i, slot, first):
        columns = normed[:, pl.ds(pl.multiple_of(i * deep, deep), deep)]
        left = jnp.concatenate([columns * widened(modes[0], deep), columns * widened(modes[1], deep)], axis=1)
        for half in range(2):
            product = dot_f32(left, stages[slot][half])
            if half == 0:
                acc[8:8 + tokens, :] = product if first else acc[8:8 + tokens, :] + product
            else:
                gate_z[...] = product if first else gate_z[...] + product

    def arrive(i, slot):
        for m in range(2):
            view_copy(i, slot, m).wait()

    def depart(i, slot):
        for m in range(2):
            for half in range(2):
                stage_copy(i, slot, half, m).start()

    def departed(i, slot):
        for m in range(2):
            for half in range(2):
                stage_copy(i, slot, half, m).wait()

    def fetch(i, slot):
        for m in range(2):
            view_copy(i, slot, m).start()

    arrive(0, 0)
    unpack(0)
    depart(0, 0)
    fetch(2, 0)
    arrive(1, 1)
    multiply(0, 0, True)
    unpack(1)
    depart(1, 1)
    fetch(3, 1)

    def looped(j, nothing):
        for slot in range(2):
            i = 2 * j + slot
            departed(i, slot)
            arrive(i + 2, slot)
            multiply(i + 1, 1 - slot, False)
            unpack(slot)
            depart(i + 2, slot)

            @pl.when(i + 4 < turns)
            def _():
                fetch(i + 4, slot)
        return nothing

    lax.fori_loop(0, turns // 2 - 1, looped, 0)
    multiply(turns - 1, 1, False)
    departed(turns - 2, 0)
    departed(turns - 1, 1)

    taps = conv_w.shape[0]

    def conv_block(i, nothing):
        base = pl.multiple_of(i * block, block)
        at = pl.ds(base, block)
        rows = acc[pl.ds(base, block + 8), :]
        doc = docs[at, :]
        total = conv_b[...] + conv_w[taps - 1:taps, :] * rows[8:8 + block, :]
        for offset in range(1, taps):
            total = total + conv_w[taps - 1 - offset:taps - offset, :] * rows[8 - offset:8 - offset + block, :] * doc[:, offset:offset + 1]
        conv_sum[at, :] = total
        active = (total * jax.nn.sigmoid(total)).astype(low)
        act_b[at, :] = active
        part = dot_f32(active * widened(modes[0, at, :], channels), x_wide[0], NT)
        part = part + dot_f32(active * widened(modes[1, at, :], channels), x_wide[1], NT)
        proj_buf[at, 0:LANES] = part[:, :LANES].astype(low)
        proj_buf[at, LANES:2 * LANES] = split_tail(part[:, LANES:], coeffs_wide)
        return nothing

    lax.fori_loop(0, tokens // block, conv_block, 0)

    def red_copy(off):
        return pltpu.make_async_remote_copy(
            src_ref=proj_buf.at[pl.ds(pl.multiple_of(((z + off) % 4) * share, share), share)], dst_ref=proj_recv.at[off - 1],
            send_sem=red_send.at[off - 1], recv_sem=red_recv.at[off - 1], device_id=z_at(off), device_id_type=MESH)

    mine = pl.ds(pl.multiple_of(z * share, share), share)

    def all_copy(off):
        return pltpu.make_async_remote_copy(
            src_ref=proj_fin.at[mine], dst_ref=proj_fin.at[mine], send_sem=all_send.at[off - 1],
            recv_sem=all_recv.at[off - 1], device_id=z_at(off), device_id_type=MESH)

    pl.semaphore_wait(barrier, 4)
    for off in (1, 2, 3):
        red_copy(off).start()
    early = [pltpu.make_async_copy(source, target, early_sems.at[i]) for i, (source, target) in enumerate((
        (conv_sum, conv_sum_out), (acc.at[pl.ds(8, tokens)], inner_x_out), (act_b, act_out), (gate_z, gate_z_out)))]
    for copy in early:
        copy.start()
    for i in range(3):
        for copy in pair_copies(i):
            copy.start()
    third = tokens // 3

    def grad_block(i):
        at = pl.ds(i * third, third)
        zero = dot_f32(out_grad[at, :], w_out[0], NT)
        one = dot_f32(out_grad[at, :], w_out[1], NT)
        gated_grad[at, :] = jnp.where(docs[at, 0:1] > 0.5, zero, one)

    for m in range(2):
        out_copy(m).wait()
    grad_block(0)
    for off in (1, 2, 3):
        red_copy(off).wait_recv()
    total = proj_buf[mine, :].astype(jnp.float32)
    for k in range(3):
        total = total + proj_recv[k].astype(jnp.float32)
    proj_fin[mine, 0:LANES] = total[:, :LANES].astype(low)
    proj_fin[mine, LANES:2 * LANES] = split_tail(join_tail(total[:, LANES:], coeffs_wide), coeffs_wide)
    for off in (1, 2, 3):
        all_copy(off).start()
    grad_block(1)
    grad_block(2)
    for off in (1, 2, 3):
        all_copy(off).wait_recv()
    rank_out[...] = proj_fin[:, 0:LANES]
    coeff_out[...] = join_tail(proj_fin[:, LANES:2 * LANES].astype(jnp.float32), coeffs_wide)
    for off in (1, 2, 3):
        red_copy(off).wait_send()
        all_copy(off).wait_send()
    for i in range(3):
        for copy in pair_copies(i):
            copy.wait()
    for copy in early:
        copy.wait()


def front(hidden, gain, conv_w, conv_b, docs, modes, x_wide, out_grad, in_proj, out_proj, coeffs_wide):
    tokens, width = hidden.shape
    channels = conv_w.shape[1]
    groups = channels // LANES
    low, f32 = jnp.bfloat16, jnp.float32
    view = in_proj.reshape(2, width, 2, groups, LANES).transpose(0, 1, 3, 2, 4).reshape(2, width * 2 * groups, LANES)
    deep = 256
    vmem, anywhere = pl.BlockSpec(memory_space=pltpu.VMEM), pl.BlockSpec(memory_space=pl.ANY)
    shape = jax.ShapeDtypeStruct
    return pl.pallas_call(
        functools.partial(front_kernel, coeffs_wide),
        in_specs=[vmem] * 8 + [anywhere] * 2,
        out_specs=[anywhere] * 5 + [vmem] + [anywhere] * 4 + [vmem] * 3,
        out_shape=[
            shape((2, width, channels), low), shape((2, width, channels), low), shape((2 * tokens, width // 2), low),
            shape((2 * tokens, width // 2), low), shape((2, 2 * tokens, LANES), low),
            shape((tokens, LANES), f32), shape((tokens, channels), f32), shape((tokens, channels), f32),
            shape((tokens, channels), low), shape((tokens, channels), f32), shape((tokens, channels), f32),
            shape((tokens, LANES), low), shape((tokens, LANES), f32),
        ],
        scratch_shapes=[
            pltpu.VMEM((tokens, width), low), pltpu.VMEM((tokens, channels), f32), pltpu.VMEM((tokens, channels), low),
            pltpu.VMEM((tokens, channels), f32),
            pltpu.VMEM((tokens + 8, channels), f32),
            pltpu.VMEM((2, deep * 2 * groups, LANES), low), pltpu.VMEM((2, deep * 2 * groups, LANES), low),
            pltpu.VMEM((2, deep * 2 * groups, LANES), f32),
            pltpu.VMEM((2, 2 * deep, channels), low), pltpu.VMEM((2, 2 * deep, channels), low),
            pltpu.VMEM((2, channels, width), low),
            pltpu.VMEM((tokens, 2 * LANES), low),
            pltpu.VMEM((3, tokens // 4, 2 * LANES), low),
            pltpu.VMEM((tokens, 2 * LANES), low),
            DMA((2, 2)), DMA((2, 2, 2)), DMA((2,)), DMA((3,)), DMA((3,)), DMA((3,)), DMA((3,)), DMA((3,)), DMA((3,)), DMA((3,)), DMA((4,)),
        ],
        cost_estimate=pl.CostEstimate(flops=20_000_000_000, bytes_accessed=80_000_000, transcendentals=1_000_000),
        compiler_params=pltpu.CompilerParams(collective_id=4, has_side_effects=True, vmem_limit_bytes=60 * 1024 * 1024),
        name="front",
    )(hidden, gain, conv_w, conv_b, docs, modes, x_wide, out_grad, view, out_proj)


def products_kernel(gated, cotan, normed, gate, modes, split, weights,
                    out0, out1, gate0, gate1, partial, normed_t,
                    left_buf, right_buf, mode_buf, split_buf, w_buf, turned, mask_buf, stage, stage_wide,
                    load_sems, w_sems, stage_sems, wide_sems, turned_sem):
    pair_tokens, channels = left_buf.shape[1:]
    tokens, deep = split_buf.shape
    low = jnp.bfloat16
    block = 128
    loads = [pltpu.make_async_copy(source, target, load_sems.at[i]) for i, (source, target) in enumerate((
        (gated, left_buf.at[0]), (cotan, right_buf.at[0]), (modes, mode_buf), (normed, left_buf.at[1]), (gate, right_buf.at[1]),
        (split, split_buf)))]
    for copy in loads:
        copy.start()
    half = w_buf.shape[0] // 2
    w_loads = [pltpu.make_async_copy(weights.at[m], w_buf.at[pl.ds(m * half, half)], w_sems.at[m]) for m in range(2)]
    for copy in w_loads:
        copy.start()
    tall = stage.shape[1]
    turns = channels // tall
    flights = [None, None]

    def turn_left(which):
        def body(i, nothing):
            at = pl.ds(pl.multiple_of(i * block, block), block)
            turned[at, :] = left_buf[which, :, at].T
            return nothing
        lax.fori_loop(0, channels // block, body, 0)

    def multiply(which, targets):
        for m in range(2):
            def mask_rows(i, nothing):
                at = pl.ds(pl.multiple_of(i * block, block), block)
                mask_buf[at, :] = right_buf[which, at, :] * widened(mode_buf[m, at, :], channels)
                return nothing
            lax.fori_loop(0, pair_tokens // block, mask_rows, 0)
            for j in range(turns):
                slot = (m * turns + j) % 2
                if flights[slot] is not None:
                    flights[slot].wait()
                stage[slot] = dot_f32(turned[pl.ds(j * tall, tall), :], mask_buf[...]).astype(low)
                flights[slot] = pltpu.make_async_copy(stage.at[slot], targets[m].at[pl.ds(j * tall, tall)], stage_sems.at[slot])
                flights[slot].start()

    for copy in loads[:3]:
        copy.wait()
    turn_left(0)
    multiply(0, (out0, out1))
    for copy in loads[3:5]:
        copy.wait()
    turn_left(1)
    out_turned = pltpu.make_async_copy(turned, normed_t, turned_sem)
    out_turned.start()
    multiply(1, (gate0, gate1))
    loads[5].wait()
    for copy in w_loads:
        copy.wait()
    part = stage_wide.shape[1]
    wide_flights = [None, None]
    for j in range(tokens // part):
        slot = j % 2
        if wide_flights[slot] is not None:
            wide_flights[slot].wait()
        stage_wide[slot] = dot_f32(split_buf[pl.ds(j * part, part), :], w_buf[...]).astype(low)
        wide_flights[slot] = pltpu.make_async_copy(stage_wide.at[slot], partial.at[pl.ds(j * part, part)], wide_sems.at[slot])
        wide_flights[slot].start()
    for copy in flights + wide_flights + [out_turned]:
        copy.wait()


def make_products(gated, cotan, normed, gate, modes, split, weights):
    pair_tokens, channels = gated.shape
    tokens, deep = split.shape
    width = weights.shape[2]
    low = jnp.bfloat16
    anywhere = pl.BlockSpec(memory_space=pl.ANY)
    square = jax.ShapeDtypeStruct((channels, channels), low)
    return pl.pallas_call(
        products_kernel,
        in_specs=[anywhere] * 7,
        out_specs=[anywhere] * 6,
        out_shape=[square] * 4 + [jax.ShapeDtypeStruct((tokens, width), low), jax.ShapeDtypeStruct((channels, pair_tokens), low)],
        scratch_shapes=[
            pltpu.VMEM((2, pair_tokens, channels), low), pltpu.VMEM((2, pair_tokens, channels), low),
            pltpu.VMEM((2, pair_tokens, LANES), low), pltpu.VMEM((tokens, deep), low), pltpu.VMEM((deep, width), low),
            pltpu.VMEM((channels, pair_tokens), low), pltpu.VMEM((pair_tokens, channels), low),
            pltpu.VMEM((2, channels // 2, channels), low), pltpu.VMEM((2, tokens // 3, width), low),
            DMA((6,)), DMA((2,)), DMA((2,)), DMA((2,)), DMA,
        ],
        cost_estimate=pl.CostEstimate(flops=20_000_000_000, bytes_accessed=45_000_000, transcendentals=0),
        compiler_params=pltpu.CompilerParams(vmem_limit_bytes=60 * 1024 * 1024),
        name="products",
    )(gated, cotan, normed, gate, modes, split, weights)


def final_kernel(side, depth, where_ref, out_shared, out_own, gate_shared, gate_own, inner_shared, inner_own,
                 hidden, out_grad, inverse, gain, summed_rows, summed_out, normed_sum,
                 out_ref, in_ref, output, input_grad, x_grad, dt_grad, *rest):
    row_grads, (narrow, wide, row_in, row_out, in_sems, out_sems, row_in_sems, row_out_sems) = rest[:-8], rest[-8:]
    x, y, core = where_ref[0], where_ref[1], where_ref[2]
    low, f32 = jnp.bfloat16, jnp.float32
    block = row_in.shape[2]
    jobs = []
    for which, (shared, own) in enumerate(((out_shared, out_own), (gate_shared, gate_own), (inner_shared, inner_own))):
        for mode in range(2):
            for owner in range(2):
                c = core if owner == 0 else 1 - core
                for k in range(4):
                    qx = x if k in (0, 1) else 1 - x
                    qy = y if k in (0, 2) else 1 - y
                    row = (qx * 2 + qy if mode == 0 else qy * 2 + qx) * side
                    if which == 0:
                        target = out_ref.at[mode, pl.ds(pl.multiple_of(row, side), side),
                                            pl.ds(pl.multiple_of(c * depth, depth), depth)]
                    else:
                        target = in_ref.at[mode, pl.ds(pl.multiple_of(c * 4 * side + row, side), side), 2 - which, :]
                    source = own.at[mode] if owner == 0 and k == 0 else shared.at[mode, owner, k]
                    jobs.append((source, target))
    slots = narrow.shape[0]
    loads = [pltpu.make_async_copy(jobs[i][0], narrow.at[i % slots], in_sems.at[i % slots]) for i in range(len(jobs))]
    stores = [pltpu.make_async_copy(wide.at[i % slots], jobs[i][1], out_sems.at[i % slots]) for i in range(len(jobs))]
    count = hidden.shape[0] // block

    def row_loads(i):
        at = pl.ds(i * block, block)
        return [pltpu.make_async_copy(ref.at[at], row_in.at[i % 2, j], row_in_sems.at[i % 2, j])
                for j, ref in enumerate((hidden, out_grad, summed_out, normed_sum))]

    def row_stores(i):
        at = pl.ds(i * block, block)
        return [pltpu.make_async_copy(row_out.at[i % 2, j], ref.at[at], row_out_sems.at[i % 2, j])
                for j, ref in enumerate((output, input_grad))]

    for copy in row_loads(0) + row_loads(1):
        copy.start()
    for i in range(slots):
        loads[i].start()
    span, rank_dim = x_grad.shape[1], dt_grad.shape[1]
    for m in range(2):
        base = m * (span + rank_dim)
        x_grad[m] = summed_rows[base:base + span, :].astype(f32)
        dt_grad[m] = summed_rows[base + span:base + span + rank_dim, :].astype(f32)
    tail_rows = summed_rows[2 * (span + rank_dim):, :].astype(f32)
    at = 0
    for ref in row_grads:
        ref[...] = tail_rows[at:at + ref.shape[0], :]
        at += ref.shape[0]
    per = -(-len(jobs) // count)
    for i in range(count):
        for copy in row_loads(i):
            copy.wait()
        if i >= 2:
            for copy in row_stores(i - 2):
                copy.wait()
        rows = row_in[i % 2, 0].astype(f32)
        scale = inverse[pl.ds(i * block, block), 0:1]
        scaled = row_in[i % 2, 3].astype(f32) * gain[...]
        mean = jnp.mean(scaled * rows, axis=1, keepdims=True)
        row_out[i % 2, 0] = (rows + row_in[i % 2, 2].astype(f32)).astype(low)
        row_out[i % 2, 1] = (row_in[i % 2, 1].astype(f32) + scale * scaled - rows * (scale * scale * scale) * mean).astype(low)
        for copy in row_stores(i):
            copy.start()
        if i + 2 < count:
            for copy in row_loads(i + 2):
                copy.start()
        for p in range(i * per, min((i + 1) * per, len(jobs))):
            loads[p].wait()
            if p >= slots:
                stores[p - slots].wait()
            wide[p % slots] = narrow[p % slots].astype(f32)
            stores[p].start()
            if p + slots < len(jobs):
                loads[p + slots].start()
    for p in range(len(jobs) - slots, len(jobs)):
        stores[p].wait()
    for i in (count - 2, count - 1):
        for copy in row_stores(i):
            copy.wait()


def final(where, out_shared, out_own, gate_shared, gate_own, inner_shared, inner_own, hidden, out_grad, inverse, gain,
          summed_rows, rank_dim, row_counts, summed_out, normed_sum):
    side, depth = out_own.shape[1:]
    tokens, width = hidden.shape
    channels = 4 * side
    low, f32 = jnp.bfloat16, jnp.float32
    anywhere, vmem = pl.BlockSpec(memory_space=pl.ANY), pl.BlockSpec(memory_space=pltpu.VMEM)
    block, slots = 128, 6
    return pl.pallas_call(
        functools.partial(final_kernel, side, depth),
        in_specs=[pl.BlockSpec(memory_space=pltpu.SMEM)] + [anywhere] * 8 + [vmem] * 3 + [anywhere] * 2,
        out_specs=[anywhere] * 4 + [vmem] * (2 + len(row_counts)),
        out_shape=[
            jax.ShapeDtypeStruct((2, channels, width), f32), jax.ShapeDtypeStruct((2, width, 2, channels), f32),
            jax.ShapeDtypeStruct((tokens, width), low), jax.ShapeDtypeStruct((tokens, width), low),
            jax.ShapeDtypeStruct((2, (summed_rows.shape[0] - 32) // 2 - rank_dim, channels), f32),
            jax.ShapeDtypeStruct((2, rank_dim, channels), f32),
        ] + [jax.ShapeDtypeStruct((n, channels), f32) for n in row_counts],
        scratch_shapes=[
            pltpu.VMEM((slots, side, depth), low), pltpu.VMEM((slots, side, depth), f32),
            pltpu.VMEM((2, 4, block, width), low), pltpu.VMEM((2, 2, block, width), low),
            DMA((slots,)), DMA((slots,)), DMA((2, 4)), DMA((2, 2)),
        ],
        cost_estimate=pl.CostEstimate(flops=50_000_000, bytes_accessed=91_000_000, transcendentals=0),
        compiler_params=pltpu.CompilerParams(vmem_limit_bytes=60 * 1024 * 1024),
        name="final_rows",
    )(where, out_shared, out_own, gate_shared, gate_own, inner_shared, inner_own, hidden, out_grad, inverse, gain,
      summed_rows, summed_out, normed_sum)


def scan_backward_kernel(states, groups, rows, unroll, count, joined,
                         bc_ref, pre_ref, act_ref, mixed_ref, keep_ref, alog_ref, skip_ref, h_ref, start_ref, *rest):
    if joined:
        prods, part_ref, rest = rest[:4], rest[4], rest[5:]
    pgrad_ref, apart_ref, bcg_ref, sum_ref, skipsum_ref = rest[:5]
    rest = rest[5:]
    if joined:
        out_own, gate_own, z_own, rest = rest[0], rest[1], rest[2], rest[3:]
    carry_ref, rate_scr, decay_scr, sk_scr, u_scr, dy_scr, w_scr, s_scr, p_scr, q_scr = rest[:10]
    rest = rest[10:]
    chunk = pl.program_id(0)
    if joined:
        line = LineReduce(part_ref, z_own, rest[0], rest[1], rest[2:5])
        outs = Reduce(prods[:2], out_own, *rest[5:8], rest[8:13])
        gate = Reduce(prods[2:], gate_own, *rest[13:16], rest[16:21])

        @pl.when(chunk == 0)
        def _():
            line.line.load().start()
            greet()
            outs.event(0)
            line.line.load().wait()
            line.line.begin((0,))

        for at in range(1, count):
            @pl.when(chunk == at)
            def _():
                if at < line.line.pieces:
                    line.line.begin((at,))
                if at == 2:
                    outs.event(1)
                elif at == 3:
                    gate.event(0)
                elif at == 5:
                    outs.event(2)
                elif at == 6:
                    outs.last()
                elif at == 8:
                    gate.event(1)
                elif at == 10:
                    gate.event(2)
                line.turn(at)

    @pl.when(chunk == 0)
    def _():
        decay = -jnp.exp(alog_ref[...])
        decay_scr[...] = decay
        rate_scr[...] = decay * LOG2E
        carry_ref[...] = jnp.zeros_like(carry_ref)
        sum_ref[...] = jnp.zeros_like(sum_ref)
        skipsum_ref[...] = jnp.zeros_like(skipsum_ref)

    step = softplus(pre_ref[...])
    act = act_ref[...].astype(jnp.float32)
    mixed = mixed_ref[...].astype(jnp.float32)
    spread_rows(u_scr, step * act, groups)
    spread_rows(dy_scr, mixed, groups)
    spread_rows(sk_scr, jnp.where(keep_ref[...] > 0.0, step, BIG), groups)
    skipsum_ref[...] += jnp.sum(mixed * act, axis=0, keepdims=True)

    def one(t, carried, before):
        at = pl.multiple_of(t * groups, groups)
        sk = sk_scr[pl.ds(at, groups), :]
        u = u_scr[pl.ds(at, groups), :]
        dy = dy_scr[pl.ds(at, groups), :]
        w = jnp.zeros_like(u)
        s = jnp.zeros_like(u)
        new, pb, pc = [], [], []
        for n in range(states):
            g = dy * bc_ref[t, states + n] + carried[n]
            pb.append(g * u)
            pc.append(dy * h_ref[t, n])
            w = w + g * bc_ref[t, n]
            fg = jnp.exp2(sk * rate_scr[n]) * g
            lg = fg * before(n)
            s = s + lg * decay_scr[n]
            sum_ref[n] += lg * sk
            new.append(fg)
        w_scr[pl.ds(at, groups), :] = w
        s_scr[pl.ds(at, groups), :] = s
        both = pb + pc
        batch = max(1, 16 // groups)
        for j in range(0, 2 * states, batch):
            p_scr[t, pl.ds(j * groups, batch * groups), :] = jnp.concatenate(
                both[j:j + batch], axis=0).astype(jnp.bfloat16)
        return tuple(new)

    def looped(i, carried):
        t = rows - 1 - i
        return one(t, carried, lambda n: h_ref[t - 1, n])

    last = lax.fori_loop(0, rows - 1, looped, tuple(carry_ref[n] for n in range(states)), unroll=unroll)
    last = one(0, last, lambda n: start_ref[0, n])
    for n in range(states):
        carry_ref[n] = last[n]

    ones = jnp.ones((16, LANES), jnp.bfloat16)

    def reduce_one(t, nothing):
        q = lax.dot_general(ones, p_scr[t], (((1,), (1,)), ((), ())), preferred_element_type=jnp.float32)
        q_scr[pl.ds(t, 1), :] = q[0:1]
        return nothing

    lax.fori_loop(0, rows, reduce_one, 0, unroll=4)
    shape = (2 * states * groups, LANES)
    pick = (lax.broadcasted_iota(jnp.int32, shape, 0) // groups == lax.broadcasted_iota(jnp.int32, shape, 1))
    pick = pick.astype(jnp.float32).astype(jnp.bfloat16)
    q = q_scr[...]
    high = q.astype(jnp.bfloat16)
    low = (q - high.astype(jnp.float32)).astype(jnp.bfloat16)
    bcg_ref[...] = (jnp.dot(high, pick, preferred_element_type=jnp.float32)
                    + jnp.dot(low, pick, preferred_element_type=jnp.float32))
    w = gather_rows(w_scr, rows, groups)
    s = gather_rows(s_scr, rows, groups)
    pgrad_ref[...] = ((act * w + s) * jax.nn.sigmoid(pre_ref[...])).astype(pgrad_ref.dtype)
    apart_ref[...] = mixed * skip_ref[...] + step * w

    if joined:
        @pl.when(chunk == count - 1)
        def _():
            gate.last()
            outs.done()
            gate.done()
            line.done()


def scan_backward(bc, pre, act, mixed, keep, a_log3, skip, h, starts, products=None, z_part=None, rows=64, unroll=7, pieces=6):
    tokens, channels = pre.shape
    groups = channels // LANES
    states = a_log3.shape[0]
    count = tokens // rows
    joined = products is not None
    wide = pl.BlockSpec((rows, channels), lambda i: (count - 1 - i, 0))
    whole3 = pl.BlockSpec((states, groups, LANES), lambda i: (0, 0, 0))
    row = pl.BlockSpec((1, channels), lambda i: (0, 0))
    anywhere = pl.BlockSpec(memory_space=pl.ANY)
    small = lambda: pltpu.VMEM((states, groups, LANES), jnp.float32)
    long = lambda: pltpu.VMEM((rows * groups, LANES), jnp.float32)
    extra, extra_shapes, extra_scratch = [], [], []
    if joined:
        side, depth = products[0].shape[0] // 4, products[0].shape[1]
        part = z_part.reshape(2, pieces, tokens // 2 // pieces, z_part.shape[1])
        extra = list(products) + [part]
        extra_shapes = [jax.ShapeDtypeStruct((2, side, depth), jnp.bfloat16)] * 2 + [jax.ShapeDtypeStruct(part.shape, jnp.bfloat16)]
        extra_scratch = LineReduce.scratch(*part.shape[1:]) + Reduce.scratch(side, depth) + Reduce.scratch(side, depth)
    settings = dict(collective_id=2, has_side_effects=True) if joined else {}
    outs = pl.pallas_call(
        functools.partial(scan_backward_kernel, states, groups, rows, unroll, count, joined),
        grid=(count,),
        in_specs=[
            pl.BlockSpec((rows, 2 * states), lambda i: (count - 1 - i, 0), memory_space=pltpu.SMEM),
            wide, wide, wide,
            pl.BlockSpec((rows, 1), lambda i: (count - 1 - i, 0)),
            whole3, row,
            pl.BlockSpec((rows, states, groups, LANES), lambda i: (count - 1 - i, 0, 0, 0)),
            pl.BlockSpec((1, states, groups, LANES), lambda i: (count - 1 - i, 0, 0, 0)),
        ] + [anywhere] * len(extra),
        out_specs=[wide, wide, pl.BlockSpec((rows, LANES), lambda i: (count - 1 - i, 0)), whole3, row]
        + [anywhere] * len(extra_shapes),
        out_shape=[
            jax.ShapeDtypeStruct((tokens, channels), jnp.bfloat16),
            jax.ShapeDtypeStruct((tokens, channels), jnp.float32),
            jax.ShapeDtypeStruct((tokens, LANES), jnp.float32),
            jax.ShapeDtypeStruct((states, groups, LANES), jnp.float32),
            jax.ShapeDtypeStruct((1, channels), jnp.float32),
        ] + extra_shapes,
        scratch_shapes=[small(), small(), small(), long(), long(), long(), long(), long(),
                        pltpu.VMEM((rows, 2 * states * groups, LANES), jnp.bfloat16),
                        pltpu.VMEM((rows, 2 * states * groups), jnp.float32)] + extra_scratch,
        cost_estimate=pl.CostEstimate(flops=60 * tokens * channels * states,
                                      bytes_accessed=4 * tokens * channels * states,
                                      transcendentals=tokens * channels * states),
        compiler_params=pltpu.CompilerParams(vmem_limit_bytes=52 * 1024 * 1024, **settings),
        name="scan_backward",
    )(bc, pre, act, mixed, keep, a_log3, skip, h, starts, *extra)
    return outs


def lagged(values, offset):
    padding = [(offset, 0)] + [(0, 0)] * (values.ndim - 1)
    return jnp.pad(values, padding)[: values.shape[0]]


def leading(values, offset):
    padding = [(0, offset)] + [(0, 0)] * (values.ndim - 1)
    return jnp.pad(values, padding)[offset:]


def pick_dot(left_side, weights, first_mode):
    first_part = jnp.dot(left_side, weights[0], preferred_element_type=jnp.float32)
    second_part = jnp.dot(left_side, weights[1], preferred_element_type=jnp.float32)
    return jnp.where(first_mode, first_part, second_part)


def pick_back(gradient, weights, first_mode):
    dims = (((1,), (1,)), ((), ()))
    first_part = lax.dot_general(gradient, weights[0], dims, preferred_element_type=jnp.float32)
    second_part = lax.dot_general(gradient, weights[1], dims, preferred_element_type=jnp.float32)
    return jnp.where(first_mode, first_part, second_part)


def weight_grads(left_side, gradient, first_mode):
    nothing = jnp.zeros_like(gradient)
    dims = (((0,), (0,)), ((), ()))
    first_part = lax.dot_general(
        left_side,
        jnp.where(first_mode, gradient, nothing),
        dims,
        preferred_element_type=jnp.float32,
    )
    second_part = lax.dot_general(
        left_side,
        jnp.where(first_mode, nothing, gradient),
        dims,
        preferred_element_type=jnp.float32,
    )
    return jnp.stack([first_part, second_part])


def finish_rows(normed_grad, hidden, inverse, cotan, norm_gain):
    scaled = normed_grad * norm_gain
    gain_terms = jnp.sum(normed_grad * hidden * inverse, axis=0)
    cubed = inverse * inverse * inverse
    rows = (
        cotan + inverse * scaled - hidden * cubed * jnp.mean(scaled * hidden, axis=1, keepdims=True)
    )
    return (rows.astype(jnp.bfloat16), gain_terms)


def swap(values, distance):
    return lax.ppermute(values, "dp", [(i, i ^ distance) for i in range(8)])


CORE = 1


def tie(values, *others):
    return lax.optimization_barrier((values,) + others)[0]


def z_sum(values, size, dtype=jnp.bfloat16):
    distance = 1
    while distance < size:
        low = values.astype(dtype)
        got = lax.ppermute(low, "tensor", [(i, i ^ distance) for i in range(size)])
        values = low.astype(jnp.float32) + got.astype(jnp.float32)
        distance *= 2
    return values


def shards(names, hidden_in, segment_ids, modality, norm_gain, in_proj, conv_weight, conv_bias, x_proj, dt_proj, dt_bias,
           a_log, skip_gain, out_proj, out_grad):
    tokens, model_width = hidden_in.shape
    conv_taps, channels = conv_weight.shape
    rank_dim = dt_proj.shape[1]
    state_dim = a_log.shape[0]
    groups = channels // LANES
    ways = names["tensor"]
    by_hand = names["dp"] == 8 and names["tensor"] == 4
    low = jnp.bfloat16
    rank = lax.axis_index("dp")
    core, x_at, y_at = rank % 2, (rank // 2) % 2, rank // 4
    where = jnp.stack([x_at, y_at, core]).astype(jnp.int32)
    first_mode = (modality == 0)[:, None]
    nothing = jnp.zeros((), low)
    dims = (((0,), (0,)), ((), ()))

    def masked_products(left, right, modes, mask_left):
        products = []
        for chosen in (modes, jnp.logical_not(modes)):
            one = jnp.where(chosen, left, nothing) if mask_left else left
            two = right if mask_left else jnp.where(chosen, right, nothing)
            products.append(lax.dot_general(one, two, dims, preferred_element_type=jnp.float32).astype(low))
        return jnp.stack(products)

    same_doc = [jnp.ones((tokens, 1), jnp.float32)]
    for offset in range(1, conv_taps):
        earlier_seg = jnp.pad(segment_ids, (offset, 0), constant_values=-1)[:tokens]
        same_doc.append((earlier_seg == segment_ids).astype(jnp.float32)[:, None])
    if by_hand:
        modes_own = jnp.broadcast_to(jnp.stack([first_mode, jnp.logical_not(first_mode)]), (2, tokens, LANES)).astype(low)
        x_wide = jnp.pad(jnp.swapaxes(x_proj, 1, 2), ((0, 0), (0, 96), (0, 0)))
        facts = jnp.concatenate([first_mode.astype(jnp.float32)] + same_doc[1:], axis=1)
        (in_inner, in_gate, normed_pair, cotan_pair, modes, inverse, conv_sum, inner_x, activated_b, gate_z, gated_grad, rank_b, coeffs) = front(
            hidden_in, norm_gain[None], conv_weight, conv_bias[None], facts, modes_own, x_wide, out_grad, in_proj, out_proj,
            2 * state_dim)
        coeffs = coeffs[:, :2 * state_dim]
    else:
        hidden = hidden_in.astype(jnp.float32)
        inverse = lax.rsqrt(jnp.mean(hidden * hidden, axis=1, keepdims=True) + EPS)
        normed_b = (hidden * inverse * norm_gain).astype(low)
        in_inner = in_proj[:, :, 0, :]
        in_gate = in_proj[:, :, 1, :]
        inner_x = pick_dot(normed_b, in_inner, first_mode)
        conv_sum = conv_bias + conv_weight[conv_taps - 1] * inner_x
        for offset in range(1, conv_taps):
            conv_sum = conv_sum + conv_weight[conv_taps - 1 - offset] * lagged(inner_x, offset) * same_doc[offset]
        activated_b = jax.nn.silu(conv_sum).astype(low)
        projected = z_sum(pick_dot(activated_b, x_proj, first_mode), ways)
        rank_b = projected[:, :rank_dim].astype(low)
        coeffs = projected[:, rank_dim:]
        gate_z = pick_dot(normed_b, in_gate, first_mode)
        gated_grad = pick_back(out_grad, out_proj, first_mode)
    step_pre = pick_dot(rank_b, dt_proj, first_mode) + jnp.where(first_mode, dt_bias[0], dt_bias[1])
    keep = same_doc[1]
    a_log3 = a_log.reshape(state_dim, groups, LANES)
    skip_row = skip_gain[None]
    forward = scan_forward(coeffs, step_pre, activated_b, gate_z, gated_grad, keep, a_log3, skip_row,
                           first_mode.astype(jnp.float32), by_hand)
    gated_b, gate_grad_b, mixed_grad, states, starts = forward[:5]
    if by_hand:
        made = make_products(gated_b, cotan_pair, normed_pair, gate_grad_b, modes, forward[5], out_proj)
        products, partial_out, normed_t = made[:4], made[4], made[5]
        back = scan_backward(coeffs, step_pre, activated_b, mixed_grad, keep, a_log3, skip_row, states, starts,
                             products, partial_out)
        out_own, gate_own, z_own = back[5:]
    else:
        partial_out = pick_dot(gated_b, out_proj, first_mode).astype(low)
        back = scan_backward(coeffs, step_pre, activated_b, mixed_grad, keep, a_log3, skip_row, states, starts)
        summed_out = lax.psum(partial_out, "tensor")
        out_proj_grad = lax.psum(weight_grads(gated_b, out_grad, first_mode).astype(low), "dp").astype(jnp.float32)
        gate_proj_grad = lax.psum(weight_grads(normed_b, gate_grad_b, first_mode).astype(low), "dp")
    pre_grad_b, act_part, coeff_grad, sums, skips = back[:5]
    a_log_grad = sums.reshape(state_dim, channels) * -jnp.exp(a_log)
    mode_rows = x_proj.shape[2] + rank_dim
    if by_hand:
        later = jnp.stack([same_doc[0]] + [leading(same_doc[k], k) for k in range(1, conv_taps)], axis=1)[:, :, 0]
        row_facts = jnp.concatenate([inverse[:, :1], first_mode.astype(jnp.float32)], axis=1)
        rows, normed_low, inner_product, out_shared, gate_shared, z_res = middle(
            pre_grad_b, act_part, coeff_grad, conv_sum, inner_x, activated_b, rank_b, dt_proj, x_wide, conv_weight, later, modes,
            gate_grad_b, normed_t, row_facts, jnp.concatenate([a_log_grad, skips], axis=0),
            hidden_in, in_gate, in_inner, out_own, gate_own, z_own)
        summed_out = z_res.reshape(tokens, model_width)
    else:
        pre_grad = pre_grad_b.astype(jnp.float32)
        dt_bias_grad = jnp.stack([
            jnp.sum(jnp.where(first_mode, pre_grad, 0.0), axis=0),
            jnp.sum(jnp.where(first_mode, 0.0, pre_grad), axis=0)])
        rank_part = pick_back(pre_grad_b, dt_proj, first_mode)
        proj_grad_b = z_sum(jnp.concatenate([rank_part, coeff_grad[:, :2 * state_dim]], axis=1), ways).astype(low)
        act_grad = act_part + pick_back(proj_grad_b, x_proj, first_mode)
        sig_conv = jax.nn.sigmoid(conv_sum)
        conv_grad = act_grad * sig_conv * (1.0 + conv_sum * (1.0 - sig_conv))
        conv_bias_grad = jnp.sum(conv_grad, axis=0)
        weight_rows = []
        x_grad = jnp.zeros_like(inner_x)
        for tap_index in range(conv_taps):
            offset = conv_taps - 1 - tap_index
            masked = conv_grad * same_doc[offset]
            weight_rows.append(jnp.sum(masked * lagged(inner_x, offset), axis=0))
            x_grad = x_grad + conv_weight[tap_index] * leading(masked, offset)
        x_grad_b = x_grad.astype(low)
        normed_part = pick_back(x_grad_b, in_inner, first_mode) + pick_back(gate_grad_b, in_gate, first_mode)
        gain_part = jnp.sum(normed_part * (hidden * inverse), axis=0).reshape(-1, channels)
        gain_part = lax.psum(gain_part, "tensor")
        small_modes = jnp.concatenate([
            weight_grads(proj_grad_b, activated_b, first_mode), weight_grads(rank_b, pre_grad_b, first_mode)], axis=1)
        rows = jnp.concatenate([small_modes.reshape(-1, channels), jnp.stack(weight_rows), conv_bias_grad[None], dt_bias_grad,
                                a_log_grad, skips, gain_part], axis=0).astype(low)
    summed_rows = lax.psum(rows, "dp")
    if by_hand:
        (inner_shared,), (inner_own,), normed_sum = tail_exchange([inner_product], normed_low)

        (out_proj_grad, in_proj_grad, output, input_grad, x_rows, dt_proj_grad, conv_weight_grad, conv_row, dt_bias_grad,
         a_log_grad, skip_row, gain_rows) = final(
            where, out_shared, out_own, gate_shared, gate_own, inner_shared, inner_own,
            hidden_in, out_grad, inverse, norm_gain[None], summed_rows, rank_dim, (conv_taps, 1, 2, state_dim, 1, model_width // channels),
            summed_out, normed_sum)
        x_proj_grad = jnp.swapaxes(x_rows, 1, 2)
        conv_bias_grad, skip_grad, norm_gain_grad = conv_row[0], skip_row[0], gain_rows.reshape(-1)
    else:
        inner_proj_grad = lax.psum(weight_grads(normed_b, x_grad_b, first_mode).astype(low), "dp")
        in_proj_grad = jnp.stack([inner_proj_grad, gate_proj_grad], axis=2).astype(jnp.float32)
        normed_sum = lax.psum(normed_part.astype(low), "tensor")
        output = (hidden + summed_out.astype(jnp.float32)).astype(low)
        cotan = out_grad.astype(jnp.float32)
        input_grad, _ = finish_rows(normed_sum.astype(jnp.float32), hidden, inverse, cotan, norm_gain)
        summed_rows = summed_rows.astype(jnp.float32)
        small_modes, rows = summed_rows[:2 * mode_rows].reshape(2, mode_rows, channels), summed_rows[2 * mode_rows:]
        x_proj_grad = jnp.swapaxes(small_modes[:, :-rank_dim], 1, 2)
        dt_proj_grad = small_modes[:, -rank_dim:]
        norm_gain_grad = rows[conv_taps + 4 + state_dim:].reshape(-1)[:model_width]
        at = conv_taps + 1
        conv_weight_grad, conv_bias_grad, dt_bias_grad = rows[:conv_taps], rows[conv_taps], rows[at:at + 2]
        a_log_grad, skip_grad = rows[at + 2:at + 2 + state_dim], rows[at + 2 + state_dim]
    return (output, input_grad, norm_gain_grad, in_proj_grad, conv_weight_grad, conv_bias_grad, x_proj_grad,
            dt_proj_grad, dt_bias_grad, a_log_grad, skip_grad, out_proj_grad)


def solution(mesh):
    in_specs = (
        P("dp", None),
        P("dp"),
        P("dp"),
        P(),
        P(None, None, None, "tensor"),
        P(None, "tensor"),
        P("tensor"),
        P(None, "tensor", None),
        P(None, None, "tensor"),
        P(None, "tensor"),
        P(None, "tensor"),
        P("tensor"),
        P(None, "tensor", None),
        P("dp", None),
    )
    out_specs = (
        P("dp", None),
        P("dp", None),
        P(),
        P(None, None, None, "tensor"),
        P(None, "tensor"),
        P("tensor"),
        P(None, "tensor", None),
        P(None, None, "tensor"),
        P(None, "tensor"),
        P(None, "tensor"),
        P("tensor"),
        P(None, "tensor", None),
    )
    names = dict(mesh.shape)
    return jax.shard_map(functools.partial(shards, names), mesh=mesh, in_specs=in_specs, out_specs=out_specs, check_vma=False)
```

```python
import functools

import jax
import jax.numpy as jnp
from jax import lax
from jax.experimental import pallas as pl
from jax.experimental.pallas import tpu as pltpu
from jax.sharding import PartitionSpec as P

EPS = 1e-05

LANES = 128
BIG = 1000.0
LOG2E = 1.4426950408889634


def softplus(v):
    return jnp.maximum(v, 0.0) + jnp.log1p(jnp.exp(-jnp.abs(v)))


def spread_rows(scratch, values, groups):
    rows = values.shape[0]
    for g in range(groups):
        scratch[pl.ds(g, rows, stride=groups), :] = values[:, g * LANES:(g + 1) * LANES]


def gather_rows(scratch, rows, groups):
    return jnp.concatenate(
        [scratch[pl.ds(g, rows, stride=groups), :] for g in range(groups)], axis=1)


def scan_forward_kernel(states, groups, rows, unroll, count, joined,
                        bc_ref, pre_ref, act_ref, z_ref, gg_ref, keep_ref, alog_ref, skip_ref, mode_ref,
                        *rest):
    chunk = pl.program_id(0)
    if joined:
        dt_ref, dt_bias_ref, rest = rest[0], rest[1], rest[2:]
    gated_ref, ggrad_ref, mixed_ref, h_ref, start_ref, *rest = rest
    if joined:
        pre_out, split_ref, rate_scr, state_scr, sk_scr, u_scr, y_scr, gated_all, ggrad_all, send_sems, recv_sems, local_sems = rest
        tokens = rows * count
        to_core = place()[4]

        def pair_copies(at, i):
            source, target = ((gated_all, gated_ref), (ggrad_all, ggrad_ref))[i]
            base = at * rows
            return (pltpu.make_async_copy(source.at[pl.ds(base, rows)], target.at[pl.ds(base, rows)], local_sems.at[at, i]),
                    pltpu.make_async_remote_copy(
                        src_ref=source.at[pl.ds(base, rows)], dst_ref=target.at[pl.ds(tokens + base, rows)],
                        send_sem=send_sems.at[at, i], recv_sem=recv_sems.at[at, i], device_id=to_core, device_id_type=MESH))

        @pl.when(chunk == 0)
        def _():
            barrier = pltpu.get_barrier_semaphore()
            pl.semaphore_signal(barrier, inc=1, device_id=to_core, device_id_type=MESH)
            pl.semaphore_wait(barrier, 1)
    else:
        rate_scr, state_scr, sk_scr, u_scr, y_scr = rest

    @pl.when(chunk == 0)
    def _():
        rate_scr[...] = jnp.exp(alog_ref[...]) * (-LOG2E)
        state_scr[...] = jnp.zeros_like(state_scr)

    if joined:
        ranks, first = pre_ref[...], mode_ref[...]
        ranks_0 = (ranks.astype(jnp.float32) * first).astype(ranks.dtype)
        pre = (jnp.dot(ranks_0, dt_ref[0], preferred_element_type=jnp.float32)
               + jnp.dot(ranks - ranks_0, dt_ref[1], preferred_element_type=jnp.float32))
        pre = pre + (first * dt_bias_ref[0:1, :] + (1.0 - first) * dt_bias_ref[1:2, :])
        pre_out[...] = pre
    else:
        pre = pre_ref[...]
    step = softplus(pre)
    act = act_ref[...].astype(jnp.float32)
    spread_rows(u_scr, step * act, groups)
    spread_rows(sk_scr, jnp.where(keep_ref[...] > 0.0, step, BIG), groups)
    start_ref[0] = state_scr[...]

    def one(t, held):
        at = pl.multiple_of(t * groups, groups)
        sk = sk_scr[pl.ds(at, groups), :]
        u = u_scr[pl.ds(at, groups), :]
        y = jnp.zeros_like(u)
        new = []
        for n in range(states):
            h = jnp.exp2(sk * rate_scr[n]) * held[n] + u * bc_ref[t, n]
            h_ref[t, n] = h
            y = y + h * bc_ref[t, states + n]
            new.append(h)
        y_scr[pl.ds(at, groups), :] = y
        return tuple(new)

    last = lax.fori_loop(0, rows, one, tuple(state_scr[n] for n in range(states)), unroll=unroll)
    for n in range(states):
        state_scr[n] = last[n]
    mixed_out = gather_rows(y_scr, rows, groups) + skip_ref[...] * act
    z = z_ref[...].astype(jnp.float32)
    gg = gg_ref[...].astype(jnp.float32)
    sig = jax.nn.sigmoid(z)
    silu = z * sig
    gated = mixed_out * silu
    gate_grad = (gg * mixed_out * sig * (1.0 + z * (1.0 - sig))).astype(ggrad_ref.dtype)
    mixed_ref[...] = gg * silu
    if joined:
        channels = gated.shape[1]
        first = mode_ref[...]
        split_ref[:, 0:channels] = (gated * first).astype(split_ref.dtype)
        split_ref[:, channels:2 * channels] = (gated * (1.0 - first)).astype(split_ref.dtype)
        at = pl.ds(pl.multiple_of(chunk * rows, rows), rows)
        gated_all[at, :] = gated.astype(gated_ref.dtype)
        ggrad_all[at, :] = gate_grad
        for k in range(count):
            @pl.when(chunk == k)
            def _():
                for i in range(2):
                    for copy in pair_copies(k, i):
                        copy.start()

        @pl.when(chunk == count - 1)
        def _():
            for k in range(count):
                for i in range(2):
                    for copy in pair_copies(k, i):
                        copy.wait()
    else:
        gated_ref[...] = gated.astype(gated_ref.dtype)
        ggrad_ref[...] = gate_grad


def scan_forward(bc, pre, act, z, gg, keep, a_log3, skip, mode, joined, dt=(), rows=64, unroll=8):
    tokens, channels = act.shape
    groups = channels // LANES
    states = a_log3.shape[0]
    count = tokens // rows
    wide = pl.BlockSpec((rows, channels), lambda i: (i, 0))
    thin = pl.BlockSpec((rows, 1), lambda i: (i, 0))
    whole3 = pl.BlockSpec((states, groups, LANES), lambda i: (0, 0, 0))
    low, f32 = jnp.bfloat16, jnp.float32
    long = lambda: pltpu.VMEM((rows * groups, LANES), f32)
    small = lambda: pltpu.VMEM((states, groups, LANES), f32)
    anywhere = pl.BlockSpec(memory_space=pl.ANY)
    tall = 2 * tokens if joined else tokens
    settings = dict(collective_id=5, has_side_effects=True) if joined else {}
    return pl.pallas_call(
        functools.partial(scan_forward_kernel, states, groups, rows, unroll, count, joined),
        grid=(count,),
        in_specs=[
            pl.BlockSpec((rows, 2 * states), lambda i: (i, 0), memory_space=pltpu.SMEM),
            pl.BlockSpec((rows, pre.shape[1]), lambda i: (i, 0)), wide, wide, wide, thin, whole3,
            pl.BlockSpec((1, channels), lambda i: (0, 0)), thin,
        ] + [pl.BlockSpec(v.shape, lambda i, n=v.ndim: (0,) * n) for v in dt],
        out_specs=[
            anywhere if joined else wide, anywhere if joined else wide, wide,
            pl.BlockSpec((rows, states, groups, LANES), lambda i: (i, 0, 0, 0)),
            pl.BlockSpec((1, states, groups, LANES), lambda i: (i, 0, 0, 0)),
        ] + ([wide, pl.BlockSpec((rows, 2 * channels), lambda i: (i, 0))] if joined else []),
        out_shape=[
            jax.ShapeDtypeStruct((tall, channels), low),
            jax.ShapeDtypeStruct((tall, channels), low),
            jax.ShapeDtypeStruct((tokens, channels), f32),
            jax.ShapeDtypeStruct((tokens, states, groups, LANES), f32),
            jax.ShapeDtypeStruct((count, states, groups, LANES), f32),
        ] + ([jax.ShapeDtypeStruct((tokens, channels), f32), jax.ShapeDtypeStruct((tokens, 2 * channels), low)] if joined else []),
        scratch_shapes=[small(), small(), long(), long(), long()] + ([
            pltpu.VMEM((tokens, channels), low), pltpu.VMEM((tokens, channels), low),
            pltpu.SemaphoreType.DMA((count, 2)), pltpu.SemaphoreType.DMA((count, 2)), pltpu.SemaphoreType.DMA((count, 2)),
        ] if joined else []),
        compiler_params=pltpu.CompilerParams(vmem_limit_bytes=48 * 1024 * 1024, **settings),
        name="scan_forward",
    )(bc, pre, act, z, gg, keep, a_log3, skip, mode, *dt)


MESH = pl.DeviceIdType.MESH
DMA = pltpu.SemaphoreType.DMA


def add_rows(target, left, right, rows, slab):
    def body(i, nothing):
        at = pl.ds(pl.multiple_of(i * slab, slab), slab)
        target[at, :] = (left[at, :].astype(jnp.float32) + right[at, :].astype(jnp.float32)).astype(jnp.bfloat16)
        return nothing
    lax.fori_loop(0, rows // slab, body, 0)


def place():
    dp = lax.axis_index("dp")
    x, y, core = (dp // 2) % 2, dp // 4, dp % 2
    return x, y, {"dp": dp + 2 - 4 * x}, {"dp": dp + 4 - 8 * y}, {"dp": dp + 1 - 2 * core}


def greet():
    z = lax.axis_index("tensor")
    barrier = pltpu.get_barrier_semaphore()
    for target in place()[2:]:
        pl.semaphore_signal(barrier, inc=1, device_id=target, device_id_type=MESH)

    @pl.when(z > 0)
    def _():
        pl.semaphore_signal(barrier, inc=1, device_id={"tensor": z - 1}, device_id_type=MESH)

    @pl.when(z < 3)
    def _():
        pl.semaphore_signal(barrier, inc=1, device_id={"tensor": z + 1}, device_id_type=MESH)

    @pl.when((z > 0) & (z < 3))
    def _():
        pl.semaphore_wait(barrier, 5)

    @pl.when((z == 0) | (z == 3))
    def _():
        pl.semaphore_wait(barrier, 4)


class Exchange:
    def __init__(self, prod, out, held, half_buf, quarter_buf, sems, summed=None):
        self.summed = summed
        self.prod, self.held, self.half_buf, self.quarter_buf = prod, held, half_buf, quarter_buf
        self.out, self.own = out
        (self.half_send, self.half_recv, self.quarter_send, self.quarter_recv,
         self.share_send, self.share_recv, self.core_send, self.core_recv, self.local) = sems
        x, y, self.to_x, self.to_y, self.to_core = place()
        self.firsts, self.seconds = (x, y), (y, x)
        self.ways = ((self.to_x, self.to_y), (self.to_y, self.to_x))
        self.side = half_buf.shape[2]

    @staticmethod
    def scratch(side, depth):
        low = jnp.bfloat16
        return [pltpu.VMEM((2, 2, side, depth), low), pltpu.VMEM((2, 2, side, depth), low), pltpu.VMEM((2, side, depth), low),
                DMA((2, 2)), DMA((2, 2)), DMA((2,)), DMA((2,)), DMA((2, 4)), DMA((2, 4)), DMA((2, 4)), DMA((2, 4)), DMA((2, 3))]

    def rows(self, mode, k, mine):
        first, second = self.firsts[mode], self.seconds[mode]
        half = first if mine else 1 - first
        quarter = 1 - second if k == 0 else second
        return pl.ds(pl.multiple_of((half * 2 + quarter) * self.side, self.side), self.side)

    def half_copy(self, mode, k):
        return pltpu.make_async_remote_copy(
            src_ref=self.prod[mode].at[self.rows(mode, k, False)], dst_ref=self.half_buf.at[mode, k],
            send_sem=self.half_send.at[mode, k], recv_sem=self.half_recv.at[mode, k],
            device_id=self.ways[mode][0], device_id_type=MESH)

    def keep_copy(self, mode, k):
        return pltpu.make_async_copy(self.prod[mode].at[self.rows(mode, k, True)], self.held.at[mode, k], self.local.at[mode, k])

    def quarter_copy(self, mode):
        return pltpu.make_async_remote_copy(
            src_ref=self.half_buf.at[mode, 0], dst_ref=self.quarter_buf.at[mode],
            send_sem=self.quarter_send.at[mode], recv_sem=self.quarter_recv.at[mode],
            device_id=self.ways[mode][1], device_id_type=MESH)

    def share_copy(self, mode, k):
        own = self.held.at[mode, 1]
        if k == 3:
            source, way = (self.out.at[mode, 0, 1], self.to_x) if mode == 0 else (self.out.at[mode, 0, 2], self.to_y)
        else:
            source, way = own, self.to_y if k == 1 else self.to_x
        return pltpu.make_async_remote_copy(
            src_ref=source, dst_ref=self.out.at[mode, 0, k], send_sem=self.share_send.at[mode, k],
            recv_sem=self.share_recv.at[mode, k], device_id=way, device_id_type=MESH)

    def core_copy(self, mode, k):
        return pltpu.make_async_remote_copy(
            src_ref=self.held.at[mode, 1] if k == 0 else self.out.at[mode, 0, k], dst_ref=self.out.at[mode, 1, k],
            send_sem=self.core_send.at[mode, k], recv_sem=self.core_recv.at[mode, k],
            device_id=self.to_core, device_id_type=MESH)

    def out_copy(self, mode):
        return pltpu.make_async_copy(self.held.at[mode, 1], self.own.at[mode], self.local.at[mode, 2])

    def start_shares(self, mode):
        for k in ((1, 2) if mode == 0 else (2, 1)):
            self.share_copy(mode, k).start()
        self.core_copy(mode, 0).start()
        self.out_copy(mode).start()

    def event(self, number):
        if number == 0:
            for k in range(2):
                for mode in range(2):
                    self.half_copy(mode, k).start()
                    self.keep_copy(mode, k).start()
        elif number == 1:
            for mode in range(2):
                self.keep_copy(mode, 0).wait()
                self.half_copy(mode, 0).wait_recv()
                add_rows(self.half_buf.at[mode, 0], self.half_buf.at[mode, 0], self.held.at[mode, 0], self.side, 32)
                self.quarter_copy(mode).start()
        elif number == 2:
            for mode in range(2):
                self.keep_copy(mode, 1).wait()
                self.half_copy(mode, 1).wait_recv()
                add_rows(self.half_buf.at[mode, 1], self.half_buf.at[mode, 1], self.held.at[mode, 1], self.side, 32)
        elif number == 3:
            for mode in range(2):
                self.quarter_copy(mode).wait_recv()
                add_rows(self.held.at[mode, 1], self.half_buf.at[mode, 1], self.quarter_buf.at[mode], self.side, 32)
                self.start_shares(mode)
        elif number == 4:
            for mode in range(2):
                k = 1 if mode == 0 else 2
                self.share_copy(mode, k).wait_recv()
                self.share_copy(mode, 3).start()
                self.core_copy(mode, k).start()
        elif number == 5:
            for mode in range(2):
                k = 2 if mode == 0 else 1
                self.share_copy(mode, k).wait_recv()
                self.core_copy(mode, k).start()
        elif number == 6:
            for mode in range(2):
                self.share_copy(mode, 3).wait_recv()
                self.core_copy(mode, 3).start()
        elif number == 8:
            for mode in range(2):
                pltpu.make_async_copy(self.prod.at[mode], self.held.at[mode, 1], self.local.at[mode, 1]).start()
        elif number == 9:
            for mode in range(2):
                pltpu.make_async_copy(self.prod.at[mode], self.held.at[mode, 1], self.local.at[mode, 1]).wait()
                self.start_shares(mode)
        elif number == 7:
            for mode in range(2):
                if self.summed is None:
                    for k in range(2):
                        self.half_copy(mode, k).wait_send()
                    self.quarter_copy(mode).wait_send()
                for k in range(1, 4):
                    self.share_copy(mode, k).wait_send()
                for k in range(4):
                    self.core_copy(mode, k).wait_send()
                    self.core_copy(mode, k).wait_recv()
                self.out_copy(mode).wait()


class Share:
    def __init__(self, own, out, sems):
        self.own, self.out = own, out
        self.share_send, self.share_recv, self.core_send, self.core_recv = sems
        _, _, self.to_x, self.to_y, self.to_core = place()

    @staticmethod
    def scratch():
        return [DMA((2, 4)), DMA((2, 4)), DMA((2, 4)), DMA((2, 4))]

    def share_copy(self, mode, k):
        if k == 3:
            source, way = (self.out.at[mode, 0, 1], self.to_x) if mode == 0 else (self.out.at[mode, 0, 2], self.to_y)
        else:
            source, way = self.own.at[mode], self.to_y if k == 1 else self.to_x
        return pltpu.make_async_remote_copy(
            src_ref=source, dst_ref=self.out.at[mode, 0, k], send_sem=self.share_send.at[mode, k],
            recv_sem=self.share_recv.at[mode, k], device_id=way, device_id_type=MESH)

    def core_copy(self, mode, k):
        return pltpu.make_async_remote_copy(
            src_ref=self.own.at[mode] if k == 0 else self.out.at[mode, 0, k], dst_ref=self.out.at[mode, 1, k],
            send_sem=self.core_send.at[mode, k], recv_sem=self.core_recv.at[mode, k],
            device_id=self.to_core, device_id_type=MESH)

    def event(self, number):
        for mode in range(2):
            early, late = (1, 2) if mode == 0 else (2, 1)
            if number == 0:
                self.share_copy(mode, early).start()
                self.share_copy(mode, late).start()
                self.core_copy(mode, 0).start()
            elif number == 1:
                self.share_copy(mode, early).wait_recv()
                self.share_copy(mode, 3).start()
                self.core_copy(mode, early).start()
            elif number == 2:
                self.share_copy(mode, late).wait_recv()
                self.core_copy(mode, late).start()
            elif number == 3:
                self.share_copy(mode, 3).wait_recv()
                self.core_copy(mode, 3).start()
            else:
                for k in range(1, 4):
                    self.share_copy(mode, k).wait_send()
                for k in range(4):
                    self.core_copy(mode, k).wait_send()
                    self.core_copy(mode, k).wait_recv()


class Reduce(Exchange):
    def __init__(self, prod, own, held, half_buf, quarter_buf, sems):
        half_send, half_recv, quarter_send, quarter_recv, keep = sems
        super().__init__(prod, (None, own), held, half_buf, quarter_buf,
                         (half_send, half_recv, quarter_send, quarter_recv, None, None, None, None, keep))

    @staticmethod
    def scratch(side, depth):
        low = jnp.bfloat16
        return [pltpu.VMEM((2, 2, side, depth), low), pltpu.VMEM((2, 2, side, depth), low), pltpu.VMEM((2, side, depth), low),
                DMA((2, 2)), DMA((2, 2)), DMA((2,)), DMA((2,)), DMA((2, 3))]

    def last(self):
        for mode in range(2):
            self.quarter_copy(mode).wait_recv()
            add_rows(self.held.at[mode, 1], self.half_buf.at[mode, 1], self.quarter_buf.at[mode], self.side, 32)
            pltpu.make_async_copy(self.held.at[mode, 1], self.own.at[mode], self.local.at[mode, 2]).start()

    def done(self):
        for mode in range(2):
            for k in range(2):
                self.half_copy(mode, k).wait_send()
            self.quarter_copy(mode).wait_send()
            pltpu.make_async_copy(self.held.at[mode, 1], self.own.at[mode], self.local.at[mode, 2]).wait()


class LineReduce:
    def __init__(self, part, own, acc, red, sems):
        red_send, red_recv, local = sems
        self.line = LineSum(part, own, acc, red, (red_send, red_recv, None, None, local))

    @staticmethod
    def scratch(pieces, rows, width):
        low = jnp.bfloat16
        return [pltpu.VMEM((2, pieces, rows, width), low), pltpu.VMEM((2, pieces, rows, width), low),
                DMA((2, pieces)), DMA((2, pieces)), DMA((2,))]

    def step(self, c, half):
        line = self.line
        begins, ends = line.place_of(half)

        @pl.when(jnp.logical_not(begins))
        def _():
            line.red_copy(half, c).wait_recv()
            add_rows(line.acc.at[half, c], line.acc.at[half, c], line.red.at[half, c], line.rows, 16)

            @pl.when(jnp.logical_not(ends))
            def _():
                line.red_copy(half, c).start()

    def turn(self, turn):
        line = self.line
        at_end = (line.z == 0) | (line.z == 3)
        if 0 <= turn - 2 < line.pieces:
            self.step(turn - 2, line.near)
        if 0 <= turn - 4 < line.pieces:
            @pl.when(jnp.logical_not(at_end))
            def _():
                self.step(turn - 4, 1 - line.near)
        if 0 <= turn - 6 < line.pieces:
            @pl.when(at_end)
            def _():
                self.step(turn - 6, 1 - line.near)

    def done(self):
        line = self.line
        for half in range(2):
            begins, ends = line.place_of(half)

            @pl.when(ends)
            def _():
                line.own(half).start()
                line.own(half).wait()

            @pl.when(jnp.logical_not(ends))
            def _():
                for c in range(line.pieces):
                    line.red_copy(half, c).wait_send()


class LineBack:
    def __init__(self, res, sems):
        self.res = res
        self.send, self.recv = sems
        self.z = lax.axis_index("tensor")
        self.near = jnp.where(self.z < 2, 1, 0)
        self.pieces = res.shape[1]

    @staticmethod
    def scratch(pieces):
        return [DMA((2, pieces)), DMA((2, pieces))]

    def place_of(self, half):
        along = jnp.where(half == 0, 3 - self.z, self.z)
        return along == 0, along == 3

    def copy(self, half, c):
        return pltpu.make_async_remote_copy(
            src_ref=self.res.at[half, c], dst_ref=self.res.at[half, c], send_sem=self.send.at[half, c],
            recv_sem=self.recv.at[half, c], device_id={"tensor": self.z - 2 * half + 1}, device_id_type=MESH)

    def begin(self, pieces):
        for half in range(2):
            _, ends = self.place_of(half)

            @pl.when(ends)
            def _():
                for c in pieces:
                    self.copy(half, c).start()

    def step(self, c, half):
        begins, ends = self.place_of(half)

        @pl.when(jnp.logical_not(ends | begins))
        def _():
            self.copy(half, c).wait_recv()
            self.copy(half, c).start()

    def some(self, pieces, far):
        for c in pieces:
            self.step(c, 1 - self.near if far else self.near)

    def done(self):
        for half in range(2):
            begins, ends = self.place_of(half)

            @pl.when(begins)
            def _():
                for c in range(self.pieces):
                    self.copy(half, c).wait_recv()

            @pl.when(jnp.logical_not(begins))
            def _():
                for c in range(self.pieces):
                    self.copy(half, c).wait_send()


AHEAD = 4


class LineSum:
    def __init__(self, part, res, acc, red, sems):
        self.part, self.res, self.acc, self.red = part, res, acc, red
        self.red_send, self.red_recv, self.back_send, self.back_recv, self.local = sems
        self.z = lax.axis_index("tensor")
        self.near = jnp.where(self.z < 2, 1, 0)
        self.pieces, self.rows = acc.shape[1], acc.shape[2]
        self.turns = self.pieces + 8

    @staticmethod
    def scratch(pieces, rows, width):
        low = jnp.bfloat16
        return [pltpu.VMEM((2, pieces, rows, width), low), pltpu.VMEM((2, pieces, rows, width), low),
                DMA((2, pieces)), DMA((2, pieces)), DMA((2, pieces)), DMA((2, pieces)), DMA((2,))]

    def place_of(self, half):
        along = jnp.where(half == 0, 3 - self.z, self.z)
        return along == 0, along == 3

    def red_copy(self, half, c):
        return pltpu.make_async_remote_copy(
            src_ref=self.acc.at[half, c], dst_ref=self.red.at[half, c], send_sem=self.red_send.at[half, c],
            recv_sem=self.red_recv.at[half, c], device_id={"tensor": self.z + 2 * half - 1}, device_id_type=MESH)

    def back_copy(self, half, c, source):
        return pltpu.make_async_remote_copy(
            src_ref=source, dst_ref=self.res.at[half, c], send_sem=self.back_send.at[half, c],
            recv_sem=self.back_recv.at[half, c], device_id={"tensor": self.z - 2 * half + 1}, device_id_type=MESH)

    def load(self):
        return pltpu.make_async_copy(self.part, self.acc, self.local.at[0])

    def own(self, half):
        return pltpu.make_async_copy(self.acc.at[half], self.res.at[half], self.local.at[1])

    def begin(self, pieces):
        for half in range(2):
            begins, _ = self.place_of(half)

            @pl.when(begins)
            def _():
                for c in pieces:
                    self.red_copy(half, c).start()

    def reduce_step(self, c, half):
        begins, ends = self.place_of(half)

        @pl.when(jnp.logical_not(begins))
        def _():
            self.red_copy(half, c).wait_recv()
            add_rows(self.acc.at[half, c], self.acc.at[half, c], self.red.at[half, c], self.rows, 16)

            @pl.when(ends)
            def _():
                self.back_copy(half, c, self.acc.at[half, c]).start()

            @pl.when(jnp.logical_not(ends))
            def _():
                self.red_copy(half, c).start()

    def back_step(self, c, half):
        begins, ends = self.place_of(half)

        @pl.when(jnp.logical_not(ends | begins))
        def _():
            self.back_copy(half, c, self.res.at[half, c]).wait_recv()
            self.back_copy(half, c, self.res.at[half, c]).start()

    def turn(self, turn):
        near, far = self.near, 1 - self.near
        if turn + AHEAD < self.pieces:
            self.begin((turn + AHEAD,))
        if turn < self.pieces:
            self.reduce_step(turn, near)
        if 1 <= turn <= self.pieces:
            self.reduce_step(turn - 1, far)
        if 0 <= turn - 6 < self.pieces:
            self.back_step(turn - 6, far)
        if 0 <= turn - 8 < self.pieces:
            self.back_step(turn - 8, near)

    def finish(self):
        for half in range(2):
            begins, ends = self.place_of(half)

            @pl.when(ends)
            def _():
                self.own(half).start()
                self.own(half).wait()

            @pl.when(begins)
            def _():
                for c in range(self.pieces):
                    self.back_copy(half, c, self.res.at[half, c]).wait_recv()

            @pl.when(jnp.logical_not(ends))
            def _():
                for c in range(self.pieces):
                    self.red_copy(half, c).wait_send()

            @pl.when(jnp.logical_not(begins))
            def _():
                for c in range(self.pieces):
                    self.back_copy(half, c, self.res.at[half, c]).wait_send()


def tail_kernel(count, *refs):
    prods, part = refs[:count], refs[count]
    outs, res, owns = refs[count + 1:2 * count + 1], refs[2 * count + 1], refs[2 * count + 2:3 * count + 2]
    scr = refs[3 * count + 2:]
    line = LineSum(part, res, scr[0], scr[1], scr[2:7])
    swaps = [Exchange([prods[i].at[0], prods[i].at[1]], (outs[i], owns[i]), *scr[7 + 12 * i:10 + 12 * i], scr[10 + 12 * i:19 + 12 * i]) for i in range(count)]
    line.load().start()
    greet()
    swaps[0].event(0)
    line.load().wait()
    line.begin(range(AHEAD))
    last = line.turns
    plan = {4: [(0, 1)], 7: [(0, 2)], 10: [(0, 3)], 12: [(0, 4)], 15: [(0, 5)], 19: [(0, 6)]}
    for turn in range(last):
        line.turn(turn)
        for which, number in plan.get(turn, []):
            swaps[which].event(number)
    for swapped in swaps:
        swapped.event(7)
    line.finish()


def tail_exchange(products, normed_part, pieces=12):
    count = len(products)
    side, depth = products[0].shape[1] // 4, products[0].shape[2]
    tokens, width = normed_part.shape
    part = normed_part.reshape(2, pieces, tokens // 2 // pieces, width)
    low = jnp.bfloat16
    anywhere = pl.BlockSpec(memory_space=pl.ANY)
    scratch = LineSum.scratch(*part.shape[1:])
    for _ in products:
        scratch = scratch + Exchange.scratch(side, depth)
    outs = pl.pallas_call(
        functools.partial(tail_kernel, count),
        in_specs=[anywhere] * (count + 1),
        out_specs=[anywhere] * (2 * count + 1),
        out_shape=[jax.ShapeDtypeStruct((2, 2, 4, side, depth), low)] * count + [jax.ShapeDtypeStruct(part.shape, low)]
        + [jax.ShapeDtypeStruct((2, side, depth), low)] * count,
        scratch_shapes=scratch,
        cost_estimate=pl.CostEstimate(flops=100_000_000, bytes_accessed=300_000_000, transcendentals=0),
        compiler_params=pltpu.CompilerParams(collective_id=1, has_side_effects=True, vmem_limit_bytes=60 * 1024 * 1024),
        name="tail_exchange",
    )(*products, part)
    return outs[:count], outs[count + 1:], outs[count].reshape(tokens, width)


NT = (((1,), (1,)), ((), ()))
TN = (((0,), (0,)), ((), ()))


def dot_f32(left, right, dims=(((1,), (0,)), ((), ()))):
    return lax.dot_general(left, right, dims, preferred_element_type=jnp.float32)


def widened(column_block, width):
    return jnp.concatenate([column_block] * (width // LANES), axis=1)


def middle_kernel(pre_grad, act_part, coeff, conv_sum, inner_x, act_b, rank_b, dt_proj, x_wide, conv_w, docs, modes,
                  gate_grads, normed_t, inv, extra, hidden, in_gate, in_inner, out_own, gate_own, z_own,
                  rows_out, normed_out, inner_prod, out_shared, gate_shared, z_res,
                  w_buf, mask_buf, pair_buf, conv_buf, stage, stage_n, hid_buf, proj_buf, proj_recv, proj_fin, gain_buf, gain_recv,
                  red_send, red_recv, all_send, all_recv, core_sems, gain_send, gain_recv_sem, w_sems, stage_sems, n_sems, hid_sems,
                  *share_sems):
    tokens, channels = pre_grad.shape
    low = jnp.bfloat16
    rank_dim = dt_proj.shape[1]
    z = lax.axis_index("tensor")
    x, y, to_x, to_y, to_core = place()
    share = tokens // 4
    outs = Share(out_own, out_shared, share_sems[0:4])
    gate = Share(gate_own, gate_shared, share_sems[4:8])
    back = LineBack(z_res, share_sems[8:10])
    width = hidden.shape[1]
    slices = width // w_buf.shape[2]
    cut = w_buf.shape[2]

    def z_at(off):
        return {"tensor": (z + off) % 4}

    barrier = pltpu.get_barrier_semaphore()
    for target in (to_x, to_y, to_core, z_at(1), z_at(2), z_at(3)):
        pl.semaphore_signal(barrier, inc=1, device_id=target, device_id_type=MESH)
    pl.semaphore_wait(barrier, 6)

    def weight_copies(i):
        slot = i % 2
        found = []
        for j, source in enumerate((in_gate, in_inner)):
            for m in range(2):
                found.append(pltpu.make_async_copy(source.at[m, pl.ds(i * cut, cut)], w_buf.at[slot, 2 * j + m],
                                                   w_sems.at[slot, 2 * j + m]))
        found.append(pltpu.make_async_copy(hidden.at[:, pl.ds(i * cut, cut)], hid_buf.at[slot], hid_sems.at[slot]))
        return found

    for i in range(2):
        for copy in weight_copies(i):
            copy.start()

    block = 128

    def proj_block(i, nothing):
        at = pl.ds(pl.multiple_of(i * block, block), block)
        grad = pre_grad[at, :]
        part = dot_f32(grad * widened(modes[0, at, :], channels), dt_proj[0], NT)
        part = part + dot_f32(grad * widened(modes[1, at, :], channels), dt_proj[1], NT)
        proj_buf[at, 0:rank_dim] = part.astype(low)
        proj_buf[at, rank_dim:rank_dim + LANES] = coeff[at, :].astype(low)
        return nothing

    lax.fori_loop(0, tokens // block, proj_block, 0)

    def red_copy(off):
        return pltpu.make_async_remote_copy(
            src_ref=proj_buf.at[pl.ds(pl.multiple_of(((z + off) % 4) * share, share), share)], dst_ref=proj_recv.at[off - 1],
            send_sem=red_send.at[off - 1], recv_sem=red_recv.at[off - 1], device_id=z_at(off), device_id_type=MESH)

    for off in (1, 2, 3):
        red_copy(off).start()
    outs.event(0)

    def product(pair, target, number):
        pair_tokens = pair.shape[0]
        tall = stage.shape[1]
        turns = normed_t.shape[0] // tall
        for m in range(2):
            def mask_rows(i, nothing):
                at = pl.ds(pl.multiple_of(i * block, block), block)
                mask_buf[at, :] = pair[at, :] * widened(modes[m, at, :], channels)
                return nothing
            lax.fori_loop(0, pair_tokens // block, mask_rows, 0)
            for j in range(turns):
                slot = (m * turns + j) % 2
                copy = pltpu.make_async_copy(stage.at[slot], target.at[m, pl.ds(j * tall, tall)], stage_sems.at[slot])
                if m * turns + j >= 2:
                    copy.wait()
                stage[slot] = dot_f32(normed_t[pl.ds(j * tall, tall), :], mask_buf[...]).astype(low)
                copy.start()
        for slot in range(2):
            pltpu.make_async_copy(stage.at[slot], target.at[0, pl.ds(0, tall)], stage_sems.at[slot]).wait()

    for off in (1, 2, 3):
        red_copy(off).wait_recv()
    mine = pl.ds(pl.multiple_of(z * share, share), share)
    total = proj_buf[mine, :].astype(jnp.float32)
    for k in range(3):
        total = total + proj_recv[k].astype(jnp.float32)
    proj_fin[mine, :] = total.astype(low)

    def all_copy(off):
        return pltpu.make_async_remote_copy(
            src_ref=proj_fin.at[mine], dst_ref=proj_fin.at[mine], send_sem=all_send.at[off - 1],
            recv_sem=all_recv.at[off - 1], device_id=z_at(off), device_id_type=MESH)

    for off in (1, 2, 3):
        all_copy(off).start()
    span = x_wide.shape[1] - 96
    mode_rows = span + rank_dim
    for m in range(2):
        ranks = rank_b[...] * modes[m, pl.ds(0, tokens), :]
        rows_out[pl.ds(m * mode_rows + span, rank_dim), :] = dot_f32(ranks, pre_grad[...], TN).astype(low)
    def dt_sums(i, carried):
        at = pl.ds(pl.multiple_of(i * block, block), block)
        grad = pre_grad[at, :].astype(jnp.float32)
        first = jnp.sum(grad * widened(modes[0, at, :].astype(jnp.float32), channels), axis=0, keepdims=True)
        return carried[0] + first, carried[1] + jnp.sum(grad, axis=0, keepdims=True) - first

    none_row = jnp.zeros((1, channels), jnp.float32)
    bias0, bias1 = lax.fori_loop(0, tokens // block, dt_sums, (none_row, none_row))
    for off in (1, 2, 3):
        all_copy(off).wait_recv()
    back.begin((0, 1))

    def act_block(i, bias):
        at = pl.ds(pl.multiple_of(i * block, block), block)
        proj = proj_fin[at, :]
        two = proj.shape[1]
        back = dot_f32(proj * widened(modes[0, at, :], two), x_wide[0])
        back = back + dot_f32(proj * widened(modes[1, at, :], two), x_wide[1])
        value = conv_sum[at, :]
        sig = jax.nn.sigmoid(value)
        grad = (act_part[at, :] + back) * sig * (1.0 + value * (1.0 - sig))
        conv_buf[at, :] = grad
        return bias + jnp.sum(grad, axis=0, keepdims=True)

    conv_buf[pl.ds(tokens, 8), :] = jnp.zeros((8, channels), jnp.float32)
    bias = lax.fori_loop(0, tokens // block, act_block, none_row)
    outs.event(1)
    gate.event(0)
    back.some((0,), True)
    back.begin((2,))
    taps = conv_w.shape[0]
    thin = 64

    def conv_block(i, sums):
        base = pl.multiple_of(i * thin, thin)
        grads = conv_buf[pl.ds(base, thin + 8), :]
        doc = docs[pl.ds(base, thin), :]
        inner = inner_x[pl.ds(base, thin), :]
        result = jnp.zeros((thin, channels), jnp.float32)
        new = []
        for offset in range(taps):
            moved = grads[offset:offset + thin, :] * doc[:, offset:offset + 1]
            tap = taps - 1 - offset
            result = result + moved * conv_w[tap:tap + 1, :]
            new.append(sums[offset] + jnp.sum(moved * inner, axis=0, keepdims=True))
        pair_buf[pl.ds(base, thin), :] = result.astype(low)
        return tuple(new)

    sums = lax.fori_loop(0, tokens // thin, conv_block, (none_row,) * taps)

    def core_copy():
        return pltpu.make_async_remote_copy(
            src_ref=pair_buf.at[pl.ds(0, tokens)], dst_ref=pair_buf.at[pl.ds(tokens, tokens)],
            send_sem=core_sems.at[0], recv_sem=core_sems.at[1], device_id=to_core, device_id_type=MESH)

    core_copy().start()
    back.some((1,), True)
    back.begin((3,))

    for i in range(slices):
        slot = i % 2
        for copy in weight_copies(i):
            copy.wait()
        third = tokens // 3
        out_copy = pltpu.make_async_copy(stage_n.at[slot], normed_out.at[:, pl.ds(i * cut, cut)], n_sems.at[slot])
        if i >= 2:
            out_copy.wait()

        def normed_rows(j, gain, slot=slot):
            at = pl.ds(pl.multiple_of(j * third, third), third)
            gate_grad, grad = gate_grads[at, :], pair_buf[at, :]
            zero = dot_f32(gate_grad, w_buf[slot, 0], NT) + dot_f32(grad, w_buf[slot, 2], NT)
            one = dot_f32(gate_grad, w_buf[slot, 1], NT) + dot_f32(grad, w_buf[slot, 3], NT)
            picked = jnp.where(inv[at, 1:2] > 0.5, zero, one)
            stage_n[slot, at, :] = picked.astype(low)
            return gain + jnp.sum(picked * hid_buf[slot, at, :].astype(jnp.float32) * inv[at, 0:1], axis=0, keepdims=True)

        gain = lax.fori_loop(0, 3, normed_rows, jnp.zeros((1, cut), jnp.float32))
        gain_buf[:, pl.ds(i * cut, cut)] = jnp.broadcast_to(gain, (8, cut))
        out_copy.start()
        if i + 2 < slices:
            for copy in weight_copies(i + 2):
                copy.start()
        if i == 0:
            back.some((2,), True)
            back.some((0,), False)
            back.begin((4,))
        elif i == 1:
            back.some((3,), True)
            back.some((1,), False)
            back.begin((5,))
        elif i == 2:
            outs.event(2)
            back.some((4,), True)
            back.some((2,), False)
        elif i == 3:
            back.some((5,), True)
            back.some((3,), False)
    for slot in range(2):
        pltpu.make_async_copy(stage_n.at[slot], normed_out.at[:, pl.ds(0, cut)], n_sems.at[slot]).wait()

    def gain_copy(off):
        return pltpu.make_async_remote_copy(
            src_ref=gain_buf, dst_ref=gain_recv.at[off - 1], send_sem=gain_send.at[off - 1],
            recv_sem=gain_recv_sem.at[off - 1], device_id=z_at(off), device_id_type=MESH)

    for off in (1, 2, 3):
        gain_copy(off).start()
    core_copy().wait_recv()
    product(pair_buf, inner_prod, 1)
    back.some((4, 5), False)
    gate.event(1)
    outs.event(3)
    for m in range(2):
        proj = proj_fin[...] * widened(modes[m, pl.ds(0, tokens), :], proj_fin.shape[1])
        rows_out[pl.ds(m * mode_rows, span), :] = dot_f32(proj, act_b[...], TN)[:span].astype(low)
    for off in (1, 2, 3):
        gain_copy(off).wait_recv()
    gain = gain_buf[0:1, :] + gain_recv[0, 0:1, :] + gain_recv[1, 0:1, :] + gain_recv[2, 0:1, :]
    gains = [gain[:, k * channels:(k + 1) * channels] for k in range(width // channels)]
    tail_rows = list(sums[::-1]) + [bias, bias0, bias1, extra[...]] + gains
    used = taps + 3 + extra.shape[0] + len(gains)
    tail_rows.append(jnp.zeros((32 - used, channels), jnp.float32))
    rows_out[pl.ds(2 * mode_rows, 32), :] = jnp.concatenate(tail_rows, axis=0).astype(low)
    gate.event(2)
    gate.event(3)
    outs.event(4)
    gate.event(4)
    back.done()
    for off in (1, 2, 3):
        red_copy(off).wait_send()
        all_copy(off).wait_send()
        gain_copy(off).wait_send()
    core_copy().wait_send()


def middle(pre_grad, act_part, coeff, conv_sum, inner_x, act_b, rank_b, dt_proj, x_wide, conv_w, docs, modes,
           gate_grads, normed_t, inv, extra, hidden, in_gate, in_inner, out_own, gate_own, z_own):
    tokens, channels = pre_grad.shape
    width = hidden.shape[1]
    low = jnp.bfloat16
    side = normed_t.shape[0] // 4
    cut = 512
    mode_rows = x_wide.shape[1] - 96 + dt_proj.shape[1]
    vmem, anywhere = pl.BlockSpec(memory_space=pltpu.VMEM), pl.BlockSpec(memory_space=pl.ANY)
    return pl.pallas_call(
        middle_kernel,
        in_specs=[vmem] * 16 + [anywhere] * 6,
        out_specs=[vmem] + [anywhere] * 5,
        out_shape=[
            jax.ShapeDtypeStruct((2 * mode_rows + 32, channels), low),
            jax.ShapeDtypeStruct((tokens, width), low),
            jax.ShapeDtypeStruct((2, 4 * side, channels), low),
            jax.ShapeDtypeStruct((2, 2, 4) + out_own.shape[1:], low),
            jax.ShapeDtypeStruct((2, 2, 4) + gate_own.shape[1:], low),
            jax.ShapeDtypeStruct(z_own.shape, low),
        ],
        scratch_shapes=[
            pltpu.VMEM((2, 4, cut, channels), low),
            pltpu.VMEM((2 * tokens, channels), low),
            pltpu.VMEM((2 * tokens, channels), low),
            pltpu.VMEM((tokens + 8, channels), jnp.float32),
            pltpu.VMEM((2, 2 * side, channels), low),
            pltpu.VMEM((2, tokens, cut), low),
            pltpu.VMEM((2, tokens, cut), low),
            pltpu.VMEM((tokens, 2 * LANES), low),
            pltpu.VMEM((3, tokens // 4, 2 * LANES), low),
            pltpu.VMEM((tokens, 2 * LANES), low),
            pltpu.VMEM((8, width), jnp.float32),
            pltpu.VMEM((3, 8, width), jnp.float32),
            DMA((3,)), DMA((3,)), DMA((3,)), DMA((3,)), DMA((2,)), DMA((3,)), DMA((3,)),
            DMA((2, 4)), DMA((2,)), DMA((2,)), DMA((2,)),
        ] + Share.scratch() + Share.scratch() + LineBack.scratch(z_own.shape[1]),
        input_output_aliases={21: 5},
        cost_estimate=pl.CostEstimate(flops=27_000_000_000, bytes_accessed=60_000_000, transcendentals=1_000_000),
        compiler_params=pltpu.CompilerParams(collective_id=3, has_side_effects=True, vmem_limit_bytes=61 * 1024 * 1024),
        name="middle",
    )(pre_grad, act_part, coeff, conv_sum, inner_x, act_b, rank_b, dt_proj, x_wide, conv_w, docs, modes,
      gate_grads, normed_t, inv, extra, hidden, in_gate, in_inner, out_own, gate_own, z_own)


def split_tail(part, count):
    lane = lax.broadcasted_iota(jnp.int32, part.shape, 1)
    high = part.astype(jnp.bfloat16).astype(jnp.float32)
    rest = pltpu.roll(part - high, count, axis=1)
    return jnp.where(lane < count, high, jnp.where(lane < 2 * count, rest, 0.0)).astype(jnp.bfloat16)


def join_tail(block, count):
    return block + pltpu.roll(block, block.shape[1] - count, axis=1)


def front_kernel(coeffs_wide, hidden, gain, conv_w, conv_b, docs, modes, x_wide, out_grad, view, out_proj,
                 w_inner, w_gate, normed_pair, cotan_pair, modes_pair,
                 inverse, conv_sum_out, inner_x_out, act_out, gate_z_out, gated_grad, rank_out, coeff_out,
                 normed, conv_sum, act_b, gate_z, acc, view_a, view_b, wide, stage_a, stage_b, w_out, proj_buf, proj_recv, proj_fin,
                 view_sems, stage_sems, out_sems, red_send, red_recv, all_send, all_recv, pair_send, pair_recv, pair_local, early_sems):
    tokens, width = hidden.shape
    channels = conv_w.shape[1]
    groups = channels // LANES
    low = jnp.bfloat16
    z = lax.axis_index("tensor")
    share = tokens // 4
    deep = stage_a.shape[1] // 2
    turns = width // deep
    views, stages = (view_a, view_b), (stage_a, stage_b)
    block = 128

    def z_at(off):
        return {"tensor": (z + off) % 4}

    barrier = pltpu.get_barrier_semaphore()
    for off in (1, 2, 3):
        pl.semaphore_signal(barrier, inc=1, device_id=z_at(off), device_id_type=MESH)
    core, to_core = lax.axis_index("dp") % 2, place()[4]
    pl.semaphore_signal(barrier, inc=1, device_id=to_core, device_id_type=MESH)

    def half_of(ref, which):
        return ref.at[:, pl.ds(pl.multiple_of(which * (width // 2), width // 2), width // 2)]

    own_rows, other_rows = pl.ds(0, tokens), pl.ds(tokens, tokens)
    pairs = ((half_of(normed, core), half_of(normed, 1 - core), normed_pair.at[own_rows], normed_pair.at[other_rows]),
             (half_of(out_grad, core), half_of(out_grad, 1 - core), cotan_pair.at[own_rows], cotan_pair.at[other_rows]),
             (modes, modes, modes_pair.at[:, own_rows], modes_pair.at[:, other_rows]))

    def pair_copies(i):
        mine, theirs, here, there = pairs[i]
        return (pltpu.make_async_copy(mine, here, pair_local.at[i]),
                pltpu.make_async_remote_copy(src_ref=theirs, dst_ref=there, send_sem=pair_send.at[i], recv_sem=pair_recv.at[i],
                                             device_id=to_core, device_id_type=MESH))

    def view_copy(i, slot, m):
        tall = deep * 2 * groups
        return pltpu.make_async_copy(view.at[m, pl.ds(pl.multiple_of(i * tall, tall), tall)], views[slot].at[m],
                                     view_sems.at[slot, m])

    def stage_copy(i, slot, half, m):
        target = w_inner if half == 0 else w_gate
        return pltpu.make_async_copy(stages[slot].at[half, pl.ds(m * deep, deep)],
                                     target.at[m, pl.ds(pl.multiple_of(i * deep, deep), deep)], stage_sems.at[slot, half, m])

    def out_copy(m):
        return pltpu.make_async_copy(out_proj.at[m], w_out.at[m], out_sems.at[m])

    for slot in range(2):
        for m in range(2):
            view_copy(slot, slot, m).start()
    for m in range(2):
        out_copy(m).start()

    def norm_block(i, nothing):
        at = pl.ds(pl.multiple_of(i * block, block), block)
        rows = hidden[at, :].astype(jnp.float32)
        scale = lax.rsqrt(jnp.mean(rows * rows, axis=1, keepdims=True) + EPS)
        inverse[at, :] = jnp.broadcast_to(scale, (block, LANES))
        normed[at, :] = (rows * scale * gain[...]).astype(low)
        return nothing

    lax.fori_loop(0, tokens // block, norm_block, 0)
    acc[0:8, :] = jnp.zeros((8, channels), jnp.float32)

    def unpack(slot):
        for m in range(2):
            wide[m] = views[slot][m].astype(jnp.float32)
            for half in range(2):
                stages[slot][half, m * deep:(m + 1) * deep, :] = jnp.concatenate(
                    [wide[m, pl.ds(g * 2 + half, deep, stride=2 * groups), :] for g in range(groups)], axis=1).astype(low)

    def multiply(i, slot, first):
        columns = normed[:, pl.ds(pl.multiple_of(i * deep, deep), deep)]
        left = jnp.concatenate([columns * widened(modes[0], deep), columns * widened(modes[1], deep)], axis=1)
        for half in range(2):
            product = dot_f32(left, stages[slot][half])
            if half == 0:
                acc[8:8 + tokens, :] = product if first else acc[8:8 + tokens, :] + product
            else:
                gate_z[...] = product if first else gate_z[...] + product

    def arrive(i, slot):
        for m in range(2):
            view_copy(i, slot, m).wait()

    def depart(i, slot):
        for m in range(2):
            for half in range(2):
                stage_copy(i, slot, half, m).start()

    def departed(i, slot):
        for m in range(2):
            for half in range(2):
                stage_copy(i, slot, half, m).wait()

    def fetch(i, slot):
        for m in range(2):
            view_copy(i, slot, m).start()

    arrive(0, 0)
    unpack(0)
    depart(0, 0)
    fetch(2, 0)
    arrive(1, 1)
    multiply(0, 0, True)
    unpack(1)
    depart(1, 1)
    fetch(3, 1)

    def looped(j, nothing):
        for slot in range(2):
            i = 2 * j + slot
            departed(i, slot)
            arrive(i + 2, slot)
            multiply(i + 1, 1 - slot, False)
            unpack(slot)
            depart(i + 2, slot)

            @pl.when(i + 4 < turns)
            def _():
                fetch(i + 4, slot)
        return nothing

    lax.fori_loop(0, turns // 2 - 1, looped, 0)
    multiply(turns - 1, 1, False)
    departed(turns - 2, 0)
    departed(turns - 1, 1)

    taps = conv_w.shape[0]

    def conv_block(i, nothing):
        base = pl.multiple_of(i * block, block)
        at = pl.ds(base, block)
        rows = acc[pl.ds(base, block + 8), :]
        doc = docs[at, :]
        total = conv_b[...] + conv_w[taps - 1:taps, :] * rows[8:8 + block, :]
        for offset in range(1, taps):
            total = total + conv_w[taps - 1 - offset:taps - offset, :] * rows[8 - offset:8 - offset + block, :] * doc[:, offset:offset + 1]
        conv_sum[at, :] = total
        active = (total * jax.nn.sigmoid(total)).astype(low)
        act_b[at, :] = active
        part = dot_f32(active * widened(modes[0, at, :], channels), x_wide[0], NT)
        part = part + dot_f32(active * widened(modes[1, at, :], channels), x_wide[1], NT)
        proj_buf[at, 0:LANES] = part[:, :LANES].astype(low)
        proj_buf[at, LANES:2 * LANES] = split_tail(part[:, LANES:], coeffs_wide)
        return nothing

    lax.fori_loop(0, tokens // block, conv_block, 0)

    def red_copy(off):
        return pltpu.make_async_remote_copy(
            src_ref=proj_buf.at[pl.ds(pl.multiple_of(((z + off) % 4) * share, share), share)], dst_ref=proj_recv.at[off - 1],
            send_sem=red_send.at[off - 1], recv_sem=red_recv.at[off - 1], device_id=z_at(off), device_id_type=MESH)

    mine = pl.ds(pl.multiple_of(z * share, share), share)

    def all_copy(off):
        return pltpu.make_async_remote_copy(
            src_ref=proj_fin.at[mine], dst_ref=proj_fin.at[mine], send_sem=all_send.at[off - 1],
            recv_sem=all_recv.at[off - 1], device_id=z_at(off), device_id_type=MESH)

    pl.semaphore_wait(barrier, 4)
    for off in (1, 2, 3):
        red_copy(off).start()
    early = [pltpu.make_async_copy(source, target, early_sems.at[i]) for i, (source, target) in enumerate((
        (conv_sum, conv_sum_out), (acc.at[pl.ds(8, tokens)], inner_x_out), (act_b, act_out), (gate_z, gate_z_out)))]
    for copy in early:
        copy.start()
    for i in range(3):
        for copy in pair_copies(i):
            copy.start()
    third = tokens // 3

    def grad_block(i):
        at = pl.ds(i * third, third)
        zero = dot_f32(out_grad[at, :], w_out[0], NT)
        one = dot_f32(out_grad[at, :], w_out[1], NT)
        gated_grad[at, :] = jnp.where(docs[at, 0:1] > 0.5, zero, one)

    for m in range(2):
        out_copy(m).wait()
    grad_block(0)
    for off in (1, 2, 3):
        red_copy(off).wait_recv()
    total = proj_buf[mine, :].astype(jnp.float32)
    for k in range(3):
        total = total + proj_recv[k].astype(jnp.float32)
    proj_fin[mine, 0:LANES] = total[:, :LANES].astype(low)
    proj_fin[mine, LANES:2 * LANES] = split_tail(join_tail(total[:, LANES:], coeffs_wide), coeffs_wide)
    for off in (1, 2, 3):
        all_copy(off).start()
    grad_block(1)
    grad_block(2)
    for off in (1, 2, 3):
        all_copy(off).wait_recv()
    rank_out[...] = proj_fin[:, 0:LANES]
    coeff_out[...] = join_tail(proj_fin[:, LANES:2 * LANES].astype(jnp.float32), coeffs_wide)
    for off in (1, 2, 3):
        red_copy(off).wait_send()
        all_copy(off).wait_send()
    for i in range(3):
        for copy in pair_copies(i):
            copy.wait()
    for copy in early:
        copy.wait()


def front(hidden, gain, conv_w, conv_b, docs, modes, x_wide, out_grad, in_proj, out_proj, coeffs_wide):
    tokens, width = hidden.shape
    channels = conv_w.shape[1]
    groups = channels // LANES
    low, f32 = jnp.bfloat16, jnp.float32
    view = in_proj.reshape(2, width, 2, groups, LANES).transpose(0, 1, 3, 2, 4).reshape(2, width * 2 * groups, LANES)
    deep = 256
    vmem, anywhere = pl.BlockSpec(memory_space=pltpu.VMEM), pl.BlockSpec(memory_space=pl.ANY)
    shape = jax.ShapeDtypeStruct
    return pl.pallas_call(
        functools.partial(front_kernel, coeffs_wide),
        in_specs=[vmem] * 8 + [anywhere] * 2,
        out_specs=[anywhere] * 5 + [vmem] + [anywhere] * 4 + [vmem] * 3,
        out_shape=[
            shape((2, width, channels), low), shape((2, width, channels), low), shape((2 * tokens, width // 2), low),
            shape((2 * tokens, width // 2), low), shape((2, 2 * tokens, LANES), low),
            shape((tokens, LANES), f32), shape((tokens, channels), f32), shape((tokens, channels), f32),
            shape((tokens, channels), low), shape((tokens, channels), f32), shape((tokens, channels), f32),
            shape((tokens, LANES), low), shape((tokens, LANES), f32),
        ],
        scratch_shapes=[
            pltpu.VMEM((tokens, width), low), pltpu.VMEM((tokens, channels), f32), pltpu.VMEM((tokens, channels), low),
            pltpu.VMEM((tokens, channels), f32),
            pltpu.VMEM((tokens + 8, channels), f32),
            pltpu.VMEM((2, deep * 2 * groups, LANES), low), pltpu.VMEM((2, deep * 2 * groups, LANES), low),
            pltpu.VMEM((2, deep * 2 * groups, LANES), f32),
            pltpu.VMEM((2, 2 * deep, channels), low), pltpu.VMEM((2, 2 * deep, channels), low),
            pltpu.VMEM((2, channels, width), low),
            pltpu.VMEM((tokens, 2 * LANES), low),
            pltpu.VMEM((3, tokens // 4, 2 * LANES), low),
            pltpu.VMEM((tokens, 2 * LANES), low),
            DMA((2, 2)), DMA((2, 2, 2)), DMA((2,)), DMA((3,)), DMA((3,)), DMA((3,)), DMA((3,)), DMA((3,)), DMA((3,)), DMA((3,)), DMA((4,)),
        ],
        cost_estimate=pl.CostEstimate(flops=20_000_000_000, bytes_accessed=80_000_000, transcendentals=1_000_000),
        compiler_params=pltpu.CompilerParams(collective_id=4, has_side_effects=True, vmem_limit_bytes=60 * 1024 * 1024),
        name="front",
    )(hidden, gain, conv_w, conv_b, docs, modes, x_wide, out_grad, view, out_proj)


def products_kernel(gated, cotan, normed, gate, modes, split, weights,
                    out0, out1, gate0, gate1, partial, normed_t,
                    left_buf, right_buf, mode_buf, split_buf, w_buf, turned, mask_buf, stage, stage_wide,
                    load_sems, w_sems, stage_sems, wide_sems, turned_sem):
    pair_tokens, channels = left_buf.shape[1:]
    tokens, deep = split_buf.shape
    low = jnp.bfloat16
    block = 128
    loads = [pltpu.make_async_copy(source, target, load_sems.at[i]) for i, (source, target) in enumerate((
        (gated, left_buf.at[0]), (cotan, right_buf.at[0]), (modes, mode_buf), (normed, left_buf.at[1]), (gate, right_buf.at[1]),
        (split, split_buf)))]
    for copy in loads:
        copy.start()
    half = w_buf.shape[0] // 2
    w_loads = [pltpu.make_async_copy(weights.at[m], w_buf.at[pl.ds(m * half, half)], w_sems.at[m]) for m in range(2)]
    for copy in w_loads:
        copy.start()
    tall = stage.shape[1]
    turns = channels // tall
    flights = [None, None]

    def turn_left(which):
        def body(i, nothing):
            at = pl.ds(pl.multiple_of(i * block, block), block)
            turned[at, :] = left_buf[which, :, at].T
            return nothing
        lax.fori_loop(0, channels // block, body, 0)

    def multiply(which, targets):
        for m in range(2):
            def mask_rows(i, nothing):
                at = pl.ds(pl.multiple_of(i * block, block), block)
                mask_buf[at, :] = right_buf[which, at, :] * widened(mode_buf[m, at, :], channels)
                return nothing
            lax.fori_loop(0, pair_tokens // block, mask_rows, 0)
            for j in range(turns):
                slot = (m * turns + j) % 2
                if flights[slot] is not None:
                    flights[slot].wait()
                stage[slot] = dot_f32(turned[pl.ds(j * tall, tall), :], mask_buf[...]).astype(low)
                flights[slot] = pltpu.make_async_copy(stage.at[slot], targets[m].at[pl.ds(j * tall, tall)], stage_sems.at[slot])
                flights[slot].start()

    for copy in loads[:3]:
        copy.wait()
    turn_left(0)
    multiply(0, (out0, out1))
    for copy in loads[3:5]:
        copy.wait()
    turn_left(1)
    out_turned = pltpu.make_async_copy(turned, normed_t, turned_sem)
    out_turned.start()
    multiply(1, (gate0, gate1))
    loads[5].wait()
    for copy in w_loads:
        copy.wait()
    part = stage_wide.shape[1]
    wide_flights = [None, None]
    for j in range(tokens // part):
        slot = j % 2
        if wide_flights[slot] is not None:
            wide_flights[slot].wait()
        stage_wide[slot] = dot_f32(split_buf[pl.ds(j * part, part), :], w_buf[...]).astype(low)
        wide_flights[slot] = pltpu.make_async_copy(stage_wide.at[slot], partial.at[pl.ds(j * part, part)], wide_sems.at[slot])
        wide_flights[slot].start()
    for copy in flights + wide_flights + [out_turned]:
        copy.wait()


def make_products(gated, cotan, normed, gate, modes, split, weights):
    pair_tokens, channels = gated.shape
    tokens, deep = split.shape
    width = weights.shape[2]
    low = jnp.bfloat16
    anywhere = pl.BlockSpec(memory_space=pl.ANY)
    square = jax.ShapeDtypeStruct((channels, channels), low)
    return pl.pallas_call(
        products_kernel,
        in_specs=[anywhere] * 7,
        out_specs=[anywhere] * 6,
        out_shape=[square] * 4 + [jax.ShapeDtypeStruct((tokens, width), low), jax.ShapeDtypeStruct((channels, pair_tokens), low)],
        scratch_shapes=[
            pltpu.VMEM((2, pair_tokens, channels), low), pltpu.VMEM((2, pair_tokens, channels), low),
            pltpu.VMEM((2, pair_tokens, LANES), low), pltpu.VMEM((tokens, deep), low), pltpu.VMEM((deep, width), low),
            pltpu.VMEM((channels, pair_tokens), low), pltpu.VMEM((pair_tokens, channels), low),
            pltpu.VMEM((2, channels // 2, channels), low), pltpu.VMEM((2, tokens // 3, width), low),
            DMA((6,)), DMA((2,)), DMA((2,)), DMA((2,)), DMA,
        ],
        cost_estimate=pl.CostEstimate(flops=20_000_000_000, bytes_accessed=45_000_000, transcendentals=0),
        compiler_params=pltpu.CompilerParams(vmem_limit_bytes=60 * 1024 * 1024),
        name="products",
    )(gated, cotan, normed, gate, modes, split, weights)


def final_kernel(side, depth, where_ref, out_shared, out_own, gate_shared, gate_own, inner_shared, inner_own,
                 hidden, out_grad, inverse, gain, summed_rows, summed_out, normed_sum,
                 out_ref, in_ref, output, input_grad, x_grad, dt_grad, *rest):
    row_grads, (narrow, wide, row_in, row_out, in_sems, out_sems, row_in_sems, row_out_sems) = rest[:-8], rest[-8:]
    x, y, core = where_ref[0], where_ref[1], where_ref[2]
    low, f32 = jnp.bfloat16, jnp.float32
    block = row_in.shape[2]
    jobs = []
    for which, (shared, own) in enumerate(((out_shared, out_own), (gate_shared, gate_own), (inner_shared, inner_own))):
        for mode in range(2):
            for owner in range(2):
                c = core if owner == 0 else 1 - core
                for k in range(4):
                    qx = x if k in (0, 1) else 1 - x
                    qy = y if k in (0, 2) else 1 - y
                    row = (qx * 2 + qy if mode == 0 else qy * 2 + qx) * side
                    if which == 0:
                        target = out_ref.at[mode, pl.ds(pl.multiple_of(row, side), side),
                                            pl.ds(pl.multiple_of(c * depth, depth), depth)]
                    else:
                        target = in_ref.at[mode, pl.ds(pl.multiple_of(c * 4 * side + row, side), side), 2 - which, :]
                    source = own.at[mode] if owner == 0 and k == 0 else shared.at[mode, owner, k]
                    jobs.append((source, target))
    slots = narrow.shape[0]
    loads = [pltpu.make_async_copy(jobs[i][0], narrow.at[i % slots], in_sems.at[i % slots]) for i in range(len(jobs))]
    stores = [pltpu.make_async_copy(wide.at[i % slots], jobs[i][1], out_sems.at[i % slots]) for i in range(len(jobs))]
    count = hidden.shape[0] // block

    def row_loads(i):
        at = pl.ds(i * block, block)
        return [pltpu.make_async_copy(ref.at[at], row_in.at[i % 2, j], row_in_sems.at[i % 2, j])
                for j, ref in enumerate((hidden, out_grad, summed_out, normed_sum))]

    def row_stores(i):
        at = pl.ds(i * block, block)
        return [pltpu.make_async_copy(row_out.at[i % 2, j], ref.at[at], row_out_sems.at[i % 2, j])
                for j, ref in enumerate((output, input_grad))]

    for copy in row_loads(0) + row_loads(1):
        copy.start()
    for i in range(slots):
        loads[i].start()
    span, rank_dim = x_grad.shape[1], dt_grad.shape[1]
    for m in range(2):
        base = m * (span + rank_dim)
        x_grad[m] = summed_rows[base:base + span, :].astype(f32)
        dt_grad[m] = summed_rows[base + span:base + span + rank_dim, :].astype(f32)
    tail_rows = summed_rows[2 * (span + rank_dim):, :].astype(f32)
    at = 0
    for ref in row_grads:
        ref[...] = tail_rows[at:at + ref.shape[0], :]
        at += ref.shape[0]
    per = -(-len(jobs) // count)
    for i in range(count):
        for copy in row_loads(i):
            copy.wait()
        if i >= 2:
            for copy in row_stores(i - 2):
                copy.wait()
        rows = row_in[i % 2, 0].astype(f32)
        scale = inverse[pl.ds(i * block, block), 0:1]
        scaled = row_in[i % 2, 3].astype(f32) * gain[...]
        mean = jnp.mean(scaled * rows, axis=1, keepdims=True)
        row_out[i % 2, 0] = (rows + row_in[i % 2, 2].astype(f32)).astype(low)
        row_out[i % 2, 1] = (row_in[i % 2, 1].astype(f32) + scale * scaled - rows * (scale * scale * scale) * mean).astype(low)
        for copy in row_stores(i):
            copy.start()
        if i + 2 < count:
            for copy in row_loads(i + 2):
                copy.start()
        for p in range(i * per, min((i + 1) * per, len(jobs))):
            loads[p].wait()
            if p >= slots:
                stores[p - slots].wait()
            wide[p % slots] = narrow[p % slots].astype(f32)
            stores[p].start()
            if p + slots < len(jobs):
                loads[p + slots].start()
    for p in range(len(jobs) - slots, len(jobs)):
        stores[p].wait()
    for i in (count - 2, count - 1):
        for copy in row_stores(i):
            copy.wait()


def final(where, out_shared, out_own, gate_shared, gate_own, inner_shared, inner_own, hidden, out_grad, inverse, gain,
          summed_rows, rank_dim, row_counts, summed_out, normed_sum):
    side, depth = out_own.shape[1:]
    tokens, width = hidden.shape
    channels = 4 * side
    low, f32 = jnp.bfloat16, jnp.float32
    anywhere, vmem = pl.BlockSpec(memory_space=pl.ANY), pl.BlockSpec(memory_space=pltpu.VMEM)
    block, slots = 128, 6
    return pl.pallas_call(
        functools.partial(final_kernel, side, depth),
        in_specs=[pl.BlockSpec(memory_space=pltpu.SMEM)] + [anywhere] * 8 + [vmem] * 3 + [anywhere] * 2,
        out_specs=[anywhere] * 4 + [vmem] * (2 + len(row_counts)),
        out_shape=[
            jax.ShapeDtypeStruct((2, channels, width), f32), jax.ShapeDtypeStruct((2, width, 2, channels), f32),
            jax.ShapeDtypeStruct((tokens, width), low), jax.ShapeDtypeStruct((tokens, width), low),
            jax.ShapeDtypeStruct((2, (summed_rows.shape[0] - 32) // 2 - rank_dim, channels), f32),
            jax.ShapeDtypeStruct((2, rank_dim, channels), f32),
        ] + [jax.ShapeDtypeStruct((n, channels), f32) for n in row_counts],
        scratch_shapes=[
            pltpu.VMEM((slots, side, depth), low), pltpu.VMEM((slots, side, depth), f32),
            pltpu.VMEM((2, 4, block, width), low), pltpu.VMEM((2, 2, block, width), low),
            DMA((slots,)), DMA((slots,)), DMA((2, 4)), DMA((2, 2)),
        ],
        cost_estimate=pl.CostEstimate(flops=50_000_000, bytes_accessed=91_000_000, transcendentals=0),
        compiler_params=pltpu.CompilerParams(vmem_limit_bytes=60 * 1024 * 1024),
        name="final_rows",
    )(where, out_shared, out_own, gate_shared, gate_own, inner_shared, inner_own, hidden, out_grad, inverse, gain,
      summed_rows, summed_out, normed_sum)


def scan_backward_kernel(states, groups, rows, unroll, count, joined,
                         bc_ref, pre_ref, act_ref, mixed_ref, keep_ref, alog_ref, skip_ref, h_ref, start_ref, *rest):
    if joined:
        prods, part_ref, rest = rest[:4], rest[4], rest[5:]
    pgrad_ref, apart_ref, bcg_ref, sum_ref, skipsum_ref = rest[:5]
    rest = rest[5:]
    if joined:
        out_own, gate_own, z_own, rest = rest[0], rest[1], rest[2], rest[3:]
    carry_ref, rate_scr, decay_scr, sk_scr, u_scr, dy_scr, w_scr, s_scr, p_scr, q_scr = rest[:10]
    rest = rest[10:]
    chunk = pl.program_id(0)
    if joined:
        line = LineReduce(part_ref, z_own, rest[0], rest[1], rest[2:5])
        outs = Reduce(prods[:2], out_own, *rest[5:8], rest[8:13])
        gate = Reduce(prods[2:], gate_own, *rest[13:16], rest[16:21])

        @pl.when(chunk == 0)
        def _():
            line.line.load().start()
            greet()
            outs.event(0)
            line.line.load().wait()
            line.line.begin((0,))

        for at in range(1, count):
            @pl.when(chunk == at)
            def _():
                if at < line.line.pieces:
                    line.line.begin((at,))
                if at == 2:
                    outs.event(1)
                elif at == 3:
                    gate.event(0)
                elif at == 5:
                    outs.event(2)
                elif at == 6:
                    outs.last()
                elif at == 8:
                    gate.event(1)
                elif at == 10:
                    gate.event(2)
                line.turn(at)

    @pl.when(chunk == 0)
    def _():
        decay = -jnp.exp(alog_ref[...])
        decay_scr[...] = decay
        rate_scr[...] = decay * LOG2E
        carry_ref[...] = jnp.zeros_like(carry_ref)
        sum_ref[...] = jnp.zeros_like(sum_ref)
        skipsum_ref[...] = jnp.zeros_like(skipsum_ref)

    step = softplus(pre_ref[...])
    act = act_ref[...].astype(jnp.float32)
    mixed = mixed_ref[...].astype(jnp.float32)
    spread_rows(u_scr, step * act, groups)
    spread_rows(dy_scr, mixed, groups)
    spread_rows(sk_scr, jnp.where(keep_ref[...] > 0.0, step, BIG), groups)
    skipsum_ref[...] += jnp.sum(mixed * act, axis=0, keepdims=True)

    def one(t, carried, before):
        at = pl.multiple_of(t * groups, groups)
        sk = sk_scr[pl.ds(at, groups), :]
        u = u_scr[pl.ds(at, groups), :]
        dy = dy_scr[pl.ds(at, groups), :]
        w = jnp.zeros_like(u)
        s = jnp.zeros_like(u)
        new, pb, pc = [], [], []
        for n in range(states):
            g = dy * bc_ref[t, states + n] + carried[n]
            pb.append(g * u)
            pc.append(dy * h_ref[t, n])
            w = w + g * bc_ref[t, n]
            fg = jnp.exp2(sk * rate_scr[n]) * g
            lg = fg * before(n)
            s = s + lg * decay_scr[n]
            sum_ref[n] += lg * sk
            new.append(fg)
        w_scr[pl.ds(at, groups), :] = w
        s_scr[pl.ds(at, groups), :] = s
        both = pb + pc
        batch = max(1, 16 // groups)
        for j in range(0, 2 * states, batch):
            p_scr[t, pl.ds(j * groups, batch * groups), :] = jnp.concatenate(
                both[j:j + batch], axis=0).astype(jnp.bfloat16)
        return tuple(new)

    def looped(i, carried):
        t = rows - 1 - i
        return one(t, carried, lambda n: h_ref[t - 1, n])

    last = lax.fori_loop(0, rows - 1, looped, tuple(carry_ref[n] for n in range(states)), unroll=unroll)
    last = one(0, last, lambda n: start_ref[0, n])
    for n in range(states):
        carry_ref[n] = last[n]

    ones = jnp.ones((16, LANES), jnp.bfloat16)

    def reduce_one(t, nothing):
        q = lax.dot_general(ones, p_scr[t], (((1,), (1,)), ((), ())), preferred_element_type=jnp.float32)
        q_scr[pl.ds(t, 1), :] = q[0:1]
        return nothing

    lax.fori_loop(0, rows, reduce_one, 0, unroll=4)
    shape = (2 * states * groups, LANES)
    pick = (lax.broadcasted_iota(jnp.int32, shape, 0) // groups == lax.broadcasted_iota(jnp.int32, shape, 1))
    pick = pick.astype(jnp.float32).astype(jnp.bfloat16)
    q = q_scr[...]
    high = q.astype(jnp.bfloat16)
    low = (q - high.astype(jnp.float32)).astype(jnp.bfloat16)
    bcg_ref[...] = (jnp.dot(high, pick, preferred_element_type=jnp.float32)
                    + jnp.dot(low, pick, preferred_element_type=jnp.float32))
    w = gather_rows(w_scr, rows, groups)
    s = gather_rows(s_scr, rows, groups)
    pgrad_ref[...] = ((act * w + s) * jax.nn.sigmoid(pre_ref[...])).astype(pgrad_ref.dtype)
    apart_ref[...] = mixed * skip_ref[...] + step * w

    if joined:
        @pl.when(chunk == count - 1)
        def _():
            gate.last()
            outs.done()
            gate.done()
            line.done()


def scan_backward(bc, pre, act, mixed, keep, a_log3, skip, h, starts, products=None, z_part=None, rows=64, unroll=7, pieces=6):
    tokens, channels = pre.shape
    groups = channels // LANES
    states = a_log3.shape[0]
    count = tokens // rows
    joined = products is not None
    wide = pl.BlockSpec((rows, channels), lambda i: (count - 1 - i, 0))
    whole3 = pl.BlockSpec((states, groups, LANES), lambda i: (0, 0, 0))
    row = pl.BlockSpec((1, channels), lambda i: (0, 0))
    anywhere = pl.BlockSpec(memory_space=pl.ANY)
    small = lambda: pltpu.VMEM((states, groups, LANES), jnp.float32)
    long = lambda: pltpu.VMEM((rows * groups, LANES), jnp.float32)
    extra, extra_shapes, extra_scratch = [], [], []
    if joined:
        side, depth = products[0].shape[0] // 4, products[0].shape[1]
        part = z_part.reshape(2, pieces, tokens // 2 // pieces, z_part.shape[1])
        extra = list(products) + [part]
        extra_shapes = [jax.ShapeDtypeStruct((2, side, depth), jnp.bfloat16)] * 2 + [jax.ShapeDtypeStruct(part.shape, jnp.bfloat16)]
        extra_scratch = LineReduce.scratch(*part.shape[1:]) + Reduce.scratch(side, depth) + Reduce.scratch(side, depth)
    settings = dict(collective_id=2, has_side_effects=True) if joined else {}
    outs = pl.pallas_call(
        functools.partial(scan_backward_kernel, states, groups, rows, unroll, count, joined),
        grid=(count,),
        in_specs=[
            pl.BlockSpec((rows, 2 * states), lambda i: (count - 1 - i, 0), memory_space=pltpu.SMEM),
            wide, wide, wide,
            pl.BlockSpec((rows, 1), lambda i: (count - 1 - i, 0)),
            whole3, row,
            pl.BlockSpec((rows, states, groups, LANES), lambda i: (count - 1 - i, 0, 0, 0)),
            pl.BlockSpec((1, states, groups, LANES), lambda i: (count - 1 - i, 0, 0, 0)),
        ] + [anywhere] * len(extra),
        out_specs=[wide, wide, pl.BlockSpec((rows, LANES), lambda i: (count - 1 - i, 0)), whole3, row]
        + [anywhere] * len(extra_shapes),
        out_shape=[
            jax.ShapeDtypeStruct((tokens, channels), jnp.bfloat16),
            jax.ShapeDtypeStruct((tokens, channels), jnp.float32),
            jax.ShapeDtypeStruct((tokens, LANES), jnp.float32),
            jax.ShapeDtypeStruct((states, groups, LANES), jnp.float32),
            jax.ShapeDtypeStruct((1, channels), jnp.float32),
        ] + extra_shapes,
        scratch_shapes=[small(), small(), small(), long(), long(), long(), long(), long(),
                        pltpu.VMEM((rows, 2 * states * groups, LANES), jnp.bfloat16),
                        pltpu.VMEM((rows, 2 * states * groups), jnp.float32)] + extra_scratch,
        cost_estimate=pl.CostEstimate(flops=60 * tokens * channels * states,
                                      bytes_accessed=4 * tokens * channels * states,
                                      transcendentals=tokens * channels * states),
        compiler_params=pltpu.CompilerParams(vmem_limit_bytes=52 * 1024 * 1024, **settings),
        name="scan_backward",
    )(bc, pre, act, mixed, keep, a_log3, skip, h, starts, *extra)
    return outs


def lagged(values, offset):
    padding = [(offset, 0)] + [(0, 0)] * (values.ndim - 1)
    return jnp.pad(values, padding)[: values.shape[0]]


def leading(values, offset):
    padding = [(0, offset)] + [(0, 0)] * (values.ndim - 1)
    return jnp.pad(values, padding)[offset:]


def pick_dot(left_side, weights, first_mode):
    first_part = jnp.dot(left_side, weights[0], preferred_element_type=jnp.float32)
    second_part = jnp.dot(left_side, weights[1], preferred_element_type=jnp.float32)
    return jnp.where(first_mode, first_part, second_part)


def pick_back(gradient, weights, first_mode):
    dims = (((1,), (1,)), ((), ()))
    first_part = lax.dot_general(gradient, weights[0], dims, preferred_element_type=jnp.float32)
    second_part = lax.dot_general(gradient, weights[1], dims, preferred_element_type=jnp.float32)
    return jnp.where(first_mode, first_part, second_part)


def weight_grads(left_side, gradient, first_mode):
    nothing = jnp.zeros_like(gradient)
    dims = (((0,), (0,)), ((), ()))
    first_part = lax.dot_general(
        left_side,
        jnp.where(first_mode, gradient, nothing),
        dims,
        preferred_element_type=jnp.float32,
    )
    second_part = lax.dot_general(
        left_side,
        jnp.where(first_mode, nothing, gradient),
        dims,
        preferred_element_type=jnp.float32,
    )
    return jnp.stack([first_part, second_part])


def finish_rows(normed_grad, hidden, inverse, cotan, norm_gain):
    scaled = normed_grad * norm_gain
    gain_terms = jnp.sum(normed_grad * hidden * inverse, axis=0)
    cubed = inverse * inverse * inverse
    rows = (
        cotan + inverse * scaled - hidden * cubed * jnp.mean(scaled * hidden, axis=1, keepdims=True)
    )
    return (rows.astype(jnp.bfloat16), gain_terms)


def swap(values, distance):
    return lax.ppermute(values, "dp", [(i, i ^ distance) for i in range(8)])


CORE = 1


def tie(values, *others):
    return lax.optimization_barrier((values,) + others)[0]


def z_sum(values, size, dtype=jnp.bfloat16):
    distance = 1
    while distance < size:
        low = values.astype(dtype)
        got = lax.ppermute(low, "tensor", [(i, i ^ distance) for i in range(size)])
        values = low.astype(jnp.float32) + got.astype(jnp.float32)
        distance *= 2
    return values


def shards(names, hidden_in, segment_ids, modality, norm_gain, in_proj, conv_weight, conv_bias, x_proj, dt_proj, dt_bias,
           a_log, skip_gain, out_proj, out_grad):
    tokens, model_width = hidden_in.shape
    conv_taps, channels = conv_weight.shape
    rank_dim = dt_proj.shape[1]
    state_dim = a_log.shape[0]
    groups = channels // LANES
    ways = names["tensor"]
    by_hand = names["dp"] == 8 and names["tensor"] == 4
    low = jnp.bfloat16
    rank = lax.axis_index("dp")
    core, x_at, y_at = rank % 2, (rank // 2) % 2, rank // 4
    where = jnp.stack([x_at, y_at, core]).astype(jnp.int32)
    first_mode = (modality == 0)[:, None]
    nothing = jnp.zeros((), low)
    dims = (((0,), (0,)), ((), ()))

    def masked_products(left, right, modes, mask_left):
        products = []
        for chosen in (modes, jnp.logical_not(modes)):
            one = jnp.where(chosen, left, nothing) if mask_left else left
            two = right if mask_left else jnp.where(chosen, right, nothing)
            products.append(lax.dot_general(one, two, dims, preferred_element_type=jnp.float32).astype(low))
        return jnp.stack(products)

    same_doc = [jnp.ones((tokens, 1), jnp.float32)]
    for offset in range(1, conv_taps):
        earlier_seg = jnp.pad(segment_ids, (offset, 0), constant_values=-1)[:tokens]
        same_doc.append((earlier_seg == segment_ids).astype(jnp.float32)[:, None])
    if by_hand:
        modes_own = jnp.broadcast_to(jnp.stack([first_mode, jnp.logical_not(first_mode)]), (2, tokens, LANES)).astype(low)
        x_wide = jnp.pad(jnp.swapaxes(x_proj, 1, 2), ((0, 0), (0, 96), (0, 0)))
        facts = jnp.concatenate([first_mode.astype(jnp.float32)] + same_doc[1:], axis=1)
        (in_inner, in_gate, normed_pair, cotan_pair, modes, inverse, conv_sum, inner_x, activated_b, gate_z, gated_grad, rank_b, coeffs) = front(
            hidden_in, norm_gain[None], conv_weight, conv_bias[None], facts, modes_own, x_wide, out_grad, in_proj, out_proj,
            2 * state_dim)
        coeffs = coeffs[:, :2 * state_dim]
    else:
        hidden = hidden_in.astype(jnp.float32)
        inverse = lax.rsqrt(jnp.mean(hidden * hidden, axis=1, keepdims=True) + EPS)
        normed_b = (hidden * inverse * norm_gain).astype(low)
        in_inner = in_proj[:, :, 0, :]
        in_gate = in_proj[:, :, 1, :]
        inner_x = pick_dot(normed_b, in_inner, first_mode)
        conv_sum = conv_bias + conv_weight[conv_taps - 1] * inner_x
        for offset in range(1, conv_taps):
            conv_sum = conv_sum + conv_weight[conv_taps - 1 - offset] * lagged(inner_x, offset) * same_doc[offset]
        activated_b = jax.nn.silu(conv_sum).astype(low)
        projected = z_sum(pick_dot(activated_b, x_proj, first_mode), ways)
        rank_b = projected[:, :rank_dim].astype(low)
        coeffs = projected[:, rank_dim:]
        gate_z = pick_dot(normed_b, in_gate, first_mode)
        gated_grad = pick_back(out_grad, out_proj, first_mode)
    step_pre, dt = rank_b, (dt_proj, dt_bias)
    if not by_hand:
        step_pre = pick_dot(rank_b, dt_proj, first_mode) + jnp.where(first_mode, dt_bias[0], dt_bias[1])
        dt = ()
    keep = same_doc[1]
    a_log3 = a_log.reshape(state_dim, groups, LANES)
    skip_row = skip_gain[None]
    forward = scan_forward(coeffs, step_pre, activated_b, gate_z, gated_grad, keep, a_log3, skip_row,
                           first_mode.astype(jnp.float32), by_hand, dt)
    gated_b, gate_grad_b, mixed_grad, states, starts = forward[:5]
    if by_hand:
        step_pre = forward[5]
        made = make_products(gated_b, cotan_pair, normed_pair, gate_grad_b, modes, forward[6], out_proj)
        products, partial_out, normed_t = made[:4], made[4], made[5]
        back = scan_backward(coeffs, step_pre, activated_b, mixed_grad, keep, a_log3, skip_row, states, starts,
                             products, partial_out)
        out_own, gate_own, z_own = back[5:]
    else:
        partial_out = pick_dot(gated_b, out_proj, first_mode).astype(low)
        back = scan_backward(coeffs, step_pre, activated_b, mixed_grad, keep, a_log3, skip_row, states, starts)
        summed_out = lax.psum(partial_out, "tensor")
        out_proj_grad = lax.psum(weight_grads(gated_b, out_grad, first_mode).astype(low), "dp").astype(jnp.float32)
        gate_proj_grad = lax.psum(weight_grads(normed_b, gate_grad_b, first_mode).astype(low), "dp")
    pre_grad_b, act_part, coeff_grad, sums, skips = back[:5]
    a_log_grad = sums.reshape(state_dim, channels) * -jnp.exp(a_log)
    mode_rows = x_proj.shape[2] + rank_dim
    if by_hand:
        later = jnp.stack([same_doc[0]] + [leading(same_doc[k], k) for k in range(1, conv_taps)], axis=1)[:, :, 0]
        row_facts = jnp.concatenate([inverse[:, :1], first_mode.astype(jnp.float32)], axis=1)
        rows, normed_low, inner_product, out_shared, gate_shared, z_res = middle(
            pre_grad_b, act_part, coeff_grad, conv_sum, inner_x, activated_b, rank_b, dt_proj, x_wide, conv_weight, later, modes,
            gate_grad_b, normed_t, row_facts, jnp.concatenate([a_log_grad, skips], axis=0),
            hidden_in, in_gate, in_inner, out_own, gate_own, z_own)
        summed_out = z_res.reshape(tokens, model_width)
    else:
        pre_grad = pre_grad_b.astype(jnp.float32)
        dt_bias_grad = jnp.stack([
            jnp.sum(jnp.where(first_mode, pre_grad, 0.0), axis=0),
            jnp.sum(jnp.where(first_mode, 0.0, pre_grad), axis=0)])
        rank_part = pick_back(pre_grad_b, dt_proj, first_mode)
        proj_grad_b = z_sum(jnp.concatenate([rank_part, coeff_grad[:, :2 * state_dim]], axis=1), ways).astype(low)
        act_grad = act_part + pick_back(proj_grad_b, x_proj, first_mode)
        sig_conv = jax.nn.sigmoid(conv_sum)
        conv_grad = act_grad * sig_conv * (1.0 + conv_sum * (1.0 - sig_conv))
        conv_bias_grad = jnp.sum(conv_grad, axis=0)
        weight_rows = []
        x_grad = jnp.zeros_like(inner_x)
        for tap_index in range(conv_taps):
            offset = conv_taps - 1 - tap_index
            masked = conv_grad * same_doc[offset]
            weight_rows.append(jnp.sum(masked * lagged(inner_x, offset), axis=0))
            x_grad = x_grad + conv_weight[tap_index] * leading(masked, offset)
        x_grad_b = x_grad.astype(low)
        normed_part = pick_back(x_grad_b, in_inner, first_mode) + pick_back(gate_grad_b, in_gate, first_mode)
        gain_part = jnp.sum(normed_part * (hidden * inverse), axis=0).reshape(-1, channels)
        gain_part = lax.psum(gain_part, "tensor")
        small_modes = jnp.concatenate([
            weight_grads(proj_grad_b, activated_b, first_mode), weight_grads(rank_b, pre_grad_b, first_mode)], axis=1)
        rows = jnp.concatenate([small_modes.reshape(-1, channels), jnp.stack(weight_rows), conv_bias_grad[None], dt_bias_grad,
                                a_log_grad, skips, gain_part], axis=0).astype(low)
    summed_rows = lax.psum(rows, "dp")
    if by_hand:
        (inner_shared,), (inner_own,), normed_sum = tail_exchange([inner_product], normed_low)

        (out_proj_grad, in_proj_grad, output, input_grad, x_rows, dt_proj_grad, conv_weight_grad, conv_row, dt_bias_grad,
         a_log_grad, skip_row, gain_rows) = final(
            where, out_shared, out_own, gate_shared, gate_own, inner_shared, inner_own,
            hidden_in, out_grad, inverse, norm_gain[None], summed_rows, rank_dim, (conv_taps, 1, 2, state_dim, 1, model_width // channels),
            summed_out, normed_sum)
        x_proj_grad = jnp.swapaxes(x_rows, 1, 2)
        conv_bias_grad, skip_grad, norm_gain_grad = conv_row[0], skip_row[0], gain_rows.reshape(-1)
    else:
        inner_proj_grad = lax.psum(weight_grads(normed_b, x_grad_b, first_mode).astype(low), "dp")
        in_proj_grad = jnp.stack([inner_proj_grad, gate_proj_grad], axis=2).astype(jnp.float32)
        normed_sum = lax.psum(normed_part.astype(low), "tensor")
        output = (hidden + summed_out.astype(jnp.float32)).astype(low)
        cotan = out_grad.astype(jnp.float32)
        input_grad, _ = finish_rows(normed_sum.astype(jnp.float32), hidden, inverse, cotan, norm_gain)
        summed_rows = summed_rows.astype(jnp.float32)
        small_modes, rows = summed_rows[:2 * mode_rows].reshape(2, mode_rows, channels), summed_rows[2 * mode_rows:]
        x_proj_grad = jnp.swapaxes(small_modes[:, :-rank_dim], 1, 2)
        dt_proj_grad = small_modes[:, -rank_dim:]
        norm_gain_grad = rows[conv_taps + 4 + state_dim:].reshape(-1)[:model_width]
        at = conv_taps + 1
        conv_weight_grad, conv_bias_grad, dt_bias_grad = rows[:conv_taps], rows[conv_taps], rows[at:at + 2]
        a_log_grad, skip_grad = rows[at + 2:at + 2 + state_dim], rows[at + 2 + state_dim]
    return (output, input_grad, norm_gain_grad, in_proj_grad, conv_weight_grad, conv_bias_grad, x_proj_grad,
            dt_proj_grad, dt_bias_grad, a_log_grad, skip_grad, out_proj_grad)


def solution(mesh):
    in_specs = (
        P("dp", None),
        P("dp"),
        P("dp"),
        P(),
        P(None, None, None, "tensor"),
        P(None, "tensor"),
        P("tensor"),
        P(None, "tensor", None),
        P(None, None, "tensor"),
        P(None, "tensor"),
        P(None, "tensor"),
        P("tensor"),
        P(None, "tensor", None),
        P("dp", None),
    )
    out_specs = (
        P("dp", None),
        P("dp", None),
        P(),
        P(None, None, None, "tensor"),
        P(None, "tensor"),
        P("tensor"),
        P(None, "tensor", None),
        P(None, None, "tensor"),
        P(None, "tensor"),
        P(None, "tensor"),
        P("tensor"),
        P(None, "tensor", None),
    )
    names = dict(mesh.shape)
    return jax.shard_map(functools.partial(shards, names), mesh=mesh, in_specs=in_specs, out_specs=out_specs, check_vma=False)
```

```python
import functools

import jax
import jax.numpy as jnp
from jax import lax
from jax.experimental import pallas as pl
from jax.experimental.pallas import tpu as pltpu
from jax.sharding import PartitionSpec as P

EPS = 1e-05

LANES = 128
BIG = 1000.0
LOG2E = 1.4426950408889634


def softplus(v):
    return jnp.maximum(v, 0.0) + jnp.log1p(jnp.exp(-jnp.abs(v)))


def spread_rows(scratch, values, groups):
    rows = values.shape[0]
    for g in range(groups):
        scratch[pl.ds(g, rows, stride=groups), :] = values[:, g * LANES:(g + 1) * LANES]


def gather_rows(scratch, rows, groups):
    return jnp.concatenate(
        [scratch[pl.ds(g, rows, stride=groups), :] for g in range(groups)], axis=1)


def scan_forward_kernel(states, groups, rows, unroll, count, joined,
                        bc_ref, pre_ref, act_ref, z_ref, gg_ref, keep_ref, alog_ref, skip_ref, mode_ref,
                        *rest):
    chunk = pl.program_id(0)
    if joined:
        dt_ref, dt_bias_ref, rest = rest[0], rest[1], rest[2:]
    gated_ref, ggrad_ref, mixed_ref, h_ref, start_ref, *rest = rest
    if joined:
        pre_out, split_ref, rate_scr, state_scr, sk_scr, u_scr, y_scr, gated_all, ggrad_all, send_sems, recv_sems, local_sems = rest
        tokens = rows * count
        to_core = place()[4]

        def pair_copies(at, i):
            source, target = ((gated_all, gated_ref), (ggrad_all, ggrad_ref))[i]
            base = at * rows
            return (pltpu.make_async_copy(source.at[pl.ds(base, rows)], target.at[pl.ds(base, rows)], local_sems.at[at, i]),
                    pltpu.make_async_remote_copy(
                        src_ref=source.at[pl.ds(base, rows)], dst_ref=target.at[pl.ds(tokens + base, rows)],
                        send_sem=send_sems.at[at, i], recv_sem=recv_sems.at[at, i], device_id=to_core, device_id_type=MESH))

        @pl.when(chunk == 0)
        def _():
            barrier = pltpu.get_barrier_semaphore()
            pl.semaphore_signal(barrier, inc=1, device_id=to_core, device_id_type=MESH)
            pl.semaphore_wait(barrier, 1)
    else:
        rate_scr, state_scr, sk_scr, u_scr, y_scr = rest

    @pl.when(chunk == 0)
    def _():
        rate_scr[...] = jnp.exp(alog_ref[...]) * (-LOG2E)
        state_scr[...] = jnp.zeros_like(state_scr)

    if joined:
        ranks, first = pre_ref[...], mode_ref[...]
        ranks_0 = (ranks.astype(jnp.float32) * first).astype(ranks.dtype)
        pre = (jnp.dot(ranks_0, dt_ref[0], preferred_element_type=jnp.float32)
               + jnp.dot(ranks - ranks_0, dt_ref[1], preferred_element_type=jnp.float32))
        pre = pre + (first * dt_bias_ref[0:1, :] + (1.0 - first) * dt_bias_ref[1:2, :])
        pre_out[...] = pre
    else:
        pre = pre_ref[...]
    step = softplus(pre)
    act = act_ref[...].astype(jnp.float32)
    spread_rows(u_scr, step * act, groups)
    spread_rows(sk_scr, jnp.where(keep_ref[...] > 0.0, step, BIG), groups)
    start_ref[0] = state_scr[...]

    def one(t, held):
        at = pl.multiple_of(t * groups, groups)
        sk = sk_scr[pl.ds(at, groups), :]
        u = u_scr[pl.ds(at, groups), :]
        y = jnp.zeros_like(u)
        new = []
        for n in range(states):
            h = jnp.exp2(sk * rate_scr[n]) * held[n] + u * bc_ref[t, n]
            h_ref[t, n] = h
            y = y + h * bc_ref[t, states + n]
            new.append(h)
        y_scr[pl.ds(at, groups), :] = y
        return tuple(new)

    last = lax.fori_loop(0, rows, one, tuple(state_scr[n] for n in range(states)), unroll=unroll)
    for n in range(states):
        state_scr[n] = last[n]
    mixed_out = gather_rows(y_scr, rows, groups) + skip_ref[...] * act
    z = z_ref[...].astype(jnp.float32)
    gg = gg_ref[...].astype(jnp.float32)
    sig = jax.nn.sigmoid(z)
    silu = z * sig
    gated = mixed_out * silu
    gate_grad = (gg * mixed_out * sig * (1.0 + z * (1.0 - sig))).astype(ggrad_ref.dtype)
    mixed_ref[...] = gg * silu
    if joined:
        channels = gated.shape[1]
        first = mode_ref[...]
        split_ref[:, 0:channels] = (gated * first).astype(split_ref.dtype)
        split_ref[:, channels:2 * channels] = (gated * (1.0 - first)).astype(split_ref.dtype)
        at = pl.ds(pl.multiple_of(chunk * rows, rows), rows)
        gated_all[at, :] = gated.astype(gated_ref.dtype)
        ggrad_all[at, :] = gate_grad
        for k in range(count):
            @pl.when(chunk == k)
            def _():
                for i in range(2):
                    for copy in pair_copies(k, i):
                        copy.start()

        @pl.when(chunk == count - 1)
        def _():
            for k in range(count):
                for i in range(2):
                    for copy in pair_copies(k, i):
                        copy.wait()
    else:
        gated_ref[...] = gated.astype(gated_ref.dtype)
        ggrad_ref[...] = gate_grad


def scan_forward(bc, pre, act, z, gg, keep, a_log3, skip, mode, joined, dt=(), rows=64, unroll=8):
    tokens, channels = act.shape
    groups = channels // LANES
    states = a_log3.shape[0]
    count = tokens // rows
    wide = pl.BlockSpec((rows, channels), lambda i: (i, 0))
    thin = pl.BlockSpec((rows, 1), lambda i: (i, 0))
    whole3 = pl.BlockSpec((states, groups, LANES), lambda i: (0, 0, 0))
    low, f32 = jnp.bfloat16, jnp.float32
    long = lambda: pltpu.VMEM((rows * groups, LANES), f32)
    small = lambda: pltpu.VMEM((states, groups, LANES), f32)
    anywhere = pl.BlockSpec(memory_space=pl.ANY)
    tall = 2 * tokens if joined else tokens
    settings = dict(collective_id=5, has_side_effects=True) if joined else {}
    return pl.pallas_call(
        functools.partial(scan_forward_kernel, states, groups, rows, unroll, count, joined),
        grid=(count,),
        in_specs=[
            pl.BlockSpec((rows, 2 * states), lambda i: (i, 0), memory_space=pltpu.SMEM),
            pl.BlockSpec((rows, pre.shape[1]), lambda i: (i, 0)), wide, wide, wide, thin, whole3,
            pl.BlockSpec((1, channels), lambda i: (0, 0)), thin,
        ] + [pl.BlockSpec(v.shape, lambda i, n=v.ndim: (0,) * n) for v in dt],
        out_specs=[
            anywhere if joined else wide, anywhere if joined else wide, wide,
            pl.BlockSpec((rows, states, groups, LANES), lambda i: (i, 0, 0, 0)),
            pl.BlockSpec((1, states, groups, LANES), lambda i: (i, 0, 0, 0)),
        ] + ([wide, pl.BlockSpec((rows, 2 * channels), lambda i: (i, 0))] if joined else []),
        out_shape=[
            jax.ShapeDtypeStruct((tall, channels), low),
            jax.ShapeDtypeStruct((tall, channels), low),
            jax.ShapeDtypeStruct((tokens, channels), f32),
            jax.ShapeDtypeStruct((tokens, states, groups, LANES), f32),
            jax.ShapeDtypeStruct((count, states, groups, LANES), f32),
        ] + ([jax.ShapeDtypeStruct((tokens, channels), f32), jax.ShapeDtypeStruct((tokens, 2 * channels), low)] if joined else []),
        scratch_shapes=[small(), small(), long(), long(), long()] + ([
            pltpu.VMEM((tokens, channels), low), pltpu.VMEM((tokens, channels), low),
            pltpu.SemaphoreType.DMA((count, 2)), pltpu.SemaphoreType.DMA((count, 2)), pltpu.SemaphoreType.DMA((count, 2)),
        ] if joined else []),
        compiler_params=pltpu.CompilerParams(vmem_limit_bytes=60 * 1024 * 1024, **settings),
        name="scan_forward",
    )(bc, pre, act, z, gg, keep, a_log3, skip, mode, *dt)


MESH = pl.DeviceIdType.MESH
DMA = pltpu.SemaphoreType.DMA


def add_rows(target, left, right, rows, slab):
    def body(i, nothing):
        at = pl.ds(pl.multiple_of(i * slab, slab), slab)
        target[at, :] = (left[at, :].astype(jnp.float32) + right[at, :].astype(jnp.float32)).astype(jnp.bfloat16)
        return nothing
    lax.fori_loop(0, rows // slab, body, 0)


def place():
    dp = lax.axis_index("dp")
    x, y, core = (dp // 2) % 2, dp // 4, dp % 2
    return x, y, {"dp": dp + 2 - 4 * x}, {"dp": dp + 4 - 8 * y}, {"dp": dp + 1 - 2 * core}


def greet():
    z = lax.axis_index("tensor")
    barrier = pltpu.get_barrier_semaphore()
    for target in place()[2:]:
        pl.semaphore_signal(barrier, inc=1, device_id=target, device_id_type=MESH)

    @pl.when(z > 0)
    def _():
        pl.semaphore_signal(barrier, inc=1, device_id={"tensor": z - 1}, device_id_type=MESH)

    @pl.when(z < 3)
    def _():
        pl.semaphore_signal(barrier, inc=1, device_id={"tensor": z + 1}, device_id_type=MESH)

    @pl.when((z > 0) & (z < 3))
    def _():
        pl.semaphore_wait(barrier, 5)

    @pl.when((z == 0) | (z == 3))
    def _():
        pl.semaphore_wait(barrier, 4)


class Exchange:
    def __init__(self, prod, out, held, half_buf, quarter_buf, sems, summed=None):
        self.summed = summed
        self.prod, self.held, self.half_buf, self.quarter_buf = prod, held, half_buf, quarter_buf
        self.out, self.own = out
        (self.half_send, self.half_recv, self.quarter_send, self.quarter_recv,
         self.share_send, self.share_recv, self.core_send, self.core_recv, self.local) = sems
        x, y, self.to_x, self.to_y, self.to_core = place()
        self.firsts, self.seconds = (x, y), (y, x)
        self.ways = ((self.to_x, self.to_y), (self.to_y, self.to_x))
        self.side = half_buf.shape[2]

    @staticmethod
    def scratch(side, depth):
        low = jnp.bfloat16
        return [pltpu.VMEM((2, 2, side, depth), low), pltpu.VMEM((2, 2, side, depth), low), pltpu.VMEM((2, side, depth), low),
                DMA((2, 2)), DMA((2, 2)), DMA((2,)), DMA((2,)), DMA((2, 4)), DMA((2, 4)), DMA((2, 4)), DMA((2, 4)), DMA((2, 3))]

    def rows(self, mode, k, mine):
        first, second = self.firsts[mode], self.seconds[mode]
        half = first if mine else 1 - first
        quarter = 1 - second if k == 0 else second
        return pl.ds(pl.multiple_of((half * 2 + quarter) * self.side, self.side), self.side)

    def half_copy(self, mode, k):
        return pltpu.make_async_remote_copy(
            src_ref=self.prod[mode].at[self.rows(mode, k, False)], dst_ref=self.half_buf.at[mode, k],
            send_sem=self.half_send.at[mode, k], recv_sem=self.half_recv.at[mode, k],
            device_id=self.ways[mode][0], device_id_type=MESH)

    def keep_copy(self, mode, k):
        return pltpu.make_async_copy(self.prod[mode].at[self.rows(mode, k, True)], self.held.at[mode, k], self.local.at[mode, k])

    def quarter_copy(self, mode):
        return pltpu.make_async_remote_copy(
            src_ref=self.half_buf.at[mode, 0], dst_ref=self.quarter_buf.at[mode],
            send_sem=self.quarter_send.at[mode], recv_sem=self.quarter_recv.at[mode],
            device_id=self.ways[mode][1], device_id_type=MESH)

    def share_copy(self, mode, k):
        own = self.held.at[mode, 1]
        if k == 3:
            source, way = (self.out.at[mode, 0, 1], self.to_x) if mode == 0 else (self.out.at[mode, 0, 2], self.to_y)
        else:
            source, way = own, self.to_y if k == 1 else self.to_x
        return pltpu.make_async_remote_copy(
            src_ref=source, dst_ref=self.out.at[mode, 0, k], send_sem=self.share_send.at[mode, k],
            recv_sem=self.share_recv.at[mode, k], device_id=way, device_id_type=MESH)

    def core_copy(self, mode, k):
        return pltpu.make_async_remote_copy(
            src_ref=self.held.at[mode, 1] if k == 0 else self.out.at[mode, 0, k], dst_ref=self.out.at[mode, 1, k],
            send_sem=self.core_send.at[mode, k], recv_sem=self.core_recv.at[mode, k],
            device_id=self.to_core, device_id_type=MESH)

    def out_copy(self, mode):
        return pltpu.make_async_copy(self.held.at[mode, 1], self.own.at[mode], self.local.at[mode, 2])

    def start_shares(self, mode):
        for k in ((1, 2) if mode == 0 else (2, 1)):
            self.share_copy(mode, k).start()
        self.core_copy(mode, 0).start()
        self.out_copy(mode).start()

    def event(self, number):
        if number == 0:
            for k in range(2):
                for mode in range(2):
                    self.half_copy(mode, k).start()
                    self.keep_copy(mode, k).start()
        elif number == 1:
            for mode in range(2):
                self.keep_copy(mode, 0).wait()
                self.half_copy(mode, 0).wait_recv()
                add_rows(self.half_buf.at[mode, 0], self.half_buf.at[mode, 0], self.held.at[mode, 0], self.side, 32)
                self.quarter_copy(mode).start()
        elif number == 2:
            for mode in range(2):
                self.keep_copy(mode, 1).wait()
                self.half_copy(mode, 1).wait_recv()
                add_rows(self.half_buf.at[mode, 1], self.half_buf.at[mode, 1], self.held.at[mode, 1], self.side, 32)
        elif number == 3:
            for mode in range(2):
                self.quarter_copy(mode).wait_recv()
                add_rows(self.held.at[mode, 1], self.half_buf.at[mode, 1], self.quarter_buf.at[mode], self.side, 32)
                self.start_shares(mode)
        elif number == 4:
            for mode in range(2):
                k = 1 if mode == 0 else 2
                self.share_copy(mode, k).wait_recv()
                self.share_copy(mode, 3).start()
                self.core_copy(mode, k).start()
        elif number == 5:
            for mode in range(2):
                k = 2 if mode == 0 else 1
                self.share_copy(mode, k).wait_recv()
                self.core_copy(mode, k).start()
        elif number == 6:
            for mode in range(2):
                self.share_copy(mode, 3).wait_recv()
                self.core_copy(mode, 3).start()
        elif number == 8:
            for mode in range(2):
                pltpu.make_async_copy(self.prod.at[mode], self.held.at[mode, 1], self.local.at[mode, 1]).start()
        elif number == 9:
            for mode in range(2):
                pltpu.make_async_copy(self.prod.at[mode], self.held.at[mode, 1], self.local.at[mode, 1]).wait()
                self.start_shares(mode)
        elif number == 7:
            for mode in range(2):
                if self.summed is None:
                    for k in range(2):
                        self.half_copy(mode, k).wait_send()
                    self.quarter_copy(mode).wait_send()
                for k in range(1, 4):
                    self.share_copy(mode, k).wait_send()
                for k in range(4):
                    self.core_copy(mode, k).wait_send()
                    self.core_copy(mode, k).wait_recv()
                self.out_copy(mode).wait()


class Share:
    def __init__(self, own, out, sems):
        self.own, self.out = own, out
        self.share_send, self.share_recv, self.core_send, self.core_recv = sems
        _, _, self.to_x, self.to_y, self.to_core = place()

    @staticmethod
    def scratch():
        return [DMA((2, 4)), DMA((2, 4)), DMA((2, 4)), DMA((2, 4))]

    def share_copy(self, mode, k):
        if k == 3:
            source, way = (self.out.at[mode, 0, 1], self.to_x) if mode == 0 else (self.out.at[mode, 0, 2], self.to_y)
        else:
            source, way = self.own.at[mode], self.to_y if k == 1 else self.to_x
        return pltpu.make_async_remote_copy(
            src_ref=source, dst_ref=self.out.at[mode, 0, k], send_sem=self.share_send.at[mode, k],
            recv_sem=self.share_recv.at[mode, k], device_id=way, device_id_type=MESH)

    def core_copy(self, mode, k):
        return pltpu.make_async_remote_copy(
            src_ref=self.own.at[mode] if k == 0 else self.out.at[mode, 0, k], dst_ref=self.out.at[mode, 1, k],
            send_sem=self.core_send.at[mode, k], recv_sem=self.core_recv.at[mode, k],
            device_id=self.to_core, device_id_type=MESH)

    def event(self, number):
        for mode in range(2):
            early, late = (1, 2) if mode == 0 else (2, 1)
            if number == 0:
                self.share_copy(mode, early).start()
                self.share_copy(mode, late).start()
                self.core_copy(mode, 0).start()
            elif number == 1:
                self.share_copy(mode, early).wait_recv()
                self.share_copy(mode, 3).start()
                self.core_copy(mode, early).start()
            elif number == 2:
                self.share_copy(mode, late).wait_recv()
                self.core_copy(mode, late).start()
            elif number == 3:
                self.share_copy(mode, 3).wait_recv()
                self.core_copy(mode, 3).start()
            else:
                for k in range(1, 4):
                    self.share_copy(mode, k).wait_send()
                for k in range(4):
                    self.core_copy(mode, k).wait_send()
                    self.core_copy(mode, k).wait_recv()


class Reduce(Exchange):
    def __init__(self, prod, own, held, half_buf, quarter_buf, sems):
        half_send, half_recv, quarter_send, quarter_recv, keep = sems
        super().__init__(prod, (None, own), held, half_buf, quarter_buf,
                         (half_send, half_recv, quarter_send, quarter_recv, None, None, None, None, keep))

    @staticmethod
    def scratch(side, depth):
        low = jnp.bfloat16
        return [pltpu.VMEM((2, 2, side, depth), low), pltpu.VMEM((2, 2, side, depth), low), pltpu.VMEM((2, side, depth), low),
                DMA((2, 2)), DMA((2, 2)), DMA((2,)), DMA((2,)), DMA((2, 3))]

    def last(self):
        for mode in range(2):
            self.quarter_copy(mode).wait_recv()
            add_rows(self.held.at[mode, 1], self.half_buf.at[mode, 1], self.quarter_buf.at[mode], self.side, 32)
            pltpu.make_async_copy(self.held.at[mode, 1], self.own.at[mode], self.local.at[mode, 2]).start()

    def done(self):
        for mode in range(2):
            for k in range(2):
                self.half_copy(mode, k).wait_send()
            self.quarter_copy(mode).wait_send()
            pltpu.make_async_copy(self.held.at[mode, 1], self.own.at[mode], self.local.at[mode, 2]).wait()


class LineReduce:
    def __init__(self, part, own, acc, red, sems):
        red_send, red_recv, local = sems
        self.line = LineSum(part, own, acc, red, (red_send, red_recv, None, None, local))

    @staticmethod
    def scratch(pieces, rows, width):
        low = jnp.bfloat16
        return [pltpu.VMEM((2, pieces, rows, width), low), pltpu.VMEM((2, pieces, rows, width), low),
                DMA((2, pieces)), DMA((2, pieces)), DMA((2,))]

    def step(self, c, half):
        line = self.line
        begins, ends = line.place_of(half)

        @pl.when(jnp.logical_not(begins))
        def _():
            line.red_copy(half, c).wait_recv()
            add_rows(line.acc.at[half, c], line.acc.at[half, c], line.red.at[half, c], line.rows, 16)

            @pl.when(jnp.logical_not(ends))
            def _():
                line.red_copy(half, c).start()

    def turn(self, turn):
        line = self.line
        at_end = (line.z == 0) | (line.z == 3)
        if 0 <= turn - 2 < line.pieces:
            self.step(turn - 2, line.near)
        if 0 <= turn - 4 < line.pieces:
            @pl.when(jnp.logical_not(at_end))
            def _():
                self.step(turn - 4, 1 - line.near)
        if 0 <= turn - 6 < line.pieces:
            @pl.when(at_end)
            def _():
                self.step(turn - 6, 1 - line.near)

    def done(self):
        line = self.line
        for half in range(2):
            begins, ends = line.place_of(half)

            @pl.when(ends)
            def _():
                line.own(half).start()
                line.own(half).wait()

            @pl.when(jnp.logical_not(ends))
            def _():
                for c in range(line.pieces):
                    line.red_copy(half, c).wait_send()


class LineBack:
    def __init__(self, res, sems):
        self.res = res
        self.send, self.recv = sems
        self.z = lax.axis_index("tensor")
        self.near = jnp.where(self.z < 2, 1, 0)
        self.pieces = res.shape[1]

    @staticmethod
    def scratch(pieces):
        return [DMA((2, pieces)), DMA((2, pieces))]

    def place_of(self, half):
        along = jnp.where(half == 0, 3 - self.z, self.z)
        return along == 0, along == 3

    def copy(self, half, c):
        return pltpu.make_async_remote_copy(
            src_ref=self.res.at[half, c], dst_ref=self.res.at[half, c], send_sem=self.send.at[half, c],
            recv_sem=self.recv.at[half, c], device_id={"tensor": self.z - 2 * half + 1}, device_id_type=MESH)

    def begin(self, pieces):
        for half in range(2):
            _, ends = self.place_of(half)

            @pl.when(ends)
            def _():
                for c in pieces:
                    self.copy(half, c).start()

    def step(self, c, half):
        begins, ends = self.place_of(half)

        @pl.when(jnp.logical_not(ends | begins))
        def _():
            self.copy(half, c).wait_recv()
            self.copy(half, c).start()

    def some(self, pieces, far):
        for c in pieces:
            self.step(c, 1 - self.near if far else self.near)

    def done(self):
        for half in range(2):
            begins, ends = self.place_of(half)

            @pl.when(begins)
            def _():
                for c in range(self.pieces):
                    self.copy(half, c).wait_recv()

            @pl.when(jnp.logical_not(begins))
            def _():
                for c in range(self.pieces):
                    self.copy(half, c).wait_send()


AHEAD = 4


class LineSum:
    def __init__(self, part, res, acc, red, sems):
        self.part, self.res, self.acc, self.red = part, res, acc, red
        self.red_send, self.red_recv, self.back_send, self.back_recv, self.local = sems
        self.z = lax.axis_index("tensor")
        self.near = jnp.where(self.z < 2, 1, 0)
        self.pieces, self.rows = acc.shape[1], acc.shape[2]
        self.turns = self.pieces + 8

    @staticmethod
    def scratch(pieces, rows, width):
        low = jnp.bfloat16
        return [pltpu.VMEM((2, pieces, rows, width), low), pltpu.VMEM((2, pieces, rows, width), low),
                DMA((2, pieces)), DMA((2, pieces)), DMA((2, pieces)), DMA((2, pieces)), DMA((2,))]

    def place_of(self, half):
        along = jnp.where(half == 0, 3 - self.z, self.z)
        return along == 0, along == 3

    def red_copy(self, half, c):
        return pltpu.make_async_remote_copy(
            src_ref=self.acc.at[half, c], dst_ref=self.red.at[half, c], send_sem=self.red_send.at[half, c],
            recv_sem=self.red_recv.at[half, c], device_id={"tensor": self.z + 2 * half - 1}, device_id_type=MESH)

    def back_copy(self, half, c, source):
        return pltpu.make_async_remote_copy(
            src_ref=source, dst_ref=self.res.at[half, c], send_sem=self.back_send.at[half, c],
            recv_sem=self.back_recv.at[half, c], device_id={"tensor": self.z - 2 * half + 1}, device_id_type=MESH)

    def load(self):
        return pltpu.make_async_copy(self.part, self.acc, self.local.at[0])

    def own(self, half):
        return pltpu.make_async_copy(self.acc.at[half], self.res.at[half], self.local.at[1])

    def begin(self, pieces):
        for half in range(2):
            begins, _ = self.place_of(half)

            @pl.when(begins)
            def _():
                for c in pieces:
                    self.red_copy(half, c).start()

    def reduce_step(self, c, half):
        begins, ends = self.place_of(half)

        @pl.when(jnp.logical_not(begins))
        def _():
            self.red_copy(half, c).wait_recv()
            add_rows(self.acc.at[half, c], self.acc.at[half, c], self.red.at[half, c], self.rows, 16)

            @pl.when(ends)
            def _():
                self.back_copy(half, c, self.acc.at[half, c]).start()

            @pl.when(jnp.logical_not(ends))
            def _():
                self.red_copy(half, c).start()

    def back_step(self, c, half):
        begins, ends = self.place_of(half)

        @pl.when(jnp.logical_not(ends | begins))
        def _():
            self.back_copy(half, c, self.res.at[half, c]).wait_recv()
            self.back_copy(half, c, self.res.at[half, c]).start()

    def turn(self, turn):
        near, far = self.near, 1 - self.near
        if turn + AHEAD < self.pieces:
            self.begin((turn + AHEAD,))
        if turn < self.pieces:
            self.reduce_step(turn, near)
        if 1 <= turn <= self.pieces:
            self.reduce_step(turn - 1, far)
        if 0 <= turn - 6 < self.pieces:
            self.back_step(turn - 6, far)
        if 0 <= turn - 8 < self.pieces:
            self.back_step(turn - 8, near)

    def finish(self):
        for half in range(2):
            begins, ends = self.place_of(half)

            @pl.when(ends)
            def _():
                self.own(half).start()
                self.own(half).wait()

            @pl.when(begins)
            def _():
                for c in range(self.pieces):
                    self.back_copy(half, c, self.res.at[half, c]).wait_recv()

            @pl.when(jnp.logical_not(ends))
            def _():
                for c in range(self.pieces):
                    self.red_copy(half, c).wait_send()

            @pl.when(jnp.logical_not(begins))
            def _():
                for c in range(self.pieces):
                    self.back_copy(half, c, self.res.at[half, c]).wait_send()


def tail_kernel(count, *refs):
    prods, part = refs[:count], refs[count]
    outs, res, owns = refs[count + 1:2 * count + 1], refs[2 * count + 1], refs[2 * count + 2:3 * count + 2]
    scr = refs[3 * count + 2:]
    line = LineSum(part, res, scr[0], scr[1], scr[2:7])
    swaps = [Exchange([prods[i].at[0], prods[i].at[1]], (outs[i], owns[i]), *scr[7 + 12 * i:10 + 12 * i], scr[10 + 12 * i:19 + 12 * i]) for i in range(count)]
    line.load().start()
    greet()
    swaps[0].event(0)
    line.load().wait()
    line.begin(range(AHEAD))
    last = line.turns
    plan = {4: [(0, 1)], 7: [(0, 2)], 10: [(0, 3)], 12: [(0, 4)], 15: [(0, 5)], 19: [(0, 6)]}
    for turn in range(last):
        line.turn(turn)
        for which, number in plan.get(turn, []):
            swaps[which].event(number)
    for swapped in swaps:
        swapped.event(7)
    line.finish()


def tail_exchange(products, normed_part, pieces=12):
    count = len(products)
    side, depth = products[0].shape[1] // 4, products[0].shape[2]
    tokens, width = normed_part.shape
    part = normed_part.reshape(2, pieces, tokens // 2 // pieces, width)
    low = jnp.bfloat16
    anywhere = pl.BlockSpec(memory_space=pl.ANY)
    scratch = LineSum.scratch(*part.shape[1:])
    for _ in products:
        scratch = scratch + Exchange.scratch(side, depth)
    outs = pl.pallas_call(
        functools.partial(tail_kernel, count),
        in_specs=[anywhere] * (count + 1),
        out_specs=[anywhere] * (2 * count + 1),
        out_shape=[jax.ShapeDtypeStruct((2, 2, 4, side, depth), low)] * count + [jax.ShapeDtypeStruct(part.shape, low)]
        + [jax.ShapeDtypeStruct((2, side, depth), low)] * count,
        scratch_shapes=scratch,
        cost_estimate=pl.CostEstimate(flops=100_000_000, bytes_accessed=300_000_000, transcendentals=0),
        compiler_params=pltpu.CompilerParams(collective_id=1, has_side_effects=True, vmem_limit_bytes=60 * 1024 * 1024),
        name="tail_exchange",
    )(*products, part)
    return outs[:count], outs[count + 1:], outs[count].reshape(tokens, width)


NT = (((1,), (1,)), ((), ()))
TN = (((0,), (0,)), ((), ()))


def dot_f32(left, right, dims=(((1,), (0,)), ((), ()))):
    return lax.dot_general(left, right, dims, preferred_element_type=jnp.float32)


def widened(column_block, width):
    return jnp.concatenate([column_block] * (width // LANES), axis=1)


def middle_kernel(pre_grad, act_part, coeff, conv_sum, inner_x, act_b, rank_b, dt_proj, x_wide, conv_w, docs, modes,
                  gate_grads, normed_t, inv, extra, hidden, in_gate, in_inner, out_own, gate_own, z_own,
                  rows_out, normed_out, inner_prod, out_shared, gate_shared, z_res,
                  w_buf, mask_buf, pair_buf, conv_buf, stage, stage_n, hid_buf, proj_buf, proj_recv, proj_fin, gain_buf, gain_recv,
                  red_send, red_recv, all_send, all_recv, core_sems, gain_send, gain_recv_sem, w_sems, stage_sems, n_sems, hid_sems,
                  *share_sems):
    tokens, channels = pre_grad.shape
    low = jnp.bfloat16
    rank_dim = dt_proj.shape[1]
    z = lax.axis_index("tensor")
    x, y, to_x, to_y, to_core = place()
    share = tokens // 4
    outs = Share(out_own, out_shared, share_sems[0:4])
    gate = Share(gate_own, gate_shared, share_sems[4:8])
    back = LineBack(z_res, share_sems[8:10])
    width = hidden.shape[1]
    slices = width // w_buf.shape[2]
    cut = w_buf.shape[2]

    def z_at(off):
        return {"tensor": (z + off) % 4}

    barrier = pltpu.get_barrier_semaphore()
    for target in (to_x, to_y, to_core, z_at(1), z_at(2), z_at(3)):
        pl.semaphore_signal(barrier, inc=1, device_id=target, device_id_type=MESH)
    pl.semaphore_wait(barrier, 6)

    def weight_copies(i):
        slot = i % 2
        found = []
        for j, source in enumerate((in_gate, in_inner)):
            for m in range(2):
                found.append(pltpu.make_async_copy(source.at[m, pl.ds(i * cut, cut)], w_buf.at[slot, 2 * j + m],
                                                   w_sems.at[slot, 2 * j + m]))
        found.append(pltpu.make_async_copy(hidden.at[:, pl.ds(i * cut, cut)], hid_buf.at[slot], hid_sems.at[slot]))
        return found

    for i in range(2):
        for copy in weight_copies(i):
            copy.start()

    block = 128

    def proj_block(i, nothing):
        at = pl.ds(pl.multiple_of(i * block, block), block)
        grad = pre_grad[at, :]
        part = dot_f32(grad * widened(modes[0, at, :], channels), dt_proj[0], NT)
        part = part + dot_f32(grad * widened(modes[1, at, :], channels), dt_proj[1], NT)
        proj_buf[at, 0:rank_dim] = part.astype(low)
        proj_buf[at, rank_dim:rank_dim + LANES] = coeff[at, :].astype(low)
        return nothing

    lax.fori_loop(0, tokens // block, proj_block, 0)

    def red_copy(off):
        return pltpu.make_async_remote_copy(
            src_ref=proj_buf.at[pl.ds(pl.multiple_of(((z + off) % 4) * share, share), share)], dst_ref=proj_recv.at[off - 1],
            send_sem=red_send.at[off - 1], recv_sem=red_recv.at[off - 1], device_id=z_at(off), device_id_type=MESH)

    for off in (1, 2, 3):
        red_copy(off).start()
    outs.event(0)

    def product(pair, target, number):
        pair_tokens = pair.shape[0]
        tall = stage.shape[1]
        turns = normed_t.shape[0] // tall
        for m in range(2):
            def mask_rows(i, nothing):
                at = pl.ds(pl.multiple_of(i * block, block), block)
                mask_buf[at, :] = pair[at, :] * widened(modes[m, at, :], channels)
                return nothing
            lax.fori_loop(0, pair_tokens // block, mask_rows, 0)
            for j in range(turns):
                slot = (m * turns + j) % 2
                copy = pltpu.make_async_copy(stage.at[slot], target.at[m, pl.ds(j * tall, tall)], stage_sems.at[slot])
                if m * turns + j >= 2:
                    copy.wait()
                stage[slot] = dot_f32(normed_t[pl.ds(j * tall, tall), :], mask_buf[...]).astype(low)
                copy.start()
        for slot in range(2):
            pltpu.make_async_copy(stage.at[slot], target.at[0, pl.ds(0, tall)], stage_sems.at[slot]).wait()

    for off in (1, 2, 3):
        red_copy(off).wait_recv()
    mine = pl.ds(pl.multiple_of(z * share, share), share)
    total = proj_buf[mine, :].astype(jnp.float32)
    for k in range(3):
        total = total + proj_recv[k].astype(jnp.float32)
    proj_fin[mine, :] = total.astype(low)

    def all_copy(off):
        return pltpu.make_async_remote_copy(
            src_ref=proj_fin.at[mine], dst_ref=proj_fin.at[mine], send_sem=all_send.at[off - 1],
            recv_sem=all_recv.at[off - 1], device_id=z_at(off), device_id_type=MESH)

    for off in (1, 2, 3):
        all_copy(off).start()
    span = x_wide.shape[1] - 96
    mode_rows = span + rank_dim
    for m in range(2):
        ranks = rank_b[...] * modes[m, pl.ds(0, tokens), :]
        rows_out[pl.ds(m * mode_rows + span, rank_dim), :] = dot_f32(ranks, pre_grad[...], TN).astype(low)
    def dt_sums(i, carried):
        at = pl.ds(pl.multiple_of(i * block, block), block)
        grad = pre_grad[at, :].astype(jnp.float32)
        first = jnp.sum(grad * widened(modes[0, at, :].astype(jnp.float32), channels), axis=0, keepdims=True)
        return carried[0] + first, carried[1] + jnp.sum(grad, axis=0, keepdims=True) - first

    none_row = jnp.zeros((1, channels), jnp.float32)
    bias0, bias1 = lax.fori_loop(0, tokens // block, dt_sums, (none_row, none_row))
    for off in (1, 2, 3):
        all_copy(off).wait_recv()
    back.begin((0, 1))

    def act_block(i, bias):
        at = pl.ds(pl.multiple_of(i * block, block), block)
        proj = proj_fin[at, :]
        two = proj.shape[1]
        back = dot_f32(proj * widened(modes[0, at, :], two), x_wide[0])
        back = back + dot_f32(proj * widened(modes[1, at, :], two), x_wide[1])
        value = conv_sum[at, :]
        sig = jax.nn.sigmoid(value)
        grad = (act_part[at, :] + back) * sig * (1.0 + value * (1.0 - sig))
        conv_buf[at, :] = grad
        return bias + jnp.sum(grad, axis=0, keepdims=True)

    conv_buf[pl.ds(tokens, 8), :] = jnp.zeros((8, channels), jnp.float32)
    bias = lax.fori_loop(0, tokens // block, act_block, none_row)
    outs.event(1)
    gate.event(0)
    back.some((0,), True)
    back.begin((2,))
    taps = conv_w.shape[0]
    thin = 64

    def conv_block(i, sums):
        base = pl.multiple_of(i * thin, thin)
        grads = conv_buf[pl.ds(base, thin + 8), :]
        doc = docs[pl.ds(base, thin), :]
        inner = inner_x[pl.ds(base, thin), :]
        result = jnp.zeros((thin, channels), jnp.float32)
        new = []
        for offset in range(taps):
            moved = grads[offset:offset + thin, :] * doc[:, offset:offset + 1]
            tap = taps - 1 - offset
            result = result + moved * conv_w[tap:tap + 1, :]
            new.append(sums[offset] + jnp.sum(moved * inner, axis=0, keepdims=True))
        pair_buf[pl.ds(base, thin), :] = result.astype(low)
        return tuple(new)

    sums = lax.fori_loop(0, tokens // thin, conv_block, (none_row,) * taps)

    def core_copy():
        return pltpu.make_async_remote_copy(
            src_ref=pair_buf.at[pl.ds(0, tokens)], dst_ref=pair_buf.at[pl.ds(tokens, tokens)],
            send_sem=core_sems.at[0], recv_sem=core_sems.at[1], device_id=to_core, device_id_type=MESH)

    core_copy().start()
    back.some((1,), True)
    back.begin((3,))

    for i in range(slices):
        slot = i % 2
        for copy in weight_copies(i):
            copy.wait()
        third = tokens // 3
        out_copy = pltpu.make_async_copy(stage_n.at[slot], normed_out.at[:, pl.ds(i * cut, cut)], n_sems.at[slot])
        if i >= 2:
            out_copy.wait()

        def normed_rows(j, gain, slot=slot):
            at = pl.ds(pl.multiple_of(j * third, third), third)
            gate_grad, grad = gate_grads[at, :], pair_buf[at, :]
            zero = dot_f32(gate_grad, w_buf[slot, 0], NT) + dot_f32(grad, w_buf[slot, 2], NT)
            one = dot_f32(gate_grad, w_buf[slot, 1], NT) + dot_f32(grad, w_buf[slot, 3], NT)
            picked = jnp.where(inv[at, 1:2] > 0.5, zero, one)
            stage_n[slot, at, :] = picked.astype(low)
            return gain + jnp.sum(picked * hid_buf[slot, at, :].astype(jnp.float32) * inv[at, 0:1], axis=0, keepdims=True)

        gain = lax.fori_loop(0, 3, normed_rows, jnp.zeros((1, cut), jnp.float32))
        gain_buf[:, pl.ds(i * cut, cut)] = jnp.broadcast_to(gain, (8, cut))
        out_copy.start()
        if i + 2 < slices:
            for copy in weight_copies(i + 2):
                copy.start()
        if i == 0:
            back.some((2,), True)
            back.some((0,), False)
            back.begin((4,))
        elif i == 1:
            back.some((3,), True)
            back.some((1,), False)
            back.begin((5,))
        elif i == 2:
            outs.event(2)
            back.some((4,), True)
            back.some((2,), False)
        elif i == 3:
            back.some((5,), True)
            back.some((3,), False)
    for slot in range(2):
        pltpu.make_async_copy(stage_n.at[slot], normed_out.at[:, pl.ds(0, cut)], n_sems.at[slot]).wait()

    def gain_copy(off):
        return pltpu.make_async_remote_copy(
            src_ref=gain_buf, dst_ref=gain_recv.at[off - 1], send_sem=gain_send.at[off - 1],
            recv_sem=gain_recv_sem.at[off - 1], device_id=z_at(off), device_id_type=MESH)

    for off in (1, 2, 3):
        gain_copy(off).start()
    core_copy().wait_recv()
    product(pair_buf, inner_prod, 1)
    back.some((4, 5), False)
    gate.event(1)
    outs.event(3)
    for m in range(2):
        proj = proj_fin[...] * widened(modes[m, pl.ds(0, tokens), :], proj_fin.shape[1])
        rows_out[pl.ds(m * mode_rows, span), :] = dot_f32(proj, act_b[...], TN)[:span].astype(low)
    for off in (1, 2, 3):
        gain_copy(off).wait_recv()
    gain = gain_buf[0:1, :] + gain_recv[0, 0:1, :] + gain_recv[1, 0:1, :] + gain_recv[2, 0:1, :]
    gains = [gain[:, k * channels:(k + 1) * channels] for k in range(width // channels)]
    tail_rows = list(sums[::-1]) + [bias, bias0, bias1, extra[...]] + gains
    used = taps + 3 + extra.shape[0] + len(gains)
    tail_rows.append(jnp.zeros((32 - used, channels), jnp.float32))
    rows_out[pl.ds(2 * mode_rows, 32), :] = jnp.concatenate(tail_rows, axis=0).astype(low)
    gate.event(2)
    gate.event(3)
    outs.event(4)
    gate.event(4)
    back.done()
    for off in (1, 2, 3):
        red_copy(off).wait_send()
        all_copy(off).wait_send()
        gain_copy(off).wait_send()
    core_copy().wait_send()


def middle(pre_grad, act_part, coeff, conv_sum, inner_x, act_b, rank_b, dt_proj, x_wide, conv_w, docs, modes,
           gate_grads, normed_t, inv, extra, hidden, in_gate, in_inner, out_own, gate_own, z_own):
    tokens, channels = pre_grad.shape
    width = hidden.shape[1]
    low = jnp.bfloat16
    side = normed_t.shape[0] // 4
    cut = 512
    mode_rows = x_wide.shape[1] - 96 + dt_proj.shape[1]
    vmem, anywhere = pl.BlockSpec(memory_space=pltpu.VMEM), pl.BlockSpec(memory_space=pl.ANY)
    return pl.pallas_call(
        middle_kernel,
        in_specs=[vmem] * 16 + [anywhere] * 6,
        out_specs=[vmem] + [anywhere] * 5,
        out_shape=[
            jax.ShapeDtypeStruct((2 * mode_rows + 32, channels), low),
            jax.ShapeDtypeStruct((tokens, width), low),
            jax.ShapeDtypeStruct((2, 4 * side, channels), low),
            jax.ShapeDtypeStruct((2, 2, 4) + out_own.shape[1:], low),
            jax.ShapeDtypeStruct((2, 2, 4) + gate_own.shape[1:], low),
            jax.ShapeDtypeStruct(z_own.shape, low),
        ],
        scratch_shapes=[
            pltpu.VMEM((2, 4, cut, channels), low),
            pltpu.VMEM((2 * tokens, channels), low),
            pltpu.VMEM((2 * tokens, channels), low),
            pltpu.VMEM((tokens + 8, channels), jnp.float32),
            pltpu.VMEM((2, 2 * side, channels), low),
            pltpu.VMEM((2, tokens, cut), low),
            pltpu.VMEM((2, tokens, cut), low),
            pltpu.VMEM((tokens, 2 * LANES), low),
            pltpu.VMEM((3, tokens // 4, 2 * LANES), low),
            pltpu.VMEM((tokens, 2 * LANES), low),
            pltpu.VMEM((8, width), jnp.float32),
            pltpu.VMEM((3, 8, width), jnp.float32),
            DMA((3,)), DMA((3,)), DMA((3,)), DMA((3,)), DMA((2,)), DMA((3,)), DMA((3,)),
            DMA((2, 4)), DMA((2,)), DMA((2,)), DMA((2,)),
        ] + Share.scratch() + Share.scratch() + LineBack.scratch(z_own.shape[1]),
        input_output_aliases={21: 5},
        cost_estimate=pl.CostEstimate(flops=27_000_000_000, bytes_accessed=60_000_000, transcendentals=1_000_000),
        compiler_params=pltpu.CompilerParams(collective_id=3, has_side_effects=True, vmem_limit_bytes=61 * 1024 * 1024),
        name="middle",
    )(pre_grad, act_part, coeff, conv_sum, inner_x, act_b, rank_b, dt_proj, x_wide, conv_w, docs, modes,
      gate_grads, normed_t, inv, extra, hidden, in_gate, in_inner, out_own, gate_own, z_own)


def split_tail(part, count):
    lane = lax.broadcasted_iota(jnp.int32, part.shape, 1)
    high = part.astype(jnp.bfloat16).astype(jnp.float32)
    rest = pltpu.roll(part - high, count, axis=1)
    return jnp.where(lane < count, high, jnp.where(lane < 2 * count, rest, 0.0)).astype(jnp.bfloat16)


def join_tail(block, count):
    return block + pltpu.roll(block, block.shape[1] - count, axis=1)


def front_kernel(coeffs_wide, hidden, gain, conv_w, conv_b, docs, modes, x_wide, out_grad, view, out_proj,
                 w_inner, w_gate, normed_pair, cotan_pair, modes_pair,
                 inverse, conv_sum_out, inner_x_out, act_out, gate_z_out, gated_grad, rank_out, coeff_out,
                 normed, conv_sum, act_b, gate_z, acc, view_a, view_b, wide, stage_a, stage_b, w_out, proj_buf, proj_recv, proj_fin,
                 view_sems, stage_sems, out_sems, red_send, red_recv, all_send, all_recv, pair_send, pair_recv, pair_local, early_sems):
    tokens, width = hidden.shape
    channels = conv_w.shape[1]
    groups = channels // LANES
    low = jnp.bfloat16
    z = lax.axis_index("tensor")
    share = tokens // 4
    deep = stage_a.shape[1] // 2
    turns = width // deep
    views, stages = (view_a, view_b), (stage_a, stage_b)
    block = 128

    def z_at(off):
        return {"tensor": (z + off) % 4}

    barrier = pltpu.get_barrier_semaphore()
    for off in (1, 2, 3):
        pl.semaphore_signal(barrier, inc=1, device_id=z_at(off), device_id_type=MESH)
    core, to_core = lax.axis_index("dp") % 2, place()[4]
    pl.semaphore_signal(barrier, inc=1, device_id=to_core, device_id_type=MESH)

    def half_of(ref, which):
        return ref.at[:, pl.ds(pl.multiple_of(which * (width // 2), width // 2), width // 2)]

    own_rows, other_rows = pl.ds(0, tokens), pl.ds(tokens, tokens)
    pairs = ((half_of(normed, core), half_of(normed, 1 - core), normed_pair.at[own_rows], normed_pair.at[other_rows]),
             (half_of(out_grad, core), half_of(out_grad, 1 - core), cotan_pair.at[own_rows], cotan_pair.at[other_rows]),
             (modes, modes, modes_pair.at[:, own_rows], modes_pair.at[:, other_rows]))

    def pair_copies(i):
        mine, theirs, here, there = pairs[i]
        return (pltpu.make_async_copy(mine, here, pair_local.at[i]),
                pltpu.make_async_remote_copy(src_ref=theirs, dst_ref=there, send_sem=pair_send.at[i], recv_sem=pair_recv.at[i],
                                             device_id=to_core, device_id_type=MESH))

    def view_copy(i, slot, m):
        tall = deep * 2 * groups
        return pltpu.make_async_copy(view.at[m, pl.ds(pl.multiple_of(i * tall, tall), tall)], views[slot].at[m],
                                     view_sems.at[slot, m])

    def stage_copy(i, slot, half, m):
        target = w_inner if half == 0 else w_gate
        return pltpu.make_async_copy(stages[slot].at[half, pl.ds(m * deep, deep)],
                                     target.at[m, pl.ds(pl.multiple_of(i * deep, deep), deep)], stage_sems.at[slot, half, m])

    def out_copy(m):
        return pltpu.make_async_copy(out_proj.at[m], w_out.at[m], out_sems.at[m])

    for slot in range(2):
        for m in range(2):
            view_copy(slot, slot, m).start()
    for m in range(2):
        out_copy(m).start()

    def norm_block(i, nothing):
        at = pl.ds(pl.multiple_of(i * block, block), block)
        rows = hidden[at, :].astype(jnp.float32)
        scale = lax.rsqrt(jnp.mean(rows * rows, axis=1, keepdims=True) + EPS)
        inverse[at, :] = jnp.broadcast_to(scale, (block, LANES))
        normed[at, :] = (rows * scale * gain[...]).astype(low)
        return nothing

    lax.fori_loop(0, tokens // block, norm_block, 0)
    acc[0:8, :] = jnp.zeros((8, channels), jnp.float32)

    def unpack(slot):
        for m in range(2):
            wide[m] = views[slot][m].astype(jnp.float32)
            for half in range(2):
                stages[slot][half, m * deep:(m + 1) * deep, :] = jnp.concatenate(
                    [wide[m, pl.ds(g * 2 + half, deep, stride=2 * groups), :] for g in range(groups)], axis=1).astype(low)

    def multiply(i, slot, first):
        columns = normed[:, pl.ds(pl.multiple_of(i * deep, deep), deep)]
        left = jnp.concatenate([columns * widened(modes[0], deep), columns * widened(modes[1], deep)], axis=1)
        for half in range(2):
            product = dot_f32(left, stages[slot][half])
            if half == 0:
                acc[8:8 + tokens, :] = product if first else acc[8:8 + tokens, :] + product
            else:
                gate_z[...] = product if first else gate_z[...] + product

    def arrive(i, slot):
        for m in range(2):
            view_copy(i, slot, m).wait()

    def depart(i, slot):
        for m in range(2):
            for half in range(2):
                stage_copy(i, slot, half, m).start()

    def departed(i, slot):
        for m in range(2):
            for half in range(2):
                stage_copy(i, slot, half, m).wait()

    def fetch(i, slot):
        for m in range(2):
            view_copy(i, slot, m).start()

    arrive(0, 0)
    unpack(0)
    depart(0, 0)
    fetch(2, 0)
    arrive(1, 1)
    multiply(0, 0, True)
    unpack(1)
    depart(1, 1)
    fetch(3, 1)

    def looped(j, nothing):
        for slot in range(2):
            i = 2 * j + slot
            departed(i, slot)
            arrive(i + 2, slot)
            multiply(i + 1, 1 - slot, False)
            unpack(slot)
            depart(i + 2, slot)

            @pl.when(i + 4 < turns)
            def _():
                fetch(i + 4, slot)
        return nothing

    lax.fori_loop(0, turns // 2 - 1, looped, 0)
    multiply(turns - 1, 1, False)
    departed(turns - 2, 0)
    departed(turns - 1, 1)

    taps = conv_w.shape[0]

    def conv_block(i, nothing):
        base = pl.multiple_of(i * block, block)
        at = pl.ds(base, block)
        rows = acc[pl.ds(base, block + 8), :]
        doc = docs[at, :]
        total = conv_b[...] + conv_w[taps - 1:taps, :] * rows[8:8 + block, :]
        for offset in range(1, taps):
            total = total + conv_w[taps - 1 - offset:taps - offset, :] * rows[8 - offset:8 - offset + block, :] * doc[:, offset:offset + 1]
        conv_sum[at, :] = total
        active = (total * jax.nn.sigmoid(total)).astype(low)
        act_b[at, :] = active
        part = dot_f32(active * widened(modes[0, at, :], channels), x_wide[0], NT)
        part = part + dot_f32(active * widened(modes[1, at, :], channels), x_wide[1], NT)
        proj_buf[at, 0:LANES] = part[:, :LANES].astype(low)
        proj_buf[at, LANES:2 * LANES] = split_tail(part[:, LANES:], coeffs_wide)
        return nothing

    lax.fori_loop(0, tokens // block, conv_block, 0)

    def red_copy(off):
        return pltpu.make_async_remote_copy(
            src_ref=proj_buf.at[pl.ds(pl.multiple_of(((z + off) % 4) * share, share), share)], dst_ref=proj_recv.at[off - 1],
            send_sem=red_send.at[off - 1], recv_sem=red_recv.at[off - 1], device_id=z_at(off), device_id_type=MESH)

    mine = pl.ds(pl.multiple_of(z * share, share), share)

    def all_copy(off):
        return pltpu.make_async_remote_copy(
            src_ref=proj_fin.at[mine], dst_ref=proj_fin.at[mine], send_sem=all_send.at[off - 1],
            recv_sem=all_recv.at[off - 1], device_id=z_at(off), device_id_type=MESH)

    pl.semaphore_wait(barrier, 4)
    for off in (1, 2, 3):
        red_copy(off).start()
    early = [pltpu.make_async_copy(source, target, early_sems.at[i]) for i, (source, target) in enumerate((
        (conv_sum, conv_sum_out), (acc.at[pl.ds(8, tokens)], inner_x_out), (act_b, act_out), (gate_z, gate_z_out)))]
    for copy in early:
        copy.start()
    for i in range(3):
        for copy in pair_copies(i):
            copy.start()
    third = tokens // 3

    def grad_block(i):
        at = pl.ds(i * third, third)
        zero = dot_f32(out_grad[at, :], w_out[0], NT)
        one = dot_f32(out_grad[at, :], w_out[1], NT)
        gated_grad[at, :] = jnp.where(docs[at, 0:1] > 0.5, zero, one)

    for m in range(2):
        out_copy(m).wait()
    grad_block(0)
    for off in (1, 2, 3):
        red_copy(off).wait_recv()
    total = proj_buf[mine, :].astype(jnp.float32)
    for k in range(3):
        total = total + proj_recv[k].astype(jnp.float32)
    proj_fin[mine, 0:LANES] = total[:, :LANES].astype(low)
    proj_fin[mine, LANES:2 * LANES] = split_tail(join_tail(total[:, LANES:], coeffs_wide), coeffs_wide)
    for off in (1, 2, 3):
        all_copy(off).start()
    grad_block(1)
    grad_block(2)
    for off in (1, 2, 3):
        all_copy(off).wait_recv()
    rank_out[...] = proj_fin[:, 0:LANES]
    coeff_out[...] = join_tail(proj_fin[:, LANES:2 * LANES].astype(jnp.float32), coeffs_wide)
    for off in (1, 2, 3):
        red_copy(off).wait_send()
        all_copy(off).wait_send()
    for i in range(3):
        for copy in pair_copies(i):
            copy.wait()
    for copy in early:
        copy.wait()


def front(hidden, gain, conv_w, conv_b, docs, modes, x_wide, out_grad, in_proj, out_proj, coeffs_wide):
    tokens, width = hidden.shape
    channels = conv_w.shape[1]
    groups = channels // LANES
    low, f32 = jnp.bfloat16, jnp.float32
    view = in_proj.reshape(2, width, 2, groups, LANES).transpose(0, 1, 3, 2, 4).reshape(2, width * 2 * groups, LANES)
    deep = 256
    vmem, anywhere = pl.BlockSpec(memory_space=pltpu.VMEM), pl.BlockSpec(memory_space=pl.ANY)
    shape = jax.ShapeDtypeStruct
    return pl.pallas_call(
        functools.partial(front_kernel, coeffs_wide),
        in_specs=[vmem] * 8 + [anywhere] * 2,
        out_specs=[anywhere] * 5 + [vmem] + [anywhere] * 4 + [vmem] * 3,
        out_shape=[
            shape((2, width, channels), low), shape((2, width, channels), low), shape((2 * tokens, width // 2), low),
            shape((2 * tokens, width // 2), low), shape((2, 2 * tokens, LANES), low),
            shape((tokens, LANES), f32), shape((tokens, channels), f32), shape((tokens, channels), f32),
            shape((tokens, channels), low), shape((tokens, channels), f32), shape((tokens, channels), f32),
            shape((tokens, LANES), low), shape((tokens, LANES), f32),
        ],
        scratch_shapes=[
            pltpu.VMEM((tokens, width), low), pltpu.VMEM((tokens, channels), f32), pltpu.VMEM((tokens, channels), low),
            pltpu.VMEM((tokens, channels), f32),
            pltpu.VMEM((tokens + 8, channels), f32),
            pltpu.VMEM((2, deep * 2 * groups, LANES), low), pltpu.VMEM((2, deep * 2 * groups, LANES), low),
            pltpu.VMEM((2, deep * 2 * groups, LANES), f32),
            pltpu.VMEM((2, 2 * deep, channels), low), pltpu.VMEM((2, 2 * deep, channels), low),
            pltpu.VMEM((2, channels, width), low),
            pltpu.VMEM((tokens, 2 * LANES), low),
            pltpu.VMEM((3, tokens // 4, 2 * LANES), low),
            pltpu.VMEM((tokens, 2 * LANES), low),
            DMA((2, 2)), DMA((2, 2, 2)), DMA((2,)), DMA((3,)), DMA((3,)), DMA((3,)), DMA((3,)), DMA((3,)), DMA((3,)), DMA((3,)), DMA((4,)),
        ],
        cost_estimate=pl.CostEstimate(flops=20_000_000_000, bytes_accessed=80_000_000, transcendentals=1_000_000),
        compiler_params=pltpu.CompilerParams(collective_id=4, has_side_effects=True, vmem_limit_bytes=60 * 1024 * 1024),
        name="front",
    )(hidden, gain, conv_w, conv_b, docs, modes, x_wide, out_grad, view, out_proj)


def products_kernel(gated, cotan, normed, gate, modes, split, weights,
                    out0, out1, gate0, gate1, partial, normed_t,
                    left_buf, right_buf, mode_buf, split_buf, w_buf, turned, mask_buf, stage, stage_wide,
                    load_sems, w_sems, stage_sems, wide_sems, turned_sem):
    pair_tokens, channels = left_buf.shape[1:]
    tokens, deep = split_buf.shape
    low = jnp.bfloat16
    block = 128
    loads = [pltpu.make_async_copy(source, target, load_sems.at[i]) for i, (source, target) in enumerate((
        (gated, left_buf.at[0]), (cotan, right_buf.at[0]), (modes, mode_buf), (normed, left_buf.at[1]), (gate, right_buf.at[1]),
        (split, split_buf)))]
    for copy in loads:
        copy.start()
    half = w_buf.shape[0] // 2
    w_loads = [pltpu.make_async_copy(weights.at[m], w_buf.at[pl.ds(m * half, half)], w_sems.at[m]) for m in range(2)]
    for copy in w_loads:
        copy.start()
    tall = stage.shape[1]
    turns = channels // tall
    flights = [None, None]

    def turn_left(which):
        def body(i, nothing):
            at = pl.ds(pl.multiple_of(i * block, block), block)
            turned[at, :] = left_buf[which, :, at].T
            return nothing
        lax.fori_loop(0, channels // block, body, 0)

    def multiply(which, targets):
        for m in range(2):
            def mask_rows(i, nothing):
                at = pl.ds(pl.multiple_of(i * block, block), block)
                mask_buf[at, :] = right_buf[which, at, :] * widened(mode_buf[m, at, :], channels)
                return nothing
            lax.fori_loop(0, pair_tokens // block, mask_rows, 0)
            for j in range(turns):
                slot = (m * turns + j) % 2
                if flights[slot] is not None:
                    flights[slot].wait()
                stage[slot] = dot_f32(turned[pl.ds(j * tall, tall), :], mask_buf[...]).astype(low)
                flights[slot] = pltpu.make_async_copy(stage.at[slot], targets[m].at[pl.ds(j * tall, tall)], stage_sems.at[slot])
                flights[slot].start()

    for copy in loads[:3]:
        copy.wait()
    turn_left(0)
    multiply(0, (out0, out1))
    for copy in loads[3:5]:
        copy.wait()
    turn_left(1)
    out_turned = pltpu.make_async_copy(turned, normed_t, turned_sem)
    out_turned.start()
    multiply(1, (gate0, gate1))
    loads[5].wait()
    for copy in w_loads:
        copy.wait()
    part = stage_wide.shape[1]
    wide_flights = [None, None]
    for j in range(tokens // part):
        slot = j % 2
        if wide_flights[slot] is not None:
            wide_flights[slot].wait()
        stage_wide[slot] = dot_f32(split_buf[pl.ds(j * part, part), :], w_buf[...]).astype(low)
        wide_flights[slot] = pltpu.make_async_copy(stage_wide.at[slot], partial.at[pl.ds(j * part, part)], wide_sems.at[slot])
        wide_flights[slot].start()
    for copy in flights + wide_flights + [out_turned]:
        copy.wait()


def make_products(gated, cotan, normed, gate, modes, split, weights):
    pair_tokens, channels = gated.shape
    tokens, deep = split.shape
    width = weights.shape[2]
    low = jnp.bfloat16
    anywhere = pl.BlockSpec(memory_space=pl.ANY)
    square = jax.ShapeDtypeStruct((channels, channels), low)
    return pl.pallas_call(
        products_kernel,
        in_specs=[anywhere] * 7,
        out_specs=[anywhere] * 6,
        out_shape=[square] * 4 + [jax.ShapeDtypeStruct((tokens, width), low), jax.ShapeDtypeStruct((channels, pair_tokens), low)],
        scratch_shapes=[
            pltpu.VMEM((2, pair_tokens, channels), low), pltpu.VMEM((2, pair_tokens, channels), low),
            pltpu.VMEM((2, pair_tokens, LANES), low), pltpu.VMEM((tokens, deep), low), pltpu.VMEM((deep, width), low),
            pltpu.VMEM((channels, pair_tokens), low), pltpu.VMEM((pair_tokens, channels), low),
            pltpu.VMEM((2, channels // 2, channels), low), pltpu.VMEM((2, tokens // 3, width), low),
            DMA((6,)), DMA((2,)), DMA((2,)), DMA((2,)), DMA,
        ],
        cost_estimate=pl.CostEstimate(flops=20_000_000_000, bytes_accessed=45_000_000, transcendentals=0),
        compiler_params=pltpu.CompilerParams(vmem_limit_bytes=60 * 1024 * 1024),
        name="products",
    )(gated, cotan, normed, gate, modes, split, weights)


def final_kernel(side, depth, where_ref, out_shared, out_own, gate_shared, gate_own, inner_shared, inner_own,
                 hidden, out_grad, inverse, gain, summed_rows, summed_out, normed_sum,
                 out_ref, in_ref, output, input_grad, x_grad, dt_grad, *rest):
    row_grads, (narrow, wide, row_in, row_out, in_sems, out_sems, row_in_sems, row_out_sems) = rest[:-8], rest[-8:]
    x, y, core = where_ref[0], where_ref[1], where_ref[2]
    low, f32 = jnp.bfloat16, jnp.float32
    block = row_in.shape[2]
    jobs = []
    for which, (shared, own) in enumerate(((out_shared, out_own), (gate_shared, gate_own), (inner_shared, inner_own))):
        for mode in range(2):
            for owner in range(2):
                c = core if owner == 0 else 1 - core
                for k in range(4):
                    qx = x if k in (0, 1) else 1 - x
                    qy = y if k in (0, 2) else 1 - y
                    row = (qx * 2 + qy if mode == 0 else qy * 2 + qx) * side
                    if which == 0:
                        target = out_ref.at[mode, pl.ds(pl.multiple_of(row, side), side),
                                            pl.ds(pl.multiple_of(c * depth, depth), depth)]
                    else:
                        target = in_ref.at[mode, pl.ds(pl.multiple_of(c * 4 * side + row, side), side), 2 - which, :]
                    source = own.at[mode] if owner == 0 and k == 0 else shared.at[mode, owner, k]
                    jobs.append((source, target))
    slots = narrow.shape[0]
    loads = [pltpu.make_async_copy(jobs[i][0], narrow.at[i % slots], in_sems.at[i % slots]) for i in range(len(jobs))]
    stores = [pltpu.make_async_copy(wide.at[i % slots], jobs[i][1], out_sems.at[i % slots]) for i in range(len(jobs))]
    count = hidden.shape[0] // block

    def row_loads(i):
        at = pl.ds(i * block, block)
        return [pltpu.make_async_copy(ref.at[at], row_in.at[i % 2, j], row_in_sems.at[i % 2, j])
                for j, ref in enumerate((hidden, out_grad, summed_out, normed_sum))]

    def row_stores(i):
        at = pl.ds(i * block, block)
        return [pltpu.make_async_copy(row_out.at[i % 2, j], ref.at[at], row_out_sems.at[i % 2, j])
                for j, ref in enumerate((output, input_grad))]

    for copy in row_loads(0) + row_loads(1):
        copy.start()
    for i in range(slots):
        loads[i].start()
    span, rank_dim = x_grad.shape[1], dt_grad.shape[1]
    for m in range(2):
        base = m * (span + rank_dim)
        x_grad[m] = summed_rows[base:base + span, :].astype(f32)
        dt_grad[m] = summed_rows[base + span:base + span + rank_dim, :].astype(f32)
    tail_rows = summed_rows[2 * (span + rank_dim):, :].astype(f32)
    at = 0
    for ref in row_grads:
        ref[...] = tail_rows[at:at + ref.shape[0], :]
        at += ref.shape[0]
    per = -(-len(jobs) // count)
    for i in range(count):
        for copy in row_loads(i):
            copy.wait()
        if i >= 2:
            for copy in row_stores(i - 2):
                copy.wait()
        rows = row_in[i % 2, 0].astype(f32)
        scale = inverse[pl.ds(i * block, block), 0:1]
        scaled = row_in[i % 2, 3].astype(f32) * gain[...]
        mean = jnp.mean(scaled * rows, axis=1, keepdims=True)
        row_out[i % 2, 0] = (rows + row_in[i % 2, 2].astype(f32)).astype(low)
        row_out[i % 2, 1] = (row_in[i % 2, 1].astype(f32) + scale * scaled - rows * (scale * scale * scale) * mean).astype(low)
        for copy in row_stores(i):
            copy.start()
        if i + 2 < count:
            for copy in row_loads(i + 2):
                copy.start()
        for p in range(i * per, min((i + 1) * per, len(jobs))):
            loads[p].wait()
            if p >= slots:
                stores[p - slots].wait()
            wide[p % slots] = narrow[p % slots].astype(f32)
            stores[p].start()
            if p + slots < len(jobs):
                loads[p + slots].start()
    for p in range(len(jobs) - slots, len(jobs)):
        stores[p].wait()
    for i in (count - 2, count - 1):
        for copy in row_stores(i):
            copy.wait()


def final(where, out_shared, out_own, gate_shared, gate_own, inner_shared, inner_own, hidden, out_grad, inverse, gain,
          summed_rows, rank_dim, row_counts, summed_out, normed_sum):
    side, depth = out_own.shape[1:]
    tokens, width = hidden.shape
    channels = 4 * side
    low, f32 = jnp.bfloat16, jnp.float32
    anywhere, vmem = pl.BlockSpec(memory_space=pl.ANY), pl.BlockSpec(memory_space=pltpu.VMEM)
    block, slots = 128, 6
    return pl.pallas_call(
        functools.partial(final_kernel, side, depth),
        in_specs=[pl.BlockSpec(memory_space=pltpu.SMEM)] + [anywhere] * 8 + [vmem] * 3 + [anywhere] * 2,
        out_specs=[anywhere] * 4 + [vmem] * (2 + len(row_counts)),
        out_shape=[
            jax.ShapeDtypeStruct((2, channels, width), f32), jax.ShapeDtypeStruct((2, width, 2, channels), f32),
            jax.ShapeDtypeStruct((tokens, width), low), jax.ShapeDtypeStruct((tokens, width), low),
            jax.ShapeDtypeStruct((2, (summed_rows.shape[0] - 32) // 2 - rank_dim, channels), f32),
            jax.ShapeDtypeStruct((2, rank_dim, channels), f32),
        ] + [jax.ShapeDtypeStruct((n, channels), f32) for n in row_counts],
        scratch_shapes=[
            pltpu.VMEM((slots, side, depth), low), pltpu.VMEM((slots, side, depth), f32),
            pltpu.VMEM((2, 4, block, width), low), pltpu.VMEM((2, 2, block, width), low),
            DMA((slots,)), DMA((slots,)), DMA((2, 4)), DMA((2, 2)),
        ],
        cost_estimate=pl.CostEstimate(flops=50_000_000, bytes_accessed=91_000_000, transcendentals=0),
        compiler_params=pltpu.CompilerParams(vmem_limit_bytes=60 * 1024 * 1024),
        name="final_rows",
    )(where, out_shared, out_own, gate_shared, gate_own, inner_shared, inner_own, hidden, out_grad, inverse, gain,
      summed_rows, summed_out, normed_sum)


def scan_backward_kernel(states, groups, rows, unroll, count, joined,
                         bc_ref, pre_ref, act_ref, mixed_ref, keep_ref, alog_ref, skip_ref, h_ref, start_ref, *rest):
    if joined:
        prods, part_ref, rest = rest[:4], rest[4], rest[5:]
    pgrad_ref, apart_ref, bcg_ref, sum_ref, skipsum_ref = rest[:5]
    rest = rest[5:]
    if joined:
        out_own, gate_own, z_own, rest = rest[0], rest[1], rest[2], rest[3:]
    carry_ref, rate_scr, decay_scr, sk_scr, u_scr, dy_scr, w_scr, s_scr, p_scr, q_scr = rest[:10]
    rest = rest[10:]
    chunk = pl.program_id(0)
    if joined:
        line = LineReduce(part_ref, z_own, rest[0], rest[1], rest[2:5])
        outs = Reduce(prods[:2], out_own, *rest[5:8], rest[8:13])
        gate = Reduce(prods[2:], gate_own, *rest[13:16], rest[16:21])

        @pl.when(chunk == 0)
        def _():
            line.line.load().start()
            greet()
            outs.event(0)
            line.line.load().wait()
            line.line.begin((0,))

        for at in range(1, count):
            @pl.when(chunk == at)
            def _():
                if at < line.line.pieces:
                    line.line.begin((at,))
                if at == 2:
                    outs.event(1)
                elif at == 3:
                    gate.event(0)
                elif at == 5:
                    outs.event(2)
                elif at == 6:
                    outs.last()
                elif at == 8:
                    gate.event(1)
                elif at == 10:
                    gate.event(2)
                line.turn(at)

    @pl.when(chunk == 0)
    def _():
        decay = -jnp.exp(alog_ref[...])
        decay_scr[...] = decay
        rate_scr[...] = decay * LOG2E
        carry_ref[...] = jnp.zeros_like(carry_ref)
        sum_ref[...] = jnp.zeros_like(sum_ref)
        skipsum_ref[...] = jnp.zeros_like(skipsum_ref)

    step = softplus(pre_ref[...])
    act = act_ref[...].astype(jnp.float32)
    mixed = mixed_ref[...].astype(jnp.float32)
    spread_rows(u_scr, step * act, groups)
    spread_rows(dy_scr, mixed, groups)
    spread_rows(sk_scr, jnp.where(keep_ref[...] > 0.0, step, BIG), groups)
    skipsum_ref[...] += jnp.sum(mixed * act, axis=0, keepdims=True)

    def one(t, carried, before):
        at = pl.multiple_of(t * groups, groups)
        sk = sk_scr[pl.ds(at, groups), :]
        u = u_scr[pl.ds(at, groups), :]
        dy = dy_scr[pl.ds(at, groups), :]
        w = jnp.zeros_like(u)
        s = jnp.zeros_like(u)
        new, pb, pc = [], [], []
        for n in range(states):
            g = dy * bc_ref[t, states + n] + carried[n]
            pb.append(g * u)
            pc.append(dy * h_ref[t, n])
            w = w + g * bc_ref[t, n]
            fg = jnp.exp2(sk * rate_scr[n]) * g
            lg = fg * before(n)
            s = s + lg * decay_scr[n]
            sum_ref[n] += lg * sk
            new.append(fg)
        w_scr[pl.ds(at, groups), :] = w
        s_scr[pl.ds(at, groups), :] = s
        both = pb + pc
        batch = max(1, 16 // groups)
        for j in range(0, 2 * states, batch):
            p_scr[t, pl.ds(j * groups, batch * groups), :] = jnp.concatenate(
                both[j:j + batch], axis=0).astype(jnp.bfloat16)
        return tuple(new)

    def looped(i, carried):
        t = rows - 1 - i
        return one(t, carried, lambda n: h_ref[t - 1, n])

    last = lax.fori_loop(0, rows - 1, looped, tuple(carry_ref[n] for n in range(states)), unroll=unroll)
    last = one(0, last, lambda n: start_ref[0, n])
    for n in range(states):
        carry_ref[n] = last[n]

    ones = jnp.ones((16, LANES), jnp.bfloat16)

    def reduce_one(t, nothing):
        q = lax.dot_general(ones, p_scr[t], (((1,), (1,)), ((), ())), preferred_element_type=jnp.float32)
        q_scr[pl.ds(t, 1), :] = q[0:1]
        return nothing

    lax.fori_loop(0, rows, reduce_one, 0, unroll=4)
    shape = (2 * states * groups, LANES)
    pick = (lax.broadcasted_iota(jnp.int32, shape, 0) // groups == lax.broadcasted_iota(jnp.int32, shape, 1))
    pick = pick.astype(jnp.float32).astype(jnp.bfloat16)
    q = q_scr[...]
    high = q.astype(jnp.bfloat16)
    low = (q - high.astype(jnp.float32)).astype(jnp.bfloat16)
    bcg_ref[...] = (jnp.dot(high, pick, preferred_element_type=jnp.float32)
                    + jnp.dot(low, pick, preferred_element_type=jnp.float32))
    w = gather_rows(w_scr, rows, groups)
    s = gather_rows(s_scr, rows, groups)
    pgrad_ref[...] = ((act * w + s) * jax.nn.sigmoid(pre_ref[...])).astype(pgrad_ref.dtype)
    apart_ref[...] = mixed * skip_ref[...] + step * w

    if joined:
        @pl.when(chunk == count - 1)
        def _():
            gate.last()
            outs.done()
            gate.done()
            line.done()


def scan_backward(bc, pre, act, mixed, keep, a_log3, skip, h, starts, products=None, z_part=None, rows=64, unroll=7, pieces=6):
    tokens, channels = pre.shape
    groups = channels // LANES
    states = a_log3.shape[0]
    count = tokens // rows
    joined = products is not None
    wide = pl.BlockSpec((rows, channels), lambda i: (count - 1 - i, 0))
    whole3 = pl.BlockSpec((states, groups, LANES), lambda i: (0, 0, 0))
    row = pl.BlockSpec((1, channels), lambda i: (0, 0))
    anywhere = pl.BlockSpec(memory_space=pl.ANY)
    small = lambda: pltpu.VMEM((states, groups, LANES), jnp.float32)
    long = lambda: pltpu.VMEM((rows * groups, LANES), jnp.float32)
    extra, extra_shapes, extra_scratch = [], [], []
    if joined:
        side, depth = products[0].shape[0] // 4, products[0].shape[1]
        part = z_part.reshape(2, pieces, tokens // 2 // pieces, z_part.shape[1])
        extra = list(products) + [part]
        extra_shapes = [jax.ShapeDtypeStruct((2, side, depth), jnp.bfloat16)] * 2 + [jax.ShapeDtypeStruct(part.shape, jnp.bfloat16)]
        extra_scratch = LineReduce.scratch(*part.shape[1:]) + Reduce.scratch(side, depth) + Reduce.scratch(side, depth)
    settings = dict(collective_id=2, has_side_effects=True) if joined else {}
    outs = pl.pallas_call(
        functools.partial(scan_backward_kernel, states, groups, rows, unroll, count, joined),
        grid=(count,),
        in_specs=[
            pl.BlockSpec((rows, 2 * states), lambda i: (count - 1 - i, 0), memory_space=pltpu.SMEM),
            wide, wide, wide,
            pl.BlockSpec((rows, 1), lambda i: (count - 1 - i, 0)),
            whole3, row,
            pl.BlockSpec((rows, states, groups, LANES), lambda i: (count - 1 - i, 0, 0, 0)),
            pl.BlockSpec((1, states, groups, LANES), lambda i: (count - 1 - i, 0, 0, 0)),
        ] + [anywhere] * len(extra),
        out_specs=[wide, wide, pl.BlockSpec((rows, LANES), lambda i: (count - 1 - i, 0)), whole3, row]
        + [anywhere] * len(extra_shapes),
        out_shape=[
            jax.ShapeDtypeStruct((tokens, channels), jnp.bfloat16),
            jax.ShapeDtypeStruct((tokens, channels), jnp.float32),
            jax.ShapeDtypeStruct((tokens, LANES), jnp.float32),
            jax.ShapeDtypeStruct((states, groups, LANES), jnp.float32),
            jax.ShapeDtypeStruct((1, channels), jnp.float32),
        ] + extra_shapes,
        scratch_shapes=[small(), small(), small(), long(), long(), long(), long(), long(),
                        pltpu.VMEM((rows, 2 * states * groups, LANES), jnp.bfloat16),
                        pltpu.VMEM((rows, 2 * states * groups), jnp.float32)] + extra_scratch,
        cost_estimate=pl.CostEstimate(flops=60 * tokens * channels * states,
                                      bytes_accessed=4 * tokens * channels * states,
                                      transcendentals=tokens * channels * states),
        compiler_params=pltpu.CompilerParams(vmem_limit_bytes=60 * 1024 * 1024, **settings),
        name="scan_backward",
    )(bc, pre, act, mixed, keep, a_log3, skip, h, starts, *extra)
    return outs


def lagged(values, offset):
    padding = [(offset, 0)] + [(0, 0)] * (values.ndim - 1)
    return jnp.pad(values, padding)[: values.shape[0]]


def leading(values, offset):
    padding = [(0, offset)] + [(0, 0)] * (values.ndim - 1)
    return jnp.pad(values, padding)[offset:]


def pick_dot(left_side, weights, first_mode):
    first_part = jnp.dot(left_side, weights[0], preferred_element_type=jnp.float32)
    second_part = jnp.dot(left_side, weights[1], preferred_element_type=jnp.float32)
    return jnp.where(first_mode, first_part, second_part)


def pick_back(gradient, weights, first_mode):
    dims = (((1,), (1,)), ((), ()))
    first_part = lax.dot_general(gradient, weights[0], dims, preferred_element_type=jnp.float32)
    second_part = lax.dot_general(gradient, weights[1], dims, preferred_element_type=jnp.float32)
    return jnp.where(first_mode, first_part, second_part)


def weight_grads(left_side, gradient, first_mode):
    nothing = jnp.zeros_like(gradient)
    dims = (((0,), (0,)), ((), ()))
    first_part = lax.dot_general(
        left_side,
        jnp.where(first_mode, gradient, nothing),
        dims,
        preferred_element_type=jnp.float32,
    )
    second_part = lax.dot_general(
        left_side,
        jnp.where(first_mode, nothing, gradient),
        dims,
        preferred_element_type=jnp.float32,
    )
    return jnp.stack([first_part, second_part])


def finish_rows(normed_grad, hidden, inverse, cotan, norm_gain):
    scaled = normed_grad * norm_gain
    gain_terms = jnp.sum(normed_grad * hidden * inverse, axis=0)
    cubed = inverse * inverse * inverse
    rows = (
        cotan + inverse * scaled - hidden * cubed * jnp.mean(scaled * hidden, axis=1, keepdims=True)
    )
    return (rows.astype(jnp.bfloat16), gain_terms)


def swap(values, distance):
    return lax.ppermute(values, "dp", [(i, i ^ distance) for i in range(8)])


CORE = 1


def tie(values, *others):
    return lax.optimization_barrier((values,) + others)[0]


def z_sum(values, size, dtype=jnp.bfloat16):
    distance = 1
    while distance < size:
        low = values.astype(dtype)
        got = lax.ppermute(low, "tensor", [(i, i ^ distance) for i in range(size)])
        values = low.astype(jnp.float32) + got.astype(jnp.float32)
        distance *= 2
    return values


def shards(names, hidden_in, segment_ids, modality, norm_gain, in_proj, conv_weight, conv_bias, x_proj, dt_proj, dt_bias,
           a_log, skip_gain, out_proj, out_grad):
    tokens, model_width = hidden_in.shape
    conv_taps, channels = conv_weight.shape
    rank_dim = dt_proj.shape[1]
    state_dim = a_log.shape[0]
    groups = channels // LANES
    ways = names["tensor"]
    by_hand = names["dp"] == 8 and names["tensor"] == 4
    low = jnp.bfloat16
    rank = lax.axis_index("dp")
    core, x_at, y_at = rank % 2, (rank // 2) % 2, rank // 4
    where = jnp.stack([x_at, y_at, core]).astype(jnp.int32)
    first_mode = (modality == 0)[:, None]
    nothing = jnp.zeros((), low)
    dims = (((0,), (0,)), ((), ()))

    def masked_products(left, right, modes, mask_left):
        products = []
        for chosen in (modes, jnp.logical_not(modes)):
            one = jnp.where(chosen, left, nothing) if mask_left else left
            two = right if mask_left else jnp.where(chosen, right, nothing)
            products.append(lax.dot_general(one, two, dims, preferred_element_type=jnp.float32).astype(low))
        return jnp.stack(products)

    same_doc = [jnp.ones((tokens, 1), jnp.float32)]
    for offset in range(1, conv_taps):
        earlier_seg = jnp.pad(segment_ids, (offset, 0), constant_values=-1)[:tokens]
        same_doc.append((earlier_seg == segment_ids).astype(jnp.float32)[:, None])
    if by_hand:
        modes_own = jnp.broadcast_to(jnp.stack([first_mode, jnp.logical_not(first_mode)]), (2, tokens, LANES)).astype(low)
        x_wide = jnp.pad(jnp.swapaxes(x_proj, 1, 2), ((0, 0), (0, 96), (0, 0)))
        facts = jnp.concatenate([first_mode.astype(jnp.float32)] + same_doc[1:], axis=1)
        (in_inner, in_gate, normed_pair, cotan_pair, modes, inverse, conv_sum, inner_x, activated_b, gate_z, gated_grad, rank_b, coeffs) = front(
            hidden_in, norm_gain[None], conv_weight, conv_bias[None], facts, modes_own, x_wide, out_grad, in_proj, out_proj,
            2 * state_dim)
        coeffs = coeffs[:, :2 * state_dim]
    else:
        hidden = hidden_in.astype(jnp.float32)
        inverse = lax.rsqrt(jnp.mean(hidden * hidden, axis=1, keepdims=True) + EPS)
        normed_b = (hidden * inverse * norm_gain).astype(low)
        in_inner = in_proj[:, :, 0, :]
        in_gate = in_proj[:, :, 1, :]
        inner_x = pick_dot(normed_b, in_inner, first_mode)
        conv_sum = conv_bias + conv_weight[conv_taps - 1] * inner_x
        for offset in range(1, conv_taps):
            conv_sum = conv_sum + conv_weight[conv_taps - 1 - offset] * lagged(inner_x, offset) * same_doc[offset]
        activated_b = jax.nn.silu(conv_sum).astype(low)
        projected = z_sum(pick_dot(activated_b, x_proj, first_mode), ways)
        rank_b = projected[:, :rank_dim].astype(low)
        coeffs = projected[:, rank_dim:]
        gate_z = pick_dot(normed_b, in_gate, first_mode)
        gated_grad = pick_back(out_grad, out_proj, first_mode)
    step_pre, dt = rank_b, (dt_proj, dt_bias)
    if not by_hand:
        step_pre = pick_dot(rank_b, dt_proj, first_mode) + jnp.where(first_mode, dt_bias[0], dt_bias[1])
        dt = ()
    keep = same_doc[1]
    a_log3 = a_log.reshape(state_dim, groups, LANES)
    skip_row = skip_gain[None]
    forward = scan_forward(coeffs, step_pre, activated_b, gate_z, gated_grad, keep, a_log3, skip_row,
                           first_mode.astype(jnp.float32), by_hand, dt)
    gated_b, gate_grad_b, mixed_grad, states, starts = forward[:5]
    if by_hand:
        step_pre = forward[5]
        made = make_products(gated_b, cotan_pair, normed_pair, gate_grad_b, modes, forward[6], out_proj)
        products, partial_out, normed_t = made[:4], made[4], made[5]
        back = scan_backward(coeffs, step_pre, activated_b, mixed_grad, keep, a_log3, skip_row, states, starts,
                             products, partial_out)
        out_own, gate_own, z_own = back[5:]
    else:
        partial_out = pick_dot(gated_b, out_proj, first_mode).astype(low)
        back = scan_backward(coeffs, step_pre, activated_b, mixed_grad, keep, a_log3, skip_row, states, starts)
        summed_out = lax.psum(partial_out, "tensor")
        out_proj_grad = lax.psum(weight_grads(gated_b, out_grad, first_mode).astype(low), "dp").astype(jnp.float32)
        gate_proj_grad = lax.psum(weight_grads(normed_b, gate_grad_b, first_mode).astype(low), "dp")
    pre_grad_b, act_part, coeff_grad, sums, skips = back[:5]
    a_log_grad = sums.reshape(state_dim, channels) * -jnp.exp(a_log)
    mode_rows = x_proj.shape[2] + rank_dim
    if by_hand:
        later = jnp.stack([same_doc[0]] + [leading(same_doc[k], k) for k in range(1, conv_taps)], axis=1)[:, :, 0]
        row_facts = jnp.concatenate([inverse[:, :1], first_mode.astype(jnp.float32)], axis=1)
        rows, normed_low, inner_product, out_shared, gate_shared, z_res = middle(
            pre_grad_b, act_part, coeff_grad, conv_sum, inner_x, activated_b, rank_b, dt_proj, x_wide, conv_weight, later, modes,
            gate_grad_b, normed_t, row_facts, jnp.concatenate([a_log_grad, skips], axis=0),
            hidden_in, in_gate, in_inner, out_own, gate_own, z_own)
        summed_out = z_res.reshape(tokens, model_width)
    else:
        pre_grad = pre_grad_b.astype(jnp.float32)
        dt_bias_grad = jnp.stack([
            jnp.sum(jnp.where(first_mode, pre_grad, 0.0), axis=0),
            jnp.sum(jnp.where(first_mode, 0.0, pre_grad), axis=0)])
        rank_part = pick_back(pre_grad_b, dt_proj, first_mode)
        proj_grad_b = z_sum(jnp.concatenate([rank_part, coeff_grad[:, :2 * state_dim]], axis=1), ways).astype(low)
        act_grad = act_part + pick_back(proj_grad_b, x_proj, first_mode)
        sig_conv = jax.nn.sigmoid(conv_sum)
        conv_grad = act_grad * sig_conv * (1.0 + conv_sum * (1.0 - sig_conv))
        conv_bias_grad = jnp.sum(conv_grad, axis=0)
        weight_rows = []
        x_grad = jnp.zeros_like(inner_x)
        for tap_index in range(conv_taps):
            offset = conv_taps - 1 - tap_index
            masked = conv_grad * same_doc[offset]
            weight_rows.append(jnp.sum(masked * lagged(inner_x, offset), axis=0))
            x_grad = x_grad + conv_weight[tap_index] * leading(masked, offset)
        x_grad_b = x_grad.astype(low)
        normed_part = pick_back(x_grad_b, in_inner, first_mode) + pick_back(gate_grad_b, in_gate, first_mode)
        gain_part = jnp.sum(normed_part * (hidden * inverse), axis=0).reshape(-1, channels)
        gain_part = lax.psum(gain_part, "tensor")
        small_modes = jnp.concatenate([
            weight_grads(proj_grad_b, activated_b, first_mode), weight_grads(rank_b, pre_grad_b, first_mode)], axis=1)
        rows = jnp.concatenate([small_modes.reshape(-1, channels), jnp.stack(weight_rows), conv_bias_grad[None], dt_bias_grad,
                                a_log_grad, skips, gain_part], axis=0).astype(low)
    summed_rows = lax.psum(rows, "dp")
    if by_hand:
        (inner_shared,), (inner_own,), normed_sum = tail_exchange([inner_product], normed_low)

        (out_proj_grad, in_proj_grad, output, input_grad, x_rows, dt_proj_grad, conv_weight_grad, conv_row, dt_bias_grad,
         a_log_grad, skip_row, gain_rows) = final(
            where, out_shared, out_own, gate_shared, gate_own, inner_shared, inner_own,
            hidden_in, out_grad, inverse, norm_gain[None], summed_rows, rank_dim, (conv_taps, 1, 2, state_dim, 1, model_width // channels),
            summed_out, normed_sum)
        x_proj_grad = jnp.swapaxes(x_rows, 1, 2)
        conv_bias_grad, skip_grad, norm_gain_grad = conv_row[0], skip_row[0], gain_rows.reshape(-1)
    else:
        inner_proj_grad = lax.psum(weight_grads(normed_b, x_grad_b, first_mode).astype(low), "dp")
        in_proj_grad = jnp.stack([inner_proj_grad, gate_proj_grad], axis=2).astype(jnp.float32)
        normed_sum = lax.psum(normed_part.astype(low), "tensor")
        output = (hidden + summed_out.astype(jnp.float32)).astype(low)
        cotan = out_grad.astype(jnp.float32)
        input_grad, _ = finish_rows(normed_sum.astype(jnp.float32), hidden, inverse, cotan, norm_gain)
        summed_rows = summed_rows.astype(jnp.float32)
        small_modes, rows = summed_rows[:2 * mode_rows].reshape(2, mode_rows, channels), summed_rows[2 * mode_rows:]
        x_proj_grad = jnp.swapaxes(small_modes[:, :-rank_dim], 1, 2)
        dt_proj_grad = small_modes[:, -rank_dim:]
        norm_gain_grad = rows[conv_taps + 4 + state_dim:].reshape(-1)[:model_width]
        at = conv_taps + 1
        conv_weight_grad, conv_bias_grad, dt_bias_grad = rows[:conv_taps], rows[conv_taps], rows[at:at + 2]
        a_log_grad, skip_grad = rows[at + 2:at + 2 + state_dim], rows[at + 2 + state_dim]
    return (output, input_grad, norm_gain_grad, in_proj_grad, conv_weight_grad, conv_bias_grad, x_proj_grad,
            dt_proj_grad, dt_bias_grad, a_log_grad, skip_grad, out_proj_grad)


def solution(mesh):
    in_specs = (
        P("dp", None),
        P("dp"),
        P("dp"),
        P(),
        P(None, None, None, "tensor"),
        P(None, "tensor"),
        P("tensor"),
        P(None, "tensor", None),
        P(None, None, "tensor"),
        P(None, "tensor"),
        P(None, "tensor"),
        P("tensor"),
        P(None, "tensor", None),
        P("dp", None),
    )
    out_specs = (
        P("dp", None),
        P("dp", None),
        P(),
        P(None, None, None, "tensor"),
        P(None, "tensor"),
        P("tensor"),
        P(None, "tensor", None),
        P(None, None, "tensor"),
        P(None, "tensor"),
        P(None, "tensor"),
        P("tensor"),
        P(None, "tensor", None),
    )
    names = dict(mesh.shape)
    return jax.shard_map(functools.partial(shards, names), mesh=mesh, in_specs=in_specs, out_specs=out_specs, check_vma=False)
```
